32 devices in a mesh: azim: 8 (over y, x, core), axial: 4 (over z).
Axes of the slice: x: 2, y: 2, z: 4, core: 2. Of those that a mesh axis runs over, the one named last changes fastest.
Arguments:
- fraction: float32 [2048, 64, 512], P('azim', 'axial'), may hold values from 0 to 1
- normals: bfloat16 [3, 2048, 64, 512], P(None, 'azim', 'axial'), may hold values from -0.63 to 0.63, as said below
- planes: bfloat16 [2048, 64, 512], P('azim', 'axial'), may hold values from 0 to 1
- cell_flags: int32 [2048, 64, 512], P('azim', 'axial'), may hold values from 0 to 2
- courant: bfloat16 [3, 2048, 64, 512], P(None, 'azim', 'axial'), may hold values from -0.29882812 to 0.29882812
- radial_basis: float32 [512, 512], replicated, may hold values from -0.25 to 0.25
- axial_basis: float32 [64, 64], replicated, may hold values from -0.75 to 0.75
- radial_rates: float32 [512], replicated, may hold values from 0.5 to 4
- axial_rates: float32 [64], replicated, may hold values from 0.2 to 2
Outputs:
- fraction_new: float32 [2048, 64, 512], P('azim', 'axial')
- pressure: float32 [2048, 64, 512], P('azim', 'axial')
The draws below stay inside these ranges and needn't reach their ends.
Inputs may be any that keep to these rules, and one draw needn't show every extreme that they name: `normals`: every component's magnitude is 0.12 or more, and a cell's three magnitudes sum to 1 within bfloat16 rounding.
All inputs are finite; a program needn't handle non-finite values.
Results may differ from the reference program's by a relative error of at most 0.0003.
Values may be sent and summed in bfloat16 or wider, within the bound.
A program may use at most 256 MiB of HBM per device.

```python
import math
import jax
import jax.numpy as jnp
from jax import lax

R = 512
A = 2048
Z = 64


def draw_normals(key, part):
    first_key, second_key = jax.random.split(key)
    uniforms = jax.random.uniform(first_key, (3, A, Z, R), jnp.float32)
    magnitudes = 0.4 + 0.6 * uniforms
    signs = jnp.where(jax.random.bernoulli(second_key, 0.5, (3, A, Z, R)), 1.0, -1.0)
    totals = magnitudes[0] + magnitudes[1] + magnitudes[2]
    return (signs * magnitudes / totals[None]).astype(jnp.bfloat16)


def plant(values, stream_key, least, top_value):
    longest = values.shape.index(max(values.shape))
    spots = []
    for shift in (0, 1):
        where = [jax.random.randint(jax.random.fold_in(stream_key, axis), (), 0, length) for axis, length in enumerate(values.shape)]
        where[longest] = (where[longest] + shift) % values.shape[longest]
        spots.append(tuple(where))
    return values.at[spots[0]].set(least).at[spots[1]].set(top_value)


def block_scale(key, shape, shards, low, largest):
    loudness = 1.0
    for dim, shards_of in shards:
        heights = jax.random.uniform(jax.random.fold_in(jax.random.fold_in(key, 6), dim), (shards_of,), jnp.float32, low / len(shards), largest / len(shards))
        loudness = loudness * jnp.repeat(jnp.exp(heights), shape[dim] // shards_of).reshape((-1,) + (1,) * (len(shape) - 1 - dim))
    return loudness


def normal_values(own_key, dims, spread, most, held_as=jnp.bfloat16):
    values = jax.random.normal(own_key, dims, jnp.float32) * spread
    return jnp.minimum(jnp.maximum(values, -most), most).astype(held_as)


def setup_inputs(seed: int = 0) -> dict:
    arg_keys = jax.random.split(jax.random.key(seed), 10)
    fraction = jnp.clip(1.0 * jax.random.uniform(arg_keys[0], (A, Z, R), jnp.float32) ** block_scale(arg_keys[0], (A, Z, R), ((0, 8), (1, 4)), -0.2, 0.2), 0.0, 1.0)
    normals = draw_normals(jax.random.fold_in(arg_keys[9], 71), 0)
    planes = jnp.clip(1.0 * jax.random.uniform(arg_keys[2], (A, Z, R), jnp.float32) ** block_scale(arg_keys[2], (A, Z, R), ((0, 8), (1, 4)), -0.2, 0.2), 0.0, 1.0).astype(jnp.bfloat16)
    cell_flags = plant(jax.random.randint(arg_keys[3], (A, Z, R), 0, 3), jax.random.fold_in(arg_keys[3], 1), 0, 2).astype(jnp.int32)
    courant = jnp.clip(jax.random.uniform(arg_keys[4], (3, A, Z, R), jnp.float32, -0.29882812, 0.29882812) * block_scale(arg_keys[4], (3, A, Z, R), ((1, 8), (2, 4)), -0.4, 0.0), -0.29882812, 0.29882812).astype(jnp.bfloat16)
    radial_basis = normal_values(arg_keys[5], (R, R), R ** -0.5, 0.25, jnp.float32)
    axial_basis = normal_values(arg_keys[6], (Z, Z), Z ** -0.5, 0.75, jnp.float32)
    radial_rates = jnp.clip(jnp.exp(jax.random.uniform(arg_keys[7], (R,), jnp.float32, math.log(0.5), math.log(4.0))), 0.5, 4.0)
    axial_rates = jnp.clip(jnp.exp(jax.random.uniform(arg_keys[8], (Z,), jnp.float32, math.log(0.2), math.log(2.0))), 0.2, 2.0)
    return dict(fraction=fraction, normals=normals, planes=planes, cell_flags=cell_flags, courant=courant, radial_basis=radial_basis, axial_basis=axial_basis, radial_rates=radial_rates, axial_rates=axial_rates)


HIGHEST = lax.Precision.HIGHEST
BUOYANCY = 0.5


def cut_volume(magnitudes, alpha_value, direction, lower_end, thickness):
    offset = alpha_value - magnitudes[direction] * lower_end
    summed = jnp.zeros_like(offset)
    for corner in range(8):
        height = offset
        parity = 1.0
        for coord_axis in range(3):
            if (corner >> coord_axis) & 1:
                parity = -parity
                if coord_axis == direction:
                    height = height - magnitudes[coord_axis] * thickness
                else:
                    height = height - magnitudes[coord_axis]
        summed = summed + parity * jnp.maximum(height, 0.0) ** 3
    return summed / (6.0 * magnitudes[0] * magnitudes[1] * magnitudes[2])


def slab_volume(cell, direction, upper_side, thickness):
    normal, alpha_value, flag_value = cell
    components = [normal[component].astype(jnp.float32) for component in range(3)]
    magnitudes = [jnp.abs(component_value) for component_value in components]
    negative = components[direction] < 0.0
    if upper_side:
        lower_end = jnp.where(negative, 0.0, 1.0 - thickness)
    else:
        lower_end = jnp.where(negative, 1.0 - thickness, 0.0)
    mixed = cut_volume(magnitudes, alpha_value.astype(jnp.float32), direction, lower_end, thickness)
    return jnp.where(flag_value == 1, thickness, jnp.where(flag_value == 2, mixed, 0.0))


def donor_flux(lower_cell, upper_cell, face_speed, direction, lower_weight, upper_weight):
    forward = jnp.maximum(face_speed, 0.0)
    backward = jnp.maximum(-face_speed, 0.0)
    from_lower = slab_volume(lower_cell, direction, True, forward) * lower_weight
    from_upper = slab_volume(upper_cell, direction, False, backward) * upper_weight
    return jnp.where(face_speed > 0.0, from_lower, jnp.where(face_speed < 0.0, -from_upper, 0.0))


def roll_next(field, direction):
    return jnp.roll(field, -1, axis=direction + field.ndim - 3)


def reference(fraction, normals, planes, cell_flags, courant, radial_basis, axial_basis, radial_rates, axial_rates):
    velocity = courant.astype(jnp.float32)
    radius = 1.0 + (jnp.arange(R, dtype=jnp.float32) + 0.5) / R
    face_radius = 1.0 + (jnp.arange(R - 1, dtype=jnp.float32) + 1.0) / R
    cell = (normals, planes, cell_flags)
    updated = fraction
    divergence = jnp.zeros_like(fraction)
    for direction in range(2):
        upper_cell = (roll_next(normals, direction), roll_next(planes, direction), roll_next(cell_flags, direction))
        face_speed = 0.5 * (velocity[direction] + roll_next(velocity[direction], direction))
        face_flux = donor_flux(cell, upper_cell, face_speed, direction, 1.0, 1.0)
        updated = updated - (face_flux - jnp.roll(face_flux, 1, axis=direction))
        divergence = divergence + (face_speed - jnp.roll(face_speed, 1, axis=direction))
    lower_cell = (normals[..., :-1], planes[..., :-1], cell_flags[..., :-1])
    upper_cell = (normals[..., 1:], planes[..., 1:], cell_flags[..., 1:])
    face_speed = 0.5 * (velocity[2][..., :-1] + velocity[2][..., 1:])
    face_flux = donor_flux(lower_cell, upper_cell, face_speed, 2, radius[:-1], radius[1:])
    zeros_col = jnp.zeros_like(fraction[..., :1])
    upper_flux = jnp.concatenate([face_flux, zeros_col], axis=-1)
    lower_flux = jnp.concatenate([zeros_col, face_flux], axis=-1)
    updated = updated - (upper_flux - lower_flux) / radius
    face_moved = face_radius * face_speed
    divergence = divergence + (jnp.concatenate([face_moved, zeros_col], axis=-1) - jnp.concatenate([zeros_col, face_moved], axis=-1)) / radius
    source = divergence + BUOYANCY * updated
    radial_modes = jnp.einsum('azr,rj->azj', source, radial_basis, precision=HIGHEST)
    both_modes = jnp.einsum('azj,zn->anj', radial_modes, axial_basis, precision=HIGHEST)
    spectrum = jnp.fft.rfft(both_modes, axis=0)
    half_count = A // 2
    coefficients = jnp.concatenate([spectrum.real, -spectrum.imag[1:half_count]], axis=0)
    mode_index = jnp.arange(A)
    wavenumber = jnp.where(mode_index <= half_count, mode_index, mode_index - half_count).astype(jnp.float32)
    azim_rates = 2.0 - 2.0 * jnp.cos(2.0 * jnp.pi * wavenumber / A)
    denominator = azim_rates[:, None, None] + axial_rates[None, :, None] + radial_rates[None, None, :]
    solved = coefficients / denominator
    cosines = solved[: half_count + 1]
    sines = jnp.concatenate([jnp.zeros_like(solved[:1]), solved[half_count + 1:], jnp.zeros_like(solved[:1])], axis=0)
    physical = jnp.fft.irfft(cosines - 1j * sines, n=A, axis=0)
    physical = jnp.einsum('anj,zn->azj', physical, axial_basis, precision=HIGHEST)
    pressure = jnp.einsum('azj,rj->azr', physical, radial_basis, precision=HIGHEST)
    return updated, pressure
```

```python
import functools

import jax
import jax.numpy as jnp
import numpy as np
from jax import lax
from jax.experimental import pallas as pl
from jax.experimental.pallas import tpu as pltpu
from jax.sharding import PartitionSpec as P

HIGH = lax.Precision.HIGH
BUOYANCY = 0.5
CODE_TOP = 32700.0


def shifted_in(edge, axis, towards_lower):
    count = lax.axis_size(axis)
    if towards_lower:
        pairs = [((i + 1) % count, i) for i in range(count)]
    else:
        pairs = [(i, (i + 1) % count) for i in range(count)]
    return lax.ppermute(edge, axis, pairs)


def cell_parts(n0, n1, n2, code):
    m0, m1, m2 = jnp.abs(n0), jnp.abs(n1), jnp.abs(n2)
    return (n0, n1, n2, code, 1.0 / (6.0 * m0 * m1 * m2))


def cube(height):
    held = jnp.maximum(height, 0.0)
    return held * held * held


def face_flux(direction, lower, upper, speed, lower_weight=None, upper_weight=None):
    forward = speed > 0.0
    signed = jnp.where(forward, lower[direction], -upper[direction])
    first, second = [d for d in range(3) if d != direction]
    along = jnp.abs(signed)
    side_a = jnp.abs(jnp.where(forward, lower[first], upper[first]))
    side_b = jnp.abs(jnp.where(forward, lower[second], upper[second]))
    code = jnp.where(forward, lower[3], upper[3])
    inverse = jnp.where(forward, lower[4], upper[4])
    width = jnp.abs(speed)
    near = code - along * jnp.where(signed < 0.0, 0.0, 1.0 - width)
    far = near - along * width
    sides = side_a + side_b
    total = (cube(near) - cube(near - side_a)) - (cube(near - side_b) - cube(near - sides))
    total = total - ((cube(far) - cube(far - side_a)) - (cube(far - side_b) - cube(far - sides)))
    volume = jnp.where(code > 3.0, width, jnp.where(code < -0.5, 0.0, total * inverse))
    if lower_weight is not None:
        volume = volume * jnp.where(forward, lower_weight, upper_weight)
    return jnp.where(forward, volume, jnp.where(speed < 0.0, -volume, 0.0))


def advect_kernel(
    fraction_ref,
    normals_ref,
    planes_ref,
    flags_ref,
    courant_ref,
    next_ref,
    high_ref,
    low_azim_ref,
    low_axial_ref,
    updated_ref,
    source_ref,
    kept,
):
    rows, layers, cells = fraction_ref.shape
    f32 = jnp.float32

    @pl.when(pl.program_id(0) == 0)
    def _():
        kept[...] = low_azim_ref[...]

    index = lax.broadcasted_iota(jnp.int32, (1, cells), 1)
    place = index.astype(f32)
    radius = 1.0 + (place + 0.5) / cells
    next_radius = 1.0 + (place + 1.5) / cells
    face_radius = 1.0 + (place + 1.0) / cells
    inverse_radius = 1.0 / radius
    inner = lax.broadcasted_iota(jnp.int32, (layers, cells), 1) < cells - 1
    layer = lax.broadcasted_iota(jnp.int32, (layers, cells), 0)
    last_layer = layer == layers - 1
    first_layer = layer == 0

    def row_parts(row):
        flags = flags_ref[row]
        code = jnp.where(
            flags == 2, planes_ref[row].astype(f32), jnp.where(flags == 1, 4.0, -1.0)
        )
        return cell_parts(
            normals_ref[0, row].astype(f32),
            normals_ref[1, row].astype(f32),
            normals_ref[2, row].astype(f32),
            code,
        )

    def one_row(row, upper, upper_speed):
        own = row_parts(row)
        moved = [courant_ref[d, row].astype(f32) for d in range(3)]
        speed = 0.5 * (moved[0] + upper_speed)
        flux = face_flux(0, own, upper, speed)
        gained = flux - kept[0]
        divergence = speed - kept[1]
        kept[0] = flux
        kept[1] = speed
        beyond = cell_parts(*[high_ref[k, row] for k in range(4)])
        above = [
            jnp.where(last_layer, high, pltpu.roll(field, layers - 1, 0))
            for field, high in zip(own, beyond)
        ]
        speed = 0.5 * (
            moved[1]
            + jnp.where(last_layer, high_ref[4, row], pltpu.roll(moved[1], layers - 1, 0))
        )
        flux = face_flux(1, own, above, speed)
        gained = gained + (
            flux - jnp.where(first_layer, low_axial_ref[0, row], pltpu.roll(flux, 1, 0))
        )
        divergence = divergence + (
            speed - jnp.where(first_layer, low_axial_ref[1, row], pltpu.roll(speed, 1, 0))
        )
        outer = [pltpu.roll(field, cells - 1, 1) for field in own]
        speed = 0.5 * (moved[2] + pltpu.roll(moved[2], cells - 1, 1))
        speed = jnp.where(inner, speed, 0.0)
        flux = face_flux(2, own, outer, speed, radius, next_radius)
        gained = gained + (flux - pltpu.roll(flux, 1, 1)) * inverse_radius
        carried = face_radius * speed
        divergence = divergence + (carried - pltpu.roll(carried, 1, 1)) * inverse_radius
        updated = fraction_ref[row] - gained
        updated_ref[row] = updated
        source_ref[row] = divergence + BUOYANCY * updated

    def step(row, _):
        one_row(row, row_parts(row + 1), courant_ref[0, row + 1].astype(f32))
        return 0

    lax.fori_loop(0, rows - 1, step, 0)
    one_row(
        rows - 1,
        cell_parts(*[next_ref[k, 0].astype(f32) for k in range(4)]),
        next_ref[4, 0].astype(f32),
    )


def plane_codes(planes, flags):
    return jnp.where(
        flags == 2, planes.astype(jnp.float32), jnp.where(flags == 1, 4.0, -1.0)
    ).astype(jnp.bfloat16)


def packed_edge(normals, planes, flags, courant, direction, pick):
    parts = [pick(normals[d]) for d in range(3)]
    parts.append(plane_codes(pick(planes), pick(flags)))
    parts.append(pick(courant[direction]))
    return jnp.stack(parts)


def low_face(direction, lower, upper):
    lower, upper = lower.astype(jnp.float32), upper.astype(jnp.float32)
    speed = 0.5 * (lower[4] + upper[4])
    flux = face_flux(direction, cell_parts(*lower[:4]), cell_parts(*upper[:4]), speed)
    return jnp.stack([flux, speed])


def advect(fraction, normals, planes, flags, courant):
    rows, layers, cells = fraction.shape
    block = 16 if rows % 16 == 0 else 1
    blocks = rows // block
    fields = (normals, planes, flags, courant)
    top_row = packed_edge(*fields, 0, lambda x: x[rows - 1])
    bottom_row = packed_edge(*fields, 0, lambda x: x[0])
    top_layer = packed_edge(*fields, 1, lambda x: x[:, layers - 1])
    bottom_layer = packed_edge(*fields, 1, lambda x: x[:, 0])
    high_row = shifted_in(bottom_row, "azim", True)
    low_row = shifted_in(top_row, "azim", False)
    high_layer = shifted_in(bottom_layer, "axial", True)
    low_layer = shifted_in(top_layer, "axial", False)
    low_azim = low_face(0, low_row, bottom_row)
    low_axial = low_face(1, low_layer, bottom_layer)[:, :, None]
    high_axial = high_layer.astype(jnp.float32)[:, :, None]
    inside = packed_edge(*fields, 0, lambda x: x[block::block])
    following = jnp.concatenate([inside, high_row[:, None]], axis=1)
    whole = pl.BlockSpec((block, layers, cells), lambda i: (i, 0, 0))
    triple = pl.BlockSpec((3, block, layers, cells), lambda i: (0, i, 0, 0))
    return pl.pallas_call(
        advect_kernel,
        grid=(blocks,),
        in_specs=[
            whole,
            triple,
            whole,
            whole,
            triple,
            pl.BlockSpec((5, 1, layers, cells), lambda i: (0, i, 0, 0)),
            pl.BlockSpec((5, block, 1, cells), lambda i: (0, i, 0, 0)),
            pl.BlockSpec((2, layers, cells), lambda i: (0, 0, 0)),
            pl.BlockSpec((2, block, 1, cells), lambda i: (0, i, 0, 0)),
        ],
        out_specs=[whole, whole],
        out_shape=[jax.ShapeDtypeStruct(fraction.shape, jnp.float32)] * 2,
        scratch_shapes=[pltpu.VMEM((2, layers, cells), jnp.float32)],
        compiler_params=pltpu.CompilerParams(vmem_limit_bytes=40 * 2**20),
    )(
        fraction,
        normals,
        planes,
        flags,
        courant,
        following,
        high_axial,
        low_azim,
        low_axial,
    )


def coded(values):
    most = jnp.max(jnp.abs(values), axis=-1)
    exponent = jnp.clip(jnp.ceil(jnp.log2(most) * 256.0) + 1.0, -30000.0, 30000.0)
    scale = CODE_TOP * jnp.exp2(exponent * (-1.0 / 256.0))
    codes = jnp.round(values * scale[..., None])
    return jnp.clip(codes, -32767.0, 32767.0).astype(jnp.int16), exponent.astype(jnp.int16)


def exchange(values):
    modes, cells = values.shape[1], values.shape[3]
    codes, exponent = coded(values)
    extra = jnp.pad(exponent.transpose(0, 2, 1), ((0, 0), (0, 0), (0, cells - modes)))
    sent = jnp.concatenate([codes, extra[:, None]], axis=1)
    got = lax.all_to_all(sent, ("azim", "axial"), split_axis=0, concat_axis=0, tiled=True)
    exponent = got[:, modes, :, :modes].transpose(0, 2, 1).astype(jnp.float32)
    scale = jnp.exp2(exponent * (1.0 / 256.0)) * (1.0 / CODE_TOP)
    return got[:, :modes].astype(jnp.float32) * scale[..., None]


@functools.lru_cache(None)
def azimuth_tables(total):
    half, quarter = total // 2, total // 4
    place = np.arange(half)

    def table(cosines, sines):
        waves = np.concatenate([cosines, sines])
        angles = 2.0 * np.pi / total * (waves[:, None] * place[None, :] % total)
        rows = np.concatenate(
            [np.cos(angles[: len(cosines)]), np.sin(angles[len(cosines) :])]
        ).astype(np.float32)
        rates = (2.0 - 2.0 * np.cos(2.0 * np.pi * waves / total)).astype(np.float32)
        ends = (waves == 0) | (waves == half)
        return rows, rates, (np.where(ends, 1.0, 2.0) / total).astype(np.float32)

    even = 2 * np.arange(quarter + 1)
    odd = 2 * np.arange(quarter) + 1
    return table(even, even[1:-1]), table(odd, odd)


def stepwise(
    fraction,
    normals,
    planes,
    cell_flags,
    courant,
    radial_basis,
    axial_basis,
    radial_rates,
    axial_rates,
):
    rows, layers, cells = fraction.shape
    around, along = lax.axis_size("azim"), lax.axis_size("axial")
    devices = around * along
    modes = cells // devices
    total = rows * around
    half = total // 2
    updated, source = advect(fraction, normals, planes, cell_flags, courant)
    radial_modes = jnp.einsum("azr,rj->jza", source, radial_basis, precision=HIGH)
    got = exchange(radial_modes.reshape(devices, modes, layers, rows))
    got = got.reshape(around, along, modes, layers, rows).transpose(2, 1, 3, 0, 4)
    got = got.reshape(modes, along * layers, total)
    both = jnp.einsum("jza,zn->jna", got, axial_basis, precision=HIGH)
    first = (lax.axis_index("azim") * along + lax.axis_index("axial")) * modes
    shifts = lax.dynamic_slice_in_dim(radial_rates, first, modes)[:, None] + axial_rates[None, :]
    low, high = both[..., :half], both[..., half:]
    solved = []
    for folded, (table, rates, weight) in zip((low + high, low - high), azimuth_tables(total)):
        coefficients = jnp.einsum("jna,ka->jnk", folded, table, precision=HIGH)
        scaled = coefficients / (rates + shifts[..., None]) * weight
        solved.append(jnp.einsum("jnk,ka->jna", scaled, table, precision=HIGH))
    physical = jnp.concatenate([solved[0] + solved[1], solved[0] - solved[1]], axis=-1)
    physical = jnp.einsum("jna,zn->jza", physical, axial_basis, precision=HIGH)
    physical = physical.reshape(modes, along, layers, around, rows).transpose(3, 1, 0, 2, 4)
    returned = exchange(physical.reshape(devices, modes, layers, rows))
    returned = returned.reshape(cells, layers, rows)
    pressure = jnp.einsum("jza,rj->azr", returned, radial_basis, precision=HIGH)
    return (updated, pressure)


CHUNK = 128
BLOCK = 16
FLUX_SCALE = 32767.0 / 0.3
F32 = jnp.float32
BF16 = jnp.bfloat16


def split(values):
    high = values.astype(BF16)
    return high, (values - high.astype(F32)).astype(BF16)


def dot(a, b, contract):
    return lax.dot_general(a, b, (contract, ((), ())), preferred_element_type=F32)


def dot3(a, b, contract=((1,), (0,))):
    return dot(a[0], b[0], contract) + (dot(a[0], b[1], contract) + dot(a[1], b[0], contract))


def donor_volume(signed, side_a, side_b, plane, inverse, width):
    along = jnp.abs(signed)
    slab = along * width
    near = plane - jnp.maximum(signed, 0.0) * (1.0 - width)
    other = (slab + (side_a + side_b)) - near
    folded = near > other
    held = jnp.maximum(jnp.minimum(near, other), 0.0)
    low, high = jnp.minimum(side_a, side_b), jnp.maximum(side_a, side_b)
    corner = low + slab
    by_low = jnp.maximum(held - low, 0.0)
    by_slab = jnp.maximum(held - slab, 0.0)
    last = jnp.maximum(held - jnp.minimum(high, corner), 0.0)
    last_cube = last * last * last
    last_cube = jnp.where(high < corner, -last_cube, last_cube)
    total = held * held * held - by_slab * by_slab * by_slab
    total = total - (by_low * by_low * by_low - last_cube)
    volume = total * inverse
    return jnp.where(folded, width - volume, volume)


def upwind_flux(direction, lower, upper, speed, lower_weight=None, upper_weight=None):
    forward = speed > 0.0
    first, second = [d for d in range(3) if d != direction]
    signed = jnp.where(forward, lower[direction], -upper[direction])
    side_a = jnp.abs(jnp.where(forward, lower[first], upper[first]))
    side_b = jnp.abs(jnp.where(forward, lower[second], upper[second]))
    plane = jnp.where(forward, lower[3], upper[3])
    inverse = jnp.where(forward, lower[4], upper[4])
    volume = donor_volume(signed, side_a, side_b, plane, inverse, jnp.abs(speed))
    if lower_weight is not None:
        volume = volume * jnp.where(forward, lower_weight, upper_weight)
    return jnp.where(forward, volume, -volume)


def inverse_of(n0, n1, n2):
    return 1.0 / (6.0 * jnp.abs(n0 * n1 * n2))


def plane_value(planes, flags):
    return jnp.where(flags == 2, planes.astype(F32), jnp.where(flags == 1, 4.0, -4.0))


def strided_rows(work, layer, rows, layers, cells):
    parts = []
    for lane in range(0, cells, 128):
        parts.append(work[lane // 128, pl.ds(layer, rows, stride=layers), :])
    return parts


def speeds_kernel(courant_ref, edge_ref, work):
    rows, layers, cells = courant_ref.shape[1:]
    for lane in range(0, cells, 128):
        work[lane // 128] = courant_ref[0, :, :, pl.ds(lane, 128)].astype(F32).reshape(rows * layers, 128)
    for side, layer in ((0, 0), (1, layers - 1)):
        for tile, got in enumerate(strided_rows(work, layer, rows, layers, cells)):
            edge_ref[side, :, pl.ds(tile * 128, 128)] = got.astype(BF16)


def edge_speeds(courant):
    _, rows, layers, cells = courant.shape
    step = 64
    return pl.pallas_call(
        speeds_kernel,
        grid=(rows // step,),
        in_specs=[pl.BlockSpec((1, step, layers, cells), lambda i: (1, i, 0, 0))],
        out_specs=pl.BlockSpec((2, step, cells), lambda i: (0, i, 0)),
        out_shape=jax.ShapeDtypeStruct((2, rows, cells), BF16),
        scratch_shapes=[pltpu.VMEM((cells // 128, step * layers, 128), F32)],
        name="edge_speeds",
    )(courant)


def fields_kernel(normals_ref, planes_ref, flags_ref, fields_ref, work):
    rows, layers, cells = planes_ref.shape
    for k in range(4):
        for lane in range(0, cells, 128):
            at = pl.ds(lane, 128)
            if k < 3:
                field = normals_ref[k, :, :, at].astype(F32)
            else:
                field = plane_value(planes_ref[:, :, at], flags_ref[:, :, at])
            work[lane // 128] = field.reshape(rows * layers, 128)
        for side, layer in ((0, 0), (1, layers - 1)):
            for tile, got in enumerate(strided_rows(work, layer, rows, layers, cells)):
                fields_ref[side, k, :, pl.ds(tile * 128, 128)] = got


def edge_fields(normals, planes, flags):
    rows, layers, cells = planes.shape
    step = 32
    whole = pl.BlockSpec((step, layers, cells), lambda i: (i, 0, 0))
    return pl.pallas_call(
        fields_kernel,
        grid=(rows // step,),
        in_specs=[
            pl.BlockSpec((3, step, layers, cells), lambda i: (0, i, 0, 0)),
            whole,
            whole,
        ],
        out_specs=pl.BlockSpec((2, 4, step, cells), lambda i: (0, 0, i, 0)),
        out_shape=jax.ShapeDtypeStruct((2, 4, rows, cells), F32),
        scratch_shapes=[pltpu.VMEM((cells // 128, step * layers, 128), F32)],
        name="edge_fields",
    )(normals, planes, flags)


def donors_kernel(fields_ref, edge_ref, below_ref, above_ref, own_ref, code_ref, speed_ref):
    for side in range(2):
        n = [fields_ref[side, k] for k in range(3)]
        beyond = (below_ref if side == 0 else above_ref)[...].astype(F32)
        speed = 0.5 * (edge_ref[side].astype(F32) + beyond)
        inverse = inverse_of(*n)
        signed = n[1] if side == 1 else -n[1]
        volume = donor_volume(
            signed, jnp.abs(n[0]), jnp.abs(n[2]), fields_ref[side, 3], inverse, jnp.abs(speed)
        )
        if side == 1:
            flux = jnp.where(speed > 0.0, volume, 0.0)
        else:
            flux = jnp.where(speed < 0.0, -volume, 0.0)
        own_ref[side] = flux
        code_ref[side] = jnp.round(flux * FLUX_SCALE).astype(jnp.int32).astype(jnp.int16)
        speed_ref[side] = speed


def donors(fields, edge, below, above):
    rows, cells = below.shape
    step = 64
    pair = pl.BlockSpec((2, step, cells), lambda i: (0, i, 0))
    one = pl.BlockSpec((step, cells), lambda i: (i, 0))
    shape = (2, rows, cells)
    return pl.pallas_call(
        donors_kernel,
        grid=(rows // step,),
        in_specs=[pl.BlockSpec((2, 4, step, cells), lambda i: (0, 0, i, 0)), pair, one, one],
        out_specs=[pair, pair, pair],
        out_shape=[
            jax.ShapeDtypeStruct(shape, F32),
            jax.ShapeDtypeStruct(shape, jnp.int16),
            jax.ShapeDtypeStruct(shape, F32),
        ],
        name="edge_donors",
    )(fields, edge, below, above)


def rows_kernel(normals_ref, planes_ref, flags_ref, courant_ref, out_ref):
    for k in range(3):
        out_ref[0, k] = normals_ref[k, 0]
    out_ref[0, 3] = plane_value(planes_ref[0], flags_ref[0]).astype(BF16)
    out_ref[0, 4] = courant_ref[0, 0]


def packed_rows(normals, planes, flags, courant, chunk):
    rows, layers, cells = planes.shape

    def place(i):
        return (i // 2) * chunk + (i % 2) * (chunk - 1)

    return pl.pallas_call(
        rows_kernel,
        grid=(2 * (rows // chunk),),
        in_specs=[
            pl.BlockSpec((3, 1, layers, cells), lambda i: (0, place(i), 0, 0)),
            pl.BlockSpec((1, layers, cells), lambda i: (place(i), 0, 0)),
            pl.BlockSpec((1, layers, cells), lambda i: (place(i), 0, 0)),
            pl.BlockSpec((1, 1, layers, cells), lambda i: (0, place(i), 0, 0)),
        ],
        out_specs=pl.BlockSpec((1, 5, layers, cells), lambda i: (i, 0, 0, 0)),
        out_shape=jax.ShapeDtypeStruct((2 * (rows // chunk), 5, layers, cells), BF16),
        name="packed_rows",
    )(normals, planes, flags, courant)


def exponent_of(most):
    return jnp.clip(jnp.ceil(jnp.log2(jnp.maximum(most, 1e-29)) * 256.0) + 1.0, -25000.0, 30000.0)


def to_codes(values):
    return jnp.round(values).astype(jnp.int32).astype(jnp.int16)


def chunk_kernel(
    around,
    has_base,
    fraction_ref,
    normals_ref,
    planes_ref,
    flags_ref,
    courant_ref,
    next_normals_ref,
    next_planes_ref,
    next_flags_ref,
    next_courant_ref,
    low_ref,
    high_ref,
    axial_flux_ref,
    axial_speed_ref,
    basis_ref,
    *rest,
):
    if has_base:
        rest = rest[1:]
    updated_ref, sent_ref, parts, kept, source, wide, scales = rest
    block, layers, cells = fraction_ref.shape
    steps = pl.num_programs(0)
    step = pl.program_id(0)
    chunk = source.shape[1] // layers
    lane_tiles = cells // 128
    backwards = lax.rem(lax.axis_index("azim"), around // 2) >= around // 4

    def put_parts(slot, normals, plane, speed):
        for k in range(3):
            parts[slot, k] = normals[k]
        parts[slot, 3] = plane
        parts[slot, 4] = inverse_of(*normals)
        parts[slot, 5] = 0.5 * speed

    def put_packed(slot, ref):
        values = [ref[0, k].astype(F32) for k in range(5)]
        put_parts(slot, values[:3], values[3], values[4])

    def own_parts(row, _):
        put_parts(
            row,
            [normals_ref[k, row].astype(F32) for k in range(3)],
            plane_value(planes_ref[row], flags_ref[row]),
            courant_ref[0, row].astype(F32),
        )
        return 0

    lax.fori_loop(0, block, own_parts, 0)

    @pl.when(step < steps - 1)
    def _():
        put_parts(
            block,
            [next_normals_ref[k, 0].astype(F32) for k in range(3)],
            plane_value(next_planes_ref[0], next_flags_ref[0]),
            next_courant_ref[0, 0].astype(F32),
        )

    @pl.when(step == steps - 1)
    def _():
        put_packed(block, high_ref)

    def read_parts(slot):
        return [parts[slot, k] for k in range(5)]

    @pl.when(step == 0)
    def _():
        put_packed(block + 1, low_ref)
        speed = parts[block + 1, 5] + parts[0, 5]
        kept[0] = upwind_flux(0, read_parts(block + 1), read_parts(0), speed)
        kept[1] = speed

    index = lax.broadcasted_iota(jnp.int32, (1, cells), 1)
    place = index.astype(F32)
    radius = 1.0 + (place + 0.5) / cells
    next_radius = 1.0 + (place + 1.5) / cells
    face_radius = 1.0 + (place + 1.0) / cells
    inverse_radius = 1.0 / radius
    inner = lax.broadcasted_iota(jnp.int32, (layers, cells), 1) < cells - 1
    layer = lax.broadcasted_iota(jnp.int32, (layers, cells), 0)
    last_layer = layer == layers - 1
    first_layer = layer == 0

    def one_row(row, _):
        own = read_parts(row)
        speed = parts[row, 5] + parts[row + 1, 5]
        flux = upwind_flux(0, own, read_parts(row + 1), speed)
        gained = flux - kept[0]
        divergence = speed - kept[1]
        kept[0] = flux
        kept[1] = speed

        half = 0.5 * courant_ref[1, row].astype(F32)
        above = [pltpu.roll(field, layers - 1, 0) for field in own]
        speed = half + pltpu.roll(half, layers - 1, 0)
        flux = upwind_flux(1, own, above, speed)
        flux = jnp.where(last_layer, axial_flux_ref[1, row], flux)
        speed = jnp.where(last_layer, axial_speed_ref[1, row], speed)
        gained = gained + (
            flux - jnp.where(first_layer, axial_flux_ref[0, row], pltpu.roll(flux, 1, 0))
        )
        divergence = divergence + (
            speed - jnp.where(first_layer, axial_speed_ref[0, row], pltpu.roll(speed, 1, 0))
        )

        half = 0.5 * courant_ref[2, row].astype(F32)
        outer = [pltpu.roll(field, cells - 1, 1) for field in own]
        speed = jnp.where(inner, half + pltpu.roll(half, cells - 1, 1), 0.0)
        flux = upwind_flux(2, own, outer, speed, radius, next_radius)
        gained = gained + (flux - pltpu.roll(flux, 1, 1)) * inverse_radius
        carried = face_radius * speed
        divergence = divergence + (carried - pltpu.roll(carried, 1, 1)) * inverse_radius
        updated = fraction_ref[row] - gained
        updated_ref[row] = updated
        result = divergence + BUOYANCY * updated
        at = step * block + row
        at = jnp.where(backwards, chunk - 1 - at, at)
        for tile in range(lane_tiles):
            source[tile, pl.ds(at, layers, stride=chunk), :] = result[
                :, tile * 128 : (tile + 1) * 128
            ]
        return 0

    lax.fori_loop(0, block, one_row, 0)

    @pl.when(step == steps - 1)
    def _():
        modes = basis_ref.shape[1]
        scales[...] = jnp.zeros_like(scales)

        def radial(z, _):
            at = pl.ds(pl.multiple_of(z * chunk, chunk), chunk)
            rows = jnp.concatenate([source[tile, at, :] for tile in range(lane_tiles)], axis=1)
            got = dot3((basis_ref[0], basis_ref[1]), split(rows), ((1,), (1,)))
            scales[...] = jnp.maximum(scales[...], jnp.abs(got))
            wide[pl.ds(z, modes, stride=layers), :] = got
            return 0

        lax.fori_loop(0, layers, radial, 0)
        exponent = exponent_of(scales[...])
        devices, _, height, lanes = sent_ref.shape
        share = modes // devices
        codes = exponent.astype(jnp.int32).astype(jnp.int16)
        sent_ref[:, share] = codes.reshape(devices, share, lanes)
        scales[...] = CODE_TOP / jnp.exp2(exponent * (1.0 / 256.0))

        def coding(device, _):
            for mode in range(share):
                row = device * share + mode
                values = wide[pl.ds(pl.multiple_of(row * layers, layers), layers), :]
                sent_ref[device, mode] = to_codes(values * scales[pl.ds(row, 1), :])
            return 0

        lax.fori_loop(0, devices, coding, 0)


def advect_chunk(arrays, low, high, axial_flux, axial_speed, basis, chunk_index, chunk, around, devices, base):
    fraction, normals, planes, flags, courant = arrays
    rows, layers, cells = fraction.shape
    block = BLOCK
    steps = chunk // block
    first = chunk_index * steps
    share = cells // devices

    def here(i):
        return first + i

    def after(i):
        return jnp.minimum((first + i + 1) * block, rows - 1)

    whole = pl.BlockSpec((block, layers, cells), lambda i: (here(i), 0, 0))
    triple = pl.BlockSpec((3, block, layers, cells), lambda i: (0, here(i), 0, 0))
    row = pl.BlockSpec((1, layers, cells), lambda i: (after(i), 0, 0))
    pack = pl.BlockSpec((1, 5, layers, cells), lambda i: (0, 0, 0, 0))
    edge = pl.BlockSpec((2, block, 1, cells), lambda i: (0, here(i), 0, 0))
    in_specs = [
        whole,
        triple,
        whole,
        whole,
        triple,
        pl.BlockSpec((3, 1, layers, cells), lambda i: (0, after(i), 0, 0)),
        row,
        row,
        pl.BlockSpec((1, 1, layers, cells), lambda i: (0, after(i), 0, 0)),
        pack,
        pack,
        edge,
        edge,
        pl.BlockSpec((2, cells, cells), lambda i: (0, 0, 0)),
    ]
    operands = [
        fraction, normals, planes, flags, courant,
        normals, planes, flags, courant,
        low, high, axial_flux, axial_speed, basis,
    ]
    aliases = {}
    if base is not None:
        in_specs.append(pl.BlockSpec(memory_space=pl.ANY))
        operands.append(base)
        aliases = {len(operands) - 1: 0}
    return pl.pallas_call(
        functools.partial(chunk_kernel, around, base is not None),
        grid=(steps,),
        in_specs=in_specs,
        out_specs=[
            whole,
            pl.BlockSpec((devices, share + 1, layers, chunk), lambda i: (0, 0, 0, 0)),
        ],
        out_shape=[
            jax.ShapeDtypeStruct(fraction.shape, F32),
            jax.ShapeDtypeStruct((devices, share + 1, layers, chunk), jnp.int16),
        ],
        scratch_shapes=[
            pltpu.VMEM((block + 2, 6, layers, cells), F32),
            pltpu.VMEM((2, layers, cells), F32),
            pltpu.VMEM((cells // 128, layers * chunk, 128), F32),
            pltpu.VMEM((cells * layers, chunk), F32),
            pltpu.VMEM((cells, chunk), F32),
        ],
        input_output_aliases=aliases,
        compiler_params=pltpu.CompilerParams(vmem_limit_bytes=48 * 2**20),
        cost_estimate=pl.CostEstimate(
            flops=40000 * chunk * layers * cells, bytes_accessed=30 * chunk * layers * cells, transcendentals=0
        ),
        name="advect_chunk",
    )(*operands)


@functools.lru_cache(None)
def folded_tables(total):
    quarter = total // 4
    place = np.arange(quarter) + 0.5

    def halves(x):
        high = x.astype(jnp.bfloat16)
        return np.stack([high, (x - high.astype(np.float64)).astype(jnp.bfloat16)])

    tables, rates, weights = [], [], []
    for waves, wave in (
        (2 * np.arange(quarter), np.cos),
        (2 * np.arange(quarter) + 2, np.sin),
        (2 * np.arange(quarter) + 1, np.cos),
        (2 * np.arange(quarter) + 1, np.sin),
    ):
        doubled = waves[:, None] * (2 * np.arange(quarter) + 1)[None, :] % (2 * total)
        tables.append(wave(np.pi * doubled / total))
        rates.append(2.0 - 2.0 * np.cos(2.0 * np.pi * waves / total))
        weights.append(np.where((waves == 0) | (waves == total // 2), 1.0, 2.0) / total)
    tables = np.stack(tables)
    back = np.stack([halves(t) for t in tables])
    forth = np.stack([halves(t.T) for t in tables])
    return forth, back, np.stack(rates)[:, None].astype(np.float32), np.stack(weights)[:, None].astype(np.float32)


def decoded(values):
    return values.astype(jnp.int32).astype(F32)


def scale_of(codes):
    return jnp.exp2(decoded(codes) * (1.0 / 256.0)) * (1.0 / CODE_TOP)


def solve_kernel(around, along, chunks, group, *refs):
    got = refs[:chunks]
    extra = refs[chunks : 2 * chunks]
    mix, unmix, forth, back, rates, weights, shifts = refs[2 * chunks : 2 * chunks + 7]
    sent, high, low, result, scale, exponents = refs[2 * chunks + 7 :]
    devices, count, layers, lanes = got[0].shape
    share = (sent.shape[1] - 1) // chunks
    pairs = around // 4
    step = pl.program_id(0)
    first = group * share + step * count
    for chunk in range(chunks):
        scale[chunk] = scale_of(extra[chunk][:, 0])

    def spots():
        for pair in range(pairs):
            for chunk in range(chunks):
                mirror = chunks - 1 - chunk
                at = pl.ds((pair * chunks + chunk) * lanes, lanes)
                yield at, (
                    (pair, chunk),
                    (pair + 2 * pairs, chunk),
                    (2 * pairs - 1 - pair, mirror),
                    (4 * pairs - 1 - pair, mirror),
                )

    def fold(index, _):
        mode, axial = index // along, index % along
        rows = pl.ds(pl.multiple_of(index * layers, layers), layers)
        row = pl.ds(first + mode, 1)
        for at, places in spots():
            u0, u1, r0, r1 = [
                decoded(got[chunk][azim * along + axial, mode])
                * scale[chunk, azim * along + axial, row, :]
                for azim, chunk in places
            ]
            e0, o0, e1, o1 = u0 + u1, u0 - u1, r0 + r1, r0 - r1
            for k, folded in enumerate((e0 + e1, e0 - e1, o0 - o1, o0 + o1)):
                high[k, rows, at], low[k, rows, at] = split(folded)
        return 0

    lax.fori_loop(0, count * along, fold, 0)

    def waves(k, _):
        mixed = dot3((mix[0], mix[1]), (high[k], low[k]))
        spectrum = dot3(split(mixed), (forth[k, 0], forth[k, 1]))
        solved = spectrum * weights[k] / (rates[k] + shifts[...])
        physical = dot3(split(solved), (back[k, 0], back[k, 1]))
        result[k] = dot3((unmix[0], unmix[1]), split(physical))
        return 0

    lax.fori_loop(0, 4, waves, 0)

    def unfold(index, _):
        mode, axial = index // along, index % along
        rows = pl.ds(pl.multiple_of(index * layers, layers), layers)
        for at, places in spots():
            ec, es, oc, os = [result[k, rows, at] for k in range(4)]
            e0, e1, o0, o1 = ec + es, ec - es, oc + os, os - oc
            for (azim, chunk), values in zip(places, (e0 + o0, e0 - o0, e1 + o1, e1 - o1)):
                device = azim * along + axial
                slot = chunk * share + step * count + mode
                exponent = exponent_of(jnp.max(jnp.abs(values), axis=0, keepdims=True))
                exponents[device, pl.ds(slot, 1), :] = exponent
                factor = CODE_TOP / jnp.exp2(exponent * (1.0 / 256.0))
                sent[device, slot] = to_codes(values * factor)
        return 0

    lax.fori_loop(0, count * along, unfold, 0)

    @pl.when(step == pl.num_programs(0) - 1)
    def _():
        sent[:, chunks * share] = exponents[...].astype(jnp.int32).astype(jnp.int16)


def solve_group(got, mix, unmix, tables, shifts, group, groups, around, along):
    chunks = len(got)
    devices, slots, layers, lanes = got[0].shape
    modes = slots - 1
    share = modes // groups
    count = 4
    steps = share // count
    rows = count * along * layers
    forth, back, rates, weights = tables
    width = forth.shape[-1]

    def fixed(array):
        return pl.BlockSpec(array.shape, lambda i: (0,) * array.ndim, pipeline_mode=pl.Buffered(1))

    return pl.pallas_call(
        functools.partial(solve_kernel, around, along, chunks, group),
        grid=(steps,),
        in_specs=[
            pl.BlockSpec((devices, count, layers, lanes), lambda i: (0, group * steps + i, 0, 0))
        ]
        * chunks
        + [pl.BlockSpec((devices, 1, layers, lanes), lambda i: (0, modes, 0, 0))] * chunks
        + [fixed(x) for x in (mix, unmix, forth, back, rates, weights)]
        + [pl.BlockSpec((rows, 1), lambda i: (group * steps + i, 0))],
        out_specs=pl.BlockSpec((devices, slots, layers, lanes), lambda i: (0, 0, 0, 0)),
        out_shape=jax.ShapeDtypeStruct((devices, chunks * share + 1, layers, lanes), jnp.int16),
        scratch_shapes=[
            pltpu.VMEM((4, rows, width), BF16),
            pltpu.VMEM((4, rows, width), BF16),
            pltpu.VMEM((4, rows, width), F32),
            pltpu.VMEM((chunks, devices, layers, lanes), F32),
            pltpu.VMEM((devices, layers, lanes), F32),
        ],
        compiler_params=pltpu.CompilerParams(vmem_limit_bytes=48 * 2**20),
        cost_estimate=pl.CostEstimate(
            flops=60 * rows * width * width * steps, bytes_accessed=20 * 2**20, transcendentals=0
        ),
        name="solve_group",
    )(*got, *got, mix, unmix, forth, back, rates, weights, shifts)


def pressure_kernel(around, groups, *refs):
    got = refs[:groups]
    extra = refs[groups : 2 * groups]
    basis, out, flat, wide, scale = refs[2 * groups :]
    devices, share, layers, lanes = got[0].shape
    lane_tiles = out.shape[2] // 128
    chunk = pl.program_id(0)
    backwards = lax.rem(lax.axis_index("azim"), around // 2) >= around // 4
    i = lax.broadcasted_iota(jnp.int32, (lanes, lanes), 0)
    j = lax.broadcasted_iota(jnp.int32, (lanes, lanes), 1)
    turned_place = jnp.where(backwards, lanes - 1, 0) + jnp.where(backwards, -1, 1) * i
    turn = jnp.where(j == turned_place, 1.0, 0.0).astype(BF16)
    for group in range(groups):
        scale[group] = scale_of(extra[group][:, 0])

        def unpack(device, _, group=group):
            for mode in range(share):
                at = pl.multiple_of((device * share + mode) * layers, layers)
                flat[group, pl.ds(at, layers), :] = (
                    decoded(got[group][device, mode])
                    * scale[group, device, pl.ds(chunk * share + mode, 1), :]
                )
            return 0

        lax.fori_loop(0, devices, unpack, 0)

    def radial(z, _):
        total = jnp.zeros((lanes, out.shape[2]), F32)
        for group in range(groups):
            values = split(flat[group, pl.ds(z, devices * share, stride=layers), :])
            turned = [dot(turn, part, ((1,), (1,))).astype(BF16) for part in values]
            total = total + dot3(turned, (basis[0, group], basis[1, group]))
        for tile in range(lane_tiles):
            wide[tile, pl.ds(z, lanes, stride=layers), :] = total[:, tile * 128 : (tile + 1) * 128]
        return 0

    lax.fori_loop(0, layers, radial, 0)
    for tile in range(lane_tiles):
        out[:, :, tile * 128 : (tile + 1) * 128] = wide[tile].reshape(lanes, layers, 128)


def pressure_of(got, basis, around, chunks):
    groups = len(got)
    devices, slots, layers, lanes = got[0].shape
    share = (slots - 1) // chunks
    cells = basis.shape[-1]
    return pl.pallas_call(
        functools.partial(pressure_kernel, around, groups),
        grid=(chunks,),
        in_specs=[pl.BlockSpec((devices, share, layers, lanes), lambda i: (0, i, 0, 0))] * groups
        + [pl.BlockSpec((devices, 1, layers, lanes), lambda i: (0, chunks * share, 0, 0))] * groups
        + [
            pl.BlockSpec(
                basis.shape, lambda i: (0,) * basis.ndim, pipeline_mode=pl.Buffered(1)
            )
        ],
        out_specs=pl.BlockSpec((lanes, layers, cells), lambda i: (i, 0, 0)),
        out_shape=jax.ShapeDtypeStruct((lanes * chunks, layers, cells), F32),
        scratch_shapes=[
            pltpu.VMEM((groups, devices * share * layers, lanes), F32),
            pltpu.VMEM((cells // 128, lanes * layers, 128), F32),
            pltpu.VMEM((groups, devices, layers, lanes), F32),
        ],
        compiler_params=pltpu.CompilerParams(vmem_limit_bytes=48 * 2**20),
        name="pressure_of",
    )(*got, *got, basis)


def halves(values):
    high = lax.reduce_precision(values, 8, 7)
    return jnp.stack([high.astype(BF16), (values - high).astype(BF16)])


def exchanged(sent):
    return lax.all_to_all(sent, ("azim", "axial"), split_axis=0, concat_axis=0, tiled=True)


def following_kernel(values_ref, earlier_ref, out_ref):
    del values_ref, earlier_ref, out_ref


def following(values, earlier):
    anywhere = pl.BlockSpec(memory_space=pl.ANY)
    return pl.pallas_call(
        following_kernel,
        in_specs=[anywhere, anywhere],
        out_specs=anywhere,
        out_shape=jax.ShapeDtypeStruct(values.shape, values.dtype),
        input_output_aliases={0: 0},
        name="following",
    )(values, earlier)


def overlapped(
    fraction,
    normals,
    planes,
    cell_flags,
    courant,
    radial_basis,
    axial_basis,
    radial_rates,
    axial_rates,
):
    rows, layers, cells = fraction.shape
    around, along = lax.axis_size("azim"), lax.axis_size("axial")
    devices = around * along
    modes = cells // devices
    chunks, groups = rows // CHUNK, 2
    edge = edge_speeds(courant)
    below = shifted_in(edge[1], "axial", False)
    above = shifted_in(edge[0], "axial", True)
    packs = packed_rows(normals, planes, cell_flags, courant, CHUNK)
    low_row = shifted_in(packs[-1:], "azim", False)
    high_row = shifted_in(packs[:1], "azim", True)
    fields = edge_fields(normals, planes, cell_flags)
    own, code, speed = donors(fields, edge, below, above)
    from_below = shifted_in(code[1], "axial", False)
    from_above = shifted_in(code[0], "axial", True)
    axial_flux = own + jnp.stack([from_below, from_above]).astype(F32) * (1.0 / FLUX_SCALE)
    axial_flux, axial_speed = axial_flux[:, :, None], speed[:, :, None]
    forward_basis = halves(radial_basis.T)
    arrays = (fraction, normals, planes, cell_flags, courant)
    updated, got = None, []
    for chunk in range(chunks):
        low = low_row if chunk == 0 else packs[2 * chunk - 1 : 2 * chunk]
        high = high_row if chunk == chunks - 1 else packs[2 * chunk + 2 : 2 * chunk + 3]
        updated, sent = advect_chunk(
            arrays, low, high, axial_flux, axial_speed, forward_basis, chunk, CHUNK, around, devices, updated
        )
        got.append(exchanged(following(sent, got[-1]) if got else sent))
    count = jnp.eye(4, dtype=F32)
    mix, unmix = halves(jnp.kron(count, axial_basis.T)), halves(jnp.kron(count, axial_basis))
    first = (lax.axis_index("azim") * along + lax.axis_index("axial")) * modes
    shifts = lax.dynamic_slice_in_dim(radial_rates, first, modes)[:, None] + axial_rates[None, :]
    shifts = shifts.reshape(modes * along * layers, 1)
    tables = [jnp.asarray(x) for x in folded_tables(rows * around)]
    returned = []
    for group in range(groups):
        sent = solve_group(got, mix, unmix, tables, shifts, group, groups, around, along)
        returned.append(exchanged(sent))
    back_basis = radial_basis.T.reshape(devices, groups, modes // groups, cells)
    back_basis = halves(back_basis.transpose(1, 0, 2, 3).reshape(groups, -1, cells))
    pressure = pressure_of(returned, back_basis, around, chunks)
    return (updated, pressure)


def fits(fraction):
    rows, layers, cells = fraction.shape
    around, along = lax.axis_size("azim"), lax.axis_size("axial")
    modes = cells // (around * along)
    chunks = rows // CHUNK
    return (
        rows % CHUNK == 0
        and layers == 16
        and modes == 16
        and modes // 2 * chunks == layers
        and cells % 128 == 0
        and around % 4 == 0
    )


def local(*arguments):
    return overlapped(*arguments) if fits(arguments[0]) else stepwise(*arguments)


def solution(mesh):
    placed = (
        P("azim", "axial", None),
        P(None, "azim", "axial", None),
        P("azim", "axial", None),
        P("azim", "axial", None),
        P(None, "azim", "axial", None),
        P(),
        P(),
        P(),
        P(),
    )
    return jax.shard_map(
        local,
        mesh=mesh,
        in_specs=placed,
        out_specs=(P("azim", "axial", None), P("azim", "axial", None)),
        check_vma=False,
    )
```

```python
import functools

import jax
import jax.numpy as jnp
import numpy as np
from jax import lax
from jax.experimental import pallas as pl
from jax.experimental.pallas import tpu as pltpu
from jax.sharding import PartitionSpec as P

HIGH = lax.Precision.HIGH
BUOYANCY = 0.5
CODE_TOP = 32700.0


def shifted_in(edge, axis, towards_lower):
    count = lax.axis_size(axis)
    if towards_lower:
        pairs = [((i + 1) % count, i) for i in range(count)]
    else:
        pairs = [(i, (i + 1) % count) for i in range(count)]
    return lax.ppermute(edge, axis, pairs)


def cell_parts(n0, n1, n2, code):
    m0, m1, m2 = jnp.abs(n0), jnp.abs(n1), jnp.abs(n2)
    return (n0, n1, n2, code, 1.0 / (6.0 * m0 * m1 * m2))


def cube(height):
    held = jnp.maximum(height, 0.0)
    return held * held * held


def face_flux(direction, lower, upper, speed, lower_weight=None, upper_weight=None):
    forward = speed > 0.0
    signed = jnp.where(forward, lower[direction], -upper[direction])
    first, second = [d for d in range(3) if d != direction]
    along = jnp.abs(signed)
    side_a = jnp.abs(jnp.where(forward, lower[first], upper[first]))
    side_b = jnp.abs(jnp.where(forward, lower[second], upper[second]))
    code = jnp.where(forward, lower[3], upper[3])
    inverse = jnp.where(forward, lower[4], upper[4])
    width = jnp.abs(speed)
    near = code - along * jnp.where(signed < 0.0, 0.0, 1.0 - width)
    far = near - along * width
    sides = side_a + side_b
    total = (cube(near) - cube(near - side_a)) - (cube(near - side_b) - cube(near - sides))
    total = total - ((cube(far) - cube(far - side_a)) - (cube(far - side_b) - cube(far - sides)))
    volume = jnp.where(code > 3.0, width, jnp.where(code < -0.5, 0.0, total * inverse))
    if lower_weight is not None:
        volume = volume * jnp.where(forward, lower_weight, upper_weight)
    return jnp.where(forward, volume, jnp.where(speed < 0.0, -volume, 0.0))


def advect_kernel(
    fraction_ref,
    normals_ref,
    planes_ref,
    flags_ref,
    courant_ref,
    next_ref,
    high_ref,
    low_azim_ref,
    low_axial_ref,
    updated_ref,
    source_ref,
    kept,
):
    rows, layers, cells = fraction_ref.shape
    f32 = jnp.float32

    @pl.when(pl.program_id(0) == 0)
    def _():
        kept[...] = low_azim_ref[...]

    index = lax.broadcasted_iota(jnp.int32, (1, cells), 1)
    place = index.astype(f32)
    radius = 1.0 + (place + 0.5) / cells
    next_radius = 1.0 + (place + 1.5) / cells
    face_radius = 1.0 + (place + 1.0) / cells
    inverse_radius = 1.0 / radius
    inner = lax.broadcasted_iota(jnp.int32, (layers, cells), 1) < cells - 1
    layer = lax.broadcasted_iota(jnp.int32, (layers, cells), 0)
    last_layer = layer == layers - 1
    first_layer = layer == 0

    def row_parts(row):
        flags = flags_ref[row]
        code = jnp.where(
            flags == 2, planes_ref[row].astype(f32), jnp.where(flags == 1, 4.0, -1.0)
        )
        return cell_parts(
            normals_ref[0, row].astype(f32),
            normals_ref[1, row].astype(f32),
            normals_ref[2, row].astype(f32),
            code,
        )

    def one_row(row, upper, upper_speed):
        own = row_parts(row)
        moved = [courant_ref[d, row].astype(f32) for d in range(3)]
        speed = 0.5 * (moved[0] + upper_speed)
        flux = face_flux(0, own, upper, speed)
        gained = flux - kept[0]
        divergence = speed - kept[1]
        kept[0] = flux
        kept[1] = speed
        beyond = cell_parts(*[high_ref[k, row] for k in range(4)])
        above = [
            jnp.where(last_layer, high, pltpu.roll(field, layers - 1, 0))
            for field, high in zip(own, beyond)
        ]
        speed = 0.5 * (
            moved[1]
            + jnp.where(last_layer, high_ref[4, row], pltpu.roll(moved[1], layers - 1, 0))
        )
        flux = face_flux(1, own, above, speed)
        gained = gained + (
            flux - jnp.where(first_layer, low_axial_ref[0, row], pltpu.roll(flux, 1, 0))
        )
        divergence = divergence + (
            speed - jnp.where(first_layer, low_axial_ref[1, row], pltpu.roll(speed, 1, 0))
        )
        outer = [pltpu.roll(field, cells - 1, 1) for field in own]
        speed = 0.5 * (moved[2] + pltpu.roll(moved[2], cells - 1, 1))
        speed = jnp.where(inner, speed, 0.0)
        flux = face_flux(2, own, outer, speed, radius, next_radius)
        gained = gained + (flux - pltpu.roll(flux, 1, 1)) * inverse_radius
        carried = face_radius * speed
        divergence = divergence + (carried - pltpu.roll(carried, 1, 1)) * inverse_radius
        updated = fraction_ref[row] - gained
        updated_ref[row] = updated
        source_ref[row] = divergence + BUOYANCY * updated

    def step(row, _):
        one_row(row, row_parts(row + 1), courant_ref[0, row + 1].astype(f32))
        return 0

    lax.fori_loop(0, rows - 1, step, 0)
    one_row(
        rows - 1,
        cell_parts(*[next_ref[k, 0].astype(f32) for k in range(4)]),
        next_ref[4, 0].astype(f32),
    )


def plane_codes(planes, flags):
    return jnp.where(
        flags == 2, planes.astype(jnp.float32), jnp.where(flags == 1, 4.0, -1.0)
    ).astype(jnp.bfloat16)


def packed_edge(normals, planes, flags, courant, direction, pick):
    parts = [pick(normals[d]) for d in range(3)]
    parts.append(plane_codes(pick(planes), pick(flags)))
    parts.append(pick(courant[direction]))
    return jnp.stack(parts)


def low_face(direction, lower, upper):
    lower, upper = lower.astype(jnp.float32), upper.astype(jnp.float32)
    speed = 0.5 * (lower[4] + upper[4])
    flux = face_flux(direction, cell_parts(*lower[:4]), cell_parts(*upper[:4]), speed)
    return jnp.stack([flux, speed])


def advect(fraction, normals, planes, flags, courant):
    rows, layers, cells = fraction.shape
    block = 16 if rows % 16 == 0 else 1
    blocks = rows // block
    fields = (normals, planes, flags, courant)
    top_row = packed_edge(*fields, 0, lambda x: x[rows - 1])
    bottom_row = packed_edge(*fields, 0, lambda x: x[0])
    top_layer = packed_edge(*fields, 1, lambda x: x[:, layers - 1])
    bottom_layer = packed_edge(*fields, 1, lambda x: x[:, 0])
    high_row = shifted_in(bottom_row, "azim", True)
    low_row = shifted_in(top_row, "azim", False)
    high_layer = shifted_in(bottom_layer, "axial", True)
    low_layer = shifted_in(top_layer, "axial", False)
    low_azim = low_face(0, low_row, bottom_row)
    low_axial = low_face(1, low_layer, bottom_layer)[:, :, None]
    high_axial = high_layer.astype(jnp.float32)[:, :, None]
    inside = packed_edge(*fields, 0, lambda x: x[block::block])
    following = jnp.concatenate([inside, high_row[:, None]], axis=1)
    whole = pl.BlockSpec((block, layers, cells), lambda i: (i, 0, 0))
    triple = pl.BlockSpec((3, block, layers, cells), lambda i: (0, i, 0, 0))
    return pl.pallas_call(
        advect_kernel,
        grid=(blocks,),
        in_specs=[
            whole,
            triple,
            whole,
            whole,
            triple,
            pl.BlockSpec((5, 1, layers, cells), lambda i: (0, i, 0, 0)),
            pl.BlockSpec((5, block, 1, cells), lambda i: (0, i, 0, 0)),
            pl.BlockSpec((2, layers, cells), lambda i: (0, 0, 0)),
            pl.BlockSpec((2, block, 1, cells), lambda i: (0, i, 0, 0)),
        ],
        out_specs=[whole, whole],
        out_shape=[jax.ShapeDtypeStruct(fraction.shape, jnp.float32)] * 2,
        scratch_shapes=[pltpu.VMEM((2, layers, cells), jnp.float32)],
        compiler_params=pltpu.CompilerParams(vmem_limit_bytes=40 * 2**20),
    )(
        fraction,
        normals,
        planes,
        flags,
        courant,
        following,
        high_axial,
        low_azim,
        low_axial,
    )


def coded(values):
    most = jnp.max(jnp.abs(values), axis=-1)
    exponent = jnp.clip(jnp.ceil(jnp.log2(most) * 256.0) + 1.0, -30000.0, 30000.0)
    scale = CODE_TOP * jnp.exp2(exponent * (-1.0 / 256.0))
    codes = jnp.round(values * scale[..., None])
    return jnp.clip(codes, -32767.0, 32767.0).astype(jnp.int16), exponent.astype(jnp.int16)


def exchange(values):
    modes, cells = values.shape[1], values.shape[3]
    codes, exponent = coded(values)
    extra = jnp.pad(exponent.transpose(0, 2, 1), ((0, 0), (0, 0), (0, cells - modes)))
    sent = jnp.concatenate([codes, extra[:, None]], axis=1)
    got = lax.all_to_all(sent, ("azim", "axial"), split_axis=0, concat_axis=0, tiled=True)
    exponent = got[:, modes, :, :modes].transpose(0, 2, 1).astype(jnp.float32)
    scale = jnp.exp2(exponent * (1.0 / 256.0)) * (1.0 / CODE_TOP)
    return got[:, :modes].astype(jnp.float32) * scale[..., None]


@functools.lru_cache(None)
def azimuth_tables(total):
    half, quarter = total // 2, total // 4
    place = np.arange(half)

    def table(cosines, sines):
        waves = np.concatenate([cosines, sines])
        angles = 2.0 * np.pi / total * (waves[:, None] * place[None, :] % total)
        rows = np.concatenate(
            [np.cos(angles[: len(cosines)]), np.sin(angles[len(cosines) :])]
        ).astype(np.float32)
        rates = (2.0 - 2.0 * np.cos(2.0 * np.pi * waves / total)).astype(np.float32)
        ends = (waves == 0) | (waves == half)
        return rows, rates, (np.where(ends, 1.0, 2.0) / total).astype(np.float32)

    even = 2 * np.arange(quarter + 1)
    odd = 2 * np.arange(quarter) + 1
    return table(even, even[1:-1]), table(odd, odd)


def stepwise(
    fraction,
    normals,
    planes,
    cell_flags,
    courant,
    radial_basis,
    axial_basis,
    radial_rates,
    axial_rates,
):
    rows, layers, cells = fraction.shape
    around, along = lax.axis_size("azim"), lax.axis_size("axial")
    devices = around * along
    modes = cells // devices
    total = rows * around
    half = total // 2
    updated, source = advect(fraction, normals, planes, cell_flags, courant)
    radial_modes = jnp.einsum("azr,rj->jza", source, radial_basis, precision=HIGH)
    got = exchange(radial_modes.reshape(devices, modes, layers, rows))
    got = got.reshape(around, along, modes, layers, rows).transpose(2, 1, 3, 0, 4)
    got = got.reshape(modes, along * layers, total)
    both = jnp.einsum("jza,zn->jna", got, axial_basis, precision=HIGH)
    first = (lax.axis_index("azim") * along + lax.axis_index("axial")) * modes
    shifts = lax.dynamic_slice_in_dim(radial_rates, first, modes)[:, None] + axial_rates[None, :]
    low, high = both[..., :half], both[..., half:]
    solved = []
    for folded, (table, rates, weight) in zip((low + high, low - high), azimuth_tables(total)):
        coefficients = jnp.einsum("jna,ka->jnk", folded, table, precision=HIGH)
        scaled = coefficients / (rates + shifts[..., None]) * weight
        solved.append(jnp.einsum("jnk,ka->jna", scaled, table, precision=HIGH))
    physical = jnp.concatenate([solved[0] + solved[1], solved[0] - solved[1]], axis=-1)
    physical = jnp.einsum("jna,zn->jza", physical, axial_basis, precision=HIGH)
    physical = physical.reshape(modes, along, layers, around, rows).transpose(3, 1, 0, 2, 4)
    returned = exchange(physical.reshape(devices, modes, layers, rows))
    returned = returned.reshape(cells, layers, rows)
    pressure = jnp.einsum("jza,rj->azr", returned, radial_basis, precision=HIGH)
    return (updated, pressure)


CHUNK = 128
BLOCK = 16
FLUX_SCALE = 32767.0 / 0.3
F32 = jnp.float32
BF16 = jnp.bfloat16


def split(values):
    high = values.astype(BF16)
    return high, (values - high.astype(F32)).astype(BF16)


def dot(a, b, contract):
    return lax.dot_general(a, b, (contract, ((), ())), preferred_element_type=F32)


def dot3(a, b, contract=((1,), (0,))):
    return dot(a[0], b[0], contract) + (dot(a[0], b[1], contract) + dot(a[1], b[0], contract))


def slab_flux(normal, side_a, side_b, plane, inverse, speed):
    along = jnp.abs(normal)
    reach = normal * speed
    slab = jnp.abs(reach)
    near = plane - jnp.where(reach > 0.0, along - slab, 0.0)
    other = (slab + (side_a + side_b)) - near
    folded = near > other
    held = jnp.maximum(jnp.minimum(near, other), 0.0)
    low, high = jnp.minimum(side_a, side_b), jnp.maximum(side_a, side_b)
    by_low = jnp.maximum(held - low, 0.0)
    by_slab = jnp.maximum(held - slab, 0.0)
    last = jnp.maximum(held - (low + slab), 0.0) - jnp.maximum(held - high, 0.0)
    total = held * held * held - by_slab * by_slab * by_slab
    total = total - (by_low * by_low * by_low - last * last * last)
    flux = total * inverse
    return jnp.where(folded, speed - flux, flux)


def upwind_flux(direction, lower, upper, speed, lower_weight=None, upper_weight=None):
    forward = speed > 0.0
    first, second = [d for d in range(3) if d != direction]
    normal = jnp.where(forward, lower[direction], upper[direction])
    side_a = jnp.abs(jnp.where(forward, lower[first], upper[first]))
    side_b = jnp.abs(jnp.where(forward, lower[second], upper[second]))
    plane = jnp.where(forward, lower[3], upper[3])
    inverse = jnp.where(forward, lower[4], upper[5])
    flux = slab_flux(normal, side_a, side_b, plane, inverse, speed)
    if lower_weight is not None:
        flux = flux * jnp.where(forward, lower_weight, upper_weight)
    return flux


def inverse_of(n0, n1, n2):
    return 1.0 / (6.0 * jnp.abs(n0 * n1 * n2))


def plane_value(planes, flags):
    return jnp.where(flags == 2, planes.astype(F32), jnp.where(flags == 1, 4.0, -4.0))


def strided_rows(work, layer, rows, layers, cells):
    parts = []
    for lane in range(0, cells, 128):
        parts.append(work[lane // 128, pl.ds(layer, rows, stride=layers), :])
    return parts


def speeds_kernel(courant_ref, edge_ref, work):
    rows, layers, cells = courant_ref.shape[1:]
    for lane in range(0, cells, 128):
        work[lane // 128] = courant_ref[0, :, :, pl.ds(lane, 128)].astype(F32).reshape(rows * layers, 128)
    for side, layer in ((0, 0), (1, layers - 1)):
        for tile, got in enumerate(strided_rows(work, layer, rows, layers, cells)):
            edge_ref[side, :, pl.ds(tile * 128, 128)] = got.astype(BF16)


def edge_speeds(courant):
    _, rows, layers, cells = courant.shape
    step = 64
    return pl.pallas_call(
        speeds_kernel,
        grid=(rows // step,),
        in_specs=[pl.BlockSpec((1, step, layers, cells), lambda i: (1, i, 0, 0))],
        out_specs=pl.BlockSpec((2, step, cells), lambda i: (0, i, 0)),
        out_shape=jax.ShapeDtypeStruct((2, rows, cells), BF16),
        scratch_shapes=[pltpu.VMEM((cells // 128, step * layers, 128), F32)],
        name="edge_speeds",
    )(courant)


def fields_kernel(normals_ref, planes_ref, flags_ref, fields_ref, work):
    rows, layers, cells = planes_ref.shape
    for k in range(4):
        for lane in range(0, cells, 128):
            at = pl.ds(lane, 128)
            if k < 3:
                field = normals_ref[k, :, :, at].astype(F32)
            else:
                field = plane_value(planes_ref[:, :, at], flags_ref[:, :, at])
            work[lane // 128] = field.reshape(rows * layers, 128)
        for side, layer in ((0, 0), (1, layers - 1)):
            for tile, got in enumerate(strided_rows(work, layer, rows, layers, cells)):
                fields_ref[side, k, :, pl.ds(tile * 128, 128)] = got


def edge_fields(normals, planes, flags):
    rows, layers, cells = planes.shape
    step = 32
    whole = pl.BlockSpec((step, layers, cells), lambda i: (i, 0, 0))
    return pl.pallas_call(
        fields_kernel,
        grid=(rows // step,),
        in_specs=[
            pl.BlockSpec((3, step, layers, cells), lambda i: (0, i, 0, 0)),
            whole,
            whole,
        ],
        out_specs=pl.BlockSpec((2, 4, step, cells), lambda i: (0, 0, i, 0)),
        out_shape=jax.ShapeDtypeStruct((2, 4, rows, cells), F32),
        scratch_shapes=[pltpu.VMEM((cells // 128, step * layers, 128), F32)],
        name="edge_fields",
    )(normals, planes, flags)


def donors_kernel(fields_ref, edge_ref, below_ref, above_ref, own_ref, code_ref, speed_ref):
    for side in range(2):
        n = [fields_ref[side, k] for k in range(3)]
        beyond = (below_ref if side == 0 else above_ref)[...].astype(F32)
        speed = 0.5 * (edge_ref[side].astype(F32) + beyond)
        inverse = inverse_of(*n)
        inverse = inverse if side == 1 else -inverse
        flux = slab_flux(n[1], jnp.abs(n[0]), jnp.abs(n[2]), fields_ref[side, 3], inverse, speed)
        flux = jnp.where(speed > 0.0 if side == 1 else speed < 0.0, flux, 0.0)
        own_ref[side] = flux
        code_ref[side] = jnp.round(flux * FLUX_SCALE).astype(jnp.int32).astype(jnp.int16)
        speed_ref[side] = speed


def donors(fields, edge, below, above):
    rows, cells = below.shape
    step = 64
    pair = pl.BlockSpec((2, step, cells), lambda i: (0, i, 0))
    one = pl.BlockSpec((step, cells), lambda i: (i, 0))
    shape = (2, rows, cells)
    return pl.pallas_call(
        donors_kernel,
        grid=(rows // step,),
        in_specs=[pl.BlockSpec((2, 4, step, cells), lambda i: (0, 0, i, 0)), pair, one, one],
        out_specs=[pair, pair, pair],
        out_shape=[
            jax.ShapeDtypeStruct(shape, F32),
            jax.ShapeDtypeStruct(shape, jnp.int16),
            jax.ShapeDtypeStruct(shape, F32),
        ],
        name="edge_donors",
    )(fields, edge, below, above)


def rows_kernel(normals_ref, planes_ref, flags_ref, courant_ref, out_ref):
    for k in range(3):
        out_ref[0, k] = normals_ref[k, 0]
    out_ref[0, 3] = plane_value(planes_ref[0], flags_ref[0]).astype(BF16)
    out_ref[0, 4] = courant_ref[0, 0]


def packed_rows(normals, planes, flags, courant, chunk):
    rows, layers, cells = planes.shape

    def place(i):
        return (i // 2) * chunk + (i % 2) * (chunk - 1)

    return pl.pallas_call(
        rows_kernel,
        grid=(2 * (rows // chunk),),
        in_specs=[
            pl.BlockSpec((3, 1, layers, cells), lambda i: (0, place(i), 0, 0)),
            pl.BlockSpec((1, layers, cells), lambda i: (place(i), 0, 0)),
            pl.BlockSpec((1, layers, cells), lambda i: (place(i), 0, 0)),
            pl.BlockSpec((1, 1, layers, cells), lambda i: (0, place(i), 0, 0)),
        ],
        out_specs=pl.BlockSpec((1, 5, layers, cells), lambda i: (i, 0, 0, 0)),
        out_shape=jax.ShapeDtypeStruct((2 * (rows // chunk), 5, layers, cells), BF16),
        name="packed_rows",
    )(normals, planes, flags, courant)


def exponent_of(most):
    return jnp.clip(jnp.ceil(jnp.log2(jnp.maximum(most, 1e-29)) * 256.0) + 1.0, -25000.0, 30000.0)


def to_codes(values):
    return jnp.round(values).astype(jnp.int32).astype(jnp.int16)


def chunk_kernel(
    around,
    has_base,
    fraction_ref,
    normals_ref,
    planes_ref,
    flags_ref,
    courant_ref,
    next_normals_ref,
    next_planes_ref,
    next_flags_ref,
    next_courant_ref,
    low_ref,
    high_ref,
    axial_flux_ref,
    axial_speed_ref,
    basis_ref,
    *rest,
):
    if has_base:
        rest = rest[1:]
    updated_ref, sent_ref, parts, kept, source, wide, scales = rest
    block, layers, cells = fraction_ref.shape
    steps = pl.num_programs(0)
    step = pl.program_id(0)
    chunk = source.shape[1] // layers
    lane_tiles = cells // 128
    backwards = lax.rem(lax.axis_index("azim"), around // 2) >= around // 4

    def put_parts(slot, normals, plane, speed):
        for k in range(3):
            parts[slot, k] = normals[k]
        parts[slot, 3] = plane
        inverse = inverse_of(*normals)
        parts[slot, 4] = inverse
        parts[slot, 5] = -inverse
        parts[slot, 6] = 0.5 * speed

    def put_packed(slot, ref):
        values = [ref[0, k].astype(F32) for k in range(5)]
        put_parts(slot, values[:3], values[3], values[4])

    def own_parts(row, _):
        put_parts(
            row,
            [normals_ref[k, row].astype(F32) for k in range(3)],
            plane_value(planes_ref[row], flags_ref[row]),
            courant_ref[0, row].astype(F32),
        )
        return 0

    lax.fori_loop(0, block, own_parts, 0)

    @pl.when(step < steps - 1)
    def _():
        put_parts(
            block,
            [next_normals_ref[k, 0].astype(F32) for k in range(3)],
            plane_value(next_planes_ref[0], next_flags_ref[0]),
            next_courant_ref[0, 0].astype(F32),
        )

    @pl.when(step == steps - 1)
    def _():
        put_packed(block, high_ref)

    def read_parts(slot):
        return [parts[slot, k] for k in range(6)]

    @pl.when(step == 0)
    def _():
        put_packed(block + 1, low_ref)
        speed = parts[block + 1, 6] + parts[0, 6]
        kept[0] = upwind_flux(0, read_parts(block + 1), read_parts(0), speed)
        kept[1] = speed

    index = lax.broadcasted_iota(jnp.int32, (1, cells), 1)
    place = index.astype(F32)
    radius = 1.0 + (place + 0.5) / cells
    next_radius = 1.0 + (place + 1.5) / cells
    face_radius = 1.0 + (place + 1.0) / cells
    inverse_radius = 1.0 / radius
    inner = lax.broadcasted_iota(jnp.int32, (layers, cells), 1) < cells - 1
    layer = lax.broadcasted_iota(jnp.int32, (layers, cells), 0)
    last_layer = layer == layers - 1
    first_layer = layer == 0

    def one_row(row, _):
        own = read_parts(row)
        speed = parts[row, 6] + parts[row + 1, 6]
        flux = upwind_flux(0, own, read_parts(row + 1), speed)
        gained = flux - kept[0]
        divergence = speed - kept[1]
        kept[0] = flux
        kept[1] = speed

        half = 0.5 * courant_ref[1, row].astype(F32)
        above = [None if k == 4 else pltpu.roll(field, layers - 1, 0) for k, field in enumerate(own)]
        speed = half + pltpu.roll(half, layers - 1, 0)
        flux = upwind_flux(1, own, above, speed)
        flux = jnp.where(last_layer, axial_flux_ref[1, row], flux)
        speed = jnp.where(last_layer, axial_speed_ref[1, row], speed)
        gained = gained + (
            flux - jnp.where(first_layer, axial_flux_ref[0, row], pltpu.roll(flux, 1, 0))
        )
        divergence = divergence + (
            speed - jnp.where(first_layer, axial_speed_ref[0, row], pltpu.roll(speed, 1, 0))
        )

        half = 0.5 * courant_ref[2, row].astype(F32)
        outer = [None if k == 4 else pltpu.roll(field, cells - 1, 1) for k, field in enumerate(own)]
        speed = jnp.where(inner, half + pltpu.roll(half, cells - 1, 1), 0.0)
        flux = upwind_flux(2, own, outer, speed, radius, next_radius)
        gained = gained + (flux - pltpu.roll(flux, 1, 1)) * inverse_radius
        carried = face_radius * speed
        divergence = divergence + (carried - pltpu.roll(carried, 1, 1)) * inverse_radius
        updated = fraction_ref[row] - gained
        updated_ref[row] = updated
        result = divergence + BUOYANCY * updated
        at = step * block + row
        at = jnp.where(backwards, chunk - 1 - at, at)
        for tile in range(lane_tiles):
            source[tile, pl.ds(at, layers, stride=chunk), :] = result[
                :, tile * 128 : (tile + 1) * 128
            ]
        return 0

    lax.fori_loop(0, block, one_row, 0)

    @pl.when(step == steps - 1)
    def _():
        modes = basis_ref.shape[1]
        scales[...] = jnp.zeros_like(scales)

        def radial(z, _):
            at = pl.ds(pl.multiple_of(z * 2 * chunk, 2 * chunk), 2 * chunk)
            rows = jnp.concatenate([source[tile, at, :] for tile in range(lane_tiles)], axis=1)
            both = dot3((basis_ref[0], basis_ref[1]), split(rows), ((1,), (1,)))
            for half in range(2):
                got = both[:, half * chunk : (half + 1) * chunk]
                scales[...] = jnp.maximum(scales[...], jnp.abs(got))
                wide[pl.ds(z * 2 + half, modes, stride=layers), :] = got
            return 0

        lax.fori_loop(0, layers // 2, radial, 0)
        exponent = exponent_of(scales[...])
        devices, _, height, lanes = sent_ref.shape
        share = modes // devices
        codes = exponent.astype(jnp.int32).astype(jnp.int16)
        sent_ref[:, share] = codes.reshape(devices, share, lanes)
        scales[...] = CODE_TOP / jnp.exp2(exponent * (1.0 / 256.0))

        def coding(device, _):
            for mode in range(share):
                row = device * share + mode
                values = wide[pl.ds(pl.multiple_of(row * layers, layers), layers), :]
                sent_ref[device, mode] = to_codes(values * scales[pl.ds(row, 1), :])
            return 0

        lax.fori_loop(0, devices, coding, 0)


def advect_chunk(arrays, ends, axial_flux, axial_speed, basis, chunk_index, chunk, around, devices, base):
    fraction, normals, planes, flags, courant = arrays
    rows, layers, cells = fraction.shape
    block = BLOCK
    steps = chunk // block
    first = chunk_index * steps
    share = cells // devices

    def here(i):
        return first + i

    def after(i):
        return jnp.minimum((first + i + 1) * block, rows - 1)

    whole = pl.BlockSpec((block, layers, cells), lambda i: (here(i), 0, 0))
    triple = pl.BlockSpec((3, block, layers, cells), lambda i: (0, here(i), 0, 0))
    row = pl.BlockSpec((1, layers, cells), lambda i: (after(i), 0, 0))
    low = pl.BlockSpec((1, 5, layers, cells), lambda i: (2 * chunk_index, 0, 0, 0))
    high = pl.BlockSpec((1, 5, layers, cells), lambda i: (2 * chunk_index + 3, 0, 0, 0))
    edge = pl.BlockSpec((2, block, 1, cells), lambda i: (0, here(i), 0, 0))
    in_specs = [
        whole,
        triple,
        whole,
        whole,
        triple,
        pl.BlockSpec((3, 1, layers, cells), lambda i: (0, after(i), 0, 0)),
        row,
        row,
        pl.BlockSpec((1, 1, layers, cells), lambda i: (0, after(i), 0, 0)),
        low,
        high,
        edge,
        edge,
        pl.BlockSpec((2, cells, cells), lambda i: (0, 0, 0)),
    ]
    operands = [
        fraction, normals, planes, flags, courant,
        normals, planes, flags, courant,
        ends, ends, axial_flux, axial_speed, basis,
    ]
    aliases = {}
    if base is not None:
        in_specs.append(pl.BlockSpec(memory_space=pl.ANY))
        operands.append(base)
        aliases = {len(operands) - 1: 0}
    return pl.pallas_call(
        functools.partial(chunk_kernel, around, base is not None),
        grid=(steps,),
        in_specs=in_specs,
        out_specs=[
            whole,
            pl.BlockSpec((devices, share + 1, layers, chunk), lambda i: (0, 0, 0, 0)),
        ],
        out_shape=[
            jax.ShapeDtypeStruct(fraction.shape, F32),
            jax.ShapeDtypeStruct((devices, share + 1, layers, chunk), jnp.int16),
        ],
        scratch_shapes=[
            pltpu.VMEM((block + 2, 7, layers, cells), F32),
            pltpu.VMEM((2, layers, cells), F32),
            pltpu.VMEM((cells // 128, layers * chunk, 128), F32),
            pltpu.VMEM((cells * layers, chunk), F32),
            pltpu.VMEM((cells, chunk), F32),
        ],
        input_output_aliases=aliases,
        compiler_params=pltpu.CompilerParams(vmem_limit_bytes=48 * 2**20),
        cost_estimate=pl.CostEstimate(
            flops=40000 * chunk * layers * cells, bytes_accessed=30 * chunk * layers * cells, transcendentals=0
        ),
        name="advect_chunk",
    )(*operands)


@functools.lru_cache(None)
def folded_tables(total):
    quarter = total // 4
    place = np.arange(quarter) + 0.5

    def halves(x):
        high = x.astype(jnp.bfloat16)
        return np.stack([high, (x - high.astype(np.float64)).astype(jnp.bfloat16)])

    tables, rates, weights = [], [], []
    for waves, wave in (
        (2 * np.arange(quarter), np.cos),
        (2 * np.arange(quarter) + 2, np.sin),
        (2 * np.arange(quarter) + 1, np.cos),
        (2 * np.arange(quarter) + 1, np.sin),
    ):
        doubled = waves[:, None] * (2 * np.arange(quarter) + 1)[None, :] % (2 * total)
        tables.append(wave(np.pi * doubled / total))
        rates.append(2.0 - 2.0 * np.cos(2.0 * np.pi * waves / total))
        weights.append(np.where((waves == 0) | (waves == total // 2), 1.0, 2.0) / total)
    tables = np.stack(tables)
    back = np.stack([halves(t) for t in tables])
    forth = np.stack([halves(t.T) for t in tables])
    return forth, back, np.stack(rates)[:, None].astype(np.float32), np.stack(weights)[:, None].astype(np.float32)


def decoded(values):
    return values.astype(jnp.int32).astype(F32)


def scale_of(codes):
    return jnp.exp2(decoded(codes) * (1.0 / 256.0)) * (1.0 / CODE_TOP)


def solve_kernel(around, along, chunks, group, *refs):
    got = refs[:chunks]
    extra = refs[chunks : 2 * chunks]
    mix, unmix, forth_ref, back_ref, rates, weights, shifts = refs[2 * chunks : 2 * chunks + 7]
    sent, high, low, result, scale, exponents, forth, back, arrived = refs[2 * chunks + 7 :]
    copies = [
        pltpu.make_async_copy(forth_ref, forth, arrived.at[0]),
        pltpu.make_async_copy(back_ref, back, arrived.at[1]),
    ]

    @pl.when(pl.program_id(0) == 0)
    def _():
        for copy in copies:
            copy.start()

    devices, count, layers, lanes = got[0].shape
    share = (sent.shape[1] - 1) // chunks
    pairs = around // 4
    step = pl.program_id(0)
    first = group * share + step * count
    for chunk in range(chunks):
        scale[chunk] = scale_of(extra[chunk][:, 0])

    def spots():
        for pair in range(pairs):
            for chunk in range(chunks):
                mirror = chunks - 1 - chunk
                at = pl.ds((pair * chunks + chunk) * lanes, lanes)
                yield at, (
                    (pair, chunk),
                    (pair + 2 * pairs, chunk),
                    (2 * pairs - 1 - pair, mirror),
                    (4 * pairs - 1 - pair, mirror),
                )

    def fold(index, _):
        mode, axial = index // along, index % along
        rows = pl.ds(pl.multiple_of(index * layers, layers), layers)
        row = pl.ds(first + mode, 1)
        for at, places in spots():
            u0, u1, r0, r1 = [
                decoded(got[chunk][azim * along + axial, mode])
                * scale[chunk, azim * along + axial, row, :]
                for azim, chunk in places
            ]
            e0, o0, e1, o1 = u0 + u1, u0 - u1, r0 + r1, r0 - r1
            for k, folded in enumerate((e0 + e1, e0 - e1, o0 - o1, o0 + o1)):
                high[k, rows, at], low[k, rows, at] = split(folded)
        return 0

    lax.fori_loop(0, count * along, fold, 0)

    @pl.when(pl.program_id(0) == 0)
    def _():
        for copy in copies:
            copy.wait()

    height = mix.shape[1]
    parts = [pl.ds(at, height) for at in range(0, high.shape[1], height)]

    def waves(k, _):
        for at in parts:
            high[k, at], low[k, at] = split(
                dot3((mix[0], mix[1]), (high[k, at], low[k, at]))
            )
        spectrum = dot3((high[k], low[k]), (forth[k, 0], forth[k, 1]))
        high[k], low[k] = split(spectrum * weights[k] / (rates[k] + shifts[...]))
        high[k], low[k] = split(dot3((high[k], low[k]), (back[k, 0], back[k, 1])))
        for at in parts:
            result[k, at] = dot3((unmix[0], unmix[1]), (high[k, at], low[k, at]))
        return 0

    lax.fori_loop(0, 4, waves, 0)

    def unfold(index, _):
        mode, axial = index // along, index % along
        rows = pl.ds(pl.multiple_of(index * layers, layers), layers)
        for at, places in spots():
            ec, es, oc, os = [result[k, rows, at] for k in range(4)]
            e0, e1, o0, o1 = ec + es, ec - es, oc + os, os - oc
            for (azim, chunk), values in zip(places, (e0 + o0, e0 - o0, e1 + o1, e1 - o1)):
                device = azim * along + axial
                slot = chunk * share + step * count + mode
                exponent = exponent_of(jnp.max(jnp.abs(values), axis=0, keepdims=True))
                exponents[device, pl.ds(slot, 1), :] = exponent
                factor = CODE_TOP / jnp.exp2(exponent * (1.0 / 256.0))
                sent[device, slot] = to_codes(values * factor)
        return 0

    lax.fori_loop(0, count * along, unfold, 0)

    @pl.when(step == pl.num_programs(0) - 1)
    def _():
        sent[:, chunks * share] = exponents[...].astype(jnp.int32).astype(jnp.int16)


def solve_group(got, mix, unmix, tables, shifts, group, groups, around, along):
    chunks = len(got)
    devices, slots, layers, lanes = got[0].shape
    modes = slots - 1
    share = modes // groups
    count = share
    steps = share // count
    rows = count * along * layers
    forth, back, rates, weights = tables
    width = forth.shape[-1]

    def fixed(array):
        return pl.BlockSpec(array.shape, lambda i: (0,) * array.ndim, pipeline_mode=pl.Buffered(1))

    return pl.pallas_call(
        functools.partial(solve_kernel, around, along, chunks, group),
        grid=(steps,),
        in_specs=[
            pl.BlockSpec((devices, count, layers, lanes), lambda i: (0, group * steps + i, 0, 0))
        ]
        * chunks
        + [pl.BlockSpec((devices, 1, layers, lanes), lambda i: (0, modes, 0, 0))] * chunks
        + [fixed(mix), fixed(unmix)]
        + [pl.BlockSpec(memory_space=pl.ANY)] * 2
        + [fixed(rates), fixed(weights)]
        + [pl.BlockSpec((rows, 1), lambda i: (group * steps + i, 0))],
        out_specs=pl.BlockSpec((devices, slots, layers, lanes), lambda i: (0, 0, 0, 0)),
        out_shape=jax.ShapeDtypeStruct((devices, chunks * share + 1, layers, lanes), jnp.int16),
        scratch_shapes=[
            pltpu.VMEM((4, rows, width), BF16),
            pltpu.VMEM((4, rows, width), BF16),
            pltpu.VMEM((4, rows, width), F32),
            pltpu.VMEM((chunks, devices, layers, lanes), F32),
            pltpu.VMEM((devices, layers, lanes), F32),
            pltpu.VMEM(forth.shape, BF16),
            pltpu.VMEM(back.shape, BF16),
            pltpu.SemaphoreType.DMA((2,)),
        ],
        compiler_params=pltpu.CompilerParams(vmem_limit_bytes=48 * 2**20),
        cost_estimate=pl.CostEstimate(
            flops=60 * rows * width * width * steps, bytes_accessed=20 * 2**20, transcendentals=0
        ),
        name="solve_group",
    )(*got, *got, mix, unmix, forth, back, rates, weights, shifts)


def pressure_kernel(around, groups, *refs):
    got = refs[:groups]
    extra = refs[groups : 2 * groups]
    basis, out, flat, wide, scale, high, low = refs[2 * groups :]
    devices, share, layers, lanes = got[0].shape
    lane_tiles = out.shape[2] // 128
    chunk = pl.program_id(0)
    backwards = lax.rem(lax.axis_index("azim"), around // 2) >= around // 4
    i = lax.broadcasted_iota(jnp.int32, (lanes, lanes), 0)
    j = lax.broadcasted_iota(jnp.int32, (lanes, lanes), 1)
    turned_place = jnp.where(backwards, lanes - 1, 0) + jnp.where(backwards, -1, 1) * i
    turn = jnp.where(j == turned_place, 1.0, 0.0).astype(BF16)
    for group in range(groups):
        scale[group] = scale_of(extra[group][:, 0])

        def unpack(device, _, group=group):
            for mode in range(share):
                at = pl.multiple_of((device * share + mode) * layers, layers)
                flat[group, pl.ds(at, layers), :] = (
                    decoded(got[group][device, mode])
                    * scale[group, device, pl.ds(chunk * share + mode, 1), :]
                )
            return 0

        lax.fori_loop(0, devices, unpack, 0)

    together = high.shape[0] // lanes

    def radial(batch, _):
        for part in range(together):
            for group in range(groups):
                z = batch * together + part
                values = split(flat[group, pl.ds(z, devices * share, stride=layers), :])
                at = pl.ds(group * devices * share, devices * share)
                for target, value in zip((high, low), values):
                    target[part * lanes : (part + 1) * lanes, at] = dot(
                        turn, value, ((1,), (1,))
                    ).astype(BF16)
        total = dot3((high[...], low[...]), (basis[0], basis[1]))
        for part in range(together):
            for tile in range(lane_tiles):
                wide[tile, pl.ds(batch * together + part, lanes, stride=layers), :] = total[
                    part * lanes : (part + 1) * lanes, tile * 128 : (tile + 1) * 128
                ]
        return 0

    lax.fori_loop(0, layers // together, radial, 0)
    for tile in range(lane_tiles):
        out[:, :, tile * 128 : (tile + 1) * 128] = wide[tile].reshape(lanes, layers, 128)


def pressure_of(got, basis, around, chunks):
    groups = len(got)
    devices, slots, layers, lanes = got[0].shape
    share = (slots - 1) // chunks
    cells = basis.shape[-1]
    return pl.pallas_call(
        functools.partial(pressure_kernel, around, groups),
        grid=(chunks,),
        in_specs=[pl.BlockSpec((devices, share, layers, lanes), lambda i: (0, i, 0, 0))] * groups
        + [pl.BlockSpec((devices, 1, layers, lanes), lambda i: (0, chunks * share, 0, 0))] * groups
        + [
            pl.BlockSpec(
                basis.shape, lambda i: (0,) * basis.ndim, pipeline_mode=pl.Buffered(1)
            )
        ],
        out_specs=pl.BlockSpec((lanes, layers, cells), lambda i: (i, 0, 0)),
        out_shape=jax.ShapeDtypeStruct((lanes * chunks, layers, cells), F32),
        scratch_shapes=[
            pltpu.VMEM((groups, devices * share * layers, lanes), F32),
            pltpu.VMEM((cells // 128, lanes * layers, 128), F32),
            pltpu.VMEM((groups, devices, layers, lanes), F32),
            pltpu.VMEM((4 * lanes, groups * devices * share), BF16),
            pltpu.VMEM((4 * lanes, groups * devices * share), BF16),
        ],
        compiler_params=pltpu.CompilerParams(vmem_limit_bytes=48 * 2**20),
        name="pressure_of",
    )(*got, *got, basis)


def halves(values):
    high = lax.reduce_precision(values, 8, 7)
    return jnp.stack([high.astype(BF16), (values - high).astype(BF16)])


def exchanged(sent):
    return lax.all_to_all(sent, ("azim", "axial"), split_axis=0, concat_axis=0, tiled=True)


def following_kernel(values_ref, earlier_ref, out_ref):
    del values_ref, earlier_ref, out_ref


def following(values, earlier):
    anywhere = pl.BlockSpec(memory_space=pl.ANY)
    return pl.pallas_call(
        following_kernel,
        in_specs=[anywhere, anywhere],
        out_specs=anywhere,
        out_shape=jax.ShapeDtypeStruct(values.shape, values.dtype),
        input_output_aliases={0: 0},
        name="following",
    )(values, earlier)


def overlapped(
    fraction,
    normals,
    planes,
    cell_flags,
    courant,
    radial_basis,
    axial_basis,
    radial_rates,
    axial_rates,
):
    rows, layers, cells = fraction.shape
    around, along = lax.axis_size("azim"), lax.axis_size("axial")
    devices = around * along
    modes = cells // devices
    chunks, groups = rows // CHUNK, 2
    edge = edge_speeds(courant)
    below = shifted_in(edge[1], "axial", False)
    above = shifted_in(edge[0], "axial", True)
    packs = packed_rows(normals, planes, cell_flags, courant, CHUNK)
    low_row = shifted_in(packs[-1:], "azim", False)
    high_row = shifted_in(packs[:1], "azim", True)
    fields = edge_fields(normals, planes, cell_flags)
    own, code, speed = donors(fields, edge, below, above)
    from_below = shifted_in(code[1], "axial", False)
    from_above = shifted_in(code[0], "axial", True)
    axial_flux = own + jnp.stack([from_below, from_above]).astype(F32) * (1.0 / FLUX_SCALE)
    axial_flux, axial_speed = axial_flux[:, :, None], speed[:, :, None]
    forward_basis = halves(radial_basis.T)
    arrays = (fraction, normals, planes, cell_flags, courant)
    updated, got = None, []
    ends = jnp.concatenate([low_row, packs, high_row])
    for chunk in range(chunks):
        updated, sent = advect_chunk(
            arrays, ends, axial_flux, axial_speed, forward_basis, chunk, CHUNK, around, devices, updated
        )
        got.append(exchanged(following(sent, got[-1]) if got else sent))
    count = jnp.eye(4, dtype=F32)
    mix, unmix = halves(jnp.kron(count, axial_basis.T)), halves(jnp.kron(count, axial_basis))
    first = (lax.axis_index("azim") * along + lax.axis_index("axial")) * modes
    shifts = lax.dynamic_slice_in_dim(radial_rates, first, modes)[:, None] + axial_rates[None, :]
    shifts = shifts.reshape(modes * along * layers, 1)
    tables = [jnp.asarray(x) for x in folded_tables(rows * around)]
    returned = []
    for group in range(groups):
        sent = solve_group(got, mix, unmix, tables, shifts, group, groups, around, along)
        returned.append(exchanged(sent))
    back_basis = radial_basis.T.reshape(devices, groups, modes // groups, cells)
    back_basis = halves(back_basis.transpose(1, 0, 2, 3).reshape(-1, cells))
    pressure = pressure_of(returned, back_basis, around, chunks)
    return (updated, pressure)


def fits(fraction):
    rows, layers, cells = fraction.shape
    around, along = lax.axis_size("azim"), lax.axis_size("axial")
    modes = cells // (around * along)
    chunks = rows // CHUNK
    return (
        rows % CHUNK == 0
        and layers == 16
        and modes == 16
        and modes // 2 * chunks == layers
        and cells % 128 == 0
        and around % 4 == 0
    )


def local(*arguments):
    return overlapped(*arguments) if fits(arguments[0]) else stepwise(*arguments)


def solution(mesh):
    placed = (
        P("azim", "axial", None),
        P(None, "azim", "axial", None),
        P("azim", "axial", None),
        P("azim", "axial", None),
        P(None, "azim", "axial", None),
        P(),
        P(),
        P(),
        P(),
    )
    return jax.shard_map(
        local,
        mesh=mesh,
        in_specs=placed,
        out_specs=(P("azim", "axial", None), P("azim", "axial", None)),
        check_vma=False,
    )
```

```python
import functools

import jax
import jax.numpy as jnp
import numpy as np
from jax import lax
from jax.experimental import pallas as pl
from jax.experimental.pallas import tpu as pltpu
from jax.sharding import PartitionSpec as P

HIGH = lax.Precision.HIGH
BUOYANCY = 0.5
CODE_TOP = 32700.0


def shifted_in(edge, axis, towards_lower):
    count = lax.axis_size(axis)
    if towards_lower:
        pairs = [((i + 1) % count, i) for i in range(count)]
    else:
        pairs = [(i, (i + 1) % count) for i in range(count)]
    return lax.ppermute(edge, axis, pairs)


def cell_parts(n0, n1, n2, code):
    m0, m1, m2 = jnp.abs(n0), jnp.abs(n1), jnp.abs(n2)
    return (n0, n1, n2, code, 1.0 / (6.0 * m0 * m1 * m2))


def cube(height):
    held = jnp.maximum(height, 0.0)
    return held * held * held


def face_flux(direction, lower, upper, speed, lower_weight=None, upper_weight=None):
    forward = speed > 0.0
    signed = jnp.where(forward, lower[direction], -upper[direction])
    first, second = [d for d in range(3) if d != direction]
    along = jnp.abs(signed)
    side_a = jnp.abs(jnp.where(forward, lower[first], upper[first]))
    side_b = jnp.abs(jnp.where(forward, lower[second], upper[second]))
    code = jnp.where(forward, lower[3], upper[3])
    inverse = jnp.where(forward, lower[4], upper[4])
    width = jnp.abs(speed)
    near = code - along * jnp.where(signed < 0.0, 0.0, 1.0 - width)
    far = near - along * width
    sides = side_a + side_b
    total = (cube(near) - cube(near - side_a)) - (cube(near - side_b) - cube(near - sides))
    total = total - ((cube(far) - cube(far - side_a)) - (cube(far - side_b) - cube(far - sides)))
    volume = jnp.where(code > 3.0, width, jnp.where(code < -0.5, 0.0, total * inverse))
    if lower_weight is not None:
        volume = volume * jnp.where(forward, lower_weight, upper_weight)
    return jnp.where(forward, volume, jnp.where(speed < 0.0, -volume, 0.0))


def advect_kernel(
    fraction_ref,
    normals_ref,
    planes_ref,
    flags_ref,
    courant_ref,
    next_ref,
    high_ref,
    low_azim_ref,
    low_axial_ref,
    updated_ref,
    source_ref,
    kept,
):
    rows, layers, cells = fraction_ref.shape
    f32 = jnp.float32

    @pl.when(pl.program_id(0) == 0)
    def _():
        kept[...] = low_azim_ref[...]

    index = lax.broadcasted_iota(jnp.int32, (1, cells), 1)
    place = index.astype(f32)
    radius = 1.0 + (place + 0.5) / cells
    next_radius = 1.0 + (place + 1.5) / cells
    face_radius = 1.0 + (place + 1.0) / cells
    inverse_radius = 1.0 / radius
    inner = lax.broadcasted_iota(jnp.int32, (layers, cells), 1) < cells - 1
    layer = lax.broadcasted_iota(jnp.int32, (layers, cells), 0)
    last_layer = layer == layers - 1
    first_layer = layer == 0

    def row_parts(row):
        flags = flags_ref[row]
        code = jnp.where(
            flags == 2, planes_ref[row].astype(f32), jnp.where(flags == 1, 4.0, -1.0)
        )
        return cell_parts(
            normals_ref[0, row].astype(f32),
            normals_ref[1, row].astype(f32),
            normals_ref[2, row].astype(f32),
            code,
        )

    def one_row(row, upper, upper_speed):
        own = row_parts(row)
        moved = [courant_ref[d, row].astype(f32) for d in range(3)]
        speed = 0.5 * (moved[0] + upper_speed)
        flux = face_flux(0, own, upper, speed)
        gained = flux - kept[0]
        divergence = speed - kept[1]
        kept[0] = flux
        kept[1] = speed
        beyond = cell_parts(*[high_ref[k, row] for k in range(4)])
        above = [
            jnp.where(last_layer, high, pltpu.roll(field, layers - 1, 0))
            for field, high in zip(own, beyond)
        ]
        speed = 0.5 * (
            moved[1]
            + jnp.where(last_layer, high_ref[4, row], pltpu.roll(moved[1], layers - 1, 0))
        )
        flux = face_flux(1, own, above, speed)
        gained = gained + (
            flux - jnp.where(first_layer, low_axial_ref[0, row], pltpu.roll(flux, 1, 0))
        )
        divergence = divergence + (
            speed - jnp.where(first_layer, low_axial_ref[1, row], pltpu.roll(speed, 1, 0))
        )
        outer = [pltpu.roll(field, cells - 1, 1) for field in own]
        speed = 0.5 * (moved[2] + pltpu.roll(moved[2], cells - 1, 1))
        speed = jnp.where(inner, speed, 0.0)
        flux = face_flux(2, own, outer, speed, radius, next_radius)
        gained = gained + (flux - pltpu.roll(flux, 1, 1)) * inverse_radius
        carried = face_radius * speed
        divergence = divergence + (carried - pltpu.roll(carried, 1, 1)) * inverse_radius
        updated = fraction_ref[row] - gained
        updated_ref[row] = updated
        source_ref[row] = divergence + BUOYANCY * updated

    def step(row, _):
        one_row(row, row_parts(row + 1), courant_ref[0, row + 1].astype(f32))
        return 0

    lax.fori_loop(0, rows - 1, step, 0)
    one_row(
        rows - 1,
        cell_parts(*[next_ref[k, 0].astype(f32) for k in range(4)]),
        next_ref[4, 0].astype(f32),
    )


def plane_codes(planes, flags):
    return jnp.where(
        flags == 2, planes.astype(jnp.float32), jnp.where(flags == 1, 4.0, -1.0)
    ).astype(jnp.bfloat16)


def packed_edge(normals, planes, flags, courant, direction, pick):
    parts = [pick(normals[d]) for d in range(3)]
    parts.append(plane_codes(pick(planes), pick(flags)))
    parts.append(pick(courant[direction]))
    return jnp.stack(parts)


def low_face(direction, lower, upper):
    lower, upper = lower.astype(jnp.float32), upper.astype(jnp.float32)
    speed = 0.5 * (lower[4] + upper[4])
    flux = face_flux(direction, cell_parts(*lower[:4]), cell_parts(*upper[:4]), speed)
    return jnp.stack([flux, speed])


def advect(fraction, normals, planes, flags, courant):
    rows, layers, cells = fraction.shape
    block = 16 if rows % 16 == 0 else 1
    blocks = rows // block
    fields = (normals, planes, flags, courant)
    top_row = packed_edge(*fields, 0, lambda x: x[rows - 1])
    bottom_row = packed_edge(*fields, 0, lambda x: x[0])
    top_layer = packed_edge(*fields, 1, lambda x: x[:, layers - 1])
    bottom_layer = packed_edge(*fields, 1, lambda x: x[:, 0])
    high_row = shifted_in(bottom_row, "azim", True)
    low_row = shifted_in(top_row, "azim", False)
    high_layer = shifted_in(bottom_layer, "axial", True)
    low_layer = shifted_in(top_layer, "axial", False)
    low_azim = low_face(0, low_row, bottom_row)
    low_axial = low_face(1, low_layer, bottom_layer)[:, :, None]
    high_axial = high_layer.astype(jnp.float32)[:, :, None]
    inside = packed_edge(*fields, 0, lambda x: x[block::block])
    following = jnp.concatenate([inside, high_row[:, None]], axis=1)
    whole = pl.BlockSpec((block, layers, cells), lambda i: (i, 0, 0))
    triple = pl.BlockSpec((3, block, layers, cells), lambda i: (0, i, 0, 0))
    return pl.pallas_call(
        advect_kernel,
        grid=(blocks,),
        in_specs=[
            whole,
            triple,
            whole,
            whole,
            triple,
            pl.BlockSpec((5, 1, layers, cells), lambda i: (0, i, 0, 0)),
            pl.BlockSpec((5, block, 1, cells), lambda i: (0, i, 0, 0)),
            pl.BlockSpec((2, layers, cells), lambda i: (0, 0, 0)),
            pl.BlockSpec((2, block, 1, cells), lambda i: (0, i, 0, 0)),
        ],
        out_specs=[whole, whole],
        out_shape=[jax.ShapeDtypeStruct(fraction.shape, jnp.float32)] * 2,
        scratch_shapes=[pltpu.VMEM((2, layers, cells), jnp.float32)],
        compiler_params=pltpu.CompilerParams(vmem_limit_bytes=40 * 2**20),
    )(
        fraction,
        normals,
        planes,
        flags,
        courant,
        following,
        high_axial,
        low_azim,
        low_axial,
    )


def coded(values):
    most = jnp.max(jnp.abs(values), axis=-1)
    exponent = jnp.clip(jnp.ceil(jnp.log2(most) * 256.0) + 1.0, -30000.0, 30000.0)
    scale = CODE_TOP * jnp.exp2(exponent * (-1.0 / 256.0))
    codes = jnp.round(values * scale[..., None])
    return jnp.clip(codes, -32767.0, 32767.0).astype(jnp.int16), exponent.astype(jnp.int16)


def exchange(values):
    modes, cells = values.shape[1], values.shape[3]
    codes, exponent = coded(values)
    extra = jnp.pad(exponent.transpose(0, 2, 1), ((0, 0), (0, 0), (0, cells - modes)))
    sent = jnp.concatenate([codes, extra[:, None]], axis=1)
    got = lax.all_to_all(sent, ("azim", "axial"), split_axis=0, concat_axis=0, tiled=True)
    exponent = got[:, modes, :, :modes].transpose(0, 2, 1).astype(jnp.float32)
    scale = jnp.exp2(exponent * (1.0 / 256.0)) * (1.0 / CODE_TOP)
    return got[:, :modes].astype(jnp.float32) * scale[..., None]


@functools.lru_cache(None)
def azimuth_tables(total):
    half, quarter = total // 2, total // 4
    place = np.arange(half)

    def table(cosines, sines):
        waves = np.concatenate([cosines, sines])
        angles = 2.0 * np.pi / total * (waves[:, None] * place[None, :] % total)
        rows = np.concatenate(
            [np.cos(angles[: len(cosines)]), np.sin(angles[len(cosines) :])]
        ).astype(np.float32)
        rates = (2.0 - 2.0 * np.cos(2.0 * np.pi * waves / total)).astype(np.float32)
        ends = (waves == 0) | (waves == half)
        return rows, rates, (np.where(ends, 1.0, 2.0) / total).astype(np.float32)

    even = 2 * np.arange(quarter + 1)
    odd = 2 * np.arange(quarter) + 1
    return table(even, even[1:-1]), table(odd, odd)


def stepwise(
    fraction,
    normals,
    planes,
    cell_flags,
    courant,
    radial_basis,
    axial_basis,
    radial_rates,
    axial_rates,
):
    rows, layers, cells = fraction.shape
    around, along = lax.axis_size("azim"), lax.axis_size("axial")
    devices = around * along
    modes = cells // devices
    total = rows * around
    half = total // 2
    updated, source = advect(fraction, normals, planes, cell_flags, courant)
    radial_modes = jnp.einsum("azr,rj->jza", source, radial_basis, precision=HIGH)
    got = exchange(radial_modes.reshape(devices, modes, layers, rows))
    got = got.reshape(around, along, modes, layers, rows).transpose(2, 1, 3, 0, 4)
    got = got.reshape(modes, along * layers, total)
    both = jnp.einsum("jza,zn->jna", got, axial_basis, precision=HIGH)
    first = (lax.axis_index("azim") * along + lax.axis_index("axial")) * modes
    shifts = lax.dynamic_slice_in_dim(radial_rates, first, modes)[:, None] + axial_rates[None, :]
    low, high = both[..., :half], both[..., half:]
    solved = []
    for folded, (table, rates, weight) in zip((low + high, low - high), azimuth_tables(total)):
        coefficients = jnp.einsum("jna,ka->jnk", folded, table, precision=HIGH)
        scaled = coefficients / (rates + shifts[..., None]) * weight
        solved.append(jnp.einsum("jnk,ka->jna", scaled, table, precision=HIGH))
    physical = jnp.concatenate([solved[0] + solved[1], solved[0] - solved[1]], axis=-1)
    physical = jnp.einsum("jna,zn->jza", physical, axial_basis, precision=HIGH)
    physical = physical.reshape(modes, along, layers, around, rows).transpose(3, 1, 0, 2, 4)
    returned = exchange(physical.reshape(devices, modes, layers, rows))
    returned = returned.reshape(cells, layers, rows)
    pressure = jnp.einsum("jza,rj->azr", returned, radial_basis, precision=HIGH)
    return (updated, pressure)


CHUNK = 128
BLOCK = 16
FLUX_SCALE = 32767.0 / 0.3
F32 = jnp.float32
BF16 = jnp.bfloat16


def split(values):
    high = values.astype(BF16)
    return high, (values - high.astype(F32)).astype(BF16)


def dot(a, b, contract):
    return lax.dot_general(a, b, (contract, ((), ())), preferred_element_type=F32)


def dot3(a, b, contract=((1,), (0,))):
    return dot(a[0], b[0], contract) + (dot(a[0], b[1], contract) + dot(a[1], b[0], contract))


def slab_flux(normal, side_a, side_b, plane, inverse, speed):
    along = jnp.abs(normal)
    reach = normal * speed
    slab = jnp.abs(reach)
    near = plane - jnp.where(reach > 0.0, along - slab, 0.0)
    other = (slab + (side_a + side_b)) - near
    folded = near > other
    held = jnp.maximum(jnp.minimum(near, other), 0.0)
    low, high = jnp.minimum(side_a, side_b), jnp.maximum(side_a, side_b)
    by_low = jnp.maximum(held - low, 0.0)
    by_slab = jnp.maximum(held - slab, 0.0)
    last = jnp.maximum(held - (low + slab), 0.0) - jnp.maximum(held - high, 0.0)
    total = held * held * held - by_slab * by_slab * by_slab
    total = total - (by_low * by_low * by_low - last * last * last)
    flux = total * inverse
    return jnp.where(folded, speed - flux, flux)


def upwind_flux(direction, lower, upper, speed, lower_weight=None, upper_weight=None):
    forward = speed > 0.0
    first, second = [d for d in range(3) if d != direction]
    normal = jnp.where(forward, lower[direction], upper[direction])
    side_a = jnp.abs(jnp.where(forward, lower[first], upper[first]))
    side_b = jnp.abs(jnp.where(forward, lower[second], upper[second]))
    plane = jnp.where(forward, lower[3], upper[3])
    inverse = jnp.where(forward, lower[4], upper[5])
    flux = slab_flux(normal, side_a, side_b, plane, inverse, speed)
    if lower_weight is not None:
        flux = flux * jnp.where(forward, lower_weight, upper_weight)
    return flux


def inverse_of(n0, n1, n2):
    return 1.0 / (6.0 * jnp.abs(n0 * n1 * n2))


def plane_value(planes, flags):
    return jnp.where(flags == 2, planes.astype(F32), jnp.where(flags == 1, 4.0, -4.0))


def halo_kernel(
    courant_ref,
    normals_ref,
    planes_ref,
    flags_ref,
    first_normals_ref,
    first_planes_ref,
    first_flags_ref,
    first_courant_ref,
    last_normals_ref,
    last_planes_ref,
    last_flags_ref,
    last_courant_ref,
    flux_ref,
    speed_ref,
    ends_ref,
    work,
    edge,
    edge_in,
    fields,
    code,
    code_in,
    packs,
    packs_in,
    row_send,
    row_recv,
    edge_send,
    edge_recv,
    code_send,
    code_recv,
):
    step = pl.program_id(0)
    half = pl.num_programs(0) // 2
    span, layers, cells = planes_ref.shape
    groups, group = code_send.shape[1], code.shape[2]
    tiles = cells // 128
    neighbours = []
    for axis in ("azim", "axial"):
        count, me = lax.axis_size(axis), lax.axis_index(axis)
        neighbours.append(
            ({axis: lax.rem(me + count - 1, count)}, {axis: lax.rem(me + 1, count)})
        )

    def remote(source, target, send, recv, device):
        return pltpu.make_async_remote_copy(
            src_ref=source,
            dst_ref=target,
            send_sem=send,
            recv_sem=recv,
            device_id=device,
            device_id_type=pl.DeviceIdType.MESH,
        )

    row_copies = [
        remote(packs.at[s], packs_in.at[1 - s], row_send.at[s], row_recv.at[1 - s], neighbours[0][s])
        for s in range(2)
    ]
    edge_copies = [
        remote(edge.at[s], edge_in.at[1 - s], edge_send.at[s], edge_recv.at[1 - s], neighbours[1][s])
        for s in range(2)
    ]

    def code_copy(s, g):
        return remote(
            code.at[s, g],
            code_in.at[1 - s, g],
            code_send.at[s, g],
            code_recv.at[1 - s, g],
            neighbours[1][s],
        )

    @pl.when(step == 0)
    def _():
        barrier = pltpu.get_barrier_semaphore()
        for pair in neighbours:
            for device in pair:
                pl.semaphore_signal(
                    barrier, inc=1, device_id=device, device_id_type=pl.DeviceIdType.MESH
                )
        pl.semaphore_wait(barrier, 4)
        for s, (normals, planes, flags, courant) in enumerate(
            (
                (first_normals_ref, first_planes_ref, first_flags_ref, first_courant_ref),
                (last_normals_ref, last_planes_ref, last_flags_ref, last_courant_ref),
            )
        ):
            for k in range(3):
                packs[s, k] = normals[k, 0]
            packs[s, 3] = plane_value(planes[0], flags[0]).astype(BF16)
            packs[s, 4] = courant[0, 0]
        for copy in row_copies:
            copy.start()

    def layer_rows(tile, layer):
        return work[tile, pl.ds(layer, span, stride=layers), :]

    @pl.when(step < half)
    def _():
        at = pl.ds(pl.multiple_of(step * span, span), span)
        for tile in range(tiles):
            lanes = pl.ds(tile * 128, 128)
            work[tile] = courant_ref[0, :, :, lanes].astype(F32).reshape(span * layers, 128)
            for s, layer in ((0, 0), (1, layers - 1)):
                edge[s, at, lanes] = layer_rows(tile, layer).astype(BF16)

    @pl.when(step == half - 1)
    def _():
        for copy in edge_copies:
            copy.start()

    @pl.when(step >= half)
    def _():
        at = pl.ds(pl.multiple_of((step - half) * span, span), span)
        for k in range(4):
            for tile in range(tiles):
                lanes = pl.ds(tile * 128, 128)
                if k < 3:
                    field = normals_ref[k, :, :, lanes].astype(F32)
                else:
                    field = plane_value(planes_ref[:, :, lanes], flags_ref[:, :, lanes])
                work[tile] = field.reshape(span * layers, 128)
                for s, layer in ((0, 0), (1, layers - 1)):
                    fields[s, k, at, lanes] = layer_rows(tile, layer)

    @pl.when(step == 2 * half - 1)
    def _():
        for copy in edge_copies:
            copy.wait()
        for g in range(groups):
            for s in range(2):

                def donate(piece, _, g=g, s=s):
                    inside = pl.ds(pl.multiple_of(piece * 16, 16), 16)
                    at = pl.ds(pl.multiple_of(g * group + piece * 16, 16), 16)
                    normals = [fields[s, k, at, :] for k in range(3)]
                    speed = 0.5 * (edge[s, at, :].astype(F32) + edge_in[s, at, :].astype(F32))
                    inverse = inverse_of(*normals)
                    flux = slab_flux(
                        normals[1],
                        jnp.abs(normals[0]),
                        jnp.abs(normals[2]),
                        fields[s, 3, at, :],
                        inverse if s == 1 else -inverse,
                        speed,
                    )
                    flux = jnp.where(speed > 0.0 if s == 1 else speed < 0.0, flux, 0.0)
                    flux_ref[s, at, :] = flux
                    speed_ref[s, at, :] = speed
                    code[s, g, inside, :] = to_codes(flux * FLUX_SCALE)
                    return 0

                lax.fori_loop(0, group // 16, donate, 0)
                code_copy(s, g).start()
        for copy in row_copies:
            copy.wait()
        ends_ref[...] = packs_in[...]
        for g in range(groups):
            for s in range(2):
                code_copy(s, g).wait()
            for s in range(2):
                at = pl.ds(g * group, group)
                received = code_in[s, g].astype(jnp.int32).astype(F32)
                flux_ref[s, at, :] += received * (1.0 / FLUX_SCALE)


def halos(normals, planes, flags, courant):
    rows, layers, cells = planes.shape
    span, groups = 32, 4
    half = rows // span

    def later(i):
        return jnp.maximum(i - half, 0)

    whole = pl.BlockSpec((span, layers, cells), lambda i: (later(i), 0, 0))
    in_specs = [
        pl.BlockSpec((1, span, layers, cells), lambda i: (1, jnp.minimum(i, half - 1), 0, 0)),
        pl.BlockSpec((3, span, layers, cells), lambda i: (0, later(i), 0, 0)),
        whole,
        whole,
    ]
    for row in (0, rows - 1):
        one = pl.BlockSpec((1, layers, cells), lambda i, row=row: (row, 0, 0))
        in_specs += [
            pl.BlockSpec((3, 1, layers, cells), lambda i, row=row: (0, row, 0, 0)),
            one,
            one,
            pl.BlockSpec((1, 1, layers, cells), lambda i, row=row: (0, row, 0, 0)),
        ]
    pair = pl.BlockSpec((2, rows, cells), lambda i: (0, 0, 0))
    ends = (2, 5, layers, cells)
    split_shape = (2, groups, rows // groups, cells)
    dma = pltpu.SemaphoreType.DMA
    return pl.pallas_call(
        halo_kernel,
        grid=(2 * half,),
        in_specs=in_specs,
        out_specs=[pair, pair, pl.BlockSpec(ends, lambda i: (0, 0, 0, 0))],
        out_shape=[
            jax.ShapeDtypeStruct((2, rows, cells), F32),
            jax.ShapeDtypeStruct((2, rows, cells), F32),
            jax.ShapeDtypeStruct(ends, BF16),
        ],
        scratch_shapes=[
            pltpu.VMEM((cells // 128, span * layers, 128), F32),
            pltpu.VMEM((2, rows, cells), BF16),
            pltpu.VMEM((2, rows, cells), BF16),
            pltpu.VMEM((2, 4, rows, cells), F32),
            pltpu.VMEM(split_shape, jnp.int16),
            pltpu.VMEM(split_shape, jnp.int16),
            pltpu.VMEM(ends, BF16),
            pltpu.VMEM(ends, BF16),
            dma((2,)),
            dma((2,)),
            dma((2,)),
            dma((2,)),
            dma((2, groups)),
            dma((2, groups)),
        ],
        compiler_params=pltpu.CompilerParams(
            collective_id=0, has_side_effects=True, vmem_limit_bytes=60 * 2**20
        ),
        name="halos",
    )(courant, normals, planes, flags, *(normals, planes, flags, courant) * 2)


def exponent_of(most):
    return jnp.clip(jnp.ceil(jnp.log2(jnp.maximum(most, 1e-29)) * 256.0) + 1.0, -25000.0, 30000.0)


def to_codes(values):
    return jnp.round(values).astype(jnp.int32).astype(jnp.int16)


def chunk_kernel(
    around,
    chunk_index,
    chunks,
    fraction_ref,
    normals_ref,
    planes_ref,
    flags_ref,
    courant_ref,
    next_normals_ref,
    next_planes_ref,
    next_flags_ref,
    next_courant_ref,
    last_normals_ref,
    last_planes_ref,
    last_flags_ref,
    last_courant_ref,
    ends_ref,
    axial_flux_ref,
    axial_speed_ref,
    basis_ref,
    *rest,
):
    if chunk_index:
        rest = rest[1:]
    updated_ref, sent_ref, parts, kept, source, wide, scales = rest
    block, layers, cells = fraction_ref.shape
    steps = pl.num_programs(0)
    step = pl.program_id(0)
    chunk = source.shape[1] // layers
    lane_tiles = cells // 128
    backwards = lax.rem(lax.axis_index("azim"), around // 2) >= around // 4

    def put_field(slot, k, value):
        at = pl.ds(pl.multiple_of(slot * layers, layers), layers)
        for tile in range(lane_tiles):
            parts[k, tile, at, :] = value[:, tile * 128 : (tile + 1) * 128]

    def get_field(slot, k, shift=0):
        at = pl.ds(slot * layers + shift, layers)
        return jnp.concatenate([parts[k, tile, at, :] for tile in range(lane_tiles)], axis=1)

    def put_parts(slot, normals, plane, speed):
        inverse = inverse_of(*normals)
        for k, value in enumerate((*normals, plane, inverse, -inverse, 0.5 * speed)):
            put_field(slot, k, value)

    def put_packed(slot, side):
        values = [ends_ref[side, k].astype(F32) for k in range(5)]
        put_parts(slot, values[:3], values[3], values[4])

    def own_parts(row, _):
        put_parts(
            row,
            [normals_ref[k, row].astype(F32) for k in range(3)],
            plane_value(planes_ref[row], flags_ref[row]),
            courant_ref[0, row].astype(F32),
        )
        put_field(row, 7, 0.5 * courant_ref[1, row].astype(F32))
        return 0

    lax.fori_loop(0, block, own_parts, 0, unroll=2)

    def put_row(slot, normals, planes, flags, courant):
        put_parts(
            slot,
            [normals[k, 0].astype(F32) for k in range(3)],
            plane_value(planes[0], flags[0]),
            courant[0, 0].astype(F32),
        )

    def put_next():
        put_row(block, next_normals_ref, next_planes_ref, next_flags_ref, next_courant_ref)

    if chunk_index < chunks - 1:
        put_next()
    else:
        pl.when(step < steps - 1)(put_next)

        @pl.when(step == steps - 1)
        def _():
            put_packed(block, 1)

    def read_parts(slot):
        return [get_field(slot, k) for k in range(6)]

    @pl.when(step == 0)
    def _():
        if chunk_index == 0:
            put_packed(block + 1, 0)
        else:
            put_row(
                block + 1, last_normals_ref, last_planes_ref, last_flags_ref, last_courant_ref
            )
        speed = get_field(block + 1, 6) + get_field(0, 6)
        kept[0] = upwind_flux(0, read_parts(block + 1), read_parts(0), speed)
        kept[1] = speed

    index = lax.broadcasted_iota(jnp.int32, (1, cells), 1)
    place = index.astype(F32)
    radius = 1.0 + (place + 0.5) / cells
    next_radius = 1.0 + (place + 1.5) / cells
    face_radius = 1.0 + (place + 1.0) / cells
    inverse_radius = 1.0 / radius
    inner = lax.broadcasted_iota(jnp.int32, (layers, cells), 1) < cells - 1
    layer = lax.broadcasted_iota(jnp.int32, (layers, cells), 0)
    last_layer = layer == layers - 1
    first_layer = layer == 0

    def one_row(row, _):
        own = read_parts(row)
        speed = get_field(row, 6) + get_field(row + 1, 6)
        flux = upwind_flux(0, own, read_parts(row + 1), speed)
        gained = flux - kept[0]
        divergence = speed - kept[1]
        kept[0] = flux
        kept[1] = speed

        above = [None if k == 4 else get_field(row, k, 1) for k in range(6)]
        speed = get_field(row, 7) + get_field(row, 7, 1)
        flux = upwind_flux(1, own, above, speed)
        flux = jnp.where(last_layer, axial_flux_ref[1, pl.ds(row, 1), :], flux)
        speed = jnp.where(last_layer, axial_speed_ref[1, pl.ds(row, 1), :], speed)
        gained = gained + (
            flux - jnp.where(first_layer, axial_flux_ref[0, pl.ds(row, 1), :], pltpu.roll(flux, 1, 0))
        )
        divergence = divergence + (
            speed - jnp.where(first_layer, axial_speed_ref[0, pl.ds(row, 1), :], pltpu.roll(speed, 1, 0))
        )

        half = 0.5 * courant_ref[2, row].astype(F32)
        outer = [None if k == 4 else pltpu.roll(field, cells - 1, 1) for k, field in enumerate(own)]
        speed = jnp.where(inner, half + pltpu.roll(half, cells - 1, 1), 0.0)
        flux = upwind_flux(2, own, outer, speed, radius, next_radius)
        gained = gained + (flux - pltpu.roll(flux, 1, 1)) * inverse_radius
        carried = face_radius * speed
        divergence = divergence + (carried - pltpu.roll(carried, 1, 1)) * inverse_radius
        updated = fraction_ref[row] - gained
        updated_ref[row] = updated
        result = divergence + BUOYANCY * updated
        at = step * block + row
        at = jnp.where(backwards, chunk - 1 - at, at)
        for tile in range(lane_tiles):
            source[tile, pl.ds(at, layers, stride=chunk), :] = result[
                :, tile * 128 : (tile + 1) * 128
            ]
        return 0

    lax.fori_loop(0, block, one_row, 0, unroll=2)

    @pl.when(step == steps - 1)
    def _():
        modes = basis_ref.shape[1]
        scales[...] = jnp.zeros_like(scales)

        def radial(z, _):
            at = pl.ds(pl.multiple_of(z * 2 * chunk, 2 * chunk), 2 * chunk)
            rows = jnp.concatenate([source[tile, at, :] for tile in range(lane_tiles)], axis=1)
            both = dot3((basis_ref[0], basis_ref[1]), split(rows), ((1,), (1,)))
            for half in range(2):
                got = both[:, half * chunk : (half + 1) * chunk]
                scales[...] = jnp.maximum(scales[...], jnp.abs(got))
                wide[pl.ds(z * 2 + half, modes, stride=layers), :] = got
            return 0

        lax.fori_loop(0, layers // 2, radial, 0)
        exponent = exponent_of(scales[...])
        devices, _, height, lanes = sent_ref.shape
        share = modes // devices
        codes = exponent.astype(jnp.int32).astype(jnp.int16)
        sent_ref[:, share] = codes.reshape(devices, share, lanes)
        scales[...] = CODE_TOP / jnp.exp2(exponent * (1.0 / 256.0))

        def coding(device, _):
            for mode in range(share):
                row = device * share + mode
                values = wide[pl.ds(pl.multiple_of(row * layers, layers), layers), :]
                sent_ref[device, mode] = to_codes(values * scales[pl.ds(row, 1), :])
            return 0

        lax.fori_loop(0, devices, coding, 0)


def advect_chunk(arrays, ends, axial_flux, axial_speed, basis, chunk_index, chunk, around, devices, base):
    fraction, normals, planes, flags, courant = arrays
    rows, layers, cells = fraction.shape
    block = BLOCK
    steps = chunk // block
    first = chunk_index * steps
    share = cells // devices

    def here(i):
        return first + i

    def after(i):
        return jnp.minimum((first + i + 1) * block, rows - 1)

    whole = pl.BlockSpec((block, layers, cells), lambda i: (here(i), 0, 0))
    triple = pl.BlockSpec((3, block, layers, cells), lambda i: (0, here(i), 0, 0))
    row = pl.BlockSpec((1, layers, cells), lambda i: (after(i), 0, 0))
    before = max(first * block - 1, 0)
    last_row = pl.BlockSpec((1, layers, cells), lambda i: (before, 0, 0))
    edge = pl.BlockSpec((2, block, cells), lambda i: (0, here(i), 0))
    in_specs = [
        whole,
        triple,
        whole,
        whole,
        triple,
        pl.BlockSpec((3, 1, layers, cells), lambda i: (0, after(i), 0, 0)),
        row,
        row,
        pl.BlockSpec((1, 1, layers, cells), lambda i: (0, after(i), 0, 0)),
        pl.BlockSpec((3, 1, layers, cells), lambda i: (0, before, 0, 0)),
        last_row,
        last_row,
        pl.BlockSpec((1, 1, layers, cells), lambda i: (0, before, 0, 0)),
        pl.BlockSpec(ends.shape, lambda i: (0, 0, 0, 0)),
        edge,
        edge,
        pl.BlockSpec((2, cells, cells), lambda i: (0, 0, 0)),
    ]
    operands = [
        fraction, normals, planes, flags, courant,
        normals, planes, flags, courant,
        normals, planes, flags, courant,
        ends, axial_flux, axial_speed, basis,
    ]
    aliases = {}
    if base is not None:
        in_specs.append(pl.BlockSpec(memory_space=pl.ANY))
        operands.append(base)
        aliases = {len(operands) - 1: 0}
    return pl.pallas_call(
        functools.partial(chunk_kernel, around, chunk_index, rows // chunk),
        grid=(steps,),
        in_specs=in_specs,
        out_specs=[
            whole,
            pl.BlockSpec((devices, share + 1, layers, chunk), lambda i: (0, 0, 0, 0)),
        ],
        out_shape=[
            jax.ShapeDtypeStruct(fraction.shape, F32),
            jax.ShapeDtypeStruct((devices, share + 1, layers, chunk), jnp.int16),
        ],
        scratch_shapes=[
            pltpu.VMEM((8, cells // 128, (block + 2) * layers, 128), F32),
            pltpu.VMEM((2, layers, cells), F32),
            pltpu.VMEM((cells // 128, layers * chunk, 128), F32),
            pltpu.VMEM((cells * layers, chunk), F32),
            pltpu.VMEM((cells, chunk), F32),
        ],
        input_output_aliases=aliases,
        compiler_params=pltpu.CompilerParams(vmem_limit_bytes=60 * 2**20),
        cost_estimate=pl.CostEstimate(
            flops=40000 * chunk * layers * cells, bytes_accessed=30 * chunk * layers * cells, transcendentals=0
        ),
        name="advect_chunk",
    )(*operands)


@functools.lru_cache(None)
def folded_tables(total):
    quarter = total // 4
    place = np.arange(quarter) + 0.5

    def halves(x):
        high = x.astype(jnp.bfloat16)
        return np.stack([high, (x - high.astype(np.float64)).astype(jnp.bfloat16)])

    tables, rates, weights = [], [], []
    for waves, wave in (
        (2 * np.arange(quarter), np.cos),
        (2 * np.arange(quarter) + 2, np.sin),
        (2 * np.arange(quarter) + 1, np.cos),
        (2 * np.arange(quarter) + 1, np.sin),
    ):
        doubled = waves[:, None] * (2 * np.arange(quarter) + 1)[None, :] % (2 * total)
        tables.append(wave(np.pi * doubled / total))
        rates.append(2.0 - 2.0 * np.cos(2.0 * np.pi * waves / total))
        weights.append(np.where((waves == 0) | (waves == total // 2), 1.0, 2.0) / total)
    tables = np.stack(tables)
    back = np.stack([halves(t) for t in tables])
    forth = np.stack([halves(t.T) for t in tables])
    return forth, back, np.stack(rates)[:, None].astype(np.float32), np.stack(weights)[:, None].astype(np.float32)


def decoded(values):
    return values.astype(jnp.int32).astype(F32)


def scale_of(codes):
    return jnp.exp2(decoded(codes) * (1.0 / 256.0)) * (1.0 / CODE_TOP)


def solve_kernel(around, along, chunks, group, *refs):
    got = refs[:chunks]
    extra = refs[chunks : 2 * chunks]
    mix, unmix, forth_ref, back_ref, rates, weights, shifts = refs[2 * chunks : 2 * chunks + 7]
    sent, high, low, result, scale, exponents, forth, back, arrived = refs[2 * chunks + 7 :]
    copies = [
        pltpu.make_async_copy(forth_ref, forth, arrived.at[0]),
        pltpu.make_async_copy(back_ref, back, arrived.at[1]),
    ]

    @pl.when(pl.program_id(0) == 0)
    def _():
        for copy in copies:
            copy.start()

    devices, count, layers, lanes = got[0].shape
    share = (sent.shape[1] - 1) // chunks
    pairs = around // 4
    step = pl.program_id(0)
    first = group * share + step * count
    for chunk in range(chunks):
        scale[chunk] = scale_of(extra[chunk][:, 0])

    def spots():
        for pair in range(pairs):
            for chunk in range(chunks):
                mirror = chunks - 1 - chunk
                at = pl.ds((pair * chunks + chunk) * lanes, lanes)
                yield at, (
                    (pair, chunk),
                    (pair + 2 * pairs, chunk),
                    (2 * pairs - 1 - pair, mirror),
                    (4 * pairs - 1 - pair, mirror),
                )

    def fold(index, _):
        mode, axial = index // along, index % along
        rows = pl.ds(pl.multiple_of(index * layers, layers), layers)
        row = pl.ds(first + mode, 1)
        for at, places in spots():
            u0, u1, r0, r1 = [
                decoded(got[chunk][azim * along + axial, mode])
                * scale[chunk, azim * along + axial, row, :]
                for azim, chunk in places
            ]
            e0, o0, e1, o1 = u0 + u1, u0 - u1, r0 + r1, r0 - r1
            for k, folded in enumerate((e0 + e1, e0 - e1, o0 - o1, o0 + o1)):
                high[k, rows, at], low[k, rows, at] = split(folded)
        return 0

    lax.fori_loop(0, count * along, fold, 0)

    @pl.when(pl.program_id(0) == 0)
    def _():
        for copy in copies:
            copy.wait()

    height = mix.shape[1]
    parts = [pl.ds(at, height) for at in range(0, high.shape[1], height)]

    def waves(k, _):
        for at in parts:
            high[k, at], low[k, at] = split(
                dot3((mix[0], mix[1]), (high[k, at], low[k, at]))
            )
        spectrum = dot3((high[k], low[k]), (forth[k, 0], forth[k, 1]))
        high[k], low[k] = split(spectrum * weights[k] / (rates[k] + shifts[...]))
        high[k], low[k] = split(dot3((high[k], low[k]), (back[k, 0], back[k, 1])))
        for at in parts:
            result[k, at] = dot3((unmix[0], unmix[1]), (high[k, at], low[k, at]))
        return 0

    lax.fori_loop(0, 4, waves, 0)

    def unfold(index, _):
        mode, axial = index // along, index % along
        rows = pl.ds(pl.multiple_of(index * layers, layers), layers)
        for at, places in spots():
            ec, es, oc, os = [result[k, rows, at] for k in range(4)]
            e0, e1, o0, o1 = ec + es, ec - es, oc + os, os - oc
            for (azim, chunk), values in zip(places, (e0 + o0, e0 - o0, e1 + o1, e1 - o1)):
                device = azim * along + axial
                slot = chunk * share + step * count + mode
                exponent = exponent_of(jnp.max(jnp.abs(values), axis=0, keepdims=True))
                exponents[device, pl.ds(slot, 1), :] = exponent
                factor = CODE_TOP / jnp.exp2(exponent * (1.0 / 256.0))
                sent[device, slot] = to_codes(values * factor)
        return 0

    lax.fori_loop(0, count * along, unfold, 0)

    @pl.when(step == pl.num_programs(0) - 1)
    def _():
        sent[:, chunks * share] = exponents[...].astype(jnp.int32).astype(jnp.int16)


def solve_group(got, mix, unmix, tables, shifts, group, groups, around, along):
    chunks = len(got)
    devices, slots, layers, lanes = got[0].shape
    modes = slots - 1
    share = modes // groups
    count = share
    steps = share // count
    rows = count * along * layers
    forth, back, rates, weights = tables
    width = forth.shape[-1]

    def fixed(array):
        return pl.BlockSpec(array.shape, lambda i: (0,) * array.ndim, pipeline_mode=pl.Buffered(1))

    return pl.pallas_call(
        functools.partial(solve_kernel, around, along, chunks, group),
        grid=(steps,),
        in_specs=[
            pl.BlockSpec((devices, count, layers, lanes), lambda i: (0, group * steps + i, 0, 0))
        ]
        * chunks
        + [pl.BlockSpec((devices, 1, layers, lanes), lambda i: (0, modes, 0, 0))] * chunks
        + [fixed(mix), fixed(unmix)]
        + [pl.BlockSpec(memory_space=pl.ANY)] * 2
        + [fixed(rates), fixed(weights)]
        + [pl.BlockSpec((rows, 1), lambda i: (group * steps + i, 0))],
        out_specs=pl.BlockSpec((devices, slots, layers, lanes), lambda i: (0, 0, 0, 0)),
        out_shape=jax.ShapeDtypeStruct((devices, chunks * share + 1, layers, lanes), jnp.int16),
        scratch_shapes=[
            pltpu.VMEM((4, rows, width), BF16),
            pltpu.VMEM((4, rows, width), BF16),
            pltpu.VMEM((4, rows, width), F32),
            pltpu.VMEM((chunks, devices, layers, lanes), F32),
            pltpu.VMEM((devices, layers, lanes), F32),
            pltpu.VMEM(forth.shape, BF16),
            pltpu.VMEM(back.shape, BF16),
            pltpu.SemaphoreType.DMA((2,)),
        ],
        compiler_params=pltpu.CompilerParams(vmem_limit_bytes=60 * 2**20),
        cost_estimate=pl.CostEstimate(
            flops=60 * rows * width * width * steps, bytes_accessed=20 * 2**20, transcendentals=0
        ),
        name="solve_group",
    )(*got, *got, mix, unmix, forth, back, rates, weights, shifts)


def pressure_kernel(around, groups, *refs):
    got = refs[:groups]
    extra = refs[groups : 2 * groups]
    basis, out, flat, wide, scale, high, low = refs[2 * groups :]
    devices, share, layers, lanes = got[0].shape
    lane_tiles = out.shape[2] // 128
    chunk = pl.program_id(0)
    backwards = lax.rem(lax.axis_index("azim"), around // 2) >= around // 4
    i = lax.broadcasted_iota(jnp.int32, (lanes, lanes), 0)
    j = lax.broadcasted_iota(jnp.int32, (lanes, lanes), 1)
    turned_place = jnp.where(backwards, lanes - 1, 0) + jnp.where(backwards, -1, 1) * i
    turn = jnp.where(j == turned_place, 1.0, 0.0).astype(BF16)
    for group in range(groups):
        scale[group] = scale_of(extra[group][:, 0])

        def unpack(device, _, group=group):
            for mode in range(share):
                at = pl.multiple_of((device * share + mode) * layers, layers)
                flat[group, pl.ds(at, layers), :] = (
                    decoded(got[group][device, mode])
                    * scale[group, device, pl.ds(chunk * share + mode, 1), :]
                )
            return 0

        lax.fori_loop(0, devices, unpack, 0)

    together = high.shape[0] // lanes

    def radial(batch, _):
        for part in range(together):
            for group in range(groups):
                z = batch * together + part
                values = split(flat[group, pl.ds(z, devices * share, stride=layers), :])
                at = pl.ds(group * devices * share, devices * share)
                for target, value in zip((high, low), values):
                    target[part * lanes : (part + 1) * lanes, at] = dot(
                        turn, value, ((1,), (1,))
                    ).astype(BF16)
        total = dot3((high[...], low[...]), (basis[0], basis[1]))
        for part in range(together):
            for tile in range(lane_tiles):
                wide[tile, pl.ds(batch * together + part, lanes, stride=layers), :] = total[
                    part * lanes : (part + 1) * lanes, tile * 128 : (tile + 1) * 128
                ]
        return 0

    lax.fori_loop(0, layers // together, radial, 0)
    for tile in range(lane_tiles):
        out[:, :, tile * 128 : (tile + 1) * 128] = wide[tile].reshape(lanes, layers, 128)


def pressure_of(got, basis, around, chunks):
    groups = len(got)
    devices, slots, layers, lanes = got[0].shape
    share = (slots - 1) // chunks
    cells = basis.shape[-1]
    return pl.pallas_call(
        functools.partial(pressure_kernel, around, groups),
        grid=(chunks,),
        in_specs=[pl.BlockSpec((devices, share, layers, lanes), lambda i: (0, i, 0, 0))] * groups
        + [pl.BlockSpec((devices, 1, layers, lanes), lambda i: (0, chunks * share, 0, 0))] * groups
        + [
            pl.BlockSpec(
                basis.shape, lambda i: (0,) * basis.ndim, pipeline_mode=pl.Buffered(1)
            )
        ],
        out_specs=pl.BlockSpec((lanes, layers, cells), lambda i: (i, 0, 0)),
        out_shape=jax.ShapeDtypeStruct((lanes * chunks, layers, cells), F32),
        scratch_shapes=[
            pltpu.VMEM((groups, devices * share * layers, lanes), F32),
            pltpu.VMEM((cells // 128, lanes * layers, 128), F32),
            pltpu.VMEM((groups, devices, layers, lanes), F32),
            pltpu.VMEM((4 * lanes, groups * devices * share), BF16),
            pltpu.VMEM((4 * lanes, groups * devices * share), BF16),
        ],
        compiler_params=pltpu.CompilerParams(vmem_limit_bytes=60 * 2**20),
        name="pressure_of",
    )(*got, *got, basis)


def halves(values):
    high = lax.reduce_precision(values, 8, 7)
    return jnp.stack([high.astype(BF16), (values - high).astype(BF16)])


def exchanged(sent):
    return lax.all_to_all(sent, ("azim", "axial"), split_axis=0, concat_axis=0, tiled=True)


def following_kernel(values_ref, earlier_ref, out_ref):
    del values_ref, earlier_ref, out_ref


def following(values, earlier):
    anywhere = pl.BlockSpec(memory_space=pl.ANY)
    return pl.pallas_call(
        following_kernel,
        in_specs=[anywhere, anywhere],
        out_specs=anywhere,
        out_shape=jax.ShapeDtypeStruct(values.shape, values.dtype),
        input_output_aliases={0: 0},
        name="following",
    )(values, earlier)


def overlapped(
    fraction,
    normals,
    planes,
    cell_flags,
    courant,
    radial_basis,
    axial_basis,
    radial_rates,
    axial_rates,
):
    rows, layers, cells = fraction.shape
    around, along = lax.axis_size("azim"), lax.axis_size("axial")
    devices = around * along
    modes = cells // devices
    chunks, groups = rows // CHUNK, 2
    axial_flux, axial_speed, ends = halos(normals, planes, cell_flags, courant)
    forward_basis = halves(radial_basis.T)
    arrays = (fraction, normals, planes, cell_flags, courant)
    updated, got = None, []
    for chunk in range(chunks):
        updated, sent = advect_chunk(
            arrays, ends, axial_flux, axial_speed, forward_basis, chunk, CHUNK, around, devices, updated
        )
        got.append(exchanged(following(sent, got[-1]) if got else sent))
    count = jnp.eye(4, dtype=F32)
    mix, unmix = halves(jnp.kron(count, axial_basis.T)), halves(jnp.kron(count, axial_basis))
    first = (lax.axis_index("azim") * along + lax.axis_index("axial")) * modes
    shifts = lax.dynamic_slice_in_dim(radial_rates, first, modes)[:, None] + axial_rates[None, :]
    shifts = shifts.reshape(modes * along * layers, 1)
    tables = [jnp.asarray(x) for x in folded_tables(rows * around)]
    returned = []
    for group in range(groups):
        sent = solve_group(got, mix, unmix, tables, shifts, group, groups, around, along)
        returned.append(exchanged(sent))
    back_basis = radial_basis.T.reshape(devices, groups, modes // groups, cells)
    back_basis = halves(back_basis.transpose(1, 0, 2, 3).reshape(-1, cells))
    pressure = pressure_of(returned, back_basis, around, chunks)
    return (updated, pressure)


def fits(fraction):
    rows, layers, cells = fraction.shape
    around, along = lax.axis_size("azim"), lax.axis_size("axial")
    modes = cells // (around * along)
    chunks = rows // CHUNK
    return (
        rows % CHUNK == 0
        and layers == 16
        and modes == 16
        and modes // 2 * chunks == layers
        and cells % 128 == 0
        and around % 4 == 0
        and along > 2
    )


def local(*arguments):
    return overlapped(*arguments) if fits(arguments[0]) else stepwise(*arguments)


def solution(mesh):
    placed = (
        P("azim", "axial", None),
        P(None, "azim", "axial", None),
        P("azim", "axial", None),
        P("azim", "axial", None),
        P(None, "azim", "axial", None),
        P(),
        P(),
        P(),
        P(),
    )
    return jax.shard_map(
        local,
        mesh=mesh,
        in_specs=placed,
        out_specs=(P("azim", "axial", None), P("azim", "axial", None)),
        check_vma=False,
    )
```

```python
import functools

import jax
import jax.numpy as jnp
import numpy as np
from jax import lax
from jax.experimental import pallas as pl
from jax.experimental.pallas import tpu as pltpu
from jax.sharding import PartitionSpec as P

HIGH = lax.Precision.HIGH
BUOYANCY = 0.5
CODE_TOP = 32700.0


def shifted_in(edge, axis, towards_lower):
    count = lax.axis_size(axis)
    if towards_lower:
        pairs = [((i + 1) % count, i) for i in range(count)]
    else:
        pairs = [(i, (i + 1) % count) for i in range(count)]
    return lax.ppermute(edge, axis, pairs)


def cell_parts(n0, n1, n2, code):
    m0, m1, m2 = jnp.abs(n0), jnp.abs(n1), jnp.abs(n2)
    return (n0, n1, n2, code, 1.0 / (6.0 * m0 * m1 * m2))


def cube(height):
    held = jnp.maximum(height, 0.0)
    return held * held * held


def face_flux(direction, lower, upper, speed, lower_weight=None, upper_weight=None):
    forward = speed > 0.0
    signed = jnp.where(forward, lower[direction], -upper[direction])
    first, second = [d for d in range(3) if d != direction]
    along = jnp.abs(signed)
    side_a = jnp.abs(jnp.where(forward, lower[first], upper[first]))
    side_b = jnp.abs(jnp.where(forward, lower[second], upper[second]))
    code = jnp.where(forward, lower[3], upper[3])
    inverse = jnp.where(forward, lower[4], upper[4])
    width = jnp.abs(speed)
    near = code - along * jnp.where(signed < 0.0, 0.0, 1.0 - width)
    far = near - along * width
    sides = side_a + side_b
    total = (cube(near) - cube(near - side_a)) - (cube(near - side_b) - cube(near - sides))
    total = total - ((cube(far) - cube(far - side_a)) - (cube(far - side_b) - cube(far - sides)))
    volume = jnp.where(code > 3.0, width, jnp.where(code < -0.5, 0.0, total * inverse))
    if lower_weight is not None:
        volume = volume * jnp.where(forward, lower_weight, upper_weight)
    return jnp.where(forward, volume, jnp.where(speed < 0.0, -volume, 0.0))


def advect_kernel(
    fraction_ref,
    normals_ref,
    planes_ref,
    flags_ref,
    courant_ref,
    next_ref,
    high_ref,
    low_azim_ref,
    low_axial_ref,
    updated_ref,
    source_ref,
    kept,
):
    rows, layers, cells = fraction_ref.shape
    f32 = jnp.float32

    @pl.when(pl.program_id(0) == 0)
    def _():
        kept[...] = low_azim_ref[...]

    index = lax.broadcasted_iota(jnp.int32, (1, cells), 1)
    place = index.astype(f32)
    radius = 1.0 + (place + 0.5) / cells
    next_radius = 1.0 + (place + 1.5) / cells
    face_radius = 1.0 + (place + 1.0) / cells
    inverse_radius = 1.0 / radius
    inner = lax.broadcasted_iota(jnp.int32, (layers, cells), 1) < cells - 1
    layer = lax.broadcasted_iota(jnp.int32, (layers, cells), 0)
    last_layer = layer == layers - 1
    first_layer = layer == 0

    def row_parts(row):
        flags = flags_ref[row]
        code = jnp.where(
            flags == 2, planes_ref[row].astype(f32), jnp.where(flags == 1, 4.0, -1.0)
        )
        return cell_parts(
            normals_ref[0, row].astype(f32),
            normals_ref[1, row].astype(f32),
            normals_ref[2, row].astype(f32),
            code,
        )

    def one_row(row, upper, upper_speed):
        own = row_parts(row)
        moved = [courant_ref[d, row].astype(f32) for d in range(3)]
        speed = 0.5 * (moved[0] + upper_speed)
        flux = face_flux(0, own, upper, speed)
        gained = flux - kept[0]
        divergence = speed - kept[1]
        kept[0] = flux
        kept[1] = speed
        beyond = cell_parts(*[high_ref[k, row] for k in range(4)])
        above = [
            jnp.where(last_layer, high, pltpu.roll(field, layers - 1, 0))
            for field, high in zip(own, beyond)
        ]
        speed = 0.5 * (
            moved[1]
            + jnp.where(last_layer, high_ref[4, row], pltpu.roll(moved[1], layers - 1, 0))
        )
        flux = face_flux(1, own, above, speed)
        gained = gained + (
            flux - jnp.where(first_layer, low_axial_ref[0, row], pltpu.roll(flux, 1, 0))
        )
        divergence = divergence + (
            speed - jnp.where(first_layer, low_axial_ref[1, row], pltpu.roll(speed, 1, 0))
        )
        outer = [pltpu.roll(field, cells - 1, 1) for field in own]
        speed = 0.5 * (moved[2] + pltpu.roll(moved[2], cells - 1, 1))
        speed = jnp.where(inner, speed, 0.0)
        flux = face_flux(2, own, outer, speed, radius, next_radius)
        gained = gained + (flux - pltpu.roll(flux, 1, 1)) * inverse_radius
        carried = face_radius * speed
        divergence = divergence + (carried - pltpu.roll(carried, 1, 1)) * inverse_radius
        updated = fraction_ref[row] - gained
        updated_ref[row] = updated
        source_ref[row] = divergence + BUOYANCY * updated

    def step(row, _):
        one_row(row, row_parts(row + 1), courant_ref[0, row + 1].astype(f32))
        return 0

    lax.fori_loop(0, rows - 1, step, 0)
    one_row(
        rows - 1,
        cell_parts(*[next_ref[k, 0].astype(f32) for k in range(4)]),
        next_ref[4, 0].astype(f32),
    )


def plane_codes(planes, flags):
    return jnp.where(
        flags == 2, planes.astype(jnp.float32), jnp.where(flags == 1, 4.0, -1.0)
    ).astype(jnp.bfloat16)


def packed_edge(normals, planes, flags, courant, direction, pick):
    parts = [pick(normals[d]) for d in range(3)]
    parts.append(plane_codes(pick(planes), pick(flags)))
    parts.append(pick(courant[direction]))
    return jnp.stack(parts)


def low_face(direction, lower, upper):
    lower, upper = lower.astype(jnp.float32), upper.astype(jnp.float32)
    speed = 0.5 * (lower[4] + upper[4])
    flux = face_flux(direction, cell_parts(*lower[:4]), cell_parts(*upper[:4]), speed)
    return jnp.stack([flux, speed])


def advect(fraction, normals, planes, flags, courant):
    rows, layers, cells = fraction.shape
    block = 16 if rows % 16 == 0 else 1
    blocks = rows // block
    fields = (normals, planes, flags, courant)
    top_row = packed_edge(*fields, 0, lambda x: x[rows - 1])
    bottom_row = packed_edge(*fields, 0, lambda x: x[0])
    top_layer = packed_edge(*fields, 1, lambda x: x[:, layers - 1])
    bottom_layer = packed_edge(*fields, 1, lambda x: x[:, 0])
    high_row = shifted_in(bottom_row, "azim", True)
    low_row = shifted_in(top_row, "azim", False)
    high_layer = shifted_in(bottom_layer, "axial", True)
    low_layer = shifted_in(top_layer, "axial", False)
    low_azim = low_face(0, low_row, bottom_row)
    low_axial = low_face(1, low_layer, bottom_layer)[:, :, None]
    high_axial = high_layer.astype(jnp.float32)[:, :, None]
    inside = packed_edge(*fields, 0, lambda x: x[block::block])
    following = jnp.concatenate([inside, high_row[:, None]], axis=1)
    whole = pl.BlockSpec((block, layers, cells), lambda i: (i, 0, 0))
    triple = pl.BlockSpec((3, block, layers, cells), lambda i: (0, i, 0, 0))
    return pl.pallas_call(
        advect_kernel,
        grid=(blocks,),
        in_specs=[
            whole,
            triple,
            whole,
            whole,
            triple,
            pl.BlockSpec((5, 1, layers, cells), lambda i: (0, i, 0, 0)),
            pl.BlockSpec((5, block, 1, cells), lambda i: (0, i, 0, 0)),
            pl.BlockSpec((2, layers, cells), lambda i: (0, 0, 0)),
            pl.BlockSpec((2, block, 1, cells), lambda i: (0, i, 0, 0)),
        ],
        out_specs=[whole, whole],
        out_shape=[jax.ShapeDtypeStruct(fraction.shape, jnp.float32)] * 2,
        scratch_shapes=[pltpu.VMEM((2, layers, cells), jnp.float32)],
        compiler_params=pltpu.CompilerParams(vmem_limit_bytes=40 * 2**20),
    )(
        fraction,
        normals,
        planes,
        flags,
        courant,
        following,
        high_axial,
        low_azim,
        low_axial,
    )


def coded(values):
    most = jnp.max(jnp.abs(values), axis=-1)
    exponent = jnp.clip(jnp.ceil(jnp.log2(most) * 256.0) + 1.0, -30000.0, 30000.0)
    scale = CODE_TOP * jnp.exp2(exponent * (-1.0 / 256.0))
    codes = jnp.round(values * scale[..., None])
    return jnp.clip(codes, -32767.0, 32767.0).astype(jnp.int16), exponent.astype(jnp.int16)


def exchange(values):
    modes, cells = values.shape[1], values.shape[3]
    codes, exponent = coded(values)
    extra = jnp.pad(exponent.transpose(0, 2, 1), ((0, 0), (0, 0), (0, cells - modes)))
    sent = jnp.concatenate([codes, extra[:, None]], axis=1)
    got = lax.all_to_all(sent, ("azim", "axial"), split_axis=0, concat_axis=0, tiled=True)
    exponent = got[:, modes, :, :modes].transpose(0, 2, 1).astype(jnp.float32)
    scale = jnp.exp2(exponent * (1.0 / 256.0)) * (1.0 / CODE_TOP)
    return got[:, :modes].astype(jnp.float32) * scale[..., None]


@functools.lru_cache(None)
def azimuth_tables(total):
    half, quarter = total // 2, total // 4
    place = np.arange(half)

    def table(cosines, sines):
        waves = np.concatenate([cosines, sines])
        angles = 2.0 * np.pi / total * (waves[:, None] * place[None, :] % total)
        rows = np.concatenate(
            [np.cos(angles[: len(cosines)]), np.sin(angles[len(cosines) :])]
        ).astype(np.float32)
        rates = (2.0 - 2.0 * np.cos(2.0 * np.pi * waves / total)).astype(np.float32)
        ends = (waves == 0) | (waves == half)
        return rows, rates, (np.where(ends, 1.0, 2.0) / total).astype(np.float32)

    even = 2 * np.arange(quarter + 1)
    odd = 2 * np.arange(quarter) + 1
    return table(even, even[1:-1]), table(odd, odd)


def stepwise(
    fraction,
    normals,
    planes,
    cell_flags,
    courant,
    radial_basis,
    axial_basis,
    radial_rates,
    axial_rates,
):
    rows, layers, cells = fraction.shape
    around, along = lax.axis_size("azim"), lax.axis_size("axial")
    devices = around * along
    modes = cells // devices
    total = rows * around
    half = total // 2
    updated, source = advect(fraction, normals, planes, cell_flags, courant)
    radial_modes = jnp.einsum("azr,rj->jza", source, radial_basis, precision=HIGH)
    got = exchange(radial_modes.reshape(devices, modes, layers, rows))
    got = got.reshape(around, along, modes, layers, rows).transpose(2, 1, 3, 0, 4)
    got = got.reshape(modes, along * layers, total)
    both = jnp.einsum("jza,zn->jna", got, axial_basis, precision=HIGH)
    first = (lax.axis_index("azim") * along + lax.axis_index("axial")) * modes
    shifts = lax.dynamic_slice_in_dim(radial_rates, first, modes)[:, None] + axial_rates[None, :]
    low, high = both[..., :half], both[..., half:]
    solved = []
    for folded, (table, rates, weight) in zip((low + high, low - high), azimuth_tables(total)):
        coefficients = jnp.einsum("jna,ka->jnk", folded, table, precision=HIGH)
        scaled = coefficients / (rates + shifts[..., None]) * weight
        solved.append(jnp.einsum("jnk,ka->jna", scaled, table, precision=HIGH))
    physical = jnp.concatenate([solved[0] + solved[1], solved[0] - solved[1]], axis=-1)
    physical = jnp.einsum("jna,zn->jza", physical, axial_basis, precision=HIGH)
    physical = physical.reshape(modes, along, layers, around, rows).transpose(3, 1, 0, 2, 4)
    returned = exchange(physical.reshape(devices, modes, layers, rows))
    returned = returned.reshape(cells, layers, rows)
    pressure = jnp.einsum("jza,rj->azr", returned, radial_basis, precision=HIGH)
    return (updated, pressure)


CHUNK = 128
BLOCK = 16
SOLVED = ((0, 4), (8, 8), (4, 4))
FLUX_SCALE = 32767.0 / 0.3
F32 = jnp.float32
BF16 = jnp.bfloat16


def split(values):
    high = values.astype(BF16)
    return high, (values - high.astype(F32)).astype(BF16)


def dot(a, b, contract):
    return lax.dot_general(a, b, (contract, ((), ())), preferred_element_type=F32)


def dot3(a, b, contract=((1,), (0,))):
    return dot(a[0], b[0], contract) + (dot(a[0], b[1], contract) + dot(a[1], b[0], contract))


def slab_flux(normal, side_a, side_b, plane, inverse, speed):
    along = jnp.abs(normal)
    reach = normal * speed
    slab = jnp.abs(reach)
    near = plane - jnp.where(reach > 0.0, along - slab, 0.0)
    other = (slab + (side_a + side_b)) - near
    folded = near > other
    held = jnp.maximum(jnp.minimum(near, other), 0.0)
    low, high = jnp.minimum(side_a, side_b), jnp.maximum(side_a, side_b)
    by_low = jnp.maximum(held - low, 0.0)
    by_slab = jnp.maximum(held - slab, 0.0)
    last = jnp.maximum(held - (low + slab), 0.0) - jnp.maximum(held - high, 0.0)
    total = held * held * held - by_slab * by_slab * by_slab
    total = total - (by_low * by_low * by_low - last * last * last)
    flux = total * inverse
    return jnp.where(folded, speed - flux, flux)


def upwind_flux(direction, lower, upper, speed, lower_weight=None, upper_weight=None):
    forward = speed > 0.0
    first, second = [d for d in range(3) if d != direction]
    normal = jnp.where(forward, lower[direction], upper[direction])
    side_a = jnp.abs(jnp.where(forward, lower[first], upper[first]))
    side_b = jnp.abs(jnp.where(forward, lower[second], upper[second]))
    plane = jnp.where(forward, lower[3], upper[3])
    inverse = jnp.where(forward, lower[4], upper[5])
    flux = slab_flux(normal, side_a, side_b, plane, inverse, speed)
    if lower_weight is not None:
        flux = flux * jnp.where(forward, lower_weight, upper_weight)
    return flux


def inverse_of(n0, n1, n2):
    return 1.0 / (6.0 * jnp.abs(n0 * n1 * n2))


def plane_value(planes, flags):
    return jnp.where(flags == 2, planes.astype(F32), jnp.where(flags == 1, 4.0, -4.0))


def halo_kernel(
    courant_ref,
    normals_ref,
    planes_ref,
    flags_ref,
    first_normals_ref,
    first_planes_ref,
    first_flags_ref,
    first_courant_ref,
    last_normals_ref,
    last_planes_ref,
    last_flags_ref,
    last_courant_ref,
    flux_ref,
    speed_ref,
    ends_ref,
    work,
    edge,
    edge_in,
    fields,
    code,
    code_in,
    packs,
    packs_in,
    row_send,
    row_recv,
    edge_send,
    edge_recv,
    code_send,
    code_recv,
):
    step = pl.program_id(0)
    half = pl.num_programs(0) // 2
    span, layers, cells = planes_ref.shape
    groups, group = code.shape[1:3]
    per_group = group // span
    tiles = cells // 128
    neighbours = []
    for axis in ("azim", "axial"):
        count, me = lax.axis_size(axis), lax.axis_index(axis)
        neighbours.append(
            ({axis: lax.rem(me + count - 1, count)}, {axis: lax.rem(me + 1, count)})
        )

    def remote(source, target, send, recv, device):
        return pltpu.make_async_remote_copy(
            src_ref=source,
            dst_ref=target,
            send_sem=send,
            recv_sem=recv,
            device_id=device,
            device_id_type=pl.DeviceIdType.MESH,
        )

    row_copies = [
        remote(packs.at[s], packs_in.at[1 - s], row_send.at[s], row_recv.at[1 - s], neighbours[0][s])
        for s in range(2)
    ]
    def edge_copy(s, g):
        return remote(
            edge.at[s, g],
            edge_in.at[1 - s, g],
            edge_send.at[s, g],
            edge_recv.at[1 - s, g],
            neighbours[1][s],
        )

    def code_copy(s, g):
        return remote(
            code.at[s, g],
            code_in.at[1 - s, g],
            code_send.at[s, g],
            code_recv.at[1 - s, g],
            neighbours[1][s],
        )

    @pl.when(step == 0)
    def _():
        barrier = pltpu.get_barrier_semaphore()
        for pair in neighbours:
            for device in pair:
                pl.semaphore_signal(
                    barrier, inc=1, device_id=device, device_id_type=pl.DeviceIdType.MESH
                )
        pl.semaphore_wait(barrier, 4)
        for s, (normals, planes, flags, courant) in enumerate(
            (
                (first_normals_ref, first_planes_ref, first_flags_ref, first_courant_ref),
                (last_normals_ref, last_planes_ref, last_flags_ref, last_courant_ref),
            )
        ):
            for k in range(3):
                packs[s, k] = normals[k, 0]
            packs[s, 3] = plane_value(planes[0], flags[0]).astype(BF16)
            packs[s, 4] = courant[0, 0]
        for copy in row_copies:
            copy.start()

    def layer_rows(tile, layer):
        return work[tile, pl.ds(layer, span, stride=layers), :]

    @pl.when(step < half)
    def _():
        place = step // per_group
        at = pl.ds(pl.multiple_of(lax.rem(step, per_group) * span, span), span)
        for tile in range(tiles):
            lanes = pl.ds(tile * 128, 128)
            work[tile] = courant_ref[0, :, :, lanes].astype(F32).reshape(span * layers, 128)
            for s, layer in ((0, 0), (1, layers - 1)):
                edge[s, place, at, lanes] = layer_rows(tile, layer).astype(BF16)

    for g in range(groups):

        @pl.when(step == (g + 1) * per_group - 1)
        def _(g=g):
            for s in range(2):
                edge_copy(s, g).start()

    @pl.when(step >= half)
    def _():
        at = pl.ds(pl.multiple_of((step - half) * span, span), span)
        for k in range(4):
            for tile in range(tiles):
                lanes = pl.ds(tile * 128, 128)
                if k < 3:
                    field = normals_ref[k, :, :, lanes].astype(F32)
                else:
                    field = plane_value(planes_ref[:, :, lanes], flags_ref[:, :, lanes])
                work[tile] = field.reshape(span * layers, 128)
                for s, layer in ((0, 0), (1, layers - 1)):
                    fields[s, k, at, lanes] = layer_rows(tile, layer)

    for g in range(groups):

        @pl.when(step == half + (g + 1) * per_group - 1)
        def _(g=g):
            for s in range(2):
                edge_copy(s, g).wait()
            for s in range(2):

                def donate(piece, _, s=s):
                    inside = pl.ds(pl.multiple_of(piece * 16, 16), 16)
                    at = pl.ds(pl.multiple_of(g * group + piece * 16, 16), 16)
                    normals = [fields[s, k, at, :] for k in range(3)]
                    own, beyond = edge[s, g, inside, :], edge_in[s, g, inside, :]
                    speed = 0.5 * (own.astype(F32) + beyond.astype(F32))
                    inverse = inverse_of(*normals)
                    flux = slab_flux(
                        normals[1],
                        jnp.abs(normals[0]),
                        jnp.abs(normals[2]),
                        fields[s, 3, at, :],
                        inverse if s == 1 else -inverse,
                        speed,
                    )
                    flux = jnp.where(speed > 0.0 if s == 1 else speed < 0.0, flux, 0.0)
                    flux_ref[s, at, :] = flux
                    speed_ref[s, at, :] = speed
                    code[s, g, inside, :] = to_codes(flux * FLUX_SCALE)
                    return 0

                lax.fori_loop(0, group // 16, donate, 0)
                code_copy(s, g).start()

    @pl.when(step == 2 * half - 1)
    def _():
        for copy in row_copies:
            copy.wait()
        ends_ref[...] = packs_in[...]
        for g in range(groups):
            for s in range(2):
                code_copy(s, g).wait()
            for s in range(2):
                at = pl.ds(g * group, group)
                received = code_in[s, g].astype(jnp.int32).astype(F32)
                flux_ref[s, at, :] += received * (1.0 / FLUX_SCALE)


def halos(normals, planes, flags, courant):
    rows, layers, cells = planes.shape
    span, groups = 32, 4
    half = rows // span

    def later(i):
        return jnp.maximum(i - half, 0)

    whole = pl.BlockSpec((span, layers, cells), lambda i: (later(i), 0, 0))
    in_specs = [
        pl.BlockSpec((1, span, layers, cells), lambda i: (1, jnp.minimum(i, half - 1), 0, 0)),
        pl.BlockSpec((3, span, layers, cells), lambda i: (0, later(i), 0, 0)),
        whole,
        whole,
    ]
    for row in (0, rows - 1):
        one = pl.BlockSpec((1, layers, cells), lambda i, row=row: (row, 0, 0))
        in_specs += [
            pl.BlockSpec((3, 1, layers, cells), lambda i, row=row: (0, row, 0, 0)),
            one,
            one,
            pl.BlockSpec((1, 1, layers, cells), lambda i, row=row: (0, row, 0, 0)),
        ]
    pair = pl.BlockSpec((2, rows, cells), lambda i: (0, 0, 0))
    ends = (2, 5, layers, cells)
    split_shape = (2, groups, rows // groups, cells)
    dma = pltpu.SemaphoreType.DMA
    return pl.pallas_call(
        halo_kernel,
        grid=(2 * half,),
        in_specs=in_specs,
        out_specs=[pair, pair, pl.BlockSpec(ends, lambda i: (0, 0, 0, 0))],
        out_shape=[
            jax.ShapeDtypeStruct((2, rows, cells), F32),
            jax.ShapeDtypeStruct((2, rows, cells), F32),
            jax.ShapeDtypeStruct(ends, BF16),
        ],
        scratch_shapes=[
            pltpu.VMEM((cells // 128, span * layers, 128), F32),
            pltpu.VMEM(split_shape, BF16),
            pltpu.VMEM(split_shape, BF16),
            pltpu.VMEM((2, 4, rows, cells), F32),
            pltpu.VMEM(split_shape, jnp.int16),
            pltpu.VMEM(split_shape, jnp.int16),
            pltpu.VMEM(ends, BF16),
            pltpu.VMEM(ends, BF16),
            dma((2,)),
            dma((2,)),
            dma((2, groups)),
            dma((2, groups)),
            dma((2, groups)),
            dma((2, groups)),
        ],
        compiler_params=pltpu.CompilerParams(
            collective_id=0, has_side_effects=True, vmem_limit_bytes=60 * 2**20
        ),
        name="halos",
    )(courant, normals, planes, flags, *(normals, planes, flags, courant) * 2)


def exponent_of(most):
    return jnp.clip(jnp.ceil(jnp.log2(jnp.maximum(most, 1e-29)) * 256.0) + 1.0, -25000.0, 30000.0)


def to_codes(values):
    return jnp.round(values).astype(jnp.int32).astype(jnp.int16)


def chunk_kernel(
    around,
    chunk_index,
    chunks,
    fraction_ref,
    normals_ref,
    planes_ref,
    flags_ref,
    courant_ref,
    next_normals_ref,
    next_planes_ref,
    next_flags_ref,
    next_courant_ref,
    last_normals_ref,
    last_planes_ref,
    last_flags_ref,
    last_courant_ref,
    ends_ref,
    axial_flux_ref,
    axial_speed_ref,
    basis_ref,
    *rest,
):
    if chunk_index:
        rest = rest[1:]
    updated_ref, sent_ref, parts, kept, source, wide, scales = rest
    block, layers, cells = fraction_ref.shape
    steps = pl.num_programs(0)
    step = pl.program_id(0)
    chunk = source.shape[1] // layers
    lane_tiles = cells // 128
    backwards = lax.rem(lax.axis_index("azim"), around // 2) >= around // 4

    def put_field(slot, k, value):
        at = pl.ds(pl.multiple_of(slot * layers, layers), layers)
        for tile in range(lane_tiles):
            parts[k, tile, at, :] = value[:, tile * 128 : (tile + 1) * 128]

    def get_field(slot, k, shift=0):
        at = pl.ds(slot * layers + shift, layers)
        return jnp.concatenate([parts[k, tile, at, :] for tile in range(lane_tiles)], axis=1)

    def put_parts(slot, normals, plane, speed):
        inverse = inverse_of(*normals)
        for k, value in enumerate((*normals, plane, inverse, -inverse, 0.5 * speed)):
            put_field(slot, k, value)

    def put_packed(slot, side):
        values = [ends_ref[side, k].astype(F32) for k in range(5)]
        put_parts(slot, values[:3], values[3], values[4])

    def own_parts(row, _):
        put_parts(
            row,
            [normals_ref[k, row].astype(F32) for k in range(3)],
            plane_value(planes_ref[row], flags_ref[row]),
            courant_ref[0, row].astype(F32),
        )
        put_field(row, 7, 0.5 * courant_ref[1, row].astype(F32))
        return 0

    lax.fori_loop(0, block, own_parts, 0, unroll=2)

    def put_row(slot, normals, planes, flags, courant):
        put_parts(
            slot,
            [normals[k, 0].astype(F32) for k in range(3)],
            plane_value(planes[0], flags[0]),
            courant[0, 0].astype(F32),
        )

    def put_next():
        put_row(block, next_normals_ref, next_planes_ref, next_flags_ref, next_courant_ref)

    if chunk_index < chunks - 1:
        put_next()
    else:
        pl.when(step < steps - 1)(put_next)

        @pl.when(step == steps - 1)
        def _():
            put_packed(block, 1)

    def read_parts(slot):
        return [get_field(slot, k) for k in range(6)]

    @pl.when(step == 0)
    def _():
        if chunk_index == 0:
            put_packed(block + 1, 0)
        else:
            put_row(
                block + 1, last_normals_ref, last_planes_ref, last_flags_ref, last_courant_ref
            )
        speed = get_field(block + 1, 6) + get_field(0, 6)
        kept[0] = upwind_flux(0, read_parts(block + 1), read_parts(0), speed)
        kept[1] = speed

    index = lax.broadcasted_iota(jnp.int32, (1, cells), 1)
    place = index.astype(F32)
    radius = 1.0 + (place + 0.5) / cells
    next_radius = 1.0 + (place + 1.5) / cells
    face_radius = 1.0 + (place + 1.0) / cells
    inverse_radius = 1.0 / radius
    inner = lax.broadcasted_iota(jnp.int32, (layers, cells), 1) < cells - 1
    layer = lax.broadcasted_iota(jnp.int32, (layers, cells), 0)
    last_layer = layer == layers - 1
    first_layer = layer == 0

    def one_row(row, _):
        own = read_parts(row)
        speed = get_field(row, 6) + get_field(row + 1, 6)
        flux = upwind_flux(0, own, read_parts(row + 1), speed)
        gained = flux - kept[0]
        divergence = speed - kept[1]
        kept[0] = flux
        kept[1] = speed

        above = [None if k == 4 else get_field(row, k, 1) for k in range(6)]
        speed = get_field(row, 7) + get_field(row, 7, 1)
        flux = upwind_flux(1, own, above, speed)
        flux = jnp.where(last_layer, axial_flux_ref[1, pl.ds(row, 1), :], flux)
        speed = jnp.where(last_layer, axial_speed_ref[1, pl.ds(row, 1), :], speed)
        gained = gained + (
            flux - jnp.where(first_layer, axial_flux_ref[0, pl.ds(row, 1), :], pltpu.roll(flux, 1, 0))
        )
        divergence = divergence + (
            speed - jnp.where(first_layer, axial_speed_ref[0, pl.ds(row, 1), :], pltpu.roll(speed, 1, 0))
        )

        half = 0.5 * courant_ref[2, row].astype(F32)
        outer = [None if k == 4 else pltpu.roll(field, cells - 1, 1) for k, field in enumerate(own)]
        speed = jnp.where(inner, half + pltpu.roll(half, cells - 1, 1), 0.0)
        flux = upwind_flux(2, own, outer, speed, radius, next_radius)
        gained = gained + (flux - pltpu.roll(flux, 1, 1)) * inverse_radius
        carried = face_radius * speed
        divergence = divergence + (carried - pltpu.roll(carried, 1, 1)) * inverse_radius
        updated = fraction_ref[row] - gained
        updated_ref[row] = updated
        result = divergence + BUOYANCY * updated
        at = step * block + row
        at = jnp.where(backwards, chunk - 1 - at, at)
        for tile in range(lane_tiles):
            source[tile, pl.ds(at, layers, stride=chunk), :] = result[
                :, tile * 128 : (tile + 1) * 128
            ]
        return 0

    lax.fori_loop(0, block, one_row, 0, unroll=2)

    @pl.when(step == steps - 1)
    def _():
        modes = basis_ref.shape[1]
        scales[...] = jnp.zeros_like(scales)

        def radial(z, _):
            at = pl.ds(pl.multiple_of(z * 2 * chunk, 2 * chunk), 2 * chunk)
            rows = jnp.concatenate([source[tile, at, :] for tile in range(lane_tiles)], axis=1)
            both = dot3((basis_ref[0], basis_ref[1]), split(rows), ((1,), (1,)))
            for half in range(2):
                got = both[:, half * chunk : (half + 1) * chunk]
                scales[...] = jnp.maximum(scales[...], jnp.abs(got))
                wide[pl.ds(z * 2 + half, modes, stride=layers), :] = got
            return 0

        lax.fori_loop(0, layers // 2, radial, 0)
        exponent = exponent_of(scales[...])
        devices, _, height, lanes = sent_ref.shape
        share = modes // devices
        codes = exponent.astype(jnp.int32).astype(jnp.int16)
        sent_ref[:, share] = codes.reshape(devices, share, lanes)
        scales[...] = CODE_TOP / jnp.exp2(exponent * (1.0 / 256.0))

        def coding(device, _):
            for mode in range(share):
                row = device * share + mode
                values = wide[pl.ds(pl.multiple_of(row * layers, layers), layers), :]
                sent_ref[device, mode] = to_codes(values * scales[pl.ds(row, 1), :])
            return 0

        lax.fori_loop(0, devices, coding, 0)


def advect_chunk(arrays, ends, axial_flux, axial_speed, basis, chunk_index, chunk, around, devices, base):
    fraction, normals, planes, flags, courant = arrays
    rows, layers, cells = fraction.shape
    block = BLOCK
    steps = chunk // block
    first = chunk_index * steps
    share = cells // devices

    def here(i):
        return first + i

    def after(i):
        return jnp.minimum((first + i + 1) * block, rows - 1)

    whole = pl.BlockSpec((block, layers, cells), lambda i: (here(i), 0, 0))
    triple = pl.BlockSpec((3, block, layers, cells), lambda i: (0, here(i), 0, 0))
    row = pl.BlockSpec((1, layers, cells), lambda i: (after(i), 0, 0))
    before = max(first * block - 1, 0)
    last_row = pl.BlockSpec((1, layers, cells), lambda i: (before, 0, 0))
    edge = pl.BlockSpec((2, block, cells), lambda i: (0, here(i), 0))
    in_specs = [
        whole,
        triple,
        whole,
        whole,
        triple,
        pl.BlockSpec((3, 1, layers, cells), lambda i: (0, after(i), 0, 0)),
        row,
        row,
        pl.BlockSpec((1, 1, layers, cells), lambda i: (0, after(i), 0, 0)),
        pl.BlockSpec((3, 1, layers, cells), lambda i: (0, before, 0, 0)),
        last_row,
        last_row,
        pl.BlockSpec((1, 1, layers, cells), lambda i: (0, before, 0, 0)),
        pl.BlockSpec(ends.shape, lambda i: (0, 0, 0, 0)),
        edge,
        edge,
        pl.BlockSpec((2, cells, cells), lambda i: (0, 0, 0)),
    ]
    operands = [
        fraction, normals, planes, flags, courant,
        normals, planes, flags, courant,
        normals, planes, flags, courant,
        ends, axial_flux, axial_speed, basis,
    ]
    aliases = {}
    if base is not None:
        in_specs.append(pl.BlockSpec(memory_space=pl.ANY))
        operands.append(base)
        aliases = {len(operands) - 1: 0}
    return pl.pallas_call(
        functools.partial(chunk_kernel, around, chunk_index, rows // chunk),
        grid=(steps,),
        in_specs=in_specs,
        out_specs=[
            whole,
            pl.BlockSpec((devices, share + 1, layers, chunk), lambda i: (0, 0, 0, 0)),
        ],
        out_shape=[
            jax.ShapeDtypeStruct(fraction.shape, F32),
            jax.ShapeDtypeStruct((devices, share + 1, layers, chunk), jnp.int16),
        ],
        scratch_shapes=[
            pltpu.VMEM((8, cells // 128, (block + 2) * layers, 128), F32),
            pltpu.VMEM((2, layers, cells), F32),
            pltpu.VMEM((cells // 128, layers * chunk, 128), F32),
            pltpu.VMEM((cells * layers, chunk), F32),
            pltpu.VMEM((cells, chunk), F32),
        ],
        input_output_aliases=aliases,
        compiler_params=pltpu.CompilerParams(vmem_limit_bytes=60 * 2**20),
        cost_estimate=pl.CostEstimate(
            flops=40000 * chunk * layers * cells, bytes_accessed=30 * chunk * layers * cells, transcendentals=0
        ),
        name="advect_chunk",
    )(*operands)


@functools.lru_cache(None)
def folded_tables(total):
    quarter = total // 4
    place = np.arange(quarter) + 0.5

    def halves(x):
        high = x.astype(jnp.bfloat16)
        return np.stack([high, (x - high.astype(np.float64)).astype(jnp.bfloat16)])

    tables, rates, weights = [], [], []
    for waves, wave in (
        (2 * np.arange(quarter), np.cos),
        (2 * np.arange(quarter) + 2, np.sin),
        (2 * np.arange(quarter) + 1, np.cos),
        (2 * np.arange(quarter) + 1, np.sin),
    ):
        doubled = waves[:, None] * (2 * np.arange(quarter) + 1)[None, :] % (2 * total)
        tables.append(wave(np.pi * doubled / total))
        rates.append(2.0 - 2.0 * np.cos(2.0 * np.pi * waves / total))
        weights.append(np.where((waves == 0) | (waves == total // 2), 1.0, 2.0) / total)
    tables = np.stack(tables)
    back = np.stack([halves(t) for t in tables])
    forth = np.stack([halves(t.T) for t in tables])
    return forth, back, np.stack(rates)[:, None].astype(np.float32), np.stack(weights)[:, None].astype(np.float32)


def decoded(values):
    return values.astype(jnp.int32).astype(F32)


def scale_of(codes):
    return jnp.exp2(decoded(codes) * (1.0 / 256.0)) * (1.0 / CODE_TOP)


def solve_kernel(around, along, chunks, start, *refs):
    got = refs[:chunks]
    extra = refs[chunks : 2 * chunks]
    mix, unmix, forth_ref, back_ref, rates, weights, shifts = refs[2 * chunks : 2 * chunks + 7]
    sent, high, low, result, scale, exponents, forth, back, arrived = refs[2 * chunks + 7 :]
    copies = [
        pltpu.make_async_copy(forth_ref, forth, arrived.at[0]),
        pltpu.make_async_copy(back_ref, back, arrived.at[1]),
    ]

    @pl.when(pl.program_id(0) == 0)
    def _():
        for copy in copies:
            copy.start()

    devices, count, layers, lanes = got[0].shape
    share = (sent.shape[1] - 1) // chunks
    pairs = around // 4
    step = pl.program_id(0)
    first = start + step * count
    for chunk in range(chunks):
        scale[chunk] = scale_of(extra[chunk][:, 0])
    if chunks * share < layers:
        exponents[...] = jnp.zeros_like(exponents)

    def spots():
        for pair in range(pairs):
            for chunk in range(chunks):
                mirror = chunks - 1 - chunk
                at = pl.ds((pair * chunks + chunk) * lanes, lanes)
                yield at, (
                    (pair, chunk),
                    (pair + 2 * pairs, chunk),
                    (2 * pairs - 1 - pair, mirror),
                    (4 * pairs - 1 - pair, mirror),
                )

    def fold(index, _):
        mode, axial = index // along, index % along
        rows = pl.ds(pl.multiple_of(index * layers, layers), layers)
        row = pl.ds(first + mode, 1)
        for at, places in spots():
            u0, u1, r0, r1 = [
                decoded(got[chunk][azim * along + axial, mode])
                * scale[chunk, azim * along + axial, row, :]
                for azim, chunk in places
            ]
            e0, o0, e1, o1 = u0 + u1, u0 - u1, r0 + r1, r0 - r1
            for k, folded in enumerate((e0 + e1, e0 - e1, o0 - o1, o0 + o1)):
                high[k, rows, at], low[k, rows, at] = split(folded)
        return 0

    lax.fori_loop(0, count * along, fold, 0)

    @pl.when(pl.program_id(0) == 0)
    def _():
        for copy in copies:
            copy.wait()

    height = mix.shape[1]
    parts = [pl.ds(at, height) for at in range(0, high.shape[1], height)]

    def waves(k, _):
        for at in parts:
            high[k, at], low[k, at] = split(
                dot3((mix[0], mix[1]), (high[k, at], low[k, at]))
            )
        spectrum = dot3((high[k], low[k]), (forth[k, 0], forth[k, 1]))
        high[k], low[k] = split(spectrum * weights[k] / (rates[k] + shifts[...]))
        high[k], low[k] = split(dot3((high[k], low[k]), (back[k, 0], back[k, 1])))
        for at in parts:
            result[k, at] = dot3((unmix[0], unmix[1]), (high[k, at], low[k, at]))
        return 0

    lax.fori_loop(0, 4, waves, 0)

    def unfold(index, _):
        mode, axial = index // along, index % along
        rows = pl.ds(pl.multiple_of(index * layers, layers), layers)
        for at, places in spots():
            ec, es, oc, os = [result[k, rows, at] for k in range(4)]
            e0, e1, o0, o1 = ec + es, ec - es, oc + os, os - oc
            for (azim, chunk), values in zip(places, (e0 + o0, e0 - o0, e1 + o1, e1 - o1)):
                device = azim * along + axial
                slot = chunk * share + step * count + mode
                exponent = exponent_of(jnp.max(jnp.abs(values), axis=0, keepdims=True))
                exponents[device, pl.ds(slot, 1), :] = exponent
                factor = CODE_TOP / jnp.exp2(exponent * (1.0 / 256.0))
                sent[device, slot] = to_codes(values * factor)
        return 0

    lax.fori_loop(0, count * along, unfold, 0)

    @pl.when(step == pl.num_programs(0) - 1)
    def _():
        sent[:, chunks * share] = exponents[...].astype(jnp.int32).astype(jnp.int16)


def solve_group(got, mix, unmix, tables, shifts, start, share, around, along):
    chunks = len(got)
    devices, slots, layers, lanes = got[0].shape
    modes = slots - 1
    count = share
    steps = share // count
    block = start // count
    rows = count * along * layers
    forth, back, rates, weights = tables
    width = forth.shape[-1]

    def fixed(array):
        return pl.BlockSpec(array.shape, lambda i: (0,) * array.ndim, pipeline_mode=pl.Buffered(1))

    return pl.pallas_call(
        functools.partial(solve_kernel, around, along, chunks, start),
        grid=(steps,),
        in_specs=[
            pl.BlockSpec((devices, count, layers, lanes), lambda i: (0, block + i, 0, 0))
        ]
        * chunks
        + [pl.BlockSpec((devices, 1, layers, lanes), lambda i: (0, modes, 0, 0))] * chunks
        + [fixed(mix), fixed(unmix)]
        + [pl.BlockSpec(memory_space=pl.ANY)] * 2
        + [fixed(rates), fixed(weights)]
        + [pl.BlockSpec((rows, 1), lambda i: (block + i, 0))],
        out_specs=pl.BlockSpec(
            (devices, chunks * share + 1, layers, lanes), lambda i: (0, 0, 0, 0)
        ),
        out_shape=jax.ShapeDtypeStruct((devices, chunks * share + 1, layers, lanes), jnp.int16),
        scratch_shapes=[
            pltpu.VMEM((4, rows, width), BF16),
            pltpu.VMEM((4, rows, width), BF16),
            pltpu.VMEM((4, rows, width), F32),
            pltpu.VMEM((chunks, devices, layers, lanes), F32),
            pltpu.VMEM((devices, layers, lanes), F32),
            pltpu.VMEM(forth.shape, BF16),
            pltpu.VMEM(back.shape, BF16),
            pltpu.SemaphoreType.DMA((2,)),
        ],
        compiler_params=pltpu.CompilerParams(vmem_limit_bytes=60 * 2**20),
        cost_estimate=pl.CostEstimate(
            flops=60 * rows * width * width * steps, bytes_accessed=20 * 2**20, transcendentals=0
        ),
        name="solve_group",
    )(*got, *got, mix, unmix, forth, back, rates, weights, shifts)


def pressure_kernel(around, groups, *refs):
    got = refs[:groups]
    extra = refs[groups : 2 * groups]
    basis = refs[2 * groups]
    base = refs[2 * groups + 1 : -6]
    out, flat, wide, scale, high, low = refs[-6:]
    devices, _, layers, lanes = got[0].shape
    lane_tiles = out.shape[2] // 128
    chunk = pl.program_id(0)
    backwards = lax.rem(lax.axis_index("azim"), around // 2) >= around // 4
    i = lax.broadcasted_iota(jnp.int32, (lanes, lanes), 0)
    j = lax.broadcasted_iota(jnp.int32, (lanes, lanes), 1)
    turned_place = jnp.where(backwards, lanes - 1, 0) + jnp.where(backwards, -1, 1) * i
    turn = jnp.where(j == turned_place, 1.0, 0.0).astype(BF16)
    spans, filled = [], 0
    for group in range(groups):
        share = got[group].shape[1]
        spans.append((filled, devices * share))
        scale[group] = scale_of(extra[group][:, 0])

        def unpack(device, _, group=group, share=share, filled=filled):
            for mode in range(share):
                at = pl.multiple_of((filled + device * share + mode) * layers, layers)
                flat[pl.ds(at, layers), :] = (
                    decoded(got[group][device, mode])
                    * scale[group, device, pl.ds(chunk * share + mode, 1), :]
                )
            return 0

        lax.fori_loop(0, devices, unpack, 0)
        filled += devices * share

    together = high.shape[0] // lanes

    def radial(batch, _):
        for part in range(together):
            for offset, height in spans:
                z = batch * together + part
                values = split(flat[pl.ds(offset * layers + z, height, stride=layers), :])
                at = pl.ds(offset, height)
                for target, value in zip((high, low), values):
                    target[part * lanes : (part + 1) * lanes, at] = dot(
                        turn, value, ((1,), (1,))
                    ).astype(BF16)
        total = dot3((high[...], low[...]), (basis[0], basis[1]))
        for part in range(together):
            for tile in range(lane_tiles):
                wide[tile, pl.ds(batch * together + part, lanes, stride=layers), :] = total[
                    part * lanes : (part + 1) * lanes, tile * 128 : (tile + 1) * 128
                ]
        return 0

    lax.fori_loop(0, layers // together, radial, 0)
    for tile in range(lane_tiles):
        at = slice(tile * 128, (tile + 1) * 128)
        result = wide[tile].reshape(lanes, layers, 128)
        out[:, :, at] = result + base[0][:, :, at] if base else result


def pressure_of(got, basis, around, chunks, base=None):
    groups = len(got)
    devices, _, layers, lanes = got[0].shape
    shares = [(x.shape[1] - 1) // chunks for x in got]
    inner, cells = basis.shape[1:]
    whole = pl.BlockSpec((lanes, layers, cells), lambda i: (i, 0, 0))
    return pl.pallas_call(
        functools.partial(pressure_kernel, around, groups),
        grid=(chunks,),
        in_specs=[pl.BlockSpec((devices, share, layers, lanes), lambda i: (0, i, 0, 0)) for share in shares]
        + [
            pl.BlockSpec((devices, 1, layers, lanes), lambda i, share=share: (0, chunks * share, 0, 0))
            for share in shares
        ]
        + [pl.BlockSpec(basis.shape, lambda i: (0, 0, 0), pipeline_mode=pl.Buffered(1))]
        + ([] if base is None else [whole]),
        out_specs=whole,
        out_shape=jax.ShapeDtypeStruct((lanes * chunks, layers, cells), F32),
        scratch_shapes=[
            pltpu.VMEM((inner * layers, lanes), F32),
            pltpu.VMEM((cells // 128, lanes * layers, 128), F32),
            pltpu.VMEM((groups, devices, layers, lanes), F32),
            pltpu.VMEM((4 * lanes, inner), BF16),
            pltpu.VMEM((4 * lanes, inner), BF16),
        ],
        compiler_params=pltpu.CompilerParams(vmem_limit_bytes=60 * 2**20),
        cost_estimate=pl.CostEstimate(
            flops=20 * lanes * chunks * layers * cells * inner,
            bytes_accessed=20 * 2**20,
            transcendentals=0,
        ),
        name="pressure_of",
    )(*got, *got, basis, *([] if base is None else [base]))


def halves(values):
    high = lax.reduce_precision(values, 8, 7)
    return jnp.stack([high.astype(BF16), (values - high).astype(BF16)])


def exchanged(sent):
    return lax.all_to_all(sent, ("azim", "axial"), split_axis=0, concat_axis=0, tiled=True)


def following_kernel(values_ref, earlier_ref, out_ref):
    del values_ref, earlier_ref, out_ref


def following(values, earlier):
    anywhere = pl.BlockSpec(memory_space=pl.ANY)
    return pl.pallas_call(
        following_kernel,
        in_specs=[anywhere, anywhere],
        out_specs=anywhere,
        out_shape=jax.ShapeDtypeStruct(values.shape, values.dtype),
        input_output_aliases={0: 0},
        name="following",
    )(values, earlier)


def overlapped(
    fraction,
    normals,
    planes,
    cell_flags,
    courant,
    radial_basis,
    axial_basis,
    radial_rates,
    axial_rates,
):
    rows, layers, cells = fraction.shape
    around, along = lax.axis_size("azim"), lax.axis_size("axial")
    devices = around * along
    modes = cells // devices
    chunks = rows // CHUNK
    axial_flux, axial_speed, ends = halos(normals, planes, cell_flags, courant)
    forward_basis = halves(radial_basis.T)
    arrays = (fraction, normals, planes, cell_flags, courant)
    updated, got = None, []
    for chunk in range(chunks):
        updated, sent = advect_chunk(
            arrays, ends, axial_flux, axial_speed, forward_basis, chunk, CHUNK, around, devices, updated
        )
        got.append(exchanged(following(sent, got[-1]) if got else sent))
    count = jnp.eye(4, dtype=F32)
    mix, unmix = halves(jnp.kron(count, axial_basis.T)), halves(jnp.kron(count, axial_basis))
    first = (lax.axis_index("azim") * along + lax.axis_index("axial")) * modes
    shifts = lax.dynamic_slice_in_dim(radial_rates, first, modes)[:, None] + axial_rates[None, :]
    shifts = shifts.reshape(modes * along * layers, 1)
    tables = [jnp.asarray(x) for x in folded_tables(rows * around)]
    returned, bases = [], []
    for start, share in SOLVED:
        sent = solve_group(got, mix, unmix, tables, shifts, start, share, around, along)
        returned.append(exchanged(following(sent, returned[-1]) if returned else sent))
        rows_of = radial_basis.T.reshape(devices, modes, cells)[:, start : start + share]
        bases.append(rows_of.reshape(devices * share, cells))
    pressure = pressure_of(returned[:-1], halves(jnp.concatenate(bases[:-1])), around, chunks)
    pressure = pressure_of(returned[-1:], halves(bases[-1]), around, chunks, pressure)
    return (updated, pressure)


def fits(fraction):
    rows, layers, cells = fraction.shape
    around, along = lax.axis_size("azim"), lax.axis_size("axial")
    modes = cells // (around * along)
    chunks = rows // CHUNK
    return (
        rows % CHUNK == 0
        and layers == 16
        and modes == 16
        and modes // 2 * chunks == layers
        and cells % 128 == 0
        and around % 4 == 0
        and along > 2
    )


def local(*arguments):
    return overlapped(*arguments) if fits(arguments[0]) else stepwise(*arguments)


def solution(mesh):
    placed = (
        P("azim", "axial", None),
        P(None, "azim", "axial", None),
        P("azim", "axial", None),
        P("azim", "axial", None),
        P(None, "azim", "axial", None),
        P(),
        P(),
        P(),
        P(),
    )
    return jax.shard_map(
        local,
        mesh=mesh,
        in_specs=placed,
        out_specs=(P("azim", "axial", None), P("azim", "axial", None)),
        check_vma=False,
    )
```

```python
import functools

import jax
import jax.numpy as jnp
import numpy as np
from jax import lax
from jax.experimental import pallas as pl
from jax.experimental.pallas import tpu as pltpu
from jax.sharding import PartitionSpec as P

HIGH = lax.Precision.HIGH
BUOYANCY = 0.5
CODE_TOP = 32700.0


def shifted_in(edge, axis, towards_lower):
    count = lax.axis_size(axis)
    if towards_lower:
        pairs = [((i + 1) % count, i) for i in range(count)]
    else:
        pairs = [(i, (i + 1) % count) for i in range(count)]
    return lax.ppermute(edge, axis, pairs)


def cell_parts(n0, n1, n2, code):
    m0, m1, m2 = jnp.abs(n0), jnp.abs(n1), jnp.abs(n2)
    return (n0, n1, n2, code, 1.0 / (6.0 * m0 * m1 * m2))


def cube(height):
    held = jnp.maximum(height, 0.0)
    return held * held * held


def face_flux(direction, lower, upper, speed, lower_weight=None, upper_weight=None):
    forward = speed > 0.0
    signed = jnp.where(forward, lower[direction], -upper[direction])
    first, second = [d for d in range(3) if d != direction]
    along = jnp.abs(signed)
    side_a = jnp.abs(jnp.where(forward, lower[first], upper[first]))
    side_b = jnp.abs(jnp.where(forward, lower[second], upper[second]))
    code = jnp.where(forward, lower[3], upper[3])
    inverse = jnp.where(forward, lower[4], upper[4])
    width = jnp.abs(speed)
    near = code - along * jnp.where(signed < 0.0, 0.0, 1.0 - width)
    far = near - along * width
    sides = side_a + side_b
    total = (cube(near) - cube(near - side_a)) - (cube(near - side_b) - cube(near - sides))
    total = total - ((cube(far) - cube(far - side_a)) - (cube(far - side_b) - cube(far - sides)))
    volume = jnp.where(code > 3.0, width, jnp.where(code < -0.5, 0.0, total * inverse))
    if lower_weight is not None:
        volume = volume * jnp.where(forward, lower_weight, upper_weight)
    return jnp.where(forward, volume, jnp.where(speed < 0.0, -volume, 0.0))


def advect_kernel(
    fraction_ref,
    normals_ref,
    planes_ref,
    flags_ref,
    courant_ref,
    next_ref,
    high_ref,
    low_azim_ref,
    low_axial_ref,
    updated_ref,
    source_ref,
    kept,
):
    rows, layers, cells = fraction_ref.shape
    f32 = jnp.float32

    @pl.when(pl.program_id(0) == 0)
    def _():
        kept[...] = low_azim_ref[...]

    index = lax.broadcasted_iota(jnp.int32, (1, cells), 1)
    place = index.astype(f32)
    radius = 1.0 + (place + 0.5) / cells
    next_radius = 1.0 + (place + 1.5) / cells
    face_radius = 1.0 + (place + 1.0) / cells
    inverse_radius = 1.0 / radius
    inner = lax.broadcasted_iota(jnp.int32, (layers, cells), 1) < cells - 1
    layer = lax.broadcasted_iota(jnp.int32, (layers, cells), 0)
    last_layer = layer == layers - 1
    first_layer = layer == 0

    def row_parts(row):
        flags = flags_ref[row]
        code = jnp.where(
            flags == 2, planes_ref[row].astype(f32), jnp.where(flags == 1, 4.0, -1.0)
        )
        return cell_parts(
            normals_ref[0, row].astype(f32),
            normals_ref[1, row].astype(f32),
            normals_ref[2, row].astype(f32),
            code,
        )

    def one_row(row, upper, upper_speed):
        own = row_parts(row)
        moved = [courant_ref[d, row].astype(f32) for d in range(3)]
        speed = 0.5 * (moved[0] + upper_speed)
        flux = face_flux(0, own, upper, speed)
        gained = flux - kept[0]
        divergence = speed - kept[1]
        kept[0] = flux
        kept[1] = speed
        beyond = cell_parts(*[high_ref[k, row] for k in range(4)])
        above = [
            jnp.where(last_layer, high, pltpu.roll(field, layers - 1, 0))
            for field, high in zip(own, beyond)
        ]
        speed = 0.5 * (
            moved[1]
            + jnp.where(last_layer, high_ref[4, row], pltpu.roll(moved[1], layers - 1, 0))
        )
        flux = face_flux(1, own, above, speed)
        gained = gained + (
            flux - jnp.where(first_layer, low_axial_ref[0, row], pltpu.roll(flux, 1, 0))
        )
        divergence = divergence + (
            speed - jnp.where(first_layer, low_axial_ref[1, row], pltpu.roll(speed, 1, 0))
        )
        outer = [pltpu.roll(field, cells - 1, 1) for field in own]
        speed = 0.5 * (moved[2] + pltpu.roll(moved[2], cells - 1, 1))
        speed = jnp.where(inner, speed, 0.0)
        flux = face_flux(2, own, outer, speed, radius, next_radius)
        gained = gained + (flux - pltpu.roll(flux, 1, 1)) * inverse_radius
        carried = face_radius * speed
        divergence = divergence + (carried - pltpu.roll(carried, 1, 1)) * inverse_radius
        updated = fraction_ref[row] - gained
        updated_ref[row] = updated
        source_ref[row] = divergence + BUOYANCY * updated

    def step(row, _):
        one_row(row, row_parts(row + 1), courant_ref[0, row + 1].astype(f32))
        return 0

    lax.fori_loop(0, rows - 1, step, 0)
    one_row(
        rows - 1,
        cell_parts(*[next_ref[k, 0].astype(f32) for k in range(4)]),
        next_ref[4, 0].astype(f32),
    )


def plane_codes(planes, flags):
    return jnp.where(
        flags == 2, planes.astype(jnp.float32), jnp.where(flags == 1, 4.0, -1.0)
    ).astype(jnp.bfloat16)


def packed_edge(normals, planes, flags, courant, direction, pick):
    parts = [pick(normals[d]) for d in range(3)]
    parts.append(plane_codes(pick(planes), pick(flags)))
    parts.append(pick(courant[direction]))
    return jnp.stack(parts)


def low_face(direction, lower, upper):
    lower, upper = lower.astype(jnp.float32), upper.astype(jnp.float32)
    speed = 0.5 * (lower[4] + upper[4])
    flux = face_flux(direction, cell_parts(*lower[:4]), cell_parts(*upper[:4]), speed)
    return jnp.stack([flux, speed])


def advect(fraction, normals, planes, flags, courant):
    rows, layers, cells = fraction.shape
    block = 16 if rows % 16 == 0 else 1
    blocks = rows // block
    fields = (normals, planes, flags, courant)
    top_row = packed_edge(*fields, 0, lambda x: x[rows - 1])
    bottom_row = packed_edge(*fields, 0, lambda x: x[0])
    top_layer = packed_edge(*fields, 1, lambda x: x[:, layers - 1])
    bottom_layer = packed_edge(*fields, 1, lambda x: x[:, 0])
    high_row = shifted_in(bottom_row, "azim", True)
    low_row = shifted_in(top_row, "azim", False)
    high_layer = shifted_in(bottom_layer, "axial", True)
    low_layer = shifted_in(top_layer, "axial", False)
    low_azim = low_face(0, low_row, bottom_row)
    low_axial = low_face(1, low_layer, bottom_layer)[:, :, None]
    high_axial = high_layer.astype(jnp.float32)[:, :, None]
    inside = packed_edge(*fields, 0, lambda x: x[block::block])
    following = jnp.concatenate([inside, high_row[:, None]], axis=1)
    whole = pl.BlockSpec((block, layers, cells), lambda i: (i, 0, 0))
    triple = pl.BlockSpec((3, block, layers, cells), lambda i: (0, i, 0, 0))
    return pl.pallas_call(
        advect_kernel,
        grid=(blocks,),
        in_specs=[
            whole,
            triple,
            whole,
            whole,
            triple,
            pl.BlockSpec((5, 1, layers, cells), lambda i: (0, i, 0, 0)),
            pl.BlockSpec((5, block, 1, cells), lambda i: (0, i, 0, 0)),
            pl.BlockSpec((2, layers, cells), lambda i: (0, 0, 0)),
            pl.BlockSpec((2, block, 1, cells), lambda i: (0, i, 0, 0)),
        ],
        out_specs=[whole, whole],
        out_shape=[jax.ShapeDtypeStruct(fraction.shape, jnp.float32)] * 2,
        scratch_shapes=[pltpu.VMEM((2, layers, cells), jnp.float32)],
        compiler_params=pltpu.CompilerParams(vmem_limit_bytes=40 * 2**20),
    )(
        fraction,
        normals,
        planes,
        flags,
        courant,
        following,
        high_axial,
        low_azim,
        low_axial,
    )


def coded(values):
    most = jnp.max(jnp.abs(values), axis=-1)
    exponent = jnp.clip(jnp.ceil(jnp.log2(most) * 256.0) + 1.0, -30000.0, 30000.0)
    scale = CODE_TOP * jnp.exp2(exponent * (-1.0 / 256.0))
    codes = jnp.round(values * scale[..., None])
    return jnp.clip(codes, -32767.0, 32767.0).astype(jnp.int16), exponent.astype(jnp.int16)


def exchange(values):
    modes, cells = values.shape[1], values.shape[3]
    codes, exponent = coded(values)
    extra = jnp.pad(exponent.transpose(0, 2, 1), ((0, 0), (0, 0), (0, cells - modes)))
    sent = jnp.concatenate([codes, extra[:, None]], axis=1)
    got = lax.all_to_all(sent, ("azim", "axial"), split_axis=0, concat_axis=0, tiled=True)
    exponent = got[:, modes, :, :modes].transpose(0, 2, 1).astype(jnp.float32)
    scale = jnp.exp2(exponent * (1.0 / 256.0)) * (1.0 / CODE_TOP)
    return got[:, :modes].astype(jnp.float32) * scale[..., None]


@functools.lru_cache(None)
def azimuth_tables(total):
    half, quarter = total // 2, total // 4
    place = np.arange(half)

    def table(cosines, sines):
        waves = np.concatenate([cosines, sines])
        angles = 2.0 * np.pi / total * (waves[:, None] * place[None, :] % total)
        rows = np.concatenate(
            [np.cos(angles[: len(cosines)]), np.sin(angles[len(cosines) :])]
        ).astype(np.float32)
        rates = (2.0 - 2.0 * np.cos(2.0 * np.pi * waves / total)).astype(np.float32)
        ends = (waves == 0) | (waves == half)
        return rows, rates, (np.where(ends, 1.0, 2.0) / total).astype(np.float32)

    even = 2 * np.arange(quarter + 1)
    odd = 2 * np.arange(quarter) + 1
    return table(even, even[1:-1]), table(odd, odd)


def stepwise(
    fraction,
    normals,
    planes,
    cell_flags,
    courant,
    radial_basis,
    axial_basis,
    radial_rates,
    axial_rates,
):
    rows, layers, cells = fraction.shape
    around, along = lax.axis_size("azim"), lax.axis_size("axial")
    devices = around * along
    modes = cells // devices
    total = rows * around
    half = total // 2
    updated, source = advect(fraction, normals, planes, cell_flags, courant)
    radial_modes = jnp.einsum("azr,rj->jza", source, radial_basis, precision=HIGH)
    got = exchange(radial_modes.reshape(devices, modes, layers, rows))
    got = got.reshape(around, along, modes, layers, rows).transpose(2, 1, 3, 0, 4)
    got = got.reshape(modes, along * layers, total)
    both = jnp.einsum("jza,zn->jna", got, axial_basis, precision=HIGH)
    first = (lax.axis_index("azim") * along + lax.axis_index("axial")) * modes
    shifts = lax.dynamic_slice_in_dim(radial_rates, first, modes)[:, None] + axial_rates[None, :]
    low, high = both[..., :half], both[..., half:]
    solved = []
    for folded, (table, rates, weight) in zip((low + high, low - high), azimuth_tables(total)):
        coefficients = jnp.einsum("jna,ka->jnk", folded, table, precision=HIGH)
        scaled = coefficients / (rates + shifts[..., None]) * weight
        solved.append(jnp.einsum("jnk,ka->jna", scaled, table, precision=HIGH))
    physical = jnp.concatenate([solved[0] + solved[1], solved[0] - solved[1]], axis=-1)
    physical = jnp.einsum("jna,zn->jza", physical, axial_basis, precision=HIGH)
    physical = physical.reshape(modes, along, layers, around, rows).transpose(3, 1, 0, 2, 4)
    returned = exchange(physical.reshape(devices, modes, layers, rows))
    returned = returned.reshape(cells, layers, rows)
    pressure = jnp.einsum("jza,rj->azr", returned, radial_basis, precision=HIGH)
    return (updated, pressure)


CHUNK = 128
BLOCK = 16
SOLVED = ((0, 4), (8, 8), (4, 4))
FLUX_SCALE = 32767.0 / 0.3
F32 = jnp.float32
BF16 = jnp.bfloat16


def split(values):
    high = values.astype(BF16)
    return high, (values - high.astype(F32)).astype(BF16)


def dot(a, b, contract):
    return lax.dot_general(a, b, (contract, ((), ())), preferred_element_type=F32)


def dot3(a, b, contract=((1,), (0,))):
    return dot(a[0], b[0], contract) + (dot(a[0], b[1], contract) + dot(a[1], b[0], contract))


def slab_flux(normal, side_a, side_b, plane, inverse, speed):
    along = jnp.abs(normal)
    reach = normal * speed
    slab = jnp.abs(reach)
    near = plane - jnp.where(reach > 0.0, along - slab, 0.0)
    other = (slab + (side_a + side_b)) - near
    folded = near > other
    held = jnp.maximum(jnp.minimum(near, other), 0.0)
    low, high = jnp.minimum(side_a, side_b), jnp.maximum(side_a, side_b)
    by_low = jnp.maximum(held - low, 0.0)
    by_slab = jnp.maximum(held - slab, 0.0)
    last = jnp.maximum(held - (low + slab), 0.0) - jnp.maximum(held - high, 0.0)
    total = held * held * held - by_slab * by_slab * by_slab
    total = total - (by_low * by_low * by_low - last * last * last)
    flux = total * inverse
    return jnp.where(folded, speed - flux, flux)


def upwind_flux(direction, lower, upper, speed, lower_weight=None, upper_weight=None):
    forward = speed > 0.0
    first, second = [d for d in range(3) if d != direction]
    normal = jnp.where(forward, lower[direction], upper[direction])
    side_a = jnp.abs(jnp.where(forward, lower[first], upper[first]))
    side_b = jnp.abs(jnp.where(forward, lower[second], upper[second]))
    plane = jnp.where(forward, lower[3], upper[3])
    inverse = jnp.where(forward, lower[4], upper[5])
    flux = slab_flux(normal, side_a, side_b, plane, inverse, speed)
    if lower_weight is not None:
        flux = flux * jnp.where(forward, lower_weight, upper_weight)
    return flux


def inverse_of(n0, n1, n2):
    return 1.0 / (6.0 * jnp.abs(n0 * n1 * n2))


def plane_value(planes, flags):
    return jnp.where(flags == 2, planes.astype(F32), jnp.where(flags == 1, 4.0, -4.0))


def halo_kernel(
    courant_ref,
    normals_ref,
    planes_ref,
    flags_ref,
    first_normals_ref,
    first_planes_ref,
    first_flags_ref,
    first_courant_ref,
    last_normals_ref,
    last_planes_ref,
    last_flags_ref,
    last_courant_ref,
    flux_ref,
    speed_ref,
    ends_ref,
    work,
    edge,
    edge_in,
    fields,
    code,
    code_in,
    packs,
    packs_in,
    row_send,
    row_recv,
    edge_send,
    edge_recv,
    code_send,
    code_recv,
):
    step = pl.program_id(0)
    half = pl.num_programs(0) // 2
    span, layers, cells = planes_ref.shape
    groups, group = code.shape[1:3]
    per_group = group // span
    tiles = cells // 128
    neighbours = []
    for axis in ("azim", "axial"):
        count, me = lax.axis_size(axis), lax.axis_index(axis)
        neighbours.append(
            ({axis: lax.rem(me + count - 1, count)}, {axis: lax.rem(me + 1, count)})
        )

    def remote(source, target, send, recv, device):
        return pltpu.make_async_remote_copy(
            src_ref=source,
            dst_ref=target,
            send_sem=send,
            recv_sem=recv,
            device_id=device,
            device_id_type=pl.DeviceIdType.MESH,
        )

    row_copies = [
        remote(packs.at[s], packs_in.at[1 - s], row_send.at[s], row_recv.at[1 - s], neighbours[0][s])
        for s in range(2)
    ]
    def edge_copy(s, g):
        return remote(
            edge.at[s, g],
            edge_in.at[1 - s, g],
            edge_send.at[s, g],
            edge_recv.at[1 - s, g],
            neighbours[1][s],
        )

    def code_copy(s, g):
        return remote(
            code.at[s, g],
            code_in.at[1 - s, g],
            code_send.at[s, g],
            code_recv.at[1 - s, g],
            neighbours[1][s],
        )

    @pl.when(step == 0)
    def _():
        barrier = pltpu.get_barrier_semaphore()
        for pair in neighbours:
            for device in pair:
                pl.semaphore_signal(
                    barrier, inc=1, device_id=device, device_id_type=pl.DeviceIdType.MESH
                )
        pl.semaphore_wait(barrier, 4)
        for s, (normals, planes, flags, courant) in enumerate(
            (
                (first_normals_ref, first_planes_ref, first_flags_ref, first_courant_ref),
                (last_normals_ref, last_planes_ref, last_flags_ref, last_courant_ref),
            )
        ):
            for k in range(3):
                packs[s, k] = normals[k, 0]
            packs[s, 3] = plane_value(planes[0], flags[0]).astype(BF16)
            packs[s, 4] = courant[0, 0]
        for copy in row_copies:
            copy.start()

    def layer_rows(tile, layer):
        return work[tile, pl.ds(layer, span, stride=layers), :]

    @pl.when(step < half)
    def _():
        place = step // per_group
        at = pl.ds(pl.multiple_of(lax.rem(step, per_group) * span, span), span)
        for tile in range(tiles):
            lanes = pl.ds(tile * 128, 128)
            work[tile] = courant_ref[0, :, :, lanes].astype(F32).reshape(span * layers, 128)
            for s, layer in ((0, 0), (1, layers - 1)):
                edge[s, place, at, lanes] = layer_rows(tile, layer).astype(BF16)

    for g in range(groups):

        @pl.when(step == (g + 1) * per_group - 1)
        def _(g=g):
            for s in range(2):
                edge_copy(s, g).start()

    @pl.when(step >= half)
    def _():
        at = pl.ds(pl.multiple_of((step - half) * span, span), span)
        for k in range(4):
            for tile in range(tiles):
                lanes = pl.ds(tile * 128, 128)
                if k < 3:
                    field = normals_ref[k, :, :, lanes].astype(F32)
                else:
                    field = plane_value(planes_ref[:, :, lanes], flags_ref[:, :, lanes])
                work[tile] = field.reshape(span * layers, 128)
                for s, layer in ((0, 0), (1, layers - 1)):
                    fields[s, k, at, lanes] = layer_rows(tile, layer)

    for g in range(groups):

        @pl.when(step == half + (g + 1) * per_group - 1)
        def _(g=g):
            for s in range(2):
                edge_copy(s, g).wait()
            for s in range(2):

                def donate(piece, _, s=s):
                    inside = pl.ds(pl.multiple_of(piece * 16, 16), 16)
                    at = pl.ds(pl.multiple_of(g * group + piece * 16, 16), 16)
                    normals = [fields[s, k, at, :] for k in range(3)]
                    own, beyond = edge[s, g, inside, :], edge_in[s, g, inside, :]
                    speed = 0.5 * (own.astype(F32) + beyond.astype(F32))
                    inverse = inverse_of(*normals)
                    flux = slab_flux(
                        normals[1],
                        jnp.abs(normals[0]),
                        jnp.abs(normals[2]),
                        fields[s, 3, at, :],
                        inverse if s == 1 else -inverse,
                        speed,
                    )
                    flux = jnp.where(speed > 0.0 if s == 1 else speed < 0.0, flux, 0.0)
                    flux_ref[s, at, :] = flux
                    speed_ref[s, at, :] = speed
                    code[s, g, inside, :] = to_codes(flux * FLUX_SCALE)
                    return 0

                lax.fori_loop(0, group // 16, donate, 0)
                code_copy(s, g).start()

    @pl.when(step == 2 * half - 1)
    def _():
        for copy in row_copies:
            copy.wait()
        ends_ref[...] = packs_in[...]
        for g in range(groups):
            for s in range(2):
                code_copy(s, g).wait()
            for s in range(2):
                at = pl.ds(g * group, group)
                received = code_in[s, g].astype(jnp.int32).astype(F32)
                flux_ref[s, at, :] += received * (1.0 / FLUX_SCALE)


def halos(normals, planes, flags, courant):
    rows, layers, cells = planes.shape
    span, groups = 32, 4
    half = rows // span

    def later(i):
        return jnp.maximum(i - half, 0)

    whole = pl.BlockSpec((span, layers, cells), lambda i: (later(i), 0, 0))
    in_specs = [
        pl.BlockSpec((1, span, layers, cells), lambda i: (1, jnp.minimum(i, half - 1), 0, 0)),
        pl.BlockSpec((3, span, layers, cells), lambda i: (0, later(i), 0, 0)),
        whole,
        whole,
    ]
    for row in (0, rows - 1):
        one = pl.BlockSpec((1, layers, cells), lambda i, row=row: (row, 0, 0))
        in_specs += [
            pl.BlockSpec((3, 1, layers, cells), lambda i, row=row: (0, row, 0, 0)),
            one,
            one,
            pl.BlockSpec((1, 1, layers, cells), lambda i, row=row: (0, row, 0, 0)),
        ]
    pair = pl.BlockSpec((2, rows, cells), lambda i: (0, 0, 0))
    ends = (2, 5, layers, cells)
    split_shape = (2, groups, rows // groups, cells)
    dma = pltpu.SemaphoreType.DMA
    return pl.pallas_call(
        halo_kernel,
        grid=(2 * half,),
        in_specs=in_specs,
        out_specs=[pair, pair, pl.BlockSpec(ends, lambda i: (0, 0, 0, 0))],
        out_shape=[
            jax.ShapeDtypeStruct((2, rows, cells), F32),
            jax.ShapeDtypeStruct((2, rows, cells), F32),
            jax.ShapeDtypeStruct(ends, BF16),
        ],
        scratch_shapes=[
            pltpu.VMEM((cells // 128, span * layers, 128), F32),
            pltpu.VMEM(split_shape, BF16),
            pltpu.VMEM(split_shape, BF16),
            pltpu.VMEM((2, 4, rows, cells), F32),
            pltpu.VMEM(split_shape, jnp.int16),
            pltpu.VMEM(split_shape, jnp.int16),
            pltpu.VMEM(ends, BF16),
            pltpu.VMEM(ends, BF16),
            dma((2,)),
            dma((2,)),
            dma((2, groups)),
            dma((2, groups)),
            dma((2, groups)),
            dma((2, groups)),
        ],
        compiler_params=pltpu.CompilerParams(
            collective_id=0, has_side_effects=True, vmem_limit_bytes=60 * 2**20
        ),
        name="halos",
    )(courant, normals, planes, flags, *(normals, planes, flags, courant) * 2)


def exponent_of(most):
    return jnp.clip(jnp.ceil(jnp.log2(jnp.maximum(most, 1e-29)) * 256.0) + 1.0, -25000.0, 30000.0)


def to_codes(values):
    return jnp.round(values).astype(jnp.int32).astype(jnp.int16)


def chunk_kernel(
    around,
    chunk_index,
    chunks,
    fraction_ref,
    normals_ref,
    planes_ref,
    flags_ref,
    courant_ref,
    next_normals_ref,
    next_planes_ref,
    next_flags_ref,
    next_courant_ref,
    last_normals_ref,
    last_planes_ref,
    last_flags_ref,
    last_courant_ref,
    ends_ref,
    axial_flux_ref,
    axial_speed_ref,
    basis_ref,
    *rest,
):
    if chunk_index:
        rest = rest[1:]
    updated_ref, sent_ref, parts, kept, source, wide, scales = rest
    block, layers, cells = fraction_ref.shape
    steps = pl.num_programs(0)
    step = pl.program_id(0)
    chunk = source.shape[1] // layers
    lane_tiles = cells // 128
    backwards = lax.rem(lax.axis_index("azim"), around // 2) >= around // 4

    def put_field(slot, k, value):
        at = pl.ds(pl.multiple_of(slot * layers, layers), layers)
        for tile in range(lane_tiles):
            parts[k, tile, at, :] = value[:, tile * 128 : (tile + 1) * 128]

    def get_field(slot, k, shift=0):
        at = pl.ds(slot * layers + shift, layers)
        return jnp.concatenate([parts[k, tile, at, :] for tile in range(lane_tiles)], axis=1)

    def put_parts(slot, normals, plane, speed):
        inverse = inverse_of(*normals)
        for k, value in enumerate((*normals, plane, inverse, -inverse, 0.5 * speed)):
            put_field(slot, k, value)

    def put_packed(slot, side):
        values = [ends_ref[side, k].astype(F32) for k in range(5)]
        put_parts(slot, values[:3], values[3], values[4])

    def own_parts(row, _):
        put_parts(
            row,
            [normals_ref[k, row].astype(F32) for k in range(3)],
            plane_value(planes_ref[row], flags_ref[row]),
            courant_ref[0, row].astype(F32),
        )
        put_field(row, 7, 0.5 * courant_ref[1, row].astype(F32))
        return 0

    lax.fori_loop(0, block, own_parts, 0, unroll=2)

    def put_row(slot, normals, planes, flags, courant):
        put_parts(
            slot,
            [normals[k, 0].astype(F32) for k in range(3)],
            plane_value(planes[0], flags[0]),
            courant[0, 0].astype(F32),
        )

    def put_next():
        put_row(block, next_normals_ref, next_planes_ref, next_flags_ref, next_courant_ref)

    if chunk_index < chunks - 1:
        put_next()
    else:
        pl.when(step < steps - 1)(put_next)

        @pl.when(step == steps - 1)
        def _():
            put_packed(block, 1)

    def read_parts(slot):
        return [get_field(slot, k) for k in range(6)]

    @pl.when(step == 0)
    def _():
        if chunk_index == 0:
            put_packed(block + 1, 0)
        else:
            put_row(
                block + 1, last_normals_ref, last_planes_ref, last_flags_ref, last_courant_ref
            )
        speed = get_field(block + 1, 6) + get_field(0, 6)
        kept[0] = upwind_flux(0, read_parts(block + 1), read_parts(0), speed)
        kept[1] = speed

    index = lax.broadcasted_iota(jnp.int32, (1, cells), 1)
    place = index.astype(F32)
    radius = 1.0 + (place + 0.5) / cells
    next_radius = 1.0 + (place + 1.5) / cells
    face_radius = 1.0 + (place + 1.0) / cells
    inverse_radius = 1.0 / radius
    inner = lax.broadcasted_iota(jnp.int32, (layers, cells), 1) < cells - 1
    layer = lax.broadcasted_iota(jnp.int32, (layers, cells), 0)
    last_layer = layer == layers - 1
    first_layer = layer == 0

    def one_row(row, _):
        own = read_parts(row)
        speed = get_field(row, 6) + get_field(row + 1, 6)
        flux = upwind_flux(0, own, read_parts(row + 1), speed)
        gained = flux - kept[0]
        divergence = speed - kept[1]
        kept[0] = flux
        kept[1] = speed

        above = [None if k == 4 else get_field(row, k, 1) for k in range(6)]
        speed = get_field(row, 7) + get_field(row, 7, 1)
        flux = upwind_flux(1, own, above, speed)
        flux = jnp.where(last_layer, axial_flux_ref[1, pl.ds(row, 1), :], flux)
        speed = jnp.where(last_layer, axial_speed_ref[1, pl.ds(row, 1), :], speed)
        gained = gained + (
            flux - jnp.where(first_layer, axial_flux_ref[0, pl.ds(row, 1), :], pltpu.roll(flux, 1, 0))
        )
        divergence = divergence + (
            speed - jnp.where(first_layer, axial_speed_ref[0, pl.ds(row, 1), :], pltpu.roll(speed, 1, 0))
        )

        half = 0.5 * courant_ref[2, row].astype(F32)
        outer = [None if k == 4 else pltpu.roll(field, cells - 1, 1) for k, field in enumerate(own)]
        speed = jnp.where(inner, half + pltpu.roll(half, cells - 1, 1), 0.0)
        flux = upwind_flux(2, own, outer, speed, radius, next_radius)
        gained = gained + (flux - pltpu.roll(flux, 1, 1)) * inverse_radius
        carried = face_radius * speed
        divergence = divergence + (carried - pltpu.roll(carried, 1, 1)) * inverse_radius
        updated = fraction_ref[row] - gained
        updated_ref[row] = updated
        result = divergence + BUOYANCY * updated
        at = step * block + row
        at = jnp.where(backwards, chunk - 1 - at, at)
        for tile in range(lane_tiles):
            source[tile, pl.ds(at, layers, stride=chunk), :] = result[
                :, tile * 128 : (tile + 1) * 128
            ]
        return 0

    lax.fori_loop(0, block, one_row, 0, unroll=2)

    @pl.when(step == steps - 1)
    def _():
        modes = basis_ref.shape[1]
        scales[...] = jnp.zeros_like(scales)

        def radial(z, _):
            at = pl.ds(pl.multiple_of(z * 2 * chunk, 2 * chunk), 2 * chunk)
            rows = jnp.concatenate([source[tile, at, :] for tile in range(lane_tiles)], axis=1)
            both = dot3((basis_ref[0], basis_ref[1]), split(rows), ((1,), (1,)))
            for half in range(2):
                got = both[:, half * chunk : (half + 1) * chunk]
                scales[...] = jnp.maximum(scales[...], jnp.abs(got))
                wide[pl.ds(z * 2 + half, modes, stride=layers), :] = got
            return 0

        lax.fori_loop(0, layers // 2, radial, 0)
        devices, slots, height, lanes = sent_ref.shape
        share = modes // devices
        most = scales[...].reshape(devices, share // height, height, lanes)
        exponent = exponent_of(jnp.max(most, axis=1))
        sent_ref[:, slots - 1] = exponent.astype(jnp.int32).astype(jnp.int16)
        factor = CODE_TOP / jnp.exp2(exponent * (1.0 / 256.0))
        scales[pl.ds(0, devices * height), :] = factor.reshape(devices * height, lanes)

        def coding(device, _):
            for mode in range(share):
                factor = scales[pl.ds(device * height + mode % height, 1), :]
                for part in range(layers // height):
                    at = (device * share + mode) * layers + part * height
                    values = wide[pl.ds(pl.multiple_of(at, height), height), :]
                    sent_ref[device, mode * (layers // height) + part] = to_codes(values * factor)
            return 0

        lax.fori_loop(0, devices, coding, 0)


def advect_chunk(arrays, ends, axial_flux, axial_speed, basis, chunk_index, chunk, around, devices, base):
    fraction, normals, planes, flags, courant = arrays
    rows, layers, cells = fraction.shape
    block = BLOCK
    steps = chunk // block
    first = chunk_index * steps
    share = cells // devices

    def here(i):
        return first + i

    def after(i):
        return jnp.minimum((first + i + 1) * block, rows - 1)

    whole = pl.BlockSpec((block, layers, cells), lambda i: (here(i), 0, 0))
    triple = pl.BlockSpec((3, block, layers, cells), lambda i: (0, here(i), 0, 0))
    row = pl.BlockSpec((1, layers, cells), lambda i: (after(i), 0, 0))
    before = max(first * block - 1, 0)
    last_row = pl.BlockSpec((1, layers, cells), lambda i: (before, 0, 0))
    edge = pl.BlockSpec((2, block, cells), lambda i: (0, here(i), 0))
    in_specs = [
        whole,
        triple,
        whole,
        whole,
        triple,
        pl.BlockSpec((3, 1, layers, cells), lambda i: (0, after(i), 0, 0)),
        row,
        row,
        pl.BlockSpec((1, 1, layers, cells), lambda i: (0, after(i), 0, 0)),
        pl.BlockSpec((3, 1, layers, cells), lambda i: (0, before, 0, 0)),
        last_row,
        last_row,
        pl.BlockSpec((1, 1, layers, cells), lambda i: (0, before, 0, 0)),
        pl.BlockSpec(ends.shape, lambda i: (0, 0, 0, 0)),
        edge,
        edge,
        pl.BlockSpec((2, cells, cells), lambda i: (0, 0, 0)),
    ]
    operands = [
        fraction, normals, planes, flags, courant,
        normals, planes, flags, courant,
        normals, planes, flags, courant,
        ends, axial_flux, axial_speed, basis,
    ]
    aliases = {}
    if base is not None:
        in_specs.append(pl.BlockSpec(memory_space=pl.ANY))
        operands.append(base)
        aliases = {len(operands) - 1: 0}
    return pl.pallas_call(
        functools.partial(chunk_kernel, around, chunk_index, rows // chunk),
        grid=(steps,),
        in_specs=in_specs,
        out_specs=[
            whole,
            pl.BlockSpec((devices, 2 * share + 1, layers // 2, chunk), lambda i: (0, 0, 0, 0)),
        ],
        out_shape=[
            jax.ShapeDtypeStruct(fraction.shape, F32),
            jax.ShapeDtypeStruct((devices, 2 * share + 1, layers // 2, chunk), jnp.int16),
        ],
        scratch_shapes=[
            pltpu.VMEM((8, cells // 128, (block + 2) * layers, 128), F32),
            pltpu.VMEM((2, layers, cells), F32),
            pltpu.VMEM((cells // 128, layers * chunk, 128), F32),
            pltpu.VMEM((cells * layers, chunk), F32),
            pltpu.VMEM((cells, chunk), F32),
        ],
        input_output_aliases=aliases,
        compiler_params=pltpu.CompilerParams(vmem_limit_bytes=60 * 2**20),
        cost_estimate=pl.CostEstimate(
            flops=40000 * chunk * layers * cells, bytes_accessed=30 * chunk * layers * cells, transcendentals=0
        ),
        name="advect_chunk",
    )(*operands)


@functools.lru_cache(None)
def folded_tables(total):
    quarter = total // 4
    place = np.arange(quarter) + 0.5

    def halves(x):
        high = x.astype(jnp.bfloat16)
        return np.stack([high, (x - high.astype(np.float64)).astype(jnp.bfloat16)])

    tables, rates, weights = [], [], []
    for waves, wave in (
        (2 * np.arange(quarter), np.cos),
        (2 * np.arange(quarter) + 2, np.sin),
        (2 * np.arange(quarter) + 1, np.cos),
        (2 * np.arange(quarter) + 1, np.sin),
    ):
        doubled = waves[:, None] * (2 * np.arange(quarter) + 1)[None, :] % (2 * total)
        tables.append(wave(np.pi * doubled / total))
        rates.append(2.0 - 2.0 * np.cos(2.0 * np.pi * waves / total))
        weights.append(np.where((waves == 0) | (waves == total // 2), 1.0, 2.0) / total)
    tables = np.stack(tables)
    back = np.stack([halves(t) for t in tables])
    forth = np.stack([halves(t.T) for t in tables])
    return forth, back, np.stack(rates)[:, None].astype(np.float32), np.stack(weights)[:, None].astype(np.float32)


def decoded(values):
    return values.astype(jnp.int32).astype(F32)


def scale_of(codes):
    return jnp.exp2(decoded(codes) * (1.0 / 256.0)) * (1.0 / CODE_TOP)


def solve_kernel(around, along, chunks, start, *refs):
    got = refs[:chunks]
    extra = refs[chunks : 2 * chunks]
    mix, unmix, forth_ref, back_ref, rates, weights, shifts = refs[2 * chunks : 2 * chunks + 7]
    sent, high, low, result, scale, exponents, forth, back, arrived = refs[2 * chunks + 7 :]
    copies = [
        pltpu.make_async_copy(forth_ref, forth, arrived.at[0]),
        pltpu.make_async_copy(back_ref, back, arrived.at[1]),
    ]

    @pl.when(pl.program_id(0) == 0)
    def _():
        for copy in copies:
            copy.start()

    devices, count, height, lanes = got[0].shape
    count, layers = count // 2, 2 * height
    share = (sent.shape[1] - 1) // (2 * chunks)
    together = chunks * share // height
    pairs = around // 4
    step = pl.program_id(0)
    first = start + step * count
    for chunk in range(chunks):
        scale[chunk] = scale_of(extra[chunk][:, 0])
    def spots():
        for pair in range(pairs):
            for chunk in range(chunks):
                mirror = chunks - 1 - chunk
                at = pl.ds((pair * chunks + chunk) * lanes, lanes)
                yield at, (
                    (pair, chunk),
                    (pair + 2 * pairs, chunk),
                    (2 * pairs - 1 - pair, mirror),
                    (4 * pairs - 1 - pair, mirror),
                )

    def fold(index, _):
        mode, axial = index // along, index % along
        rows = pl.ds(pl.multiple_of(index * layers, layers), layers)
        row = pl.ds(lax.rem(first + mode, height), 1)
        for at, places in spots():
            u0, u1, r0, r1 = [
                jnp.concatenate(
                    [
                        decoded(got[chunk][azim * along + axial, 2 * mode + part])
                        * scale[chunk, azim * along + axial, row, :]
                        for part in range(2)
                    ]
                )
                for azim, chunk in places
            ]
            e0, o0, e1, o1 = u0 + u1, u0 - u1, r0 + r1, r0 - r1
            for k, folded in enumerate((e0 + e1, e0 - e1, o0 - o1, o0 + o1)):
                high[k, rows, at], low[k, rows, at] = split(folded)
        return 0

    lax.fori_loop(0, count * along, fold, 0)

    @pl.when(pl.program_id(0) == 0)
    def _():
        for copy in copies:
            copy.wait()

    deep = mix.shape[1]
    parts = [pl.ds(at, deep) for at in range(0, high.shape[1], deep)]

    def waves(k, _):
        for at in parts:
            high[k, at], low[k, at] = split(
                dot3((mix[0], mix[1]), (high[k, at], low[k, at]))
            )
        spectrum = dot3((high[k], low[k]), (forth[k, 0], forth[k, 1]))
        high[k], low[k] = split(spectrum * weights[k] / (rates[k] + shifts[...]))
        high[k], low[k] = split(dot3((high[k], low[k]), (back[k, 0], back[k, 1])))
        for at in parts:
            result[k, at] = dot3((unmix[0], unmix[1]), (high[k, at], low[k, at]))
        return 0

    lax.fori_loop(0, 4, waves, 0)

    apart = count // together

    def unfold(index, _):
        mode, axial = index // along, index % along
        for at, places in spots():
            found = []
            for part in range(together):
                row = ((mode + part * apart) * along + axial) * layers
                rows = pl.ds(pl.multiple_of(row, layers), layers)
                ec, es, oc, os = [result[k, rows, at] for k in range(4)]
                e0, e1, o0, o1 = ec + es, ec - es, oc + os, os - oc
                found.append((e0 + o0, e0 - o0, e1 + o1, e1 - o1))
            for (azim, chunk), values in zip(places, zip(*found)):
                device = azim * along + axial
                most = functools.reduce(jnp.maximum, [jnp.abs(x) for x in values])
                exponent = exponent_of(jnp.max(most, axis=0, keepdims=True))
                exponents[device, pl.ds(chunk * apart + mode, 1), :] = exponent
                factor = CODE_TOP / jnp.exp2(exponent * (1.0 / 256.0))
                for part, value in enumerate(values):
                    slot = 2 * (chunk * share + mode + part * apart)
                    for half in range(2):
                        piece = value[half * height : (half + 1) * height]
                        sent[device, slot + half] = to_codes(piece * factor)
        return 0

    lax.fori_loop(0, apart * along, unfold, 0)

    @pl.when(step == pl.num_programs(0) - 1)
    def _():
        sent[:, 2 * chunks * share] = exponents[...].astype(jnp.int32).astype(jnp.int16)


def solve_group(got, mix, unmix, tables, shifts, start, share, around, along):
    chunks = len(got)
    devices, slots, height, lanes = got[0].shape
    modes, layers = (slots - 1) // 2, 2 * height
    count = share
    steps = share // count
    block = start // count
    rows = count * along * layers
    forth, back, rates, weights = tables
    width = forth.shape[-1]

    def fixed(array):
        return pl.BlockSpec(array.shape, lambda i: (0,) * array.ndim, pipeline_mode=pl.Buffered(1))

    return pl.pallas_call(
        functools.partial(solve_kernel, around, along, chunks, start),
        grid=(steps,),
        in_specs=[
            pl.BlockSpec((devices, 2 * count, height, lanes), lambda i: (0, block + i, 0, 0))
        ]
        * chunks
        + [pl.BlockSpec((devices, 1, height, lanes), lambda i: (0, 2 * modes, 0, 0))] * chunks
        + [fixed(mix), fixed(unmix)]
        + [pl.BlockSpec(memory_space=pl.ANY)] * 2
        + [fixed(rates), fixed(weights)]
        + [pl.BlockSpec((rows, 1), lambda i: (block + i, 0))],
        out_specs=pl.BlockSpec(
            (devices, 2 * chunks * share + 1, height, lanes), lambda i: (0, 0, 0, 0)
        ),
        out_shape=jax.ShapeDtypeStruct((devices, 2 * chunks * share + 1, height, lanes), jnp.int16),
        scratch_shapes=[
            pltpu.VMEM((4, rows, width), BF16),
            pltpu.VMEM((4, rows, width), BF16),
            pltpu.VMEM((4, rows, width), F32),
            pltpu.VMEM((chunks, devices, height, lanes), F32),
            pltpu.VMEM((devices, height, lanes), F32),
            pltpu.VMEM(forth.shape, BF16),
            pltpu.VMEM(back.shape, BF16),
            pltpu.SemaphoreType.DMA((2,)),
        ],
        compiler_params=pltpu.CompilerParams(vmem_limit_bytes=60 * 2**20),
        cost_estimate=pl.CostEstimate(
            flops=60 * rows * width * width * steps, bytes_accessed=20 * 2**20, transcendentals=0
        ),
        name="solve_group",
    )(*got, *got, mix, unmix, forth, back, rates, weights, shifts)


def pressure_kernel(around, groups, chunks, *refs):
    got = refs[:groups]
    extra = refs[groups : 2 * groups]
    basis = refs[2 * groups]
    base = refs[2 * groups + 1 : -6]
    out, flat, wide, scale, high, low = refs[-6:]
    devices, _, height, lanes = got[0].shape
    layers = 2 * height
    lane_tiles = out.shape[2] // 128
    chunk = pl.program_id(0)
    backwards = lax.rem(lax.axis_index("azim"), around // 2) >= around // 4
    i = lax.broadcasted_iota(jnp.int32, (lanes, lanes), 0)
    j = lax.broadcasted_iota(jnp.int32, (lanes, lanes), 1)
    turned_place = jnp.where(backwards, lanes - 1, 0) + jnp.where(backwards, -1, 1) * i
    turn = jnp.where(j == turned_place, 1.0, 0.0).astype(BF16)
    spans, filled = [], 0
    for group in range(groups):
        share = got[group].shape[1] // 2
        apart = height // chunks
        spans.append((filled, devices * share))
        scale[group] = scale_of(extra[group][:, 0])

        def unpack(device, _, group=group, share=share, filled=filled):
            for mode in range(share):
                factor = scale[group, device, pl.ds(chunk * apart + mode % apart, 1), :]
                for part in range(2):
                    at = (filled + device * share + mode) * layers + part * height
                    flat[pl.ds(pl.multiple_of(at, height), height), :] = (
                        decoded(got[group][device, 2 * mode + part]) * factor
                    )
            return 0

        lax.fori_loop(0, devices, unpack, 0)
        filled += devices * share

    together = high.shape[0] // lanes

    def radial(batch, _):
        for part in range(together):
            for offset, height in spans:
                z = batch * together + part
                values = split(flat[pl.ds(offset * layers + z, height, stride=layers), :])
                at = pl.ds(offset, height)
                for target, value in zip((high, low), values):
                    target[part * lanes : (part + 1) * lanes, at] = dot(
                        turn, value, ((1,), (1,))
                    ).astype(BF16)
        if filled > 128:
            total = dot3((high[...], low[...]), (basis[0], basis[1]))
        else:
            lower = jnp.concatenate([high[...], low[...], high[...]], axis=1)
            total = dot(lower, jnp.concatenate([basis[0], basis[0], basis[1]]), ((1,), (0,)))
        for part in range(together):
            for tile in range(lane_tiles):
                wide[tile, pl.ds(batch * together + part, lanes, stride=layers), :] = total[
                    part * lanes : (part + 1) * lanes, tile * 128 : (tile + 1) * 128
                ]
        return 0

    lax.fori_loop(0, layers // together, radial, 0)
    for tile in range(lane_tiles):
        at = slice(tile * 128, (tile + 1) * 128)
        result = wide[tile].reshape(lanes, layers, 128)
        out[:, :, at] = result + base[0][:, :, at] if base else result


def pressure_of(got, basis, around, chunks, base=None):
    groups = len(got)
    devices, _, height, lanes = got[0].shape
    layers = 2 * height
    shares = [(x.shape[1] - 1) // (2 * chunks) for x in got]
    inner, cells = basis.shape[1:]
    whole = pl.BlockSpec((lanes, layers, cells), lambda i: (i, 0, 0))
    return pl.pallas_call(
        functools.partial(pressure_kernel, around, groups, chunks),
        grid=(chunks,),
        in_specs=[pl.BlockSpec((devices, 2 * share, height, lanes), lambda i: (0, i, 0, 0)) for share in shares]
        + [
            pl.BlockSpec((devices, 1, height, lanes), lambda i, share=share: (0, 2 * chunks * share, 0, 0))
            for share in shares
        ]
        + [pl.BlockSpec(basis.shape, lambda i: (0, 0, 0), pipeline_mode=pl.Buffered(1))]
        + ([] if base is None else [whole]),
        out_specs=whole,
        out_shape=jax.ShapeDtypeStruct((lanes * chunks, layers, cells), F32),
        scratch_shapes=[
            pltpu.VMEM((inner * layers, lanes), F32),
            pltpu.VMEM((cells // 128, lanes * layers, 128), F32),
            pltpu.VMEM((groups, devices, height, lanes), F32),
            pltpu.VMEM((4 * lanes, inner), BF16),
            pltpu.VMEM((4 * lanes, inner), BF16),
        ],
        compiler_params=pltpu.CompilerParams(vmem_limit_bytes=60 * 2**20),
        cost_estimate=pl.CostEstimate(
            flops=20 * lanes * chunks * layers * cells * inner,
            bytes_accessed=20 * 2**20,
            transcendentals=0,
        ),
        name="pressure_of",
    )(*got, *got, basis, *([] if base is None else [base]))


def halves(values):
    high = lax.reduce_precision(values, 8, 7)
    return jnp.stack([high.astype(BF16), (values - high).astype(BF16)])


def exchanged(sent):
    return lax.all_to_all(sent, ("azim", "axial"), split_axis=0, concat_axis=0, tiled=True)


def following_kernel(values_ref, earlier_ref, out_ref):
    del values_ref, earlier_ref, out_ref


def following(values, earlier):
    anywhere = pl.BlockSpec(memory_space=pl.ANY)
    return pl.pallas_call(
        following_kernel,
        in_specs=[anywhere, anywhere],
        out_specs=anywhere,
        out_shape=jax.ShapeDtypeStruct(values.shape, values.dtype),
        input_output_aliases={0: 0},
        name="following",
    )(values, earlier)


def overlapped(
    fraction,
    normals,
    planes,
    cell_flags,
    courant,
    radial_basis,
    axial_basis,
    radial_rates,
    axial_rates,
):
    rows, layers, cells = fraction.shape
    around, along = lax.axis_size("azim"), lax.axis_size("axial")
    devices = around * along
    modes = cells // devices
    chunks = rows // CHUNK
    axial_flux, axial_speed, ends = halos(normals, planes, cell_flags, courant)
    forward_basis = halves(radial_basis.T)
    arrays = (fraction, normals, planes, cell_flags, courant)
    updated, got = None, []
    for chunk in range(chunks):
        updated, sent = advect_chunk(
            arrays, ends, axial_flux, axial_speed, forward_basis, chunk, CHUNK, around, devices, updated
        )
        got.append(exchanged(following(sent, got[-1]) if got else sent))
    count = jnp.eye(4, dtype=F32)
    mix, unmix = halves(jnp.kron(count, axial_basis.T)), halves(jnp.kron(count, axial_basis))
    first = (lax.axis_index("azim") * along + lax.axis_index("axial")) * modes
    shifts = lax.dynamic_slice_in_dim(radial_rates, first, modes)[:, None] + axial_rates[None, :]
    shifts = shifts.reshape(modes * along * layers, 1)
    tables = [jnp.asarray(x) for x in folded_tables(rows * around)]
    returned, bases = [], []
    for start, share in SOLVED:
        sent = solve_group(got, mix, unmix, tables, shifts, start, share, around, along)
        returned.append(exchanged(sent))
        rows_of = radial_basis.T.reshape(devices, modes, cells)[:, start : start + share]
        bases.append(rows_of.reshape(devices * share, cells))
    pressure = pressure_of(returned[:-1], halves(jnp.concatenate(bases[:-1])), around, chunks)
    pressure = pressure_of(returned[-1:], halves(bases[-1]), around, chunks, pressure)
    return (updated, pressure)


def fits(fraction):
    rows, layers, cells = fraction.shape
    around, along = lax.axis_size("azim"), lax.axis_size("axial")
    modes = cells // (around * along)
    chunks = rows // CHUNK
    return (
        rows % CHUNK == 0
        and layers == 16
        and modes == 16
        and modes // 2 * chunks == layers
        and cells % 128 == 0
        and around % 4 == 0
        and along > 2
    )


def local(*arguments):
    return overlapped(*arguments) if fits(arguments[0]) else stepwise(*arguments)


def solution(mesh):
    placed = (
        P("azim", "axial", None),
        P(None, "azim", "axial", None),
        P("azim", "axial", None),
        P("azim", "axial", None),
        P(None, "azim", "axial", None),
        P(),
        P(),
        P(),
        P(),
    )
    return jax.shard_map(
        local,
        mesh=mesh,
        in_specs=placed,
        out_specs=(P("azim", "axial", None), P("azim", "axial", None)),
        check_vma=False,
    )
```

```python
import functools

import jax
import jax.numpy as jnp
import numpy as np
from jax import lax
from jax.experimental import pallas as pl
from jax.experimental.pallas import tpu as pltpu
from jax.sharding import PartitionSpec as P

HIGH = lax.Precision.HIGH
BUOYANCY = 0.5
CODE_TOP = 32700.0


def shifted_in(edge, axis, towards_lower):
    count = lax.axis_size(axis)
    if towards_lower:
        pairs = [((i + 1) % count, i) for i in range(count)]
    else:
        pairs = [(i, (i + 1) % count) for i in range(count)]
    return lax.ppermute(edge, axis, pairs)


def cell_parts(n0, n1, n2, code):
    m0, m1, m2 = jnp.abs(n0), jnp.abs(n1), jnp.abs(n2)
    return (n0, n1, n2, code, 1.0 / (6.0 * m0 * m1 * m2))


def cube(height):
    held = jnp.maximum(height, 0.0)
    return held * held * held


def face_flux(direction, lower, upper, speed, lower_weight=None, upper_weight=None):
    forward = speed > 0.0
    signed = jnp.where(forward, lower[direction], -upper[direction])
    first, second = [d for d in range(3) if d != direction]
    along = jnp.abs(signed)
    side_a = jnp.abs(jnp.where(forward, lower[first], upper[first]))
    side_b = jnp.abs(jnp.where(forward, lower[second], upper[second]))
    code = jnp.where(forward, lower[3], upper[3])
    inverse = jnp.where(forward, lower[4], upper[4])
    width = jnp.abs(speed)
    near = code - along * jnp.where(signed < 0.0, 0.0, 1.0 - width)
    far = near - along * width
    sides = side_a + side_b
    total = (cube(near) - cube(near - side_a)) - (cube(near - side_b) - cube(near - sides))
    total = total - ((cube(far) - cube(far - side_a)) - (cube(far - side_b) - cube(far - sides)))
    volume = jnp.where(code > 3.0, width, jnp.where(code < -0.5, 0.0, total * inverse))
    if lower_weight is not None:
        volume = volume * jnp.where(forward, lower_weight, upper_weight)
    return jnp.where(forward, volume, jnp.where(speed < 0.0, -volume, 0.0))


def advect_kernel(
    fraction_ref,
    normals_ref,
    planes_ref,
    flags_ref,
    courant_ref,
    next_ref,
    high_ref,
    low_azim_ref,
    low_axial_ref,
    updated_ref,
    source_ref,
    kept,
):
    rows, layers, cells = fraction_ref.shape
    f32 = jnp.float32

    @pl.when(pl.program_id(0) == 0)
    def _():
        kept[...] = low_azim_ref[...]

    index = lax.broadcasted_iota(jnp.int32, (1, cells), 1)
    place = index.astype(f32)
    radius = 1.0 + (place + 0.5) / cells
    next_radius = 1.0 + (place + 1.5) / cells
    face_radius = 1.0 + (place + 1.0) / cells
    inverse_radius = 1.0 / radius
    inner = lax.broadcasted_iota(jnp.int32, (layers, cells), 1) < cells - 1
    layer = lax.broadcasted_iota(jnp.int32, (layers, cells), 0)
    last_layer = layer == layers - 1
    first_layer = layer == 0

    def row_parts(row):
        flags = flags_ref[row]
        code = jnp.where(
            flags == 2, planes_ref[row].astype(f32), jnp.where(flags == 1, 4.0, -1.0)
        )
        return cell_parts(
            normals_ref[0, row].astype(f32),
            normals_ref[1, row].astype(f32),
            normals_ref[2, row].astype(f32),
            code,
        )

    def one_row(row, upper, upper_speed):
        own = row_parts(row)
        moved = [courant_ref[d, row].astype(f32) for d in range(3)]
        speed = 0.5 * (moved[0] + upper_speed)
        flux = face_flux(0, own, upper, speed)
        gained = flux - kept[0]
        divergence = speed - kept[1]
        kept[0] = flux
        kept[1] = speed
        beyond = cell_parts(*[high_ref[k, row] for k in range(4)])
        above = [
            jnp.where(last_layer, high, pltpu.roll(field, layers - 1, 0))
            for field, high in zip(own, beyond)
        ]
        speed = 0.5 * (
            moved[1]
            + jnp.where(last_layer, high_ref[4, row], pltpu.roll(moved[1], layers - 1, 0))
        )
        flux = face_flux(1, own, above, speed)
        gained = gained + (
            flux - jnp.where(first_layer, low_axial_ref[0, row], pltpu.roll(flux, 1, 0))
        )
        divergence = divergence + (
            speed - jnp.where(first_layer, low_axial_ref[1, row], pltpu.roll(speed, 1, 0))
        )
        outer = [pltpu.roll(field, cells - 1, 1) for field in own]
        speed = 0.5 * (moved[2] + pltpu.roll(moved[2], cells - 1, 1))
        speed = jnp.where(inner, speed, 0.0)
        flux = face_flux(2, own, outer, speed, radius, next_radius)
        gained = gained + (flux - pltpu.roll(flux, 1, 1)) * inverse_radius
        carried = face_radius * speed
        divergence = divergence + (carried - pltpu.roll(carried, 1, 1)) * inverse_radius
        updated = fraction_ref[row] - gained
        updated_ref[row] = updated
        source_ref[row] = divergence + BUOYANCY * updated

    def step(row, _):
        one_row(row, row_parts(row + 1), courant_ref[0, row + 1].astype(f32))
        return 0

    lax.fori_loop(0, rows - 1, step, 0)
    one_row(
        rows - 1,
        cell_parts(*[next_ref[k, 0].astype(f32) for k in range(4)]),
        next_ref[4, 0].astype(f32),
    )


def plane_codes(planes, flags):
    return jnp.where(
        flags == 2, planes.astype(jnp.float32), jnp.where(flags == 1, 4.0, -1.0)
    ).astype(jnp.bfloat16)


def packed_edge(normals, planes, flags, courant, direction, pick):
    parts = [pick(normals[d]) for d in range(3)]
    parts.append(plane_codes(pick(planes), pick(flags)))
    parts.append(pick(courant[direction]))
    return jnp.stack(parts)


def low_face(direction, lower, upper):
    lower, upper = lower.astype(jnp.float32), upper.astype(jnp.float32)
    speed = 0.5 * (lower[4] + upper[4])
    flux = face_flux(direction, cell_parts(*lower[:4]), cell_parts(*upper[:4]), speed)
    return jnp.stack([flux, speed])


def advect(fraction, normals, planes, flags, courant):
    rows, layers, cells = fraction.shape
    block = 16 if rows % 16 == 0 else 1
    blocks = rows // block
    fields = (normals, planes, flags, courant)
    top_row = packed_edge(*fields, 0, lambda x: x[rows - 1])
    bottom_row = packed_edge(*fields, 0, lambda x: x[0])
    top_layer = packed_edge(*fields, 1, lambda x: x[:, layers - 1])
    bottom_layer = packed_edge(*fields, 1, lambda x: x[:, 0])
    high_row = shifted_in(bottom_row, "azim", True)
    low_row = shifted_in(top_row, "azim", False)
    high_layer = shifted_in(bottom_layer, "axial", True)
    low_layer = shifted_in(top_layer, "axial", False)
    low_azim = low_face(0, low_row, bottom_row)
    low_axial = low_face(1, low_layer, bottom_layer)[:, :, None]
    high_axial = high_layer.astype(jnp.float32)[:, :, None]
    inside = packed_edge(*fields, 0, lambda x: x[block::block])
    following = jnp.concatenate([inside, high_row[:, None]], axis=1)
    whole = pl.BlockSpec((block, layers, cells), lambda i: (i, 0, 0))
    triple = pl.BlockSpec((3, block, layers, cells), lambda i: (0, i, 0, 0))
    return pl.pallas_call(
        advect_kernel,
        grid=(blocks,),
        in_specs=[
            whole,
            triple,
            whole,
            whole,
            triple,
            pl.BlockSpec((5, 1, layers, cells), lambda i: (0, i, 0, 0)),
            pl.BlockSpec((5, block, 1, cells), lambda i: (0, i, 0, 0)),
            pl.BlockSpec((2, layers, cells), lambda i: (0, 0, 0)),
            pl.BlockSpec((2, block, 1, cells), lambda i: (0, i, 0, 0)),
        ],
        out_specs=[whole, whole],
        out_shape=[jax.ShapeDtypeStruct(fraction.shape, jnp.float32)] * 2,
        scratch_shapes=[pltpu.VMEM((2, layers, cells), jnp.float32)],
        compiler_params=pltpu.CompilerParams(vmem_limit_bytes=40 * 2**20),
    )(
        fraction,
        normals,
        planes,
        flags,
        courant,
        following,
        high_axial,
        low_azim,
        low_axial,
    )


def coded(values):
    most = jnp.max(jnp.abs(values), axis=-1)
    exponent = jnp.clip(jnp.ceil(jnp.log2(most) * 256.0) + 1.0, -30000.0, 30000.0)
    scale = CODE_TOP * jnp.exp2(exponent * (-1.0 / 256.0))
    codes = jnp.round(values * scale[..., None])
    return jnp.clip(codes, -32767.0, 32767.0).astype(jnp.int16), exponent.astype(jnp.int16)


def exchange(values):
    modes, cells = values.shape[1], values.shape[3]
    codes, exponent = coded(values)
    extra = jnp.pad(exponent.transpose(0, 2, 1), ((0, 0), (0, 0), (0, cells - modes)))
    sent = jnp.concatenate([codes, extra[:, None]], axis=1)
    got = lax.all_to_all(sent, ("azim", "axial"), split_axis=0, concat_axis=0, tiled=True)
    exponent = got[:, modes, :, :modes].transpose(0, 2, 1).astype(jnp.float32)
    scale = jnp.exp2(exponent * (1.0 / 256.0)) * (1.0 / CODE_TOP)
    return got[:, :modes].astype(jnp.float32) * scale[..., None]


@functools.lru_cache(None)
def azimuth_tables(total):
    half, quarter = total // 2, total // 4
    place = np.arange(half)

    def table(cosines, sines):
        waves = np.concatenate([cosines, sines])
        angles = 2.0 * np.pi / total * (waves[:, None] * place[None, :] % total)
        rows = np.concatenate(
            [np.cos(angles[: len(cosines)]), np.sin(angles[len(cosines) :])]
        ).astype(np.float32)
        rates = (2.0 - 2.0 * np.cos(2.0 * np.pi * waves / total)).astype(np.float32)
        ends = (waves == 0) | (waves == half)
        return rows, rates, (np.where(ends, 1.0, 2.0) / total).astype(np.float32)

    even = 2 * np.arange(quarter + 1)
    odd = 2 * np.arange(quarter) + 1
    return table(even, even[1:-1]), table(odd, odd)


def stepwise(
    fraction,
    normals,
    planes,
    cell_flags,
    courant,
    radial_basis,
    axial_basis,
    radial_rates,
    axial_rates,
):
    rows, layers, cells = fraction.shape
    around, along = lax.axis_size("azim"), lax.axis_size("axial")
    devices = around * along
    modes = cells // devices
    total = rows * around
    half = total // 2
    updated, source = advect(fraction, normals, planes, cell_flags, courant)
    radial_modes = jnp.einsum("azr,rj->jza", source, radial_basis, precision=HIGH)
    got = exchange(radial_modes.reshape(devices, modes, layers, rows))
    got = got.reshape(around, along, modes, layers, rows).transpose(2, 1, 3, 0, 4)
    got = got.reshape(modes, along * layers, total)
    both = jnp.einsum("jza,zn->jna", got, axial_basis, precision=HIGH)
    first = (lax.axis_index("azim") * along + lax.axis_index("axial")) * modes
    shifts = lax.dynamic_slice_in_dim(radial_rates, first, modes)[:, None] + axial_rates[None, :]
    low, high = both[..., :half], both[..., half:]
    solved = []
    for folded, (table, rates, weight) in zip((low + high, low - high), azimuth_tables(total)):
        coefficients = jnp.einsum("jna,ka->jnk", folded, table, precision=HIGH)
        scaled = coefficients / (rates + shifts[..., None]) * weight
        solved.append(jnp.einsum("jnk,ka->jna", scaled, table, precision=HIGH))
    physical = jnp.concatenate([solved[0] + solved[1], solved[0] - solved[1]], axis=-1)
    physical = jnp.einsum("jna,zn->jza", physical, axial_basis, precision=HIGH)
    physical = physical.reshape(modes, along, layers, around, rows).transpose(3, 1, 0, 2, 4)
    returned = exchange(physical.reshape(devices, modes, layers, rows))
    returned = returned.reshape(cells, layers, rows)
    pressure = jnp.einsum("jza,rj->azr", returned, radial_basis, precision=HIGH)
    return (updated, pressure)


CHUNK = 128
BLOCK = 16
SOLVED = ((0, 4), (8, 8), (4, 4))
FLUX_SCALE = 32767.0 / 0.3
F32 = jnp.float32
BF16 = jnp.bfloat16


def split(values):
    high = values.astype(BF16)
    return high, (values - high.astype(F32)).astype(BF16)


def dot(a, b, contract):
    return lax.dot_general(a, b, (contract, ((), ())), preferred_element_type=F32)


def dot3(a, b, contract=((1,), (0,))):
    return dot(a[0], b[0], contract) + (dot(a[0], b[1], contract) + dot(a[1], b[0], contract))


def slab_flux(normal, side_a, side_b, plane, inverse, speed):
    along = jnp.abs(normal)
    reach = normal * speed
    slab = jnp.abs(reach)
    near = plane - jnp.where(reach > 0.0, along - slab, 0.0)
    other = (slab + (side_a + side_b)) - near
    folded = near > other
    held = jnp.maximum(jnp.minimum(near, other), 0.0)
    low, high = jnp.minimum(side_a, side_b), jnp.maximum(side_a, side_b)
    by_low = jnp.maximum(held - low, 0.0)
    by_slab = jnp.maximum(held - slab, 0.0)
    last = jnp.maximum(held - (low + slab), 0.0) - jnp.maximum(held - high, 0.0)
    total = held * held * held - by_slab * by_slab * by_slab
    total = total - (by_low * by_low * by_low - last * last * last)
    flux = total * inverse
    return jnp.where(folded, speed - flux, flux)


def upwind_flux(direction, lower, upper, speed, lower_weight=None, upper_weight=None):
    forward = speed > 0.0
    first, second = [d for d in range(3) if d != direction]
    normal = jnp.where(forward, lower[direction], upper[direction])
    side_a = jnp.abs(jnp.where(forward, lower[first], upper[first]))
    side_b = jnp.abs(jnp.where(forward, lower[second], upper[second]))
    plane = jnp.where(forward, lower[3], upper[3])
    inverse = jnp.where(forward, lower[4], upper[5])
    flux = slab_flux(normal, side_a, side_b, plane, inverse, speed)
    if lower_weight is not None:
        flux = flux * jnp.where(forward, lower_weight, upper_weight)
    return flux


def inverse_of(n0, n1, n2):
    return 1.0 / (6.0 * jnp.abs(n0 * n1 * n2))


def plane_value(planes, flags):
    return jnp.where(flags == 2, planes.astype(F32), jnp.where(flags == 1, 4.0, -4.0))


def halo_kernel(
    courant_ref,
    normals_ref,
    planes_ref,
    flags_ref,
    first_normals_ref,
    first_planes_ref,
    first_flags_ref,
    first_courant_ref,
    last_normals_ref,
    last_planes_ref,
    last_flags_ref,
    last_courant_ref,
    flux_ref,
    speed_ref,
    ends_ref,
    work,
    edge,
    edge_in,
    fields,
    code,
    code_in,
    packs,
    packs_in,
    row_send,
    row_recv,
    edge_send,
    edge_recv,
    code_send,
    code_recv,
):
    step = pl.program_id(0)
    half = pl.num_programs(0) // 2
    span, layers, cells = planes_ref.shape
    groups, group = code.shape[1:3]
    per_group = group // span
    tiles = cells // 128
    neighbours = []
    for axis in ("azim", "axial"):
        count, me = lax.axis_size(axis), lax.axis_index(axis)
        neighbours.append(
            ({axis: lax.rem(me + count - 1, count)}, {axis: lax.rem(me + 1, count)})
        )

    def remote(source, target, send, recv, device):
        return pltpu.make_async_remote_copy(
            src_ref=source,
            dst_ref=target,
            send_sem=send,
            recv_sem=recv,
            device_id=device,
            device_id_type=pl.DeviceIdType.MESH,
        )

    row_copies = [
        remote(packs.at[s], packs_in.at[1 - s], row_send.at[s], row_recv.at[1 - s], neighbours[0][s])
        for s in range(2)
    ]
    def edge_copy(s, g):
        return remote(
            edge.at[s, g],
            edge_in.at[1 - s, g],
            edge_send.at[s, g],
            edge_recv.at[1 - s, g],
            neighbours[1][s],
        )

    def code_copy(s, g):
        return remote(
            code.at[s, g],
            code_in.at[1 - s, g],
            code_send.at[s, g],
            code_recv.at[1 - s, g],
            neighbours[1][s],
        )

    @pl.when(step == 0)
    def _():
        barrier = pltpu.get_barrier_semaphore()
        for pair in neighbours:
            for device in pair:
                pl.semaphore_signal(
                    barrier, inc=1, device_id=device, device_id_type=pl.DeviceIdType.MESH
                )
        pl.semaphore_wait(barrier, 4)
        for s, (normals, planes, flags, courant) in enumerate(
            (
                (first_normals_ref, first_planes_ref, first_flags_ref, first_courant_ref),
                (last_normals_ref, last_planes_ref, last_flags_ref, last_courant_ref),
            )
        ):
            for k in range(3):
                packs[s, k] = normals[k, 0]
            packs[s, 3] = plane_value(planes[0], flags[0]).astype(BF16)
            packs[s, 4] = courant[0, 0]
        for copy in row_copies:
            copy.start()

    def layer_rows(tile, layer):
        return work[tile, pl.ds(layer, span, stride=layers), :]

    @pl.when(step < half)
    def _():
        place = step // per_group
        at = pl.ds(pl.multiple_of(lax.rem(step, per_group) * span, span), span)
        for tile in range(tiles):
            lanes = pl.ds(tile * 128, 128)
            work[tile] = courant_ref[0, :, :, lanes].astype(F32).reshape(span * layers, 128)
            for s, layer in ((0, 0), (1, layers - 1)):
                edge[s, place, at, lanes] = layer_rows(tile, layer).astype(BF16)

    for g in range(groups):

        @pl.when(step == (g + 1) * per_group - 1)
        def _(g=g):
            for s in range(2):
                edge_copy(s, g).start()

    @pl.when(step >= half)
    def _():
        at = pl.ds(pl.multiple_of((step - half) * span, span), span)
        for k in range(4):
            for tile in range(tiles):
                lanes = pl.ds(tile * 128, 128)
                if k < 3:
                    field = normals_ref[k, :, :, lanes].astype(F32)
                else:
                    field = plane_value(planes_ref[:, :, lanes], flags_ref[:, :, lanes])
                work[tile] = field.reshape(span * layers, 128)
                for s, layer in ((0, 0), (1, layers - 1)):
                    fields[s, k, at, lanes] = layer_rows(tile, layer)

    for g in range(groups):

        @pl.when(step == half + (g + 1) * per_group - 1)
        def _(g=g):
            for s in range(2):
                edge_copy(s, g).wait()
            for s in range(2):

                def donate(piece, _, s=s):
                    inside = pl.ds(pl.multiple_of(piece * 16, 16), 16)
                    at = pl.ds(pl.multiple_of(g * group + piece * 16, 16), 16)
                    normals = [fields[s, k, at, :] for k in range(3)]
                    own, beyond = edge[s, g, inside, :], edge_in[s, g, inside, :]
                    speed = 0.5 * (own.astype(F32) + beyond.astype(F32))
                    inverse = inverse_of(*normals)
                    flux = slab_flux(
                        normals[1],
                        jnp.abs(normals[0]),
                        jnp.abs(normals[2]),
                        fields[s, 3, at, :],
                        inverse if s == 1 else -inverse,
                        speed,
                    )
                    flux = jnp.where(speed > 0.0 if s == 1 else speed < 0.0, flux, 0.0)
                    flux_ref[s, at, :] = flux
                    speed_ref[s, at, :] = speed
                    code[s, g, inside, :] = to_codes(flux * FLUX_SCALE)
                    return 0

                lax.fori_loop(0, group // 16, donate, 0)
                code_copy(s, g).start()

    @pl.when(step == 2 * half - 1)
    def _():
        for copy in row_copies:
            copy.wait()
        ends_ref[...] = packs_in[...]
        for g in range(groups):
            for s in range(2):
                code_copy(s, g).wait()
            for s in range(2):
                at = pl.ds(g * group, group)
                received = code_in[s, g].astype(jnp.int32).astype(F32)
                flux_ref[s, at, :] += received * (1.0 / FLUX_SCALE)


def halos(normals, planes, flags, courant):
    rows, layers, cells = planes.shape
    span, groups = 32, 4
    half = rows // span

    def later(i):
        return jnp.maximum(i - half, 0)

    whole = pl.BlockSpec((span, layers, cells), lambda i: (later(i), 0, 0))
    in_specs = [
        pl.BlockSpec((1, span, layers, cells), lambda i: (1, jnp.minimum(i, half - 1), 0, 0)),
        pl.BlockSpec((3, span, layers, cells), lambda i: (0, later(i), 0, 0)),
        whole,
        whole,
    ]
    for row in (0, rows - 1):
        one = pl.BlockSpec((1, layers, cells), lambda i, row=row: (row, 0, 0))
        in_specs += [
            pl.BlockSpec((3, 1, layers, cells), lambda i, row=row: (0, row, 0, 0)),
            one,
            one,
            pl.BlockSpec((1, 1, layers, cells), lambda i, row=row: (0, row, 0, 0)),
        ]
    pair = pl.BlockSpec((2, rows, cells), lambda i: (0, 0, 0))
    ends = (2, 5, layers, cells)
    split_shape = (2, groups, rows // groups, cells)
    dma = pltpu.SemaphoreType.DMA
    return pl.pallas_call(
        halo_kernel,
        grid=(2 * half,),
        in_specs=in_specs,
        out_specs=[pair, pair, pl.BlockSpec(ends, lambda i: (0, 0, 0, 0))],
        out_shape=[
            jax.ShapeDtypeStruct((2, rows, cells), F32),
            jax.ShapeDtypeStruct((2, rows, cells), F32),
            jax.ShapeDtypeStruct(ends, BF16),
        ],
        scratch_shapes=[
            pltpu.VMEM((cells // 128, span * layers, 128), F32),
            pltpu.VMEM(split_shape, BF16),
            pltpu.VMEM(split_shape, BF16),
            pltpu.VMEM((2, 4, rows, cells), F32),
            pltpu.VMEM(split_shape, jnp.int16),
            pltpu.VMEM(split_shape, jnp.int16),
            pltpu.VMEM(ends, BF16),
            pltpu.VMEM(ends, BF16),
            dma((2,)),
            dma((2,)),
            dma((2, groups)),
            dma((2, groups)),
            dma((2, groups)),
            dma((2, groups)),
        ],
        compiler_params=pltpu.CompilerParams(
            collective_id=0, has_side_effects=True, vmem_limit_bytes=60 * 2**20
        ),
        name="halos",
    )(courant, normals, planes, flags, *(normals, planes, flags, courant) * 2)


def exponent_of(most):
    return jnp.clip(jnp.ceil(jnp.log2(jnp.maximum(most, 1e-29)) * 256.0) + 1.0, -25000.0, 30000.0)


def to_codes(values):
    return jnp.round(values).astype(jnp.int32).astype(jnp.int16)


def chunk_kernel(
    around,
    chunk_index,
    chunks,
    fraction_ref,
    normals_ref,
    planes_ref,
    flags_ref,
    courant_ref,
    next_normals_ref,
    next_planes_ref,
    next_flags_ref,
    next_courant_ref,
    last_normals_ref,
    last_planes_ref,
    last_flags_ref,
    last_courant_ref,
    ends_ref,
    axial_flux_ref,
    axial_speed_ref,
    basis_ref,
    *rest,
):
    if chunk_index:
        rest = rest[1:]
    updated_ref, sent_ref, parts, kept, source, wide, scales = rest
    block, layers, cells = fraction_ref.shape
    steps = pl.num_programs(0)
    step = pl.program_id(0)
    chunk = source.shape[1] // layers
    lane_tiles = cells // 128
    backwards = lax.rem(lax.axis_index("azim"), around // 2) >= around // 4

    def put_field(slot, k, value):
        at = pl.ds(pl.multiple_of(slot * layers, layers), layers)
        for tile in range(lane_tiles):
            parts[k, tile, at, :] = value[:, tile * 128 : (tile + 1) * 128]

    def get_field(slot, k, shift=0):
        at = pl.ds(slot * layers + shift, layers)
        return jnp.concatenate([parts[k, tile, at, :] for tile in range(lane_tiles)], axis=1)

    def put_parts(slot, normals, plane, speed):
        inverse = inverse_of(*normals)
        for k, value in enumerate((*normals, plane, inverse, -inverse, 0.5 * speed)):
            put_field(slot, k, value)

    def put_packed(slot, side):
        values = [ends_ref[side, k].astype(F32) for k in range(5)]
        put_parts(slot, values[:3], values[3], values[4])

    def own_parts(row, _):
        put_parts(
            row,
            [normals_ref[k, row].astype(F32) for k in range(3)],
            plane_value(planes_ref[row], flags_ref[row]),
            courant_ref[0, row].astype(F32),
        )
        put_field(row, 7, 0.5 * courant_ref[1, row].astype(F32))
        return 0

    lax.fori_loop(0, block, own_parts, 0, unroll=2)

    def put_row(slot, normals, planes, flags, courant):
        put_parts(
            slot,
            [normals[k, 0].astype(F32) for k in range(3)],
            plane_value(planes[0], flags[0]),
            courant[0, 0].astype(F32),
        )

    def put_next():
        put_row(block, next_normals_ref, next_planes_ref, next_flags_ref, next_courant_ref)

    if chunk_index < chunks - 1:
        put_next()
    else:
        pl.when(step < steps - 1)(put_next)

        @pl.when(step == steps - 1)
        def _():
            put_packed(block, 1)

    def read_parts(slot):
        return [get_field(slot, k) for k in range(6)]

    @pl.when(step == 0)
    def _():
        if chunk_index == 0:
            put_packed(block + 1, 0)
        else:
            put_row(
                block + 1, last_normals_ref, last_planes_ref, last_flags_ref, last_courant_ref
            )
        speed = get_field(block + 1, 6) + get_field(0, 6)
        kept[0] = upwind_flux(0, read_parts(block + 1), read_parts(0), speed)
        kept[1] = speed

    index = lax.broadcasted_iota(jnp.int32, (1, cells), 1)
    place = index.astype(F32)
    radius = 1.0 + (place + 0.5) / cells
    next_radius = 1.0 + (place + 1.5) / cells
    face_radius = 1.0 + (place + 1.0) / cells
    inverse_radius = 1.0 / radius
    inner = lax.broadcasted_iota(jnp.int32, (layers, cells), 1) < cells - 1
    layer = lax.broadcasted_iota(jnp.int32, (layers, cells), 0)
    last_layer = layer == layers - 1
    first_layer = layer == 0

    def one_row(row, _):
        own = read_parts(row)
        speed = get_field(row, 6) + get_field(row + 1, 6)
        flux = upwind_flux(0, own, read_parts(row + 1), speed)
        gained = flux - kept[0]
        divergence = speed - kept[1]
        kept[0] = flux
        kept[1] = speed

        above = [None if k == 4 else get_field(row, k, 1) for k in range(6)]
        speed = get_field(row, 7) + get_field(row, 7, 1)
        flux = upwind_flux(1, own, above, speed)
        flux = jnp.where(last_layer, axial_flux_ref[1, pl.ds(row, 1), :], flux)
        speed = jnp.where(last_layer, axial_speed_ref[1, pl.ds(row, 1), :], speed)
        gained = gained + (
            flux - jnp.where(first_layer, axial_flux_ref[0, pl.ds(row, 1), :], pltpu.roll(flux, 1, 0))
        )
        divergence = divergence + (
            speed - jnp.where(first_layer, axial_speed_ref[0, pl.ds(row, 1), :], pltpu.roll(speed, 1, 0))
        )

        half = 0.5 * courant_ref[2, row].astype(F32)
        outer = [None if k == 4 else pltpu.roll(field, cells - 1, 1) for k, field in enumerate(own)]
        speed = jnp.where(inner, half + pltpu.roll(half, cells - 1, 1), 0.0)
        flux = upwind_flux(2, own, outer, speed, radius, next_radius)
        gained = gained + (flux - pltpu.roll(flux, 1, 1)) * inverse_radius
        carried = face_radius * speed
        divergence = divergence + (carried - pltpu.roll(carried, 1, 1)) * inverse_radius
        updated = fraction_ref[row] - gained
        updated_ref[row] = updated
        result = divergence + BUOYANCY * updated
        at = step * block + row
        at = jnp.where(backwards, chunk - 1 - at, at)
        for tile in range(lane_tiles):
            source[tile, pl.ds(at, layers, stride=chunk), :] = result[
                :, tile * 128 : (tile + 1) * 128
            ]
        return 0

    lax.fori_loop(0, block, one_row, 0, unroll=2)

    @pl.when(step == steps - 1)
    def _():
        modes = basis_ref.shape[1]
        scales[...] = jnp.zeros_like(scales)

        def radial(z, _):
            at = pl.ds(pl.multiple_of(z * 2 * chunk, 2 * chunk), 2 * chunk)
            rows = jnp.concatenate([source[tile, at, :] for tile in range(lane_tiles)], axis=1)
            both = dot3((basis_ref[0], basis_ref[1]), split(rows), ((1,), (1,)))
            for half in range(2):
                got = both[:, half * chunk : (half + 1) * chunk]
                scales[...] = jnp.maximum(scales[...], jnp.abs(got))
                wide[pl.ds(z * 2 + half, modes, stride=layers), :] = got
            return 0

        lax.fori_loop(0, layers // 2, radial, 0)
        devices, slots, height, lanes = sent_ref.shape
        share = modes // devices
        most = scales[...].reshape(devices, share // height, height, lanes)
        exponent = exponent_of(jnp.max(most, axis=1))
        sent_ref[:, slots - 1] = exponent.astype(jnp.int32).astype(jnp.int16)
        factor = CODE_TOP / jnp.exp2(exponent * (1.0 / 256.0))
        scales[pl.ds(0, devices * height), :] = factor.reshape(devices * height, lanes)

        def coding(device, _):
            for mode in range(share):
                factor = scales[pl.ds(device * height + mode % height, 1), :]
                for part in range(layers // height):
                    at = (device * share + mode) * layers + part * height
                    values = wide[pl.ds(pl.multiple_of(at, height), height), :]
                    sent_ref[device, mode * (layers // height) + part] = to_codes(values * factor)
            return 0

        lax.fori_loop(0, devices, coding, 0)


def advect_chunk(arrays, ends, axial_flux, axial_speed, basis, chunk_index, chunk, around, devices, base):
    fraction, normals, planes, flags, courant = arrays
    rows, layers, cells = fraction.shape
    block = BLOCK
    steps = chunk // block
    first = chunk_index * steps
    share = cells // devices

    def here(i):
        return first + i

    def after(i):
        return jnp.minimum((first + i + 1) * block, rows - 1)

    whole = pl.BlockSpec((block, layers, cells), lambda i: (here(i), 0, 0))
    triple = pl.BlockSpec((3, block, layers, cells), lambda i: (0, here(i), 0, 0))
    row = pl.BlockSpec((1, layers, cells), lambda i: (after(i), 0, 0))
    before = max(first * block - 1, 0)
    last_row = pl.BlockSpec((1, layers, cells), lambda i: (before, 0, 0))
    edge = pl.BlockSpec((2, block, cells), lambda i: (0, here(i), 0))
    in_specs = [
        whole,
        triple,
        whole,
        whole,
        triple,
        pl.BlockSpec((3, 1, layers, cells), lambda i: (0, after(i), 0, 0)),
        row,
        row,
        pl.BlockSpec((1, 1, layers, cells), lambda i: (0, after(i), 0, 0)),
        pl.BlockSpec((3, 1, layers, cells), lambda i: (0, before, 0, 0)),
        last_row,
        last_row,
        pl.BlockSpec((1, 1, layers, cells), lambda i: (0, before, 0, 0)),
        pl.BlockSpec(ends.shape, lambda i: (0, 0, 0, 0)),
        edge,
        edge,
        pl.BlockSpec((2, cells, cells), lambda i: (0, 0, 0)),
    ]
    operands = [
        fraction, normals, planes, flags, courant,
        normals, planes, flags, courant,
        normals, planes, flags, courant,
        ends, axial_flux, axial_speed, basis,
    ]
    aliases = {}
    if base is not None:
        in_specs.append(pl.BlockSpec(memory_space=pl.ANY))
        operands.append(base)
        aliases = {len(operands) - 1: 0}
    return pl.pallas_call(
        functools.partial(chunk_kernel, around, chunk_index, rows // chunk),
        grid=(steps,),
        in_specs=in_specs,
        out_specs=[
            whole,
            pl.BlockSpec((devices, 2 * share + 1, layers // 2, chunk), lambda i: (0, 0, 0, 0)),
        ],
        out_shape=[
            jax.ShapeDtypeStruct(fraction.shape, F32),
            jax.ShapeDtypeStruct((devices, 2 * share + 1, layers // 2, chunk), jnp.int16),
        ],
        scratch_shapes=[
            pltpu.VMEM((8, cells // 128, (block + 2) * layers, 128), F32),
            pltpu.VMEM((2, layers, cells), F32),
            pltpu.VMEM((cells // 128, layers * chunk, 128), F32),
            pltpu.VMEM((cells * layers, chunk), F32),
            pltpu.VMEM((cells, chunk), F32),
        ],
        input_output_aliases=aliases,
        compiler_params=pltpu.CompilerParams(vmem_limit_bytes=60 * 2**20),
        cost_estimate=pl.CostEstimate(
            flops=40000 * chunk * layers * cells, bytes_accessed=30 * chunk * layers * cells, transcendentals=0
        ),
        name="advect_chunk",
    )(*operands)


@functools.lru_cache(None)
def folded_tables(total):
    quarter = total // 4
    place = np.arange(quarter) + 0.5

    def halves(x):
        high = x.astype(jnp.bfloat16)
        return np.stack([high, (x - high.astype(np.float64)).astype(jnp.bfloat16)])

    tables, rates, weights = [], [], []
    for waves, wave in (
        (2 * np.arange(quarter), np.cos),
        (2 * np.arange(quarter) + 2, np.sin),
        (2 * np.arange(quarter) + 1, np.cos),
        (2 * np.arange(quarter) + 1, np.sin),
    ):
        doubled = waves[:, None] * (2 * np.arange(quarter) + 1)[None, :] % (2 * total)
        tables.append(wave(np.pi * doubled / total))
        rates.append(2.0 - 2.0 * np.cos(2.0 * np.pi * waves / total))
        weights.append(np.where((waves == 0) | (waves == total // 2), 1.0, 2.0) / total)
    tables = np.stack(tables)
    back = np.stack([halves(t) for t in tables])
    forth = np.stack([halves(t.T) for t in tables])
    return forth, back, np.stack(rates)[:, None].astype(np.float32), np.stack(weights)[:, None].astype(np.float32)


def decoded(values):
    return values.astype(jnp.int32).astype(F32)


def scale_of(codes):
    return jnp.exp2(decoded(codes) * (1.0 / 256.0)) * (1.0 / CODE_TOP)


def solve_kernel(around, along, chunks, start, *refs):
    got = refs[:chunks]
    mix, unmix, forth, back, rates, weights, shifts = refs[chunks : chunks + 7]
    sent, high, low, result, scale, exponents = refs[chunks + 7 :]
    devices, slots, height, lanes = got[0].shape
    count, layers = (sent.shape[1] - 1) // (2 * chunks), 2 * height
    share = (sent.shape[1] - 1) // (2 * chunks)
    together = chunks * share // height
    pairs = around // 4
    for chunk in range(chunks):
        scale[chunk] = scale_of(got[chunk][:, slots - 1])
    def spots():
        for pair in range(pairs):
            for chunk in range(chunks):
                mirror = chunks - 1 - chunk
                at = pl.ds((pair * chunks + chunk) * lanes, lanes)
                yield at, (
                    (pair, chunk),
                    (pair + 2 * pairs, chunk),
                    (2 * pairs - 1 - pair, mirror),
                    (4 * pairs - 1 - pair, mirror),
                )

    def fold(index, _):
        mode, axial = index // along, index % along
        rows = pl.ds(pl.multiple_of(index * layers, layers), layers)
        row = pl.ds(lax.rem(start + mode, height), 1)
        for at, places in spots():
            u0, u1, r0, r1 = [
                jnp.concatenate(
                    [
                        decoded(got[chunk][azim * along + axial, 2 * (start + mode) + part])
                        * scale[chunk, azim * along + axial, row, :]
                        for part in range(2)
                    ]
                )
                for azim, chunk in places
            ]
            e0, o0, e1, o1 = u0 + u1, u0 - u1, r0 + r1, r0 - r1
            for k, folded in enumerate((e0 + e1, e0 - e1, o0 - o1, o0 + o1)):
                high[k, rows, at], low[k, rows, at] = split(folded)
        return 0

    lax.fori_loop(0, count * along, fold, 0)

    deep = mix.shape[1]
    parts = [pl.ds(at, deep) for at in range(0, high.shape[1], deep)]

    def waves(k, _):
        for at in parts:
            high[k, at], low[k, at] = split(
                dot3((mix[0], mix[1]), (high[k, at], low[k, at]))
            )
        spectrum = dot3((high[k], low[k]), (forth[k, 0], forth[k, 1]))
        high[k], low[k] = split(spectrum * weights[k] / (rates[k] + shifts[...]))
        high[k], low[k] = split(dot3((high[k], low[k]), (back[k, 0], back[k, 1])))
        for at in parts:
            result[k, at] = dot3((unmix[0], unmix[1]), (high[k, at], low[k, at]))
        return 0

    lax.fori_loop(0, 4, waves, 0)

    apart = count // together

    def unfold(index, _):
        mode, axial = index // along, index % along
        for at, places in spots():
            found = []
            for part in range(together):
                row = ((mode + part * apart) * along + axial) * layers
                rows = pl.ds(pl.multiple_of(row, layers), layers)
                ec, es, oc, os = [result[k, rows, at] for k in range(4)]
                e0, e1, o0, o1 = ec + es, ec - es, oc + os, os - oc
                found.append((e0 + o0, e0 - o0, e1 + o1, e1 - o1))
            for (azim, chunk), values in zip(places, zip(*found)):
                device = azim * along + axial
                most = functools.reduce(jnp.maximum, [jnp.abs(x) for x in values])
                exponent = exponent_of(jnp.max(most, axis=0, keepdims=True))
                exponents[device, pl.ds(chunk * apart + mode, 1), :] = exponent
                factor = CODE_TOP / jnp.exp2(exponent * (1.0 / 256.0))
                for part, value in enumerate(values):
                    slot = 2 * (chunk * share + mode + part * apart)
                    for half in range(2):
                        piece = value[half * height : (half + 1) * height]
                        sent[device, slot + half] = to_codes(piece * factor)
        return 0

    lax.fori_loop(0, apart * along, unfold, 0)

    sent[:, 2 * chunks * share] = exponents[...].astype(jnp.int32).astype(jnp.int16)


def solve_group(got, mix, unmix, tables, shifts, start, share, around, along):
    chunks = len(got)
    devices, slots, height, lanes = got[0].shape
    rows = share * along * 2 * height
    forth, back, rates, weights = tables
    width = forth.shape[-1]
    whole = pl.BlockSpec(memory_space=pltpu.VMEM)
    shifts = lax.slice_in_dim(shifts, start * along * 2 * height, start * along * 2 * height + rows)
    return pl.pallas_call(
        functools.partial(solve_kernel, around, along, chunks, start),
        in_specs=[whole] * (chunks + 7),
        out_specs=whole,
        out_shape=jax.ShapeDtypeStruct((devices, 2 * chunks * share + 1, height, lanes), jnp.int16),
        scratch_shapes=[
            pltpu.VMEM((4, rows, width), BF16),
            pltpu.VMEM((4, rows, width), BF16),
            pltpu.VMEM((4, rows, width), F32),
            pltpu.VMEM((chunks, devices, height, lanes), F32),
            pltpu.VMEM((devices, height, lanes), F32),
        ],
        compiler_params=pltpu.CompilerParams(vmem_limit_bytes=32 * 2**20),
        cost_estimate=pl.CostEstimate(
            flops=60 * rows * width * width, bytes_accessed=20 * 2**20, transcendentals=0
        ),
        name="solve_group",
    )(*got, mix, unmix, forth, back, rates, weights, shifts)


def pressure_kernel(around, groups, chunks, *refs):
    got = refs[:groups]
    basis = refs[groups]
    base = refs[groups + 1 : -6]
    out, flat, wide, scale, high, low = refs[-6:]
    devices, _, height, lanes = got[0].shape
    layers = 2 * height
    lane_tiles = out.shape[2] // 128
    chunk = pl.program_id(0)
    backwards = lax.rem(lax.axis_index("azim"), around // 2) >= around // 4
    i = lax.broadcasted_iota(jnp.int32, (lanes, lanes), 0)
    j = lax.broadcasted_iota(jnp.int32, (lanes, lanes), 1)
    turned_place = jnp.where(backwards, lanes - 1, 0) + jnp.where(backwards, -1, 1) * i
    turn = jnp.where(j == turned_place, 1.0, 0.0).astype(BF16)
    spans, filled = [], 0
    for group in range(groups):
        share = (got[group].shape[1] - 1) // (2 * chunks)
        apart = height // chunks
        spans.append((filled, devices * share))
        scale[group] = scale_of(got[group][:, 2 * chunks * share])

        def unpack(device, _, group=group, share=share, filled=filled):
            for mode in range(share):
                factor = scale[group, device, pl.ds(chunk * apart + mode % apart, 1), :]
                for part in range(2):
                    at = (filled + device * share + mode) * layers + part * height
                    flat[pl.ds(pl.multiple_of(at, height), height), :] = (
                        decoded(got[group][device, 2 * (chunk * share + mode) + part]) * factor
                    )
            return 0

        lax.fori_loop(0, devices, unpack, 0)
        filled += devices * share

    together = high.shape[0] // lanes

    def radial(batch, _):
        for part in range(together):
            for offset, height in spans:
                z = batch * together + part
                values = split(flat[pl.ds(offset * layers + z, height, stride=layers), :])
                at = pl.ds(offset, height)
                for target, value in zip((high, low), values):
                    target[part * lanes : (part + 1) * lanes, at] = dot(
                        turn, value, ((1,), (1,))
                    ).astype(BF16)
        if filled > 128:
            total = dot3((high[...], low[...]), (basis[0], basis[1]))
        else:
            lower = jnp.concatenate([high[...], low[...], high[...]], axis=1)
            total = dot(lower, jnp.concatenate([basis[0], basis[0], basis[1]]), ((1,), (0,)))
        for part in range(together):
            for tile in range(lane_tiles):
                wide[tile, pl.ds(batch * together + part, lanes, stride=layers), :] = total[
                    part * lanes : (part + 1) * lanes, tile * 128 : (tile + 1) * 128
                ]
        return 0

    lax.fori_loop(0, layers // together, radial, 0)
    for tile in range(lane_tiles):
        at = slice(tile * 128, (tile + 1) * 128)
        result = wide[tile].reshape(lanes, layers, 128)
        out[:, :, at] = result + base[0][:, :, at] if base else result


def pressure_of(got, basis, around, chunks, base=None):
    groups = len(got)
    devices, _, height, lanes = got[0].shape
    layers = 2 * height
    inner, cells = basis.shape[1:]
    whole = pl.BlockSpec((lanes, layers, cells), lambda i: (i, 0, 0))
    return pl.pallas_call(
        functools.partial(pressure_kernel, around, groups, chunks),
        grid=(chunks,),
        in_specs=[pl.BlockSpec(memory_space=pltpu.VMEM)] * (groups + 1)
        + ([] if base is None else [whole]),
        out_specs=whole,
        out_shape=jax.ShapeDtypeStruct((lanes * chunks, layers, cells), F32),
        scratch_shapes=[
            pltpu.VMEM((inner * layers, lanes), F32),
            pltpu.VMEM((cells // 128, lanes * layers, 128), F32),
            pltpu.VMEM((groups, devices, height, lanes), F32),
            pltpu.VMEM((4 * lanes, inner), BF16),
            pltpu.VMEM((4 * lanes, inner), BF16),
        ],
        compiler_params=pltpu.CompilerParams(vmem_limit_bytes=40 * 2**20),
        cost_estimate=pl.CostEstimate(
            flops=20 * lanes * chunks * layers * cells * inner,
            bytes_accessed=20 * 2**20,
            transcendentals=0,
        ),
        name="pressure_of",
    )(*got, basis, *([] if base is None else [base]))


def halves(values):
    high = lax.reduce_precision(values, 8, 7)
    return jnp.stack([high.astype(BF16), (values - high).astype(BF16)])


def exchanged(sent):
    return lax.all_to_all(sent, ("azim", "axial"), split_axis=0, concat_axis=0, tiled=True)


def following_kernel(values_ref, earlier_ref, out_ref):
    del values_ref, earlier_ref, out_ref


def following(values, earlier):
    anywhere = pl.BlockSpec(memory_space=pl.ANY)
    return pl.pallas_call(
        following_kernel,
        in_specs=[anywhere, anywhere],
        out_specs=anywhere,
        out_shape=jax.ShapeDtypeStruct(values.shape, values.dtype),
        input_output_aliases={0: 0},
        name="following",
    )(values, earlier)


def overlapped(
    fraction,
    normals,
    planes,
    cell_flags,
    courant,
    radial_basis,
    axial_basis,
    radial_rates,
    axial_rates,
):
    rows, layers, cells = fraction.shape
    around, along = lax.axis_size("azim"), lax.axis_size("axial")
    devices = around * along
    modes = cells // devices
    chunks = rows // CHUNK
    axial_flux, axial_speed, ends = halos(normals, planes, cell_flags, courant)
    forward_basis = halves(radial_basis.T)
    arrays = (fraction, normals, planes, cell_flags, courant)
    updated, got = None, []
    for chunk in range(chunks):
        updated, sent = advect_chunk(
            arrays, ends, axial_flux, axial_speed, forward_basis, chunk, CHUNK, around, devices, updated
        )
        got.append(exchanged(following(sent, got[-1]) if got else sent))
    count = jnp.eye(4, dtype=F32)
    mix, unmix = halves(jnp.kron(count, axial_basis.T)), halves(jnp.kron(count, axial_basis))
    first = (lax.axis_index("azim") * along + lax.axis_index("axial")) * modes
    shifts = lax.dynamic_slice_in_dim(radial_rates, first, modes)[:, None] + axial_rates[None, :]
    shifts = shifts.reshape(modes * along * layers, 1)
    tables = [jnp.asarray(x) for x in folded_tables(rows * around)]
    returned, bases = [], []
    for start, share in SOLVED:
        sent = solve_group(got, mix, unmix, tables, shifts, start, share, around, along)
        returned.append(exchanged(sent))
        rows_of = radial_basis.T.reshape(devices, modes, cells)[:, start : start + share]
        bases.append(rows_of.reshape(devices * share, cells))
    pressure = pressure_of(returned[:-1], halves(jnp.concatenate(bases[:-1])), around, chunks)
    pressure = pressure_of(returned[-1:], halves(bases[-1]), around, chunks, pressure)
    return (updated, pressure)


def fits(fraction):
    rows, layers, cells = fraction.shape
    around, along = lax.axis_size("azim"), lax.axis_size("axial")
    modes = cells // (around * along)
    chunks = rows // CHUNK
    return (
        rows % CHUNK == 0
        and layers == 16
        and modes == 16
        and modes // 2 * chunks == layers
        and cells % 128 == 0
        and around % 4 == 0
        and along > 2
    )


def local(*arguments):
    return overlapped(*arguments) if fits(arguments[0]) else stepwise(*arguments)


def solution(mesh):
    placed = (
        P("azim", "axial", None),
        P(None, "azim", "axial", None),
        P("azim", "axial", None),
        P("azim", "axial", None),
        P(None, "azim", "axial", None),
        P(),
        P(),
        P(),
        P(),
    )
    return jax.shard_map(
        local,
        mesh=mesh,
        in_specs=placed,
        out_specs=(P("azim", "axial", None), P("azim", "axial", None)),
        check_vma=False,
    )
```

```python
import functools

import jax
import jax.numpy as jnp
import numpy as np
from jax import lax
from jax.experimental import pallas as pl
from jax.experimental.pallas import tpu as pltpu
from jax.sharding import PartitionSpec as P

HIGH = lax.Precision.HIGH
BUOYANCY = 0.5
CODE_TOP = 32700.0


def shifted_in(edge, axis, towards_lower):
    count = lax.axis_size(axis)
    if towards_lower:
        pairs = [((i + 1) % count, i) for i in range(count)]
    else:
        pairs = [(i, (i + 1) % count) for i in range(count)]
    return lax.ppermute(edge, axis, pairs)


def cell_parts(n0, n1, n2, code):
    m0, m1, m2 = jnp.abs(n0), jnp.abs(n1), jnp.abs(n2)
    return (n0, n1, n2, code, 1.0 / (6.0 * m0 * m1 * m2))


def cube(height):
    held = jnp.maximum(height, 0.0)
    return held * held * held


def face_flux(direction, lower, upper, speed, lower_weight=None, upper_weight=None):
    forward = speed > 0.0
    signed = jnp.where(forward, lower[direction], -upper[direction])
    first, second = [d for d in range(3) if d != direction]
    along = jnp.abs(signed)
    side_a = jnp.abs(jnp.where(forward, lower[first], upper[first]))
    side_b = jnp.abs(jnp.where(forward, lower[second], upper[second]))
    code = jnp.where(forward, lower[3], upper[3])
    inverse = jnp.where(forward, lower[4], upper[4])
    width = jnp.abs(speed)
    near = code - along * jnp.where(signed < 0.0, 0.0, 1.0 - width)
    far = near - along * width
    sides = side_a + side_b
    total = (cube(near) - cube(near - side_a)) - (cube(near - side_b) - cube(near - sides))
    total = total - ((cube(far) - cube(far - side_a)) - (cube(far - side_b) - cube(far - sides)))
    volume = jnp.where(code > 3.0, width, jnp.where(code < -0.5, 0.0, total * inverse))
    if lower_weight is not None:
        volume = volume * jnp.where(forward, lower_weight, upper_weight)
    return jnp.where(forward, volume, jnp.where(speed < 0.0, -volume, 0.0))


def advect_kernel(
    fraction_ref,
    normals_ref,
    planes_ref,
    flags_ref,
    courant_ref,
    next_ref,
    high_ref,
    low_azim_ref,
    low_axial_ref,
    updated_ref,
    source_ref,
    kept,
):
    rows, layers, cells = fraction_ref.shape
    f32 = jnp.float32

    @pl.when(pl.program_id(0) == 0)
    def _():
        kept[...] = low_azim_ref[...]

    index = lax.broadcasted_iota(jnp.int32, (1, cells), 1)
    place = index.astype(f32)
    radius = 1.0 + (place + 0.5) / cells
    next_radius = 1.0 + (place + 1.5) / cells
    face_radius = 1.0 + (place + 1.0) / cells
    inverse_radius = 1.0 / radius
    inner = lax.broadcasted_iota(jnp.int32, (layers, cells), 1) < cells - 1
    layer = lax.broadcasted_iota(jnp.int32, (layers, cells), 0)
    last_layer = layer == layers - 1
    first_layer = layer == 0

    def row_parts(row):
        flags = flags_ref[row]
        code = jnp.where(
            flags == 2, planes_ref[row].astype(f32), jnp.where(flags == 1, 4.0, -1.0)
        )
        return cell_parts(
            normals_ref[0, row].astype(f32),
            normals_ref[1, row].astype(f32),
            normals_ref[2, row].astype(f32),
            code,
        )

    def one_row(row, upper, upper_speed):
        own = row_parts(row)
        moved = [courant_ref[d, row].astype(f32) for d in range(3)]
        speed = 0.5 * (moved[0] + upper_speed)
        flux = face_flux(0, own, upper, speed)
        gained = flux - kept[0]
        divergence = speed - kept[1]
        kept[0] = flux
        kept[1] = speed
        beyond = cell_parts(*[high_ref[k, row] for k in range(4)])
        above = [
            jnp.where(last_layer, high, pltpu.roll(field, layers - 1, 0))
            for field, high in zip(own, beyond)
        ]
        speed = 0.5 * (
            moved[1]
            + jnp.where(last_layer, high_ref[4, row], pltpu.roll(moved[1], layers - 1, 0))
        )
        flux = face_flux(1, own, above, speed)
        gained = gained + (
            flux - jnp.where(first_layer, low_axial_ref[0, row], pltpu.roll(flux, 1, 0))
        )
        divergence = divergence + (
            speed - jnp.where(first_layer, low_axial_ref[1, row], pltpu.roll(speed, 1, 0))
        )
        outer = [pltpu.roll(field, cells - 1, 1) for field in own]
        speed = 0.5 * (moved[2] + pltpu.roll(moved[2], cells - 1, 1))
        speed = jnp.where(inner, speed, 0.0)
        flux = face_flux(2, own, outer, speed, radius, next_radius)
        gained = gained + (flux - pltpu.roll(flux, 1, 1)) * inverse_radius
        carried = face_radius * speed
        divergence = divergence + (carried - pltpu.roll(carried, 1, 1)) * inverse_radius
        updated = fraction_ref[row] - gained
        updated_ref[row] = updated
        source_ref[row] = divergence + BUOYANCY * updated

    def step(row, _):
        one_row(row, row_parts(row + 1), courant_ref[0, row + 1].astype(f32))
        return 0

    lax.fori_loop(0, rows - 1, step, 0)
    one_row(
        rows - 1,
        cell_parts(*[next_ref[k, 0].astype(f32) for k in range(4)]),
        next_ref[4, 0].astype(f32),
    )


def plane_codes(planes, flags):
    return jnp.where(
        flags == 2, planes.astype(jnp.float32), jnp.where(flags == 1, 4.0, -1.0)
    ).astype(jnp.bfloat16)


def packed_edge(normals, planes, flags, courant, direction, pick):
    parts = [pick(normals[d]) for d in range(3)]
    parts.append(plane_codes(pick(planes), pick(flags)))
    parts.append(pick(courant[direction]))
    return jnp.stack(parts)


def low_face(direction, lower, upper):
    lower, upper = lower.astype(jnp.float32), upper.astype(jnp.float32)
    speed = 0.5 * (lower[4] + upper[4])
    flux = face_flux(direction, cell_parts(*lower[:4]), cell_parts(*upper[:4]), speed)
    return jnp.stack([flux, speed])


def advect(fraction, normals, planes, flags, courant):
    rows, layers, cells = fraction.shape
    block = 16 if rows % 16 == 0 else 1
    blocks = rows // block
    fields = (normals, planes, flags, courant)
    top_row = packed_edge(*fields, 0, lambda x: x[rows - 1])
    bottom_row = packed_edge(*fields, 0, lambda x: x[0])
    top_layer = packed_edge(*fields, 1, lambda x: x[:, layers - 1])
    bottom_layer = packed_edge(*fields, 1, lambda x: x[:, 0])
    high_row = shifted_in(bottom_row, "azim", True)
    low_row = shifted_in(top_row, "azim", False)
    high_layer = shifted_in(bottom_layer, "axial", True)
    low_layer = shifted_in(top_layer, "axial", False)
    low_azim = low_face(0, low_row, bottom_row)
    low_axial = low_face(1, low_layer, bottom_layer)[:, :, None]
    high_axial = high_layer.astype(jnp.float32)[:, :, None]
    inside = packed_edge(*fields, 0, lambda x: x[block::block])
    following = jnp.concatenate([inside, high_row[:, None]], axis=1)
    whole = pl.BlockSpec((block, layers, cells), lambda i: (i, 0, 0))
    triple = pl.BlockSpec((3, block, layers, cells), lambda i: (0, i, 0, 0))
    return pl.pallas_call(
        advect_kernel,
        grid=(blocks,),
        in_specs=[
            whole,
            triple,
            whole,
            whole,
            triple,
            pl.BlockSpec((5, 1, layers, cells), lambda i: (0, i, 0, 0)),
            pl.BlockSpec((5, block, 1, cells), lambda i: (0, i, 0, 0)),
            pl.BlockSpec((2, layers, cells), lambda i: (0, 0, 0)),
            pl.BlockSpec((2, block, 1, cells), lambda i: (0, i, 0, 0)),
        ],
        out_specs=[whole, whole],
        out_shape=[jax.ShapeDtypeStruct(fraction.shape, jnp.float32)] * 2,
        scratch_shapes=[pltpu.VMEM((2, layers, cells), jnp.float32)],
        compiler_params=pltpu.CompilerParams(vmem_limit_bytes=40 * 2**20),
    )(
        fraction,
        normals,
        planes,
        flags,
        courant,
        following,
        high_axial,
        low_azim,
        low_axial,
    )


def coded(values):
    most = jnp.max(jnp.abs(values), axis=-1)
    exponent = jnp.clip(jnp.ceil(jnp.log2(most) * 256.0) + 1.0, -30000.0, 30000.0)
    scale = CODE_TOP * jnp.exp2(exponent * (-1.0 / 256.0))
    codes = jnp.round(values * scale[..., None])
    return jnp.clip(codes, -32767.0, 32767.0).astype(jnp.int16), exponent.astype(jnp.int16)


def exchange(values):
    modes, cells = values.shape[1], values.shape[3]
    codes, exponent = coded(values)
    extra = jnp.pad(exponent.transpose(0, 2, 1), ((0, 0), (0, 0), (0, cells - modes)))
    sent = jnp.concatenate([codes, extra[:, None]], axis=1)
    got = lax.all_to_all(sent, ("azim", "axial"), split_axis=0, concat_axis=0, tiled=True)
    exponent = got[:, modes, :, :modes].transpose(0, 2, 1).astype(jnp.float32)
    scale = jnp.exp2(exponent * (1.0 / 256.0)) * (1.0 / CODE_TOP)
    return got[:, :modes].astype(jnp.float32) * scale[..., None]


@functools.lru_cache(None)
def azimuth_tables(total):
    half, quarter = total // 2, total // 4
    place = np.arange(half)

    def table(cosines, sines):
        waves = np.concatenate([cosines, sines])
        angles = 2.0 * np.pi / total * (waves[:, None] * place[None, :] % total)
        rows = np.concatenate(
            [np.cos(angles[: len(cosines)]), np.sin(angles[len(cosines) :])]
        ).astype(np.float32)
        rates = (2.0 - 2.0 * np.cos(2.0 * np.pi * waves / total)).astype(np.float32)
        ends = (waves == 0) | (waves == half)
        return rows, rates, (np.where(ends, 1.0, 2.0) / total).astype(np.float32)

    even = 2 * np.arange(quarter + 1)
    odd = 2 * np.arange(quarter) + 1
    return table(even, even[1:-1]), table(odd, odd)


def stepwise(
    fraction,
    normals,
    planes,
    cell_flags,
    courant,
    radial_basis,
    axial_basis,
    radial_rates,
    axial_rates,
):
    rows, layers, cells = fraction.shape
    around, along = lax.axis_size("azim"), lax.axis_size("axial")
    devices = around * along
    modes = cells // devices
    total = rows * around
    half = total // 2
    updated, source = advect(fraction, normals, planes, cell_flags, courant)
    radial_modes = jnp.einsum("azr,rj->jza", source, radial_basis, precision=HIGH)
    got = exchange(radial_modes.reshape(devices, modes, layers, rows))
    got = got.reshape(around, along, modes, layers, rows).transpose(2, 1, 3, 0, 4)
    got = got.reshape(modes, along * layers, total)
    both = jnp.einsum("jza,zn->jna", got, axial_basis, precision=HIGH)
    first = (lax.axis_index("azim") * along + lax.axis_index("axial")) * modes
    shifts = lax.dynamic_slice_in_dim(radial_rates, first, modes)[:, None] + axial_rates[None, :]
    low, high = both[..., :half], both[..., half:]
    solved = []
    for folded, (table, rates, weight) in zip((low + high, low - high), azimuth_tables(total)):
        coefficients = jnp.einsum("jna,ka->jnk", folded, table, precision=HIGH)
        scaled = coefficients / (rates + shifts[..., None]) * weight
        solved.append(jnp.einsum("jnk,ka->jna", scaled, table, precision=HIGH))
    physical = jnp.concatenate([solved[0] + solved[1], solved[0] - solved[1]], axis=-1)
    physical = jnp.einsum("jna,zn->jza", physical, axial_basis, precision=HIGH)
    physical = physical.reshape(modes, along, layers, around, rows).transpose(3, 1, 0, 2, 4)
    returned = exchange(physical.reshape(devices, modes, layers, rows))
    returned = returned.reshape(cells, layers, rows)
    pressure = jnp.einsum("jza,rj->azr", returned, radial_basis, precision=HIGH)
    return (updated, pressure)


CHUNK = 128
BLOCK = 16
SOLVE_VMEM = 52
PRESSURE_VMEM = 58
SOLVED = ((0, 4), (8, 8), (4, 4))
FLUX_SCALE = 32767.0 / 0.3
F32 = jnp.float32
BF16 = jnp.bfloat16


def split(values):
    high = values.astype(BF16)
    return high, (values - high.astype(F32)).astype(BF16)


def dot(a, b, contract):
    return lax.dot_general(a, b, (contract, ((), ())), preferred_element_type=F32)


def dot3(a, b, contract=((1,), (0,))):
    return dot(a[0], b[0], contract) + (dot(a[0], b[1], contract) + dot(a[1], b[0], contract))


def slab_flux(normal, side_a, side_b, plane, inverse, speed):
    along = jnp.abs(normal)
    reach = normal * speed
    slab = jnp.abs(reach)
    near = plane - jnp.where(reach > 0.0, along - slab, 0.0)
    other = (slab + (side_a + side_b)) - near
    folded = near > other
    held = jnp.maximum(jnp.minimum(near, other), 0.0)
    low, high = jnp.minimum(side_a, side_b), jnp.maximum(side_a, side_b)
    by_low = jnp.maximum(held - low, 0.0)
    by_slab = jnp.maximum(held - slab, 0.0)
    last = jnp.maximum(held - (low + slab), 0.0) - jnp.maximum(held - high, 0.0)
    total = held * held * held - by_slab * by_slab * by_slab
    total = total - (by_low * by_low * by_low - last * last * last)
    flux = total * inverse
    return jnp.where(folded, speed - flux, flux)


def upwind_flux(direction, lower, upper, speed, lower_weight=None, upper_weight=None):
    forward = speed > 0.0
    first, second = [d for d in range(3) if d != direction]
    normal = jnp.where(forward, lower[direction], upper[direction])
    side_a = jnp.abs(jnp.where(forward, lower[first], upper[first]))
    side_b = jnp.abs(jnp.where(forward, lower[second], upper[second]))
    plane = jnp.where(forward, lower[3], upper[3])
    inverse = jnp.where(forward, lower[4], upper[5])
    flux = slab_flux(normal, side_a, side_b, plane, inverse, speed)
    if lower_weight is not None:
        flux = flux * jnp.where(forward, lower_weight, upper_weight)
    return flux


def inverse_of(n0, n1, n2):
    return 1.0 / (6.0 * jnp.abs(n0 * n1 * n2))


def plane_value(planes, flags):
    return jnp.where(flags == 2, planes.astype(F32), jnp.where(flags == 1, 4.0, -4.0))


def halo_kernel(
    courant_ref,
    normals_ref,
    planes_ref,
    flags_ref,
    first_normals_ref,
    first_planes_ref,
    first_flags_ref,
    first_courant_ref,
    last_normals_ref,
    last_planes_ref,
    last_flags_ref,
    last_courant_ref,
    flux_ref,
    speed_ref,
    ends_ref,
    work,
    edge,
    edge_in,
    fields,
    code,
    code_in,
    packs,
    packs_in,
    row_send,
    row_recv,
    edge_send,
    edge_recv,
    code_send,
    code_recv,
):
    step = pl.program_id(0)
    half = pl.num_programs(0) // 2
    span, layers, cells = planes_ref.shape
    groups, group = code.shape[1:3]
    per_group = group // span
    tiles = cells // 128
    neighbours = []
    for axis in ("azim", "axial"):
        count, me = lax.axis_size(axis), lax.axis_index(axis)
        neighbours.append(
            ({axis: lax.rem(me + count - 1, count)}, {axis: lax.rem(me + 1, count)})
        )

    def remote(source, target, send, recv, device):
        return pltpu.make_async_remote_copy(
            src_ref=source,
            dst_ref=target,
            send_sem=send,
            recv_sem=recv,
            device_id=device,
            device_id_type=pl.DeviceIdType.MESH,
        )

    row_copies = [
        remote(packs.at[s], packs_in.at[1 - s], row_send.at[s], row_recv.at[1 - s], neighbours[0][s])
        for s in range(2)
    ]
    def edge_copy(s, g):
        return remote(
            edge.at[s, g],
            edge_in.at[1 - s, g],
            edge_send.at[s, g],
            edge_recv.at[1 - s, g],
            neighbours[1][s],
        )

    def code_copy(s, g):
        return remote(
            code.at[s, g],
            code_in.at[1 - s, g],
            code_send.at[s, g],
            code_recv.at[1 - s, g],
            neighbours[1][s],
        )

    @pl.when(step == 0)
    def _():
        barrier = pltpu.get_barrier_semaphore()
        for pair in neighbours:
            for device in pair:
                pl.semaphore_signal(
                    barrier, inc=1, device_id=device, device_id_type=pl.DeviceIdType.MESH
                )
        pl.semaphore_wait(barrier, 4)
        for s, (normals, planes, flags, courant) in enumerate(
            (
                (first_normals_ref, first_planes_ref, first_flags_ref, first_courant_ref),
                (last_normals_ref, last_planes_ref, last_flags_ref, last_courant_ref),
            )
        ):
            for k in range(3):
                packs[s, k] = normals[k, 0]
            packs[s, 3] = plane_value(planes[0], flags[0]).astype(BF16)
            packs[s, 4] = courant[0, 0]
        for copy in row_copies:
            copy.start()

    def layer_rows(tile, layer):
        return work[tile, pl.ds(layer, span, stride=layers), :]

    @pl.when(step < half)
    def _():
        place = step // per_group
        at = pl.ds(pl.multiple_of(lax.rem(step, per_group) * span, span), span)
        for tile in range(tiles):
            lanes = pl.ds(tile * 128, 128)
            work[tile] = courant_ref[0, :, :, lanes].astype(F32).reshape(span * layers, 128)
            for s, layer in ((0, 0), (1, layers - 1)):
                edge[s, place, at, lanes] = layer_rows(tile, layer).astype(BF16)

    for g in range(groups):

        @pl.when(step == (g + 1) * per_group - 1)
        def _(g=g):
            for s in range(2):
                edge_copy(s, g).start()

    @pl.when(step >= half)
    def _():
        at = pl.ds(pl.multiple_of((step - half) * span, span), span)
        for k in range(4):
            for tile in range(tiles):
                lanes = pl.ds(tile * 128, 128)
                if k < 3:
                    field = normals_ref[k, :, :, lanes].astype(F32)
                else:
                    field = plane_value(planes_ref[:, :, lanes], flags_ref[:, :, lanes])
                work[tile] = field.reshape(span * layers, 128)
                for s, layer in ((0, 0), (1, layers - 1)):
                    fields[s, k, at, lanes] = layer_rows(tile, layer)

    for g in range(groups):

        @pl.when(step == half + (g + 1) * per_group - 1)
        def _(g=g):
            for s in range(2):
                edge_copy(s, g).wait()
            for s in range(2):

                def donate(piece, _, s=s):
                    inside = pl.ds(pl.multiple_of(piece * 16, 16), 16)
                    at = pl.ds(pl.multiple_of(g * group + piece * 16, 16), 16)
                    normals = [fields[s, k, at, :] for k in range(3)]
                    own, beyond = edge[s, g, inside, :], edge_in[s, g, inside, :]
                    speed = 0.5 * (own.astype(F32) + beyond.astype(F32))
                    inverse = inverse_of(*normals)
                    flux = slab_flux(
                        normals[1],
                        jnp.abs(normals[0]),
                        jnp.abs(normals[2]),
                        fields[s, 3, at, :],
                        inverse if s == 1 else -inverse,
                        speed,
                    )
                    flux = jnp.where(speed > 0.0 if s == 1 else speed < 0.0, flux, 0.0)
                    flux_ref[s, at, :] = flux
                    speed_ref[s, at, :] = speed
                    code[s, g, inside, :] = to_codes(flux * FLUX_SCALE)
                    return 0

                lax.fori_loop(0, group // 16, donate, 0)
                code_copy(s, g).start()

    @pl.when(step == 2 * half - 1)
    def _():
        for copy in row_copies:
            copy.wait()
        ends_ref[...] = packs_in[...]
        for g in range(groups):
            for s in range(2):
                code_copy(s, g).wait()
            for s in range(2):
                at = pl.ds(g * group, group)
                received = code_in[s, g].astype(jnp.int32).astype(F32)
                flux_ref[s, at, :] += received * (1.0 / FLUX_SCALE)


def halos(normals, planes, flags, courant):
    rows, layers, cells = planes.shape
    span, groups = 32, 4
    half = rows // span

    def later(i):
        return jnp.maximum(i - half, 0)

    whole = pl.BlockSpec((span, layers, cells), lambda i: (later(i), 0, 0))
    in_specs = [
        pl.BlockSpec((1, span, layers, cells), lambda i: (1, jnp.minimum(i, half - 1), 0, 0)),
        pl.BlockSpec((3, span, layers, cells), lambda i: (0, later(i), 0, 0)),
        whole,
        whole,
    ]
    for row in (0, rows - 1):
        one = pl.BlockSpec((1, layers, cells), lambda i, row=row: (row, 0, 0))
        in_specs += [
            pl.BlockSpec((3, 1, layers, cells), lambda i, row=row: (0, row, 0, 0)),
            one,
            one,
            pl.BlockSpec((1, 1, layers, cells), lambda i, row=row: (0, row, 0, 0)),
        ]
    pair = pl.BlockSpec((2, rows, cells), lambda i: (0, 0, 0))
    ends = (2, 5, layers, cells)
    split_shape = (2, groups, rows // groups, cells)
    dma = pltpu.SemaphoreType.DMA
    return pl.pallas_call(
        halo_kernel,
        grid=(2 * half,),
        in_specs=in_specs,
        out_specs=[pair, pair, pl.BlockSpec(ends, lambda i: (0, 0, 0, 0))],
        out_shape=[
            jax.ShapeDtypeStruct((2, rows, cells), F32),
            jax.ShapeDtypeStruct((2, rows, cells), F32),
            jax.ShapeDtypeStruct(ends, BF16),
        ],
        scratch_shapes=[
            pltpu.VMEM((cells // 128, span * layers, 128), F32),
            pltpu.VMEM(split_shape, BF16),
            pltpu.VMEM(split_shape, BF16),
            pltpu.VMEM((2, 4, rows, cells), F32),
            pltpu.VMEM(split_shape, jnp.int16),
            pltpu.VMEM(split_shape, jnp.int16),
            pltpu.VMEM(ends, BF16),
            pltpu.VMEM(ends, BF16),
            dma((2,)),
            dma((2,)),
            dma((2, groups)),
            dma((2, groups)),
            dma((2, groups)),
            dma((2, groups)),
        ],
        compiler_params=pltpu.CompilerParams(
            collective_id=0, has_side_effects=True, vmem_limit_bytes=60 * 2**20
        ),
        name="halos",
    )(courant, normals, planes, flags, *(normals, planes, flags, courant) * 2)


def exponent_of(most):
    return jnp.clip(jnp.ceil(jnp.log2(jnp.maximum(most, 1e-29)) * 256.0) + 1.0, -25000.0, 30000.0)


def to_codes(values):
    return jnp.round(values).astype(jnp.int32).astype(jnp.int16)


def chunk_kernel(
    around,
    chunk_index,
    chunks,
    fraction_ref,
    normals_ref,
    planes_ref,
    flags_ref,
    courant_ref,
    next_normals_ref,
    next_planes_ref,
    next_flags_ref,
    next_courant_ref,
    last_normals_ref,
    last_planes_ref,
    last_flags_ref,
    last_courant_ref,
    ends_ref,
    axial_flux_ref,
    axial_speed_ref,
    basis_ref,
    *rest,
):
    if chunk_index:
        rest = rest[1:]
    updated_ref, sent_ref, parts, kept, source, wide, scales = rest
    block, layers, cells = fraction_ref.shape
    steps = pl.num_programs(0)
    step = pl.program_id(0)
    chunk = source.shape[1] // layers
    lane_tiles = cells // 128
    backwards = lax.rem(lax.axis_index("azim"), around // 2) >= around // 4

    def put_field(slot, k, value):
        at = pl.ds(pl.multiple_of(slot * layers, layers), layers)
        for tile in range(lane_tiles):
            parts[k, tile, at, :] = value[:, tile * 128 : (tile + 1) * 128]

    def get_field(slot, k, shift=0):
        at = pl.ds(slot * layers + shift, layers)
        return jnp.concatenate([parts[k, tile, at, :] for tile in range(lane_tiles)], axis=1)

    def put_parts(slot, normals, plane, speed):
        inverse = inverse_of(*normals)
        for k, value in enumerate((*normals, plane, inverse, -inverse, 0.5 * speed)):
            put_field(slot, k, value)

    def put_packed(slot, side):
        values = [ends_ref[side, k].astype(F32) for k in range(5)]
        put_parts(slot, values[:3], values[3], values[4])

    def own_parts(row, _):
        put_parts(
            row,
            [normals_ref[k, row].astype(F32) for k in range(3)],
            plane_value(planes_ref[row], flags_ref[row]),
            courant_ref[0, row].astype(F32),
        )
        put_field(row, 7, 0.5 * courant_ref[1, row].astype(F32))
        return 0

    lax.fori_loop(0, block, own_parts, 0, unroll=2)

    def put_row(slot, normals, planes, flags, courant):
        put_parts(
            slot,
            [normals[k, 0].astype(F32) for k in range(3)],
            plane_value(planes[0], flags[0]),
            courant[0, 0].astype(F32),
        )

    def put_next():
        put_row(block, next_normals_ref, next_planes_ref, next_flags_ref, next_courant_ref)

    if chunk_index < chunks - 1:
        put_next()
    else:
        pl.when(step < steps - 1)(put_next)

        @pl.when(step == steps - 1)
        def _():
            put_packed(block, 1)

    def read_parts(slot):
        return [get_field(slot, k) for k in range(6)]

    @pl.when(step == 0)
    def _():
        if chunk_index == 0:
            put_packed(block + 1, 0)
        else:
            put_row(
                block + 1, last_normals_ref, last_planes_ref, last_flags_ref, last_courant_ref
            )
        speed = get_field(block + 1, 6) + get_field(0, 6)
        kept[0] = upwind_flux(0, read_parts(block + 1), read_parts(0), speed)
        kept[1] = speed

    index = lax.broadcasted_iota(jnp.int32, (1, cells), 1)
    place = index.astype(F32)
    radius = 1.0 + (place + 0.5) / cells
    next_radius = 1.0 + (place + 1.5) / cells
    face_radius = 1.0 + (place + 1.0) / cells
    inverse_radius = 1.0 / radius
    inner = lax.broadcasted_iota(jnp.int32, (layers, cells), 1) < cells - 1
    layer = lax.broadcasted_iota(jnp.int32, (layers, cells), 0)
    last_layer = layer == layers - 1
    first_layer = layer == 0

    def one_row(row, _):
        own = read_parts(row)
        speed = get_field(row, 6) + get_field(row + 1, 6)
        flux = upwind_flux(0, own, read_parts(row + 1), speed)
        gained = flux - kept[0]
        divergence = speed - kept[1]
        kept[0] = flux
        kept[1] = speed

        above = [None if k == 4 else get_field(row, k, 1) for k in range(6)]
        speed = get_field(row, 7) + get_field(row, 7, 1)
        flux = upwind_flux(1, own, above, speed)
        flux = jnp.where(last_layer, axial_flux_ref[1, pl.ds(row, 1), :], flux)
        speed = jnp.where(last_layer, axial_speed_ref[1, pl.ds(row, 1), :], speed)
        gained = gained + (
            flux - jnp.where(first_layer, axial_flux_ref[0, pl.ds(row, 1), :], pltpu.roll(flux, 1, 0))
        )
        divergence = divergence + (
            speed - jnp.where(first_layer, axial_speed_ref[0, pl.ds(row, 1), :], pltpu.roll(speed, 1, 0))
        )

        half = 0.5 * courant_ref[2, row].astype(F32)
        outer = [None if k == 4 else pltpu.roll(field, cells - 1, 1) for k, field in enumerate(own)]
        speed = jnp.where(inner, half + pltpu.roll(half, cells - 1, 1), 0.0)
        flux = upwind_flux(2, own, outer, speed, radius, next_radius)
        gained = gained + (flux - pltpu.roll(flux, 1, 1)) * inverse_radius
        carried = face_radius * speed
        divergence = divergence + (carried - pltpu.roll(carried, 1, 1)) * inverse_radius
        updated = fraction_ref[row] - gained
        updated_ref[row] = updated
        result = divergence + BUOYANCY * updated
        at = step * block + row
        at = jnp.where(backwards, chunk - 1 - at, at)
        for tile in range(lane_tiles):
            source[tile, pl.ds(at, layers, stride=chunk), :] = result[
                :, tile * 128 : (tile + 1) * 128
            ]
        return 0

    lax.fori_loop(0, block, one_row, 0, unroll=2)

    @pl.when(step == steps - 1)
    def _():
        modes = basis_ref.shape[1]
        scales[...] = jnp.zeros_like(scales)

        def radial(z, _):
            at = pl.ds(pl.multiple_of(z * 2 * chunk, 2 * chunk), 2 * chunk)
            rows = jnp.concatenate([source[tile, at, :] for tile in range(lane_tiles)], axis=1)
            both = dot3((basis_ref[0], basis_ref[1]), split(rows), ((1,), (1,)))
            for half in range(2):
                got = both[:, half * chunk : (half + 1) * chunk]
                scales[...] = jnp.maximum(scales[...], jnp.abs(got))
                wide[pl.ds(z * 2 + half, modes, stride=layers), :] = got
            return 0

        lax.fori_loop(0, layers // 2, radial, 0)
        devices, slots, height, lanes = sent_ref.shape
        share = modes // devices
        most = scales[...].reshape(devices, share // height, height, lanes)
        exponent = exponent_of(jnp.max(most, axis=1))
        sent_ref[:, slots - 1] = exponent.astype(jnp.int32).astype(jnp.int16)
        factor = CODE_TOP / jnp.exp2(exponent * (1.0 / 256.0))
        scales[pl.ds(0, devices * height), :] = factor.reshape(devices * height, lanes)

        def coding(device, _):
            for mode in range(share):
                factor = scales[pl.ds(device * height + mode % height, 1), :]
                for part in range(layers // height):
                    at = (device * share + mode) * layers + part * height
                    values = wide[pl.ds(pl.multiple_of(at, height), height), :]
                    sent_ref[device, mode * (layers // height) + part] = to_codes(values * factor)
            return 0

        lax.fori_loop(0, devices, coding, 0)


def advect_chunk(arrays, ends, axial_flux, axial_speed, basis, chunk_index, chunk, around, devices, base):
    fraction, normals, planes, flags, courant = arrays
    rows, layers, cells = fraction.shape
    block = BLOCK
    steps = chunk // block
    first = chunk_index * steps
    share = cells // devices

    def here(i):
        return first + i

    def after(i):
        return jnp.minimum((first + i + 1) * block, rows - 1)

    whole = pl.BlockSpec((block, layers, cells), lambda i: (here(i), 0, 0))
    triple = pl.BlockSpec((3, block, layers, cells), lambda i: (0, here(i), 0, 0))
    row = pl.BlockSpec((1, layers, cells), lambda i: (after(i), 0, 0))
    before = max(first * block - 1, 0)
    last_row = pl.BlockSpec((1, layers, cells), lambda i: (before, 0, 0))
    edge = pl.BlockSpec((2, block, cells), lambda i: (0, here(i), 0))
    in_specs = [
        whole,
        triple,
        whole,
        whole,
        triple,
        pl.BlockSpec((3, 1, layers, cells), lambda i: (0, after(i), 0, 0)),
        row,
        row,
        pl.BlockSpec((1, 1, layers, cells), lambda i: (0, after(i), 0, 0)),
        pl.BlockSpec((3, 1, layers, cells), lambda i: (0, before, 0, 0)),
        last_row,
        last_row,
        pl.BlockSpec((1, 1, layers, cells), lambda i: (0, before, 0, 0)),
        pl.BlockSpec(ends.shape, lambda i: (0, 0, 0, 0)),
        edge,
        edge,
        pl.BlockSpec((2, cells, cells), lambda i: (0, 0, 0)),
    ]
    operands = [
        fraction, normals, planes, flags, courant,
        normals, planes, flags, courant,
        normals, planes, flags, courant,
        ends, axial_flux, axial_speed, basis,
    ]
    aliases = {}
    if base is not None:
        in_specs.append(pl.BlockSpec(memory_space=pl.ANY))
        operands.append(base)
        aliases = {len(operands) - 1: 0}
    return pl.pallas_call(
        functools.partial(chunk_kernel, around, chunk_index, rows // chunk),
        grid=(steps,),
        in_specs=in_specs,
        out_specs=[
            whole,
            pl.BlockSpec((devices, 2 * share + 1, layers // 2, chunk), lambda i: (0, 0, 0, 0)),
        ],
        out_shape=[
            jax.ShapeDtypeStruct(fraction.shape, F32),
            jax.ShapeDtypeStruct((devices, 2 * share + 1, layers // 2, chunk), jnp.int16),
        ],
        scratch_shapes=[
            pltpu.VMEM((8, cells // 128, (block + 2) * layers, 128), F32),
            pltpu.VMEM((2, layers, cells), F32),
            pltpu.VMEM((cells // 128, layers * chunk, 128), F32),
            pltpu.VMEM((cells * layers, chunk), F32),
            pltpu.VMEM((cells, chunk), F32),
        ],
        input_output_aliases=aliases,
        compiler_params=pltpu.CompilerParams(vmem_limit_bytes=60 * 2**20),
        cost_estimate=pl.CostEstimate(
            flops=40000 * chunk * layers * cells, bytes_accessed=30 * chunk * layers * cells, transcendentals=0
        ),
        name="advect_chunk",
    )(*operands)


@functools.lru_cache(None)
def folded_tables(total):
    quarter = total // 4
    place = np.arange(quarter) + 0.5

    def halves(x):
        high = x.astype(jnp.bfloat16)
        return np.stack([high, (x - high.astype(np.float64)).astype(jnp.bfloat16)])

    tables, rates, weights = [], [], []
    for waves, wave in (
        (2 * np.arange(quarter), np.cos),
        (2 * np.arange(quarter) + 2, np.sin),
        (2 * np.arange(quarter) + 1, np.cos),
        (2 * np.arange(quarter) + 1, np.sin),
    ):
        doubled = waves[:, None] * (2 * np.arange(quarter) + 1)[None, :] % (2 * total)
        tables.append(wave(np.pi * doubled / total))
        rates.append(2.0 - 2.0 * np.cos(2.0 * np.pi * waves / total))
        weights.append(np.where((waves == 0) | (waves == total // 2), 1.0, 2.0) / total)
    tables = np.stack(tables)
    back = np.stack([halves(t) for t in tables])
    forth = np.stack([halves(t.T) for t in tables])
    return np.stack([forth, back]), np.stack(rates)[:, None].astype(np.float32), np.stack(weights)[:, None].astype(np.float32)


def decoded(values):
    return values.astype(jnp.int32).astype(F32)


def scale_of(codes):
    return jnp.exp2(decoded(codes) * (1.0 / 256.0)) * (1.0 / CODE_TOP)


def solve_kernel(around, along, chunks, start, *refs):
    got = refs[:chunks]
    mix, unmix, tables, rates, weights, shifts = refs[chunks : chunks + 6]
    sent, high, low, result, scale, exponents, forth, back, arrived = refs[chunks + 6 :]
    copies = [
        pltpu.make_async_copy(tables.at[0], forth, arrived.at[0]),
        pltpu.make_async_copy(tables.at[1], back, arrived.at[1]),
    ]
    for copy in copies:
        copy.start()
    devices, slots, height, lanes = got[0].shape
    count, layers = (sent.shape[1] - 1) // (2 * chunks), 2 * height
    share = (sent.shape[1] - 1) // (2 * chunks)
    together = chunks * share // height
    pairs = around // 4
    for chunk in range(chunks):
        scale[chunk] = scale_of(got[chunk][:, slots - 1])
    def spots():
        for pair in range(pairs):
            for chunk in range(chunks):
                mirror = chunks - 1 - chunk
                at = pl.ds((pair * chunks + chunk) * lanes, lanes)
                yield at, (
                    (pair, chunk),
                    (pair + 2 * pairs, chunk),
                    (2 * pairs - 1 - pair, mirror),
                    (4 * pairs - 1 - pair, mirror),
                )

    def fold(index, _):
        mode, axial = index // along, index % along
        rows = pl.ds(pl.multiple_of(index * layers, layers), layers)
        row = pl.ds(lax.rem(start + mode, height), 1)
        for at, places in spots():
            u0, u1, r0, r1 = [
                jnp.concatenate(
                    [
                        decoded(got[chunk][azim * along + axial, 2 * (start + mode) + part])
                        * scale[chunk, azim * along + axial, row, :]
                        for part in range(2)
                    ]
                )
                for azim, chunk in places
            ]
            e0, o0, e1, o1 = u0 + u1, u0 - u1, r0 + r1, r0 - r1
            for k, folded in enumerate((e0 + e1, e0 - e1, o0 - o1, o0 + o1)):
                high[k, rows, at], low[k, rows, at] = split(folded)
        return 0

    lax.fori_loop(0, count * along, fold, 0)

    copies[0].wait()
    deep = mix.shape[1]
    parts = [pl.ds(at, deep) for at in range(0, high.shape[1], deep)]

    def waves(k, _):
        for at in parts:
            high[k, at], low[k, at] = split(
                dot3((mix[0], mix[1]), (high[k, at], low[k, at]))
            )
        spectrum = dot3((high[k], low[k]), (forth[k, 0], forth[k, 1]))
        high[k], low[k] = split(spectrum * weights[k] / (rates[k] + shifts[...]))
        pl.when(k == 0)(copies[1].wait)
        high[k], low[k] = split(dot3((high[k], low[k]), (back[k, 0], back[k, 1])))
        for at in parts:
            result[k, at] = dot3((unmix[0], unmix[1]), (high[k, at], low[k, at]))
        return 0

    lax.fori_loop(0, 4, waves, 0)

    apart = count // together

    def unfold(index, _):
        mode, axial = index // along, index % along
        for at, places in spots():
            found = []
            for part in range(together):
                row = ((mode + part * apart) * along + axial) * layers
                rows = pl.ds(pl.multiple_of(row, layers), layers)
                ec, es, oc, os = [result[k, rows, at] for k in range(4)]
                e0, e1, o0, o1 = ec + es, ec - es, oc + os, os - oc
                found.append((e0 + o0, e0 - o0, e1 + o1, e1 - o1))
            for (azim, chunk), values in zip(places, zip(*found)):
                device = azim * along + axial
                most = functools.reduce(jnp.maximum, [jnp.abs(x) for x in values])
                exponent = exponent_of(jnp.max(most, axis=0, keepdims=True))
                exponents[device, pl.ds(chunk * apart + mode, 1), :] = exponent
                factor = CODE_TOP / jnp.exp2(exponent * (1.0 / 256.0))
                for part, value in enumerate(values):
                    slot = 2 * (chunk * share + mode + part * apart)
                    for half in range(2):
                        piece = value[half * height : (half + 1) * height]
                        sent[device, slot + half] = to_codes(piece * factor)
        return 0

    lax.fori_loop(0, apart * along, unfold, 0)

    sent[:, 2 * chunks * share] = exponents[...].astype(jnp.int32).astype(jnp.int16)


def solve_group(got, mix, unmix, tables, shifts, start, share, around, along):
    chunks = len(got)
    devices, slots, height, lanes = got[0].shape
    rows = share * along * 2 * height
    tables, rates, weights = tables
    width = tables.shape[-1]
    whole = pl.BlockSpec(memory_space=pltpu.VMEM)

    def fixed(array):
        return pl.BlockSpec(
            array.shape, lambda i: (0,) * len(array.shape), pipeline_mode=pl.Buffered(1)
        )

    shifts = lax.slice_in_dim(shifts, start * along * 2 * height, start * along * 2 * height + rows)
    return pl.pallas_call(
        functools.partial(solve_kernel, around, along, chunks, start),
        grid=(1,),
        in_specs=[whole] * chunks
        + [fixed(mix), fixed(unmix)]
        + [pl.BlockSpec(memory_space=pl.ANY)]
        + [fixed(rates), fixed(weights), fixed(shifts)],
        out_specs=fixed(jax.ShapeDtypeStruct((devices, 2 * chunks * share + 1, height, lanes), jnp.int16)),
        out_shape=jax.ShapeDtypeStruct((devices, 2 * chunks * share + 1, height, lanes), jnp.int16),
        scratch_shapes=[
            pltpu.VMEM((4, rows, width), BF16),
            pltpu.VMEM((4, rows, width), BF16),
            pltpu.VMEM((4, rows, width), F32),
            pltpu.VMEM((chunks, devices, height, lanes), F32),
            pltpu.VMEM((devices, height, lanes), F32),
            pltpu.VMEM(tables.shape[1:], BF16),
            pltpu.VMEM(tables.shape[1:], BF16),
            pltpu.SemaphoreType.DMA((2,)),
        ],
        compiler_params=pltpu.CompilerParams(vmem_limit_bytes=SOLVE_VMEM * 2**20),
        cost_estimate=pl.CostEstimate(
            flops=60 * rows * width * width, bytes_accessed=20 * 2**20, transcendentals=0
        ),
        name="solve_group",
    )(*got, mix, unmix, tables, rates, weights, shifts)


def pressure_kernel(around, groups, chunks, *refs):
    got = refs[:groups]
    basis = refs[groups]
    base = refs[groups + 1 : -4]
    out, flat, turned, scale = refs[-4:]
    devices, _, height, lanes = got[0].shape
    layers = 2 * height
    chunk = pl.program_id(0)
    backwards = lax.rem(lax.axis_index("azim"), around // 2) >= around // 4
    i = lax.broadcasted_iota(jnp.int32, (lanes, lanes), 0)
    j = lax.broadcasted_iota(jnp.int32, (lanes, lanes), 1)
    turned_place = jnp.where(backwards, lanes - 1, 0) + jnp.where(backwards, -1, 1) * i
    turn = jnp.where(j == turned_place, 1.0, 0.0).astype(BF16)
    spans, filled = [], 0
    for group in range(groups):
        share = (got[group].shape[1] - 1) // (2 * chunks)
        apart = height // chunks
        spans.append((filled, devices * share))
        scale[group] = scale_of(got[group][:, 2 * chunks * share])

        def unpack(device, _, group=group, share=share, filled=filled):
            for mode in range(share):
                factor = scale[group, device, pl.ds(chunk * apart + mode % apart, 1), :]
                for part in range(2):
                    at = (filled + device * share + mode) * layers + part * height
                    flat[pl.ds(pl.multiple_of(at, height), height), :] = (
                        decoded(got[group][device, 2 * (chunk * share + mode) + part]) * factor
                    )
            return 0

        lax.fori_loop(0, devices, unpack, 0)
        filled += devices * share

    def turning(z, _):
        for offset, height in spans:
            high, low = split(flat[pl.ds(offset * layers + z, height, stride=layers), :])
            rows = dot(turn, high, ((1,), (1,))) + dot(turn, low, ((1,), (1,)))
            for at in range(0, height, 128):
                turned[(offset + at) // 128, pl.ds(z, lanes, stride=layers), :] = rows[
                    :, at : at + 128
                ]
        return 0

    lax.fori_loop(0, layers, turning, 0, unroll=4)
    azimuths = 32
    height = azimuths * layers

    def radial(batch, _):
        at = pl.ds(pl.multiple_of(batch * height, height), height)
        rows = jnp.concatenate([turned[tile, at, :] for tile in range(filled // 128)], axis=1)
        high, low = split(rows)
        if filled > 128:
            total = dot3((high, low), (basis[0], basis[1]))
        else:
            rows = jnp.concatenate([high, low, high], axis=1)
            total = dot(rows, jnp.concatenate([basis[0], basis[0], basis[1]]), ((1,), (0,)))
        total = total.reshape(azimuths, layers, out.shape[2])
        at = pl.ds(pl.multiple_of(batch * azimuths, azimuths), azimuths)
        out[at] = total + base[0][at] if base else total
        return 0

    lax.fori_loop(0, lanes // azimuths, radial, 0)


def pressure_of(got, basis, around, chunks, base=None):
    groups = len(got)
    devices, _, height, lanes = got[0].shape
    layers = 2 * height
    inner, cells = basis.shape[1:]
    whole = pl.BlockSpec((lanes, layers, cells), lambda i: (i, 0, 0))
    return pl.pallas_call(
        functools.partial(pressure_kernel, around, groups, chunks),
        grid=(chunks,),
        in_specs=[pl.BlockSpec(memory_space=pltpu.VMEM)] * (groups + 1)
        + ([] if base is None else [whole]),
        out_specs=whole,
        out_shape=jax.ShapeDtypeStruct((lanes * chunks, layers, cells), F32),
        scratch_shapes=[
            pltpu.VMEM((inner * layers, lanes), F32),
            pltpu.VMEM((inner // 128, lanes * layers, 128), F32),
            pltpu.VMEM((groups, devices, height, lanes), F32),
        ],
        compiler_params=pltpu.CompilerParams(vmem_limit_bytes=PRESSURE_VMEM * 2**20),
        cost_estimate=pl.CostEstimate(
            flops=20 * lanes * chunks * layers * cells * inner,
            bytes_accessed=20 * 2**20,
            transcendentals=0,
        ),
        name="pressure_of",
    )(*got, basis, *([] if base is None else [base]))


def halves(values):
    high = lax.reduce_precision(values, 8, 7)
    return jnp.stack([high.astype(BF16), (values - high).astype(BF16)])


def exchanged(sent):
    return lax.all_to_all(sent, ("azim", "axial"), split_axis=0, concat_axis=0, tiled=True)


def following_kernel(values_ref, earlier_ref, out_ref):
    del values_ref, earlier_ref, out_ref


def following(values, earlier):
    anywhere = pl.BlockSpec(memory_space=pl.ANY)
    return pl.pallas_call(
        following_kernel,
        in_specs=[anywhere, pl.BlockSpec(memory_space=pltpu.VMEM)],
        out_specs=anywhere,
        out_shape=jax.ShapeDtypeStruct(values.shape, values.dtype),
        input_output_aliases={0: 0},
        name="following",
    )(values, earlier)


def overlapped(
    fraction,
    normals,
    planes,
    cell_flags,
    courant,
    radial_basis,
    axial_basis,
    radial_rates,
    axial_rates,
):
    rows, layers, cells = fraction.shape
    around, along = lax.axis_size("azim"), lax.axis_size("axial")
    devices = around * along
    modes = cells // devices
    chunks = rows // CHUNK
    axial_flux, axial_speed, ends = halos(normals, planes, cell_flags, courant)
    forward_basis = halves(radial_basis.T)
    arrays = (fraction, normals, planes, cell_flags, courant)
    updated, got = None, []
    for chunk in range(chunks):
        updated, sent = advect_chunk(
            arrays, ends, axial_flux, axial_speed, forward_basis, chunk, CHUNK, around, devices, updated
        )
        got.append(exchanged(following(sent, got[-1]) if got else sent))
    count = jnp.eye(4, dtype=F32)
    mix, unmix = halves(jnp.kron(count, axial_basis.T)), halves(jnp.kron(count, axial_basis))
    first = (lax.axis_index("azim") * along + lax.axis_index("axial")) * modes
    shifts = lax.dynamic_slice_in_dim(radial_rates, first, modes)[:, None] + axial_rates[None, :]
    shifts = shifts.reshape(modes * along * layers, 1)
    tables = [jnp.asarray(x) for x in folded_tables(rows * around)]
    returned, bases = [], []
    for start, share in SOLVED:
        sent = solve_group(got, mix, unmix, tables, shifts, start, share, around, along)
        returned.append(exchanged(sent))
        rows_of = radial_basis.T.reshape(devices, modes, cells)[:, start : start + share]
        bases.append(rows_of.reshape(devices * share, cells))
    pressure = pressure_of(returned[:-1], halves(jnp.concatenate(bases[:-1])), around, chunks)
    pressure = pressure_of(returned[-1:], halves(bases[-1]), around, chunks, pressure)
    return (updated, pressure)


def fits(fraction):
    rows, layers, cells = fraction.shape
    around, along = lax.axis_size("azim"), lax.axis_size("axial")
    modes = cells // (around * along)
    chunks = rows // CHUNK
    return (
        rows % CHUNK == 0
        and layers == 16
        and modes == 16
        and modes // 2 * chunks == layers
        and cells % 128 == 0
        and around % 4 == 0
        and along > 2
    )


def local(*arguments):
    return overlapped(*arguments) if fits(arguments[0]) else stepwise(*arguments)


def solution(mesh):
    placed = (
        P("azim", "axial", None),
        P(None, "azim", "axial", None),
        P("azim", "axial", None),
        P("azim", "axial", None),
        P(None, "azim", "axial", None),
        P(),
        P(),
        P(),
        P(),
    )
    return jax.shard_map(
        local,
        mesh=mesh,
        in_specs=placed,
        out_specs=(P("azim", "axial", None), P("azim", "axial", None)),
        check_vma=False,
    )
```

```python
import functools

import jax
import jax.numpy as jnp
import numpy as np
from jax import lax
from jax.experimental import pallas as pl
from jax.experimental.pallas import tpu as pltpu
from jax.sharding import PartitionSpec as P

HIGH = lax.Precision.HIGH
BUOYANCY = 0.5
CODE_TOP = 32700.0


def shifted_in(edge, axis, towards_lower):
    count = lax.axis_size(axis)
    if towards_lower:
        pairs = [((i + 1) % count, i) for i in range(count)]
    else:
        pairs = [(i, (i + 1) % count) for i in range(count)]
    return lax.ppermute(edge, axis, pairs)


def cell_parts(n0, n1, n2, code):
    m0, m1, m2 = jnp.abs(n0), jnp.abs(n1), jnp.abs(n2)
    return (n0, n1, n2, code, 1.0 / (6.0 * m0 * m1 * m2))


def cube(height):
    held = jnp.maximum(height, 0.0)
    return held * held * held


def face_flux(direction, lower, upper, speed, lower_weight=None, upper_weight=None):
    forward = speed > 0.0
    signed = jnp.where(forward, lower[direction], -upper[direction])
    first, second = [d for d in range(3) if d != direction]
    along = jnp.abs(signed)
    side_a = jnp.abs(jnp.where(forward, lower[first], upper[first]))
    side_b = jnp.abs(jnp.where(forward, lower[second], upper[second]))
    code = jnp.where(forward, lower[3], upper[3])
    inverse = jnp.where(forward, lower[4], upper[4])
    width = jnp.abs(speed)
    near = code - along * jnp.where(signed < 0.0, 0.0, 1.0 - width)
    far = near - along * width
    sides = side_a + side_b
    total = (cube(near) - cube(near - side_a)) - (cube(near - side_b) - cube(near - sides))
    total = total - ((cube(far) - cube(far - side_a)) - (cube(far - side_b) - cube(far - sides)))
    volume = jnp.where(code > 3.0, width, jnp.where(code < -0.5, 0.0, total * inverse))
    if lower_weight is not None:
        volume = volume * jnp.where(forward, lower_weight, upper_weight)
    return jnp.where(forward, volume, jnp.where(speed < 0.0, -volume, 0.0))


def advect_kernel(
    fraction_ref,
    normals_ref,
    planes_ref,
    flags_ref,
    courant_ref,
    next_ref,
    high_ref,
    low_azim_ref,
    low_axial_ref,
    updated_ref,
    source_ref,
    kept,
):
    rows, layers, cells = fraction_ref.shape
    f32 = jnp.float32

    @pl.when(pl.program_id(0) == 0)
    def _():
        kept[...] = low_azim_ref[...]

    index = lax.broadcasted_iota(jnp.int32, (1, cells), 1)
    place = index.astype(f32)
    radius = 1.0 + (place + 0.5) / cells
    next_radius = 1.0 + (place + 1.5) / cells
    face_radius = 1.0 + (place + 1.0) / cells
    inverse_radius = 1.0 / radius
    inner = lax.broadcasted_iota(jnp.int32, (layers, cells), 1) < cells - 1
    layer = lax.broadcasted_iota(jnp.int32, (layers, cells), 0)
    last_layer = layer == layers - 1
    first_layer = layer == 0

    def row_parts(row):
        flags = flags_ref[row]
        code = jnp.where(
            flags == 2, planes_ref[row].astype(f32), jnp.where(flags == 1, 4.0, -1.0)
        )
        return cell_parts(
            normals_ref[0, row].astype(f32),
            normals_ref[1, row].astype(f32),
            normals_ref[2, row].astype(f32),
            code,
        )

    def one_row(row, upper, upper_speed):
        own = row_parts(row)
        moved = [courant_ref[d, row].astype(f32) for d in range(3)]
        speed = 0.5 * (moved[0] + upper_speed)
        flux = face_flux(0, own, upper, speed)
        gained = flux - kept[0]
        divergence = speed - kept[1]
        kept[0] = flux
        kept[1] = speed
        beyond = cell_parts(*[high_ref[k, row] for k in range(4)])
        above = [
            jnp.where(last_layer, high, pltpu.roll(field, layers - 1, 0))
            for field, high in zip(own, beyond)
        ]
        speed = 0.5 * (
            moved[1]
            + jnp.where(last_layer, high_ref[4, row], pltpu.roll(moved[1], layers - 1, 0))
        )
        flux = face_flux(1, own, above, speed)
        gained = gained + (
            flux - jnp.where(first_layer, low_axial_ref[0, row], pltpu.roll(flux, 1, 0))
        )
        divergence = divergence + (
            speed - jnp.where(first_layer, low_axial_ref[1, row], pltpu.roll(speed, 1, 0))
        )
        outer = [pltpu.roll(field, cells - 1, 1) for field in own]
        speed = 0.5 * (moved[2] + pltpu.roll(moved[2], cells - 1, 1))
        speed = jnp.where(inner, speed, 0.0)
        flux = face_flux(2, own, outer, speed, radius, next_radius)
        gained = gained + (flux - pltpu.roll(flux, 1, 1)) * inverse_radius
        carried = face_radius * speed
        divergence = divergence + (carried - pltpu.roll(carried, 1, 1)) * inverse_radius
        updated = fraction_ref[row] - gained
        updated_ref[row] = updated
        source_ref[row] = divergence + BUOYANCY * updated

    def step(row, _):
        one_row(row, row_parts(row + 1), courant_ref[0, row + 1].astype(f32))
        return 0

    lax.fori_loop(0, rows - 1, step, 0)
    one_row(
        rows - 1,
        cell_parts(*[next_ref[k, 0].astype(f32) for k in range(4)]),
        next_ref[4, 0].astype(f32),
    )


def plane_codes(planes, flags):
    return jnp.where(
        flags == 2, planes.astype(jnp.float32), jnp.where(flags == 1, 4.0, -1.0)
    ).astype(jnp.bfloat16)


def packed_edge(normals, planes, flags, courant, direction, pick):
    parts = [pick(normals[d]) for d in range(3)]
    parts.append(plane_codes(pick(planes), pick(flags)))
    parts.append(pick(courant[direction]))
    return jnp.stack(parts)


def low_face(direction, lower, upper):
    lower, upper = lower.astype(jnp.float32), upper.astype(jnp.float32)
    speed = 0.5 * (lower[4] + upper[4])
    flux = face_flux(direction, cell_parts(*lower[:4]), cell_parts(*upper[:4]), speed)
    return jnp.stack([flux, speed])


def advect(fraction, normals, planes, flags, courant):
    rows, layers, cells = fraction.shape
    block = 16 if rows % 16 == 0 else 1
    blocks = rows // block
    fields = (normals, planes, flags, courant)
    top_row = packed_edge(*fields, 0, lambda x: x[rows - 1])
    bottom_row = packed_edge(*fields, 0, lambda x: x[0])
    top_layer = packed_edge(*fields, 1, lambda x: x[:, layers - 1])
    bottom_layer = packed_edge(*fields, 1, lambda x: x[:, 0])
    high_row = shifted_in(bottom_row, "azim", True)
    low_row = shifted_in(top_row, "azim", False)
    high_layer = shifted_in(bottom_layer, "axial", True)
    low_layer = shifted_in(top_layer, "axial", False)
    low_azim = low_face(0, low_row, bottom_row)
    low_axial = low_face(1, low_layer, bottom_layer)[:, :, None]
    high_axial = high_layer.astype(jnp.float32)[:, :, None]
    inside = packed_edge(*fields, 0, lambda x: x[block::block])
    following = jnp.concatenate([inside, high_row[:, None]], axis=1)
    whole = pl.BlockSpec((block, layers, cells), lambda i: (i, 0, 0))
    triple = pl.BlockSpec((3, block, layers, cells), lambda i: (0, i, 0, 0))
    return pl.pallas_call(
        advect_kernel,
        grid=(blocks,),
        in_specs=[
            whole,
            triple,
            whole,
            whole,
            triple,
            pl.BlockSpec((5, 1, layers, cells), lambda i: (0, i, 0, 0)),
            pl.BlockSpec((5, block, 1, cells), lambda i: (0, i, 0, 0)),
            pl.BlockSpec((2, layers, cells), lambda i: (0, 0, 0)),
            pl.BlockSpec((2, block, 1, cells), lambda i: (0, i, 0, 0)),
        ],
        out_specs=[whole, whole],
        out_shape=[jax.ShapeDtypeStruct(fraction.shape, jnp.float32)] * 2,
        scratch_shapes=[pltpu.VMEM((2, layers, cells), jnp.float32)],
        compiler_params=pltpu.CompilerParams(vmem_limit_bytes=40 * 2**20),
    )(
        fraction,
        normals,
        planes,
        flags,
        courant,
        following,
        high_axial,
        low_azim,
        low_axial,
    )


def coded(values):
    most = jnp.max(jnp.abs(values), axis=-1)
    exponent = jnp.clip(jnp.ceil(jnp.log2(most) * 256.0) + 1.0, -30000.0, 30000.0)
    scale = CODE_TOP * jnp.exp2(exponent * (-1.0 / 256.0))
    codes = jnp.round(values * scale[..., None])
    return jnp.clip(codes, -32767.0, 32767.0).astype(jnp.int16), exponent.astype(jnp.int16)


def exchange(values):
    modes, cells = values.shape[1], values.shape[3]
    codes, exponent = coded(values)
    extra = jnp.pad(exponent.transpose(0, 2, 1), ((0, 0), (0, 0), (0, cells - modes)))
    sent = jnp.concatenate([codes, extra[:, None]], axis=1)
    got = lax.all_to_all(sent, ("azim", "axial"), split_axis=0, concat_axis=0, tiled=True)
    exponent = got[:, modes, :, :modes].transpose(0, 2, 1).astype(jnp.float32)
    scale = jnp.exp2(exponent * (1.0 / 256.0)) * (1.0 / CODE_TOP)
    return got[:, :modes].astype(jnp.float32) * scale[..., None]


@functools.lru_cache(None)
def azimuth_tables(total):
    half, quarter = total // 2, total // 4
    place = np.arange(half)

    def table(cosines, sines):
        waves = np.concatenate([cosines, sines])
        angles = 2.0 * np.pi / total * (waves[:, None] * place[None, :] % total)
        rows = np.concatenate(
            [np.cos(angles[: len(cosines)]), np.sin(angles[len(cosines) :])]
        ).astype(np.float32)
        rates = (2.0 - 2.0 * np.cos(2.0 * np.pi * waves / total)).astype(np.float32)
        ends = (waves == 0) | (waves == half)
        return rows, rates, (np.where(ends, 1.0, 2.0) / total).astype(np.float32)

    even = 2 * np.arange(quarter + 1)
    odd = 2 * np.arange(quarter) + 1
    return table(even, even[1:-1]), table(odd, odd)


def stepwise(
    fraction,
    normals,
    planes,
    cell_flags,
    courant,
    radial_basis,
    axial_basis,
    radial_rates,
    axial_rates,
):
    rows, layers, cells = fraction.shape
    around, along = lax.axis_size("azim"), lax.axis_size("axial")
    devices = around * along
    modes = cells // devices
    total = rows * around
    half = total // 2
    updated, source = advect(fraction, normals, planes, cell_flags, courant)
    radial_modes = jnp.einsum("azr,rj->jza", source, radial_basis, precision=HIGH)
    got = exchange(radial_modes.reshape(devices, modes, layers, rows))
    got = got.reshape(around, along, modes, layers, rows).transpose(2, 1, 3, 0, 4)
    got = got.reshape(modes, along * layers, total)
    both = jnp.einsum("jza,zn->jna", got, axial_basis, precision=HIGH)
    first = (lax.axis_index("azim") * along + lax.axis_index("axial")) * modes
    shifts = lax.dynamic_slice_in_dim(radial_rates, first, modes)[:, None] + axial_rates[None, :]
    low, high = both[..., :half], both[..., half:]
    solved = []
    for folded, (table, rates, weight) in zip((low + high, low - high), azimuth_tables(total)):
        coefficients = jnp.einsum("jna,ka->jnk", folded, table, precision=HIGH)
        scaled = coefficients / (rates + shifts[..., None]) * weight
        solved.append(jnp.einsum("jnk,ka->jna", scaled, table, precision=HIGH))
    physical = jnp.concatenate([solved[0] + solved[1], solved[0] - solved[1]], axis=-1)
    physical = jnp.einsum("jna,zn->jza", physical, axial_basis, precision=HIGH)
    physical = physical.reshape(modes, along, layers, around, rows).transpose(3, 1, 0, 2, 4)
    returned = exchange(physical.reshape(devices, modes, layers, rows))
    returned = returned.reshape(cells, layers, rows)
    pressure = jnp.einsum("jza,rj->azr", returned, radial_basis, precision=HIGH)
    return (updated, pressure)


CHUNK = 128
BLOCK = 16
SOLVE_VMEM = 62
PRESSURE_VMEM = 62
SOLVED = ((0, 4), (8, 8), (4, 4))
FLUX_SCALE = 32767.0 / 0.3
F32 = jnp.float32
BF16 = jnp.bfloat16


def split(values):
    high = values.astype(BF16)
    return high, (values - high.astype(F32)).astype(BF16)


def dot(a, b, contract):
    return lax.dot_general(a, b, (contract, ((), ())), preferred_element_type=F32)


def dot3(a, b, contract=((1,), (0,))):
    return dot(a[0], b[0], contract) + (dot(a[0], b[1], contract) + dot(a[1], b[0], contract))


def slab_flux(normal, side_a, side_b, plane, inverse, speed):
    along = jnp.abs(normal)
    reach = normal * speed
    slab = jnp.abs(reach)
    near = plane - jnp.where(reach > 0.0, along - slab, 0.0)
    other = (slab + (side_a + side_b)) - near
    folded = near > other
    held = jnp.maximum(jnp.minimum(near, other), 0.0)
    low, high = jnp.minimum(side_a, side_b), jnp.maximum(side_a, side_b)
    by_low = jnp.maximum(held - low, 0.0)
    by_slab = jnp.maximum(held - slab, 0.0)
    last = jnp.maximum(held - (low + slab), 0.0) - jnp.maximum(held - high, 0.0)
    total = held * held * held - by_slab * by_slab * by_slab
    total = total - (by_low * by_low * by_low - last * last * last)
    flux = total * inverse
    return jnp.where(folded, speed - flux, flux)


def upwind_flux(direction, lower, upper, speed, lower_weight=None, upper_weight=None):
    forward = speed > 0.0
    first, second = [d for d in range(3) if d != direction]
    normal = jnp.where(forward, lower[direction], upper[direction])
    side_a = jnp.abs(jnp.where(forward, lower[first], upper[first]))
    side_b = jnp.abs(jnp.where(forward, lower[second], upper[second]))
    plane = jnp.where(forward, lower[3], upper[3])
    inverse = jnp.where(forward, lower[4], upper[5])
    flux = slab_flux(normal, side_a, side_b, plane, inverse, speed)
    if lower_weight is not None:
        flux = flux * jnp.where(forward, lower_weight, upper_weight)
    return flux


def inverse_of(n0, n1, n2):
    return 1.0 / (6.0 * jnp.abs(n0 * n1 * n2))


def plane_value(planes, flags):
    return jnp.where(flags == 2, planes.astype(F32), jnp.where(flags == 1, 4.0, -4.0))


def halo_kernel(
    courant_ref,
    normals_ref,
    planes_ref,
    flags_ref,
    first_normals_ref,
    first_planes_ref,
    first_flags_ref,
    first_courant_ref,
    last_normals_ref,
    last_planes_ref,
    last_flags_ref,
    last_courant_ref,
    flux_ref,
    speed_ref,
    ends_ref,
    work,
    edge,
    edge_in,
    fields,
    code,
    code_in,
    packs,
    packs_in,
    row_send,
    row_recv,
    edge_send,
    edge_recv,
    code_send,
    code_recv,
):
    step = pl.program_id(0)
    half = pl.num_programs(0) // 2
    span, layers, cells = planes_ref.shape
    groups, group = code.shape[1:3]
    per_group = group // span
    tiles = cells // 128
    neighbours = []
    for axis in ("azim", "axial"):
        count, me = lax.axis_size(axis), lax.axis_index(axis)
        neighbours.append(
            ({axis: lax.rem(me + count - 1, count)}, {axis: lax.rem(me + 1, count)})
        )

    def remote(source, target, send, recv, device):
        return pltpu.make_async_remote_copy(
            src_ref=source,
            dst_ref=target,
            send_sem=send,
            recv_sem=recv,
            device_id=device,
            device_id_type=pl.DeviceIdType.MESH,
        )

    row_copies = [
        remote(packs.at[s], packs_in.at[1 - s], row_send.at[s], row_recv.at[1 - s], neighbours[0][s])
        for s in range(2)
    ]
    def edge_copy(s, g):
        return remote(
            edge.at[s, g],
            edge_in.at[1 - s, g],
            edge_send.at[s, g],
            edge_recv.at[1 - s, g],
            neighbours[1][s],
        )

    def code_copy(s, g):
        return remote(
            code.at[s, g],
            code_in.at[1 - s, g],
            code_send.at[s, g],
            code_recv.at[1 - s, g],
            neighbours[1][s],
        )

    @pl.when(step == 0)
    def _():
        barrier = pltpu.get_barrier_semaphore()
        for pair in neighbours:
            for device in pair:
                pl.semaphore_signal(
                    barrier, inc=1, device_id=device, device_id_type=pl.DeviceIdType.MESH
                )
        pl.semaphore_wait(barrier, 4)
        for s, (normals, planes, flags, courant) in enumerate(
            (
                (first_normals_ref, first_planes_ref, first_flags_ref, first_courant_ref),
                (last_normals_ref, last_planes_ref, last_flags_ref, last_courant_ref),
            )
        ):
            for k in range(3):
                packs[s, k] = normals[k, 0]
            packs[s, 3] = plane_value(planes[0], flags[0]).astype(BF16)
            packs[s, 4] = courant[0, 0]
        for copy in row_copies:
            copy.start()

    def layer_rows(tile, layer):
        return work[tile, pl.ds(layer, span, stride=layers), :]

    @pl.when(step < half)
    def _():
        place = step // per_group
        at = pl.ds(pl.multiple_of(lax.rem(step, per_group) * span, span), span)
        for tile in range(tiles):
            lanes = pl.ds(tile * 128, 128)
            work[tile] = courant_ref[0, :, :, lanes].astype(F32).reshape(span * layers, 128)
            for s, layer in ((0, 0), (1, layers - 1)):
                edge[s, place, at, lanes] = layer_rows(tile, layer).astype(BF16)

    for g in range(groups):

        @pl.when(step == (g + 1) * per_group - 1)
        def _(g=g):
            for s in range(2):
                edge_copy(s, g).start()

    @pl.when(step >= half)
    def _():
        at = pl.ds(pl.multiple_of((step - half) * span, span), span)
        for k in range(4):
            for tile in range(tiles):
                lanes = pl.ds(tile * 128, 128)
                if k < 3:
                    field = normals_ref[k, :, :, lanes].astype(F32)
                else:
                    field = plane_value(planes_ref[:, :, lanes], flags_ref[:, :, lanes])
                work[tile] = field.reshape(span * layers, 128)
                for s, layer in ((0, 0), (1, layers - 1)):
                    fields[s, k, at, lanes] = layer_rows(tile, layer)

    for g in range(groups):

        @pl.when(step == half + (g + 1) * per_group - 1)
        def _(g=g):
            for s in range(2):
                edge_copy(s, g).wait()
            for s in range(2):

                def donate(piece, _, s=s):
                    inside = pl.ds(pl.multiple_of(piece * 16, 16), 16)
                    at = pl.ds(pl.multiple_of(g * group + piece * 16, 16), 16)
                    normals = [fields[s, k, at, :] for k in range(3)]
                    own, beyond = edge[s, g, inside, :], edge_in[s, g, inside, :]
                    speed = 0.5 * (own.astype(F32) + beyond.astype(F32))
                    inverse = inverse_of(*normals)
                    flux = slab_flux(
                        normals[1],
                        jnp.abs(normals[0]),
                        jnp.abs(normals[2]),
                        fields[s, 3, at, :],
                        inverse if s == 1 else -inverse,
                        speed,
                    )
                    flux = jnp.where(speed > 0.0 if s == 1 else speed < 0.0, flux, 0.0)
                    flux_ref[s, at, :] = flux
                    speed_ref[s, at, :] = speed
                    code[s, g, inside, :] = to_codes(flux * FLUX_SCALE)
                    return 0

                lax.fori_loop(0, group // 16, donate, 0)
                code_copy(s, g).start()

    @pl.when(step == 2 * half - 1)
    def _():
        for copy in row_copies:
            copy.wait()
        ends_ref[...] = packs_in[...]
        for g in range(groups):
            for s in range(2):
                code_copy(s, g).wait()
            for s in range(2):
                at = pl.ds(g * group, group)
                received = code_in[s, g].astype(jnp.int32).astype(F32)
                flux_ref[s, at, :] += received * (1.0 / FLUX_SCALE)


def halos(normals, planes, flags, courant):
    rows, layers, cells = planes.shape
    span, groups = 32, 4
    half = rows // span

    def later(i):
        return jnp.maximum(i - half, 0)

    whole = pl.BlockSpec((span, layers, cells), lambda i: (later(i), 0, 0))
    in_specs = [
        pl.BlockSpec((1, span, layers, cells), lambda i: (1, jnp.minimum(i, half - 1), 0, 0)),
        pl.BlockSpec((3, span, layers, cells), lambda i: (0, later(i), 0, 0)),
        whole,
        whole,
    ]
    for row in (0, rows - 1):
        one = pl.BlockSpec((1, layers, cells), lambda i, row=row: (row, 0, 0))
        in_specs += [
            pl.BlockSpec((3, 1, layers, cells), lambda i, row=row: (0, row, 0, 0)),
            one,
            one,
            pl.BlockSpec((1, 1, layers, cells), lambda i, row=row: (0, row, 0, 0)),
        ]
    pair = pl.BlockSpec((2, rows, cells), lambda i: (0, 0, 0))
    ends = (2, 5, layers, cells)
    split_shape = (2, groups, rows // groups, cells)
    dma = pltpu.SemaphoreType.DMA
    return pl.pallas_call(
        halo_kernel,
        grid=(2 * half,),
        in_specs=in_specs,
        out_specs=[pair, pair, pl.BlockSpec(ends, lambda i: (0, 0, 0, 0))],
        out_shape=[
            jax.ShapeDtypeStruct((2, rows, cells), F32),
            jax.ShapeDtypeStruct((2, rows, cells), F32),
            jax.ShapeDtypeStruct(ends, BF16),
        ],
        scratch_shapes=[
            pltpu.VMEM((cells // 128, span * layers, 128), F32),
            pltpu.VMEM(split_shape, BF16),
            pltpu.VMEM(split_shape, BF16),
            pltpu.VMEM((2, 4, rows, cells), F32),
            pltpu.VMEM(split_shape, jnp.int16),
            pltpu.VMEM(split_shape, jnp.int16),
            pltpu.VMEM(ends, BF16),
            pltpu.VMEM(ends, BF16),
            dma((2,)),
            dma((2,)),
            dma((2, groups)),
            dma((2, groups)),
            dma((2, groups)),
            dma((2, groups)),
        ],
        compiler_params=pltpu.CompilerParams(
            collective_id=0, has_side_effects=True, vmem_limit_bytes=62 * 2**20
        ),
        name="halos",
    )(courant, normals, planes, flags, *(normals, planes, flags, courant) * 2)


def exponent_of(most):
    return jnp.clip(jnp.ceil(jnp.log2(jnp.maximum(most, 1e-29)) * 256.0) + 1.0, -25000.0, 30000.0)


def to_codes(values):
    return jnp.round(values).astype(jnp.int32).astype(jnp.int16)


def chunk_kernel(
    around,
    chunk_index,
    chunks,
    fraction_ref,
    normals_ref,
    planes_ref,
    flags_ref,
    courant_ref,
    next_normals_ref,
    next_planes_ref,
    next_flags_ref,
    next_courant_ref,
    last_normals_ref,
    last_planes_ref,
    last_flags_ref,
    last_courant_ref,
    ends_ref,
    axial_flux_ref,
    axial_speed_ref,
    basis_ref,
    *rest,
):
    if chunk_index:
        rest = rest[1:]
    updated_ref, sent_ref, parts, kept, source, wide, scales, turned = rest
    block, layers, cells = fraction_ref.shape
    steps = pl.num_programs(0)
    step = pl.program_id(0)
    chunk = source.shape[1] // layers
    lane_tiles = cells // 128
    backwards = lax.rem(lax.axis_index("azim"), around // 2) >= around // 4

    def put_field(slot, k, value):
        at = pl.ds(pl.multiple_of(slot * layers, layers), layers)
        for tile in range(lane_tiles):
            parts[k, tile, at, :] = value[:, tile * 128 : (tile + 1) * 128]

    def get_field(slot, k, shift=0):
        at = pl.ds(slot * layers + shift, layers)
        return jnp.concatenate([parts[k, tile, at, :] for tile in range(lane_tiles)], axis=1)

    def put_parts(slot, normals, plane, speed):
        inverse = inverse_of(*normals)
        for k, value in enumerate((*normals, plane, inverse, -inverse, 0.5 * speed)):
            put_field(slot, k, value)

    def put_packed(slot, side):
        values = [ends_ref[side, k].astype(F32) for k in range(5)]
        put_parts(slot, values[:3], values[3], values[4])

    def own_parts(row, _):
        put_parts(
            row,
            [normals_ref[k, row].astype(F32) for k in range(3)],
            plane_value(planes_ref[row], flags_ref[row]),
            courant_ref[0, row].astype(F32),
        )
        put_field(row, 7, 0.5 * courant_ref[1, row].astype(F32))
        return 0

    lax.fori_loop(0, block, own_parts, 0, unroll=2)

    def put_row(slot, normals, planes, flags, courant):
        put_parts(
            slot,
            [normals[k, 0].astype(F32) for k in range(3)],
            plane_value(planes[0], flags[0]),
            courant[0, 0].astype(F32),
        )

    def put_next():
        put_row(block, next_normals_ref, next_planes_ref, next_flags_ref, next_courant_ref)

    if chunk_index < chunks - 1:
        put_next()
    else:
        pl.when(step < steps - 1)(put_next)

        @pl.when(step == steps - 1)
        def _():
            put_packed(block, 1)

    def read_parts(slot):
        return [get_field(slot, k) for k in range(6)]

    @pl.when(step == 0)
    def _():
        if chunk_index == 0:
            put_packed(block + 1, 0)
        else:
            put_row(
                block + 1, last_normals_ref, last_planes_ref, last_flags_ref, last_courant_ref
            )
        turned[0], turned[1] = split(basis_ref[...].T)
        speed = get_field(block + 1, 6) + get_field(0, 6)
        kept[0] = upwind_flux(0, read_parts(block + 1), read_parts(0), speed)
        kept[1] = speed

    index = lax.broadcasted_iota(jnp.int32, (1, cells), 1)
    place = index.astype(F32)
    radius = 1.0 + (place + 0.5) / cells
    next_radius = 1.0 + (place + 1.5) / cells
    face_radius = 1.0 + (place + 1.0) / cells
    inverse_radius = 1.0 / radius
    inner = lax.broadcasted_iota(jnp.int32, (layers, cells), 1) < cells - 1
    layer = lax.broadcasted_iota(jnp.int32, (layers, cells), 0)
    last_layer = layer == layers - 1
    first_layer = layer == 0

    def one_row(row, _):
        own = read_parts(row)
        speed = get_field(row, 6) + get_field(row + 1, 6)
        flux = upwind_flux(0, own, read_parts(row + 1), speed)
        gained = flux - kept[0]
        divergence = speed - kept[1]
        kept[0] = flux
        kept[1] = speed

        above = [None if k == 4 else get_field(row, k, 1) for k in range(6)]
        speed = get_field(row, 7) + get_field(row, 7, 1)
        flux = upwind_flux(1, own, above, speed)
        flux = jnp.where(last_layer, axial_flux_ref[1, pl.ds(row, 1), :], flux)
        speed = jnp.where(last_layer, axial_speed_ref[1, pl.ds(row, 1), :], speed)
        gained = gained + (
            flux - jnp.where(first_layer, axial_flux_ref[0, pl.ds(row, 1), :], pltpu.roll(flux, 1, 0))
        )
        divergence = divergence + (
            speed - jnp.where(first_layer, axial_speed_ref[0, pl.ds(row, 1), :], pltpu.roll(speed, 1, 0))
        )

        half = 0.5 * courant_ref[2, row].astype(F32)
        outer = [None if k == 4 else pltpu.roll(field, cells - 1, 1) for k, field in enumerate(own)]
        speed = jnp.where(inner, half + pltpu.roll(half, cells - 1, 1), 0.0)
        flux = upwind_flux(2, own, outer, speed, radius, next_radius)
        gained = gained + (flux - pltpu.roll(flux, 1, 1)) * inverse_radius
        carried = face_radius * speed
        divergence = divergence + (carried - pltpu.roll(carried, 1, 1)) * inverse_radius
        updated = fraction_ref[row] - gained
        updated_ref[row] = updated
        result = divergence + BUOYANCY * updated
        at = step * block + row
        at = jnp.where(backwards, chunk - 1 - at, at)
        for tile in range(lane_tiles):
            source[tile, pl.ds(at, layers, stride=chunk), :] = result[
                :, tile * 128 : (tile + 1) * 128
            ]
        return 0

    lax.fori_loop(0, block, one_row, 0, unroll=2)

    @pl.when(step == steps - 1)
    def _():
        modes = basis_ref.shape[1]
        scales[...] = jnp.zeros_like(scales)

        def radial(z, _):
            at = pl.ds(pl.multiple_of(z * 2 * chunk, 2 * chunk), 2 * chunk)
            rows = jnp.concatenate([source[tile, at, :] for tile in range(lane_tiles)], axis=1)
            both = dot3((turned[0], turned[1]), split(rows), ((1,), (1,)))
            for half in range(2):
                got = both[:, half * chunk : (half + 1) * chunk]
                scales[...] = jnp.maximum(scales[...], jnp.abs(got))
                wide[pl.ds(z * 2 + half, modes, stride=layers), :] = got
            return 0

        lax.fori_loop(0, layers // 2, radial, 0)
        devices, slots, height, lanes = sent_ref.shape
        share = modes // devices
        most = scales[...].reshape(devices, share // height, height, lanes)
        exponent = exponent_of(jnp.max(most, axis=1))
        sent_ref[:, slots - 1] = exponent.astype(jnp.int32).astype(jnp.int16)
        factor = CODE_TOP / jnp.exp2(exponent * (1.0 / 256.0))
        scales[pl.ds(0, devices * height), :] = factor.reshape(devices * height, lanes)

        def coding(device, _):
            for mode in range(share):
                factor = scales[pl.ds(device * height + mode % height, 1), :]
                for part in range(layers // height):
                    at = (device * share + mode) * layers + part * height
                    values = wide[pl.ds(pl.multiple_of(at, height), height), :]
                    sent_ref[device, mode * (layers // height) + part] = to_codes(values * factor)
            return 0

        lax.fori_loop(0, devices, coding, 0)


def advect_chunk(arrays, ends, axial_flux, axial_speed, basis, chunk_index, chunk, around, devices, base):
    fraction, normals, planes, flags, courant = arrays
    rows, layers, cells = fraction.shape
    block = BLOCK
    steps = chunk // block
    first = chunk_index * steps
    share = cells // devices

    def here(i):
        return first + i

    def after(i):
        return jnp.minimum((first + i + 1) * block, rows - 1)

    whole = pl.BlockSpec((block, layers, cells), lambda i: (here(i), 0, 0))
    triple = pl.BlockSpec((3, block, layers, cells), lambda i: (0, here(i), 0, 0))
    row = pl.BlockSpec((1, layers, cells), lambda i: (after(i), 0, 0))
    before = max(first * block - 1, 0)
    last_row = pl.BlockSpec((1, layers, cells), lambda i: (before, 0, 0))
    edge = pl.BlockSpec((2, block, cells), lambda i: (0, here(i), 0))
    in_specs = [
        whole,
        triple,
        whole,
        whole,
        triple,
        pl.BlockSpec((3, 1, layers, cells), lambda i: (0, after(i), 0, 0)),
        row,
        row,
        pl.BlockSpec((1, 1, layers, cells), lambda i: (0, after(i), 0, 0)),
        pl.BlockSpec((3, 1, layers, cells), lambda i: (0, before, 0, 0)),
        last_row,
        last_row,
        pl.BlockSpec((1, 1, layers, cells), lambda i: (0, before, 0, 0)),
        pl.BlockSpec(ends.shape, lambda i: (0, 0, 0, 0)),
        edge,
        edge,
        pl.BlockSpec((cells, cells), lambda i: (0, 0), pipeline_mode=pl.Buffered(1)),
    ]
    operands = [
        fraction, normals, planes, flags, courant,
        normals, planes, flags, courant,
        normals, planes, flags, courant,
        ends, axial_flux, axial_speed, basis,
    ]
    aliases = {}
    if base is not None:
        in_specs.append(pl.BlockSpec(memory_space=pl.ANY))
        operands.append(base)
        aliases = {len(operands) - 1: 0}
    return pl.pallas_call(
        functools.partial(chunk_kernel, around, chunk_index, rows // chunk),
        grid=(steps,),
        in_specs=in_specs,
        out_specs=[
            whole,
            pl.BlockSpec((devices, 2 * share + 1, layers // 2, chunk), lambda i: (0, 0, 0, 0)),
        ],
        out_shape=[
            jax.ShapeDtypeStruct(fraction.shape, F32),
            jax.ShapeDtypeStruct((devices, 2 * share + 1, layers // 2, chunk), jnp.int16),
        ],
        scratch_shapes=[
            pltpu.VMEM((8, cells // 128, (block + 2) * layers, 128), F32),
            pltpu.VMEM((2, layers, cells), F32),
            pltpu.VMEM((cells // 128, layers * chunk, 128), F32),
            pltpu.VMEM((cells * layers, chunk), F32),
            pltpu.VMEM((cells, chunk), F32),
            pltpu.VMEM((2, cells, cells), BF16),
        ],
        input_output_aliases=aliases,
        compiler_params=pltpu.CompilerParams(vmem_limit_bytes=62 * 2**20),
        cost_estimate=pl.CostEstimate(
            flops=40000 * chunk * layers * cells, bytes_accessed=30 * chunk * layers * cells, transcendentals=0
        ),
        name="advect_chunk",
    )(*operands)


@functools.lru_cache(None)
def folded_tables(total):
    quarter = total // 4
    place = np.arange(quarter) + 0.5

    def halves(x):
        high = x.astype(jnp.bfloat16)
        return np.stack([high, (x - high.astype(np.float64)).astype(jnp.bfloat16)])

    tables, rates, weights = [], [], []
    for waves, wave in (
        (2 * np.arange(quarter), np.cos),
        (2 * np.arange(quarter) + 2, np.sin),
        (2 * np.arange(quarter) + 1, np.cos),
        (2 * np.arange(quarter) + 1, np.sin),
    ):
        doubled = waves[:, None] * (2 * np.arange(quarter) + 1)[None, :] % (2 * total)
        tables.append(wave(np.pi * doubled / total))
        rates.append(2.0 - 2.0 * np.cos(2.0 * np.pi * waves / total))
        weights.append(np.where((waves == 0) | (waves == total // 2), 1.0, 2.0) / total)
    tables = np.stack(tables)
    back = np.stack([halves(t) for t in tables])
    forth = np.stack([halves(t.T) for t in tables])
    return np.stack([forth, back]), np.stack(rates)[:, None].astype(np.float32), np.stack(weights)[:, None].astype(np.float32)


def decoded(values):
    return values.astype(jnp.int32).astype(F32)


def scale_of(codes):
    return jnp.exp2(decoded(codes) * (1.0 / 256.0)) * (1.0 / CODE_TOP)


def solve_kernel(around, along, chunks, start, *refs):
    got = refs[:chunks]
    extra = refs[chunks : 2 * chunks]
    refs = refs[2 * chunks :]
    mix, unmix, tables, rates, weights, shifts = refs[:6]
    sent, high, low, result, scale, exponents, forth, back, arrived = refs[6:]
    copies = [
        pltpu.make_async_copy(tables.at[0], forth, arrived.at[0]),
        pltpu.make_async_copy(tables.at[1], back, arrived.at[1]),
    ]
    for copy in copies:
        copy.start()
    devices, _, height, lanes = got[0].shape
    count, layers = (sent.shape[1] - 1) // (2 * chunks), 2 * height
    share = (sent.shape[1] - 1) // (2 * chunks)
    together = chunks * share // height
    pairs = around // 4
    for chunk in range(chunks):
        scale[chunk] = scale_of(extra[chunk][:, 0])
    def spots():
        for pair in range(pairs):
            for chunk in range(chunks):
                mirror = chunks - 1 - chunk
                at = pl.ds((pair * chunks + chunk) * lanes, lanes)
                yield at, (
                    (pair, chunk),
                    (pair + 2 * pairs, chunk),
                    (2 * pairs - 1 - pair, mirror),
                    (4 * pairs - 1 - pair, mirror),
                )

    def fold(index, _):
        mode, axial = index // along, index % along
        rows = pl.ds(pl.multiple_of(index * layers, layers), layers)
        row = pl.ds(lax.rem(start + mode, height), 1)
        for at, places in spots():
            u0, u1, r0, r1 = [
                jnp.concatenate(
                    [
                        decoded(got[chunk][azim * along + axial, 2 * mode + part])
                        * scale[chunk, azim * along + axial, row, :]
                        for part in range(2)
                    ]
                )
                for azim, chunk in places
            ]
            e0, o0, e1, o1 = u0 + u1, u0 - u1, r0 + r1, r0 - r1
            for k, folded in enumerate((e0 + e1, e0 - e1, o0 - o1, o0 + o1)):
                high[k, rows, at], low[k, rows, at] = split(folded)
        return 0

    lax.fori_loop(0, count * along, fold, 0)

    copies[0].wait()
    deep = mix.shape[1]
    parts = [pl.ds(at, deep) for at in range(0, high.shape[1], deep)]

    def waves(k, _):
        for at in parts:
            high[k, at], low[k, at] = split(
                dot3((mix[0], mix[1]), (high[k, at], low[k, at]))
            )
        spectrum = dot3((high[k], low[k]), (forth[k, 0], forth[k, 1]))
        high[k], low[k] = split(spectrum * weights[k] / (rates[k] + shifts[...]))
        pl.when(k == 0)(copies[1].wait)
        high[k], low[k] = split(dot3((high[k], low[k]), (back[k, 0], back[k, 1])))
        for at in parts:
            result[k, at] = dot3((unmix[0], unmix[1]), (high[k, at], low[k, at]))
        return 0

    lax.fori_loop(0, 4, waves, 0)

    apart = count // together

    def unfold(index, _):
        mode, axial = index // along, index % along
        for at, places in spots():
            found = []
            for part in range(together):
                row = ((mode + part * apart) * along + axial) * layers
                rows = pl.ds(pl.multiple_of(row, layers), layers)
                ec, es, oc, os = [result[k, rows, at] for k in range(4)]
                e0, e1, o0, o1 = ec + es, ec - es, oc + os, os - oc
                found.append((e0 + o0, e0 - o0, e1 + o1, e1 - o1))
            for (azim, chunk), values in zip(places, zip(*found)):
                device = azim * along + axial
                most = functools.reduce(jnp.maximum, [jnp.abs(x) for x in values])
                exponent = exponent_of(jnp.max(most, axis=0, keepdims=True))
                exponents[device, pl.ds(chunk * apart + mode, 1), :] = exponent
                factor = CODE_TOP / jnp.exp2(exponent * (1.0 / 256.0))
                for part, value in enumerate(values):
                    slot = 2 * (chunk * share + mode + part * apart)
                    for half in range(2):
                        piece = value[half * height : (half + 1) * height]
                        sent[device, slot + half] = to_codes(piece * factor)
        return 0

    lax.fori_loop(0, apart * along, unfold, 0)

    sent[:, 2 * chunks * share] = exponents[...].astype(jnp.int32).astype(jnp.int16)


def solve_group(got, mix, unmix, tables, shifts, start, share, around, along):
    chunks = len(got)
    devices, slots, height, lanes = got[0].shape
    rows = share * along * 2 * height
    tables, rates, weights = tables
    width = tables.shape[-1]

    def fixed(array):
        return pl.BlockSpec(
            array.shape, lambda i: (0,) * len(array.shape), pipeline_mode=pl.Buffered(1)
        )

    shifts = lax.slice_in_dim(shifts, start * along * 2 * height, start * along * 2 * height + rows)
    return pl.pallas_call(
        functools.partial(solve_kernel, around, along, chunks, start),
        grid=(1,),
        in_specs=[
            pl.BlockSpec(
                (devices, 2 * share, height, lanes),
                lambda i: (0, start // share, 0, 0),
                pipeline_mode=pl.Buffered(1),
            )
        ]
        * chunks
        + [
            pl.BlockSpec(
                (devices, 1, height, lanes),
                lambda i: (0, slots - 1, 0, 0),
                pipeline_mode=pl.Buffered(1),
            )
        ]
        * chunks
        + [fixed(mix), fixed(unmix)]
        + [pl.BlockSpec(memory_space=pl.ANY)]
        + [fixed(rates), fixed(weights), fixed(shifts)],
        out_specs=fixed(jax.ShapeDtypeStruct((devices, 2 * chunks * share + 1, height, lanes), jnp.int16)),
        out_shape=jax.ShapeDtypeStruct((devices, 2 * chunks * share + 1, height, lanes), jnp.int16),
        scratch_shapes=[
            pltpu.VMEM((4, rows, width), BF16),
            pltpu.VMEM((4, rows, width), BF16),
            pltpu.VMEM((4, rows, width), F32),
            pltpu.VMEM((chunks, devices, height, lanes), F32),
            pltpu.VMEM((devices, height, lanes), F32),
            pltpu.VMEM(tables.shape[1:], BF16),
            pltpu.VMEM(tables.shape[1:], BF16),
            pltpu.SemaphoreType.DMA((2,)),
        ],
        compiler_params=pltpu.CompilerParams(vmem_limit_bytes=SOLVE_VMEM * 2**20),
        cost_estimate=pl.CostEstimate(
            flops=60 * rows * width * width, bytes_accessed=20 * 2**20, transcendentals=0
        ),
        name="solve_group",
    )(*got, *got, mix, unmix, tables, rates, weights, shifts)


def pressure_kernel(around, groups, chunks, *refs):
    got = refs[:groups]
    basis = refs[groups]
    base = refs[groups + 1 : -4]
    out, flat, turned, scale = refs[-4:]
    devices, _, height, lanes = got[0].shape
    layers = 2 * height
    chunk = pl.program_id(0)
    backwards = lax.rem(lax.axis_index("azim"), around // 2) >= around // 4
    i = lax.broadcasted_iota(jnp.int32, (lanes, lanes), 0)
    j = lax.broadcasted_iota(jnp.int32, (lanes, lanes), 1)
    turned_place = jnp.where(backwards, lanes - 1, 0) + jnp.where(backwards, -1, 1) * i
    turn = jnp.where(j == turned_place, 1.0, 0.0).astype(BF16)
    spans, filled = [], 0
    for group in range(groups):
        share = (got[group].shape[1] - 1) // (2 * chunks)
        apart = height // chunks
        spans.append((filled, devices * share))
        scale[group] = scale_of(got[group][:, 2 * chunks * share])

        def unpack(device, _, group=group, share=share, filled=filled):
            for mode in range(share):
                factor = scale[group, device, pl.ds(chunk * apart + mode % apart, 1), :]
                for part in range(2):
                    at = (filled + device * share + mode) * layers + part * height
                    flat[pl.ds(pl.multiple_of(at, height), height), :] = (
                        decoded(got[group][device, 2 * (chunk * share + mode) + part]) * factor
                    )
            return 0

        lax.fori_loop(0, devices, unpack, 0)
        filled += devices * share

    def turning(z, _):
        for offset, height in spans:
            high, low = split(flat[pl.ds(offset * layers + z, height, stride=layers), :])
            rows = dot(turn, high, ((1,), (1,))) + dot(turn, low, ((1,), (1,)))
            for at in range(0, height, 128):
                turned[(offset + at) // 128, pl.ds(z, lanes, stride=layers), :] = rows[
                    :, at : at + 128
                ]
        return 0

    lax.fori_loop(0, layers, turning, 0, unroll=4)
    azimuths = 32
    height = azimuths * layers

    def radial(batch, _):
        at = pl.ds(pl.multiple_of(batch * height, height), height)
        rows = jnp.concatenate([turned[tile, at, :] for tile in range(filled // 128)], axis=1)
        high, low = split(rows)
        if filled > 128:
            total = dot3((high, low), (basis[0], basis[1]))
        else:
            rows = jnp.concatenate([high, low, high], axis=1)
            total = dot(rows, jnp.concatenate([basis[0], basis[0], basis[1]]), ((1,), (0,)))
        total = total.reshape(azimuths, layers, out.shape[2])
        at = pl.ds(pl.multiple_of(batch * azimuths, azimuths), azimuths)
        out[at] = total + base[0][at] if base else total
        return 0

    lax.fori_loop(0, lanes // azimuths, radial, 0)


def pressure_of(got, basis, around, chunks, base=None):
    groups = len(got)
    devices, _, height, lanes = got[0].shape
    layers = 2 * height
    inner, cells = basis.shape[1:]
    whole = pl.BlockSpec((lanes, layers, cells), lambda i: (i, 0, 0))
    return pl.pallas_call(
        functools.partial(pressure_kernel, around, groups, chunks),
        grid=(chunks,),
        in_specs=[pl.BlockSpec(memory_space=pltpu.VMEM)] * (groups + 1)
        + ([] if base is None else [whole]),
        out_specs=whole,
        out_shape=jax.ShapeDtypeStruct((lanes * chunks, layers, cells), F32),
        scratch_shapes=[
            pltpu.VMEM((inner * layers, lanes), F32),
            pltpu.VMEM((inner // 128, lanes * layers, 128), F32),
            pltpu.VMEM((groups, devices, height, lanes), F32),
        ],
        compiler_params=pltpu.CompilerParams(vmem_limit_bytes=PRESSURE_VMEM * 2**20),
        cost_estimate=pl.CostEstimate(
            flops=20 * lanes * chunks * layers * cells * inner,
            bytes_accessed=20 * 2**20,
            transcendentals=0,
        ),
        name="pressure_of",
    )(*got, basis, *([] if base is None else [base]))


def halves(values):
    high = lax.reduce_precision(values, 8, 7)
    return jnp.stack([high.astype(BF16), (values - high).astype(BF16)])


def exchanged(sent):
    return lax.all_to_all(sent, ("azim", "axial"), split_axis=0, concat_axis=0, tiled=True)


def following_kernel(values_ref, earlier_ref, out_ref):
    del values_ref, earlier_ref, out_ref


def following(values, earlier):
    anywhere = pl.BlockSpec(memory_space=pl.ANY)
    return pl.pallas_call(
        following_kernel,
        grid=(1,),
        in_specs=[
            anywhere,
            pl.BlockSpec((1, 1) + earlier.shape[2:], lambda i: (0, 0, 0, 0)),
        ],
        out_specs=anywhere,
        out_shape=jax.ShapeDtypeStruct(values.shape, values.dtype),
        input_output_aliases={0: 0},
        name="following",
    )(values, earlier)


def overlapped(
    fraction,
    normals,
    planes,
    cell_flags,
    courant,
    radial_basis,
    axial_basis,
    radial_rates,
    axial_rates,
):
    rows, layers, cells = fraction.shape
    around, along = lax.axis_size("azim"), lax.axis_size("axial")
    devices = around * along
    modes = cells // devices
    chunks = rows // CHUNK
    axial_flux, axial_speed, ends = halos(normals, planes, cell_flags, courant)
    arrays = (fraction, normals, planes, cell_flags, courant)
    updated, got = None, []
    for chunk in range(chunks):
        updated, sent = advect_chunk(
            arrays, ends, axial_flux, axial_speed, radial_basis, chunk, CHUNK, around, devices, updated
        )
        got.append(exchanged(following(sent, got[-1]) if got else sent))
    count = jnp.eye(4, dtype=F32)
    mix, unmix = halves(jnp.kron(count, axial_basis.T)), halves(jnp.kron(count, axial_basis))
    first = (lax.axis_index("azim") * along + lax.axis_index("axial")) * modes
    shifts = lax.dynamic_slice_in_dim(radial_rates, first, modes)[:, None] + axial_rates[None, :]
    shifts = shifts.reshape(modes * along * layers, 1)
    tables = [jnp.asarray(x) for x in folded_tables(rows * around)]
    returned, bases = [], []
    for start, share in SOLVED:
        sent = solve_group(got, mix, unmix, tables, shifts, start, share, around, along)
        returned.append(exchanged(sent))
        rows_of = radial_basis.T.reshape(devices, modes, cells)[:, start : start + share]
        bases.append(rows_of.reshape(devices * share, cells))
    pressure = pressure_of(returned[:-1], halves(jnp.concatenate(bases[:-1])), around, chunks)
    pressure = pressure_of(returned[-1:], halves(bases[-1]), around, chunks, pressure)
    return (updated, pressure)


def fits(fraction):
    rows, layers, cells = fraction.shape
    around, along = lax.axis_size("azim"), lax.axis_size("axial")
    modes = cells // (around * along)
    chunks = rows // CHUNK
    return (
        rows % CHUNK == 0
        and layers == 16
        and modes == 16
        and modes // 2 * chunks == layers
        and cells % 128 == 0
        and around % 4 == 0
        and along > 2
    )


def local(*arguments):
    return overlapped(*arguments) if fits(arguments[0]) else stepwise(*arguments)


def solution(mesh):
    placed = (
        P("azim", "axial", None),
        P(None, "azim", "axial", None),
        P("azim", "axial", None),
        P("azim", "axial", None),
        P(None, "azim", "axial", None),
        P(),
        P(),
        P(),
        P(),
    )
    return jax.shard_map(
        local,
        mesh=mesh,
        in_specs=placed,
        out_specs=(P("azim", "axial", None), P("azim", "axial", None)),
        check_vma=False,
    )
```

```python
import functools

import jax
import jax.numpy as jnp
import numpy as np
from jax import lax
from jax.experimental import pallas as pl
from jax.experimental.pallas import tpu as pltpu
from jax.sharding import PartitionSpec as P

HIGH = lax.Precision.HIGH
BUOYANCY = 0.5
CODE_TOP = 32700.0


def shifted_in(edge, axis, towards_lower):
    count = lax.axis_size(axis)
    if towards_lower:
        pairs = [((i + 1) % count, i) for i in range(count)]
    else:
        pairs = [(i, (i + 1) % count) for i in range(count)]
    return lax.ppermute(edge, axis, pairs)


def cell_parts(n0, n1, n2, code):
    m0, m1, m2 = jnp.abs(n0), jnp.abs(n1), jnp.abs(n2)
    return (n0, n1, n2, code, 1.0 / (6.0 * m0 * m1 * m2))


def cube(height):
    held = jnp.maximum(height, 0.0)
    return held * held * held


def face_flux(direction, lower, upper, speed, lower_weight=None, upper_weight=None):
    forward = speed > 0.0
    signed = jnp.where(forward, lower[direction], -upper[direction])
    first, second = [d for d in range(3) if d != direction]
    along = jnp.abs(signed)
    side_a = jnp.abs(jnp.where(forward, lower[first], upper[first]))
    side_b = jnp.abs(jnp.where(forward, lower[second], upper[second]))
    code = jnp.where(forward, lower[3], upper[3])
    inverse = jnp.where(forward, lower[4], upper[4])
    width = jnp.abs(speed)
    near = code - along * jnp.where(signed < 0.0, 0.0, 1.0 - width)
    far = near - along * width
    sides = side_a + side_b
    total = (cube(near) - cube(near - side_a)) - (cube(near - side_b) - cube(near - sides))
    total = total - ((cube(far) - cube(far - side_a)) - (cube(far - side_b) - cube(far - sides)))
    volume = jnp.where(code > 3.0, width, jnp.where(code < -0.5, 0.0, total * inverse))
    if lower_weight is not None:
        volume = volume * jnp.where(forward, lower_weight, upper_weight)
    return jnp.where(forward, volume, jnp.where(speed < 0.0, -volume, 0.0))


def advect_kernel(
    fraction_ref,
    normals_ref,
    planes_ref,
    flags_ref,
    courant_ref,
    next_ref,
    high_ref,
    low_azim_ref,
    low_axial_ref,
    updated_ref,
    source_ref,
    kept,
):
    rows, layers, cells = fraction_ref.shape
    f32 = jnp.float32

    @pl.when(pl.program_id(0) == 0)
    def _():
        kept[...] = low_azim_ref[...]

    index = lax.broadcasted_iota(jnp.int32, (1, cells), 1)
    place = index.astype(f32)
    radius = 1.0 + (place + 0.5) / cells
    next_radius = 1.0 + (place + 1.5) / cells
    face_radius = 1.0 + (place + 1.0) / cells
    inverse_radius = 1.0 / radius
    inner = lax.broadcasted_iota(jnp.int32, (layers, cells), 1) < cells - 1
    layer = lax.broadcasted_iota(jnp.int32, (layers, cells), 0)
    last_layer = layer == layers - 1
    first_layer = layer == 0

    def row_parts(row):
        flags = flags_ref[row]
        code = jnp.where(
            flags == 2, planes_ref[row].astype(f32), jnp.where(flags == 1, 4.0, -1.0)
        )
        return cell_parts(
            normals_ref[0, row].astype(f32),
            normals_ref[1, row].astype(f32),
            normals_ref[2, row].astype(f32),
            code,
        )

    def one_row(row, upper, upper_speed):
        own = row_parts(row)
        moved = [courant_ref[d, row].astype(f32) for d in range(3)]
        speed = 0.5 * (moved[0] + upper_speed)
        flux = face_flux(0, own, upper, speed)
        gained = flux - kept[0]
        divergence = speed - kept[1]
        kept[0] = flux
        kept[1] = speed
        beyond = cell_parts(*[high_ref[k, row] for k in range(4)])
        above = [
            jnp.where(last_layer, high, pltpu.roll(field, layers - 1, 0))
            for field, high in zip(own, beyond)
        ]
        speed = 0.5 * (
            moved[1]
            + jnp.where(last_layer, high_ref[4, row], pltpu.roll(moved[1], layers - 1, 0))
        )
        flux = face_flux(1, own, above, speed)
        gained = gained + (
            flux - jnp.where(first_layer, low_axial_ref[0, row], pltpu.roll(flux, 1, 0))
        )
        divergence = divergence + (
            speed - jnp.where(first_layer, low_axial_ref[1, row], pltpu.roll(speed, 1, 0))
        )
        outer = [pltpu.roll(field, cells - 1, 1) for field in own]
        speed = 0.5 * (moved[2] + pltpu.roll(moved[2], cells - 1, 1))
        speed = jnp.where(inner, speed, 0.0)
        flux = face_flux(2, own, outer, speed, radius, next_radius)
        gained = gained + (flux - pltpu.roll(flux, 1, 1)) * inverse_radius
        carried = face_radius * speed
        divergence = divergence + (carried - pltpu.roll(carried, 1, 1)) * inverse_radius
        updated = fraction_ref[row] - gained
        updated_ref[row] = updated
        source_ref[row] = divergence + BUOYANCY * updated

    def step(row, _):
        one_row(row, row_parts(row + 1), courant_ref[0, row + 1].astype(f32))
        return 0

    lax.fori_loop(0, rows - 1, step, 0)
    one_row(
        rows - 1,
        cell_parts(*[next_ref[k, 0].astype(f32) for k in range(4)]),
        next_ref[4, 0].astype(f32),
    )


def plane_codes(planes, flags):
    return jnp.where(
        flags == 2, planes.astype(jnp.float32), jnp.where(flags == 1, 4.0, -1.0)
    ).astype(jnp.bfloat16)


def packed_edge(normals, planes, flags, courant, direction, pick):
    parts = [pick(normals[d]) for d in range(3)]
    parts.append(plane_codes(pick(planes), pick(flags)))
    parts.append(pick(courant[direction]))
    return jnp.stack(parts)


def low_face(direction, lower, upper):
    lower, upper = lower.astype(jnp.float32), upper.astype(jnp.float32)
    speed = 0.5 * (lower[4] + upper[4])
    flux = face_flux(direction, cell_parts(*lower[:4]), cell_parts(*upper[:4]), speed)
    return jnp.stack([flux, speed])


def advect(fraction, normals, planes, flags, courant):
    rows, layers, cells = fraction.shape
    block = 16 if rows % 16 == 0 else 1
    blocks = rows // block
    fields = (normals, planes, flags, courant)
    top_row = packed_edge(*fields, 0, lambda x: x[rows - 1])
    bottom_row = packed_edge(*fields, 0, lambda x: x[0])
    top_layer = packed_edge(*fields, 1, lambda x: x[:, layers - 1])
    bottom_layer = packed_edge(*fields, 1, lambda x: x[:, 0])
    high_row = shifted_in(bottom_row, "azim", True)
    low_row = shifted_in(top_row, "azim", False)
    high_layer = shifted_in(bottom_layer, "axial", True)
    low_layer = shifted_in(top_layer, "axial", False)
    low_azim = low_face(0, low_row, bottom_row)
    low_axial = low_face(1, low_layer, bottom_layer)[:, :, None]
    high_axial = high_layer.astype(jnp.float32)[:, :, None]
    inside = packed_edge(*fields, 0, lambda x: x[block::block])
    following = jnp.concatenate([inside, high_row[:, None]], axis=1)
    whole = pl.BlockSpec((block, layers, cells), lambda i: (i, 0, 0))
    triple = pl.BlockSpec((3, block, layers, cells), lambda i: (0, i, 0, 0))
    return pl.pallas_call(
        advect_kernel,
        grid=(blocks,),
        in_specs=[
            whole,
            triple,
            whole,
            whole,
            triple,
            pl.BlockSpec((5, 1, layers, cells), lambda i: (0, i, 0, 0)),
            pl.BlockSpec((5, block, 1, cells), lambda i: (0, i, 0, 0)),
            pl.BlockSpec((2, layers, cells), lambda i: (0, 0, 0)),
            pl.BlockSpec((2, block, 1, cells), lambda i: (0, i, 0, 0)),
        ],
        out_specs=[whole, whole],
        out_shape=[jax.ShapeDtypeStruct(fraction.shape, jnp.float32)] * 2,
        scratch_shapes=[pltpu.VMEM((2, layers, cells), jnp.float32)],
        compiler_params=pltpu.CompilerParams(vmem_limit_bytes=40 * 2**20),
    )(
        fraction,
        normals,
        planes,
        flags,
        courant,
        following,
        high_axial,
        low_azim,
        low_axial,
    )


def coded(values):
    most = jnp.max(jnp.abs(values), axis=-1)
    exponent = jnp.clip(jnp.ceil(jnp.log2(most) * 256.0) + 1.0, -30000.0, 30000.0)
    scale = CODE_TOP * jnp.exp2(exponent * (-1.0 / 256.0))
    codes = jnp.round(values * scale[..., None])
    return jnp.clip(codes, -32767.0, 32767.0).astype(jnp.int16), exponent.astype(jnp.int16)


def exchange(values):
    modes, cells = values.shape[1], values.shape[3]
    codes, exponent = coded(values)
    extra = jnp.pad(exponent.transpose(0, 2, 1), ((0, 0), (0, 0), (0, cells - modes)))
    sent = jnp.concatenate([codes, extra[:, None]], axis=1)
    got = lax.all_to_all(sent, ("azim", "axial"), split_axis=0, concat_axis=0, tiled=True)
    exponent = got[:, modes, :, :modes].transpose(0, 2, 1).astype(jnp.float32)
    scale = jnp.exp2(exponent * (1.0 / 256.0)) * (1.0 / CODE_TOP)
    return got[:, :modes].astype(jnp.float32) * scale[..., None]


@functools.lru_cache(None)
def azimuth_tables(total):
    half, quarter = total // 2, total // 4
    place = np.arange(half)

    def table(cosines, sines):
        waves = np.concatenate([cosines, sines])
        angles = 2.0 * np.pi / total * (waves[:, None] * place[None, :] % total)
        rows = np.concatenate(
            [np.cos(angles[: len(cosines)]), np.sin(angles[len(cosines) :])]
        ).astype(np.float32)
        rates = (2.0 - 2.0 * np.cos(2.0 * np.pi * waves / total)).astype(np.float32)
        ends = (waves == 0) | (waves == half)
        return rows, rates, (np.where(ends, 1.0, 2.0) / total).astype(np.float32)

    even = 2 * np.arange(quarter + 1)
    odd = 2 * np.arange(quarter) + 1
    return table(even, even[1:-1]), table(odd, odd)


def stepwise(
    fraction,
    normals,
    planes,
    cell_flags,
    courant,
    radial_basis,
    axial_basis,
    radial_rates,
    axial_rates,
):
    rows, layers, cells = fraction.shape
    around, along = lax.axis_size("azim"), lax.axis_size("axial")
    devices = around * along
    modes = cells // devices
    total = rows * around
    half = total // 2
    updated, source = advect(fraction, normals, planes, cell_flags, courant)
    radial_modes = jnp.einsum("azr,rj->jza", source, radial_basis, precision=HIGH)
    got = exchange(radial_modes.reshape(devices, modes, layers, rows))
    got = got.reshape(around, along, modes, layers, rows).transpose(2, 1, 3, 0, 4)
    got = got.reshape(modes, along * layers, total)
    both = jnp.einsum("jza,zn->jna", got, axial_basis, precision=HIGH)
    first = (lax.axis_index("azim") * along + lax.axis_index("axial")) * modes
    shifts = lax.dynamic_slice_in_dim(radial_rates, first, modes)[:, None] + axial_rates[None, :]
    low, high = both[..., :half], both[..., half:]
    solved = []
    for folded, (table, rates, weight) in zip((low + high, low - high), azimuth_tables(total)):
        coefficients = jnp.einsum("jna,ka->jnk", folded, table, precision=HIGH)
        scaled = coefficients / (rates + shifts[..., None]) * weight
        solved.append(jnp.einsum("jnk,ka->jna", scaled, table, precision=HIGH))
    physical = jnp.concatenate([solved[0] + solved[1], solved[0] - solved[1]], axis=-1)
    physical = jnp.einsum("jna,zn->jza", physical, axial_basis, precision=HIGH)
    physical = physical.reshape(modes, along, layers, around, rows).transpose(3, 1, 0, 2, 4)
    returned = exchange(physical.reshape(devices, modes, layers, rows))
    returned = returned.reshape(cells, layers, rows)
    pressure = jnp.einsum("jza,rj->azr", returned, radial_basis, precision=HIGH)
    return (updated, pressure)


CHUNK = 128
BLOCK = 16
SOLVE_VMEM = 62
PRESSURE_VMEM = 62
SOLVED = ((0, 4), (8, 8), (4, 4))
FLUX_SCALE = 32767.0 / 0.3
F32 = jnp.float32
BF16 = jnp.bfloat16


def split(values):
    high = values.astype(BF16)
    return high, (values - high.astype(F32)).astype(BF16)


def dot(a, b, contract):
    return lax.dot_general(a, b, (contract, ((), ())), preferred_element_type=F32)


def dot3(a, b, contract=((1,), (0,))):
    return dot(a[0], b[0], contract) + (dot(a[0], b[1], contract) + dot(a[1], b[0], contract))


def slab_flux(normal, side_a, side_b, plane, inverse, speed):
    along = jnp.abs(normal)
    reach = normal * speed
    slab = jnp.abs(reach)
    near = plane - jnp.where(reach > 0.0, along - slab, 0.0)
    other = (slab + (side_a + side_b)) - near
    folded = near > other
    held = jnp.maximum(jnp.minimum(near, other), 0.0)
    low, high = jnp.minimum(side_a, side_b), jnp.maximum(side_a, side_b)
    by_low = jnp.maximum(held - low, 0.0)
    by_slab = jnp.maximum(held - slab, 0.0)
    last = jnp.maximum(held - (low + slab), 0.0) - jnp.maximum(held - high, 0.0)
    total = held * held * held - by_slab * by_slab * by_slab
    total = total - (by_low * by_low * by_low - last * last * last)
    flux = total * inverse
    return jnp.where(folded, speed - flux, flux)


def upwind_flux(direction, lower, upper, speed, lower_weight=None, upper_weight=None):
    forward = speed > 0.0
    first, second = [d for d in range(3) if d != direction]
    normal = jnp.where(forward, lower[direction], upper[direction])
    side_a = jnp.abs(jnp.where(forward, lower[first], upper[first]))
    side_b = jnp.abs(jnp.where(forward, lower[second], upper[second]))
    plane = jnp.where(forward, lower[3], upper[3])
    inverse = jnp.where(forward, lower[4], upper[5])
    flux = slab_flux(normal, side_a, side_b, plane, inverse, speed)
    if lower_weight is not None:
        flux = flux * jnp.where(forward, lower_weight, upper_weight)
    return flux


def inverse_of(n0, n1, n2):
    return 1.0 / (6.0 * jnp.abs(n0 * n1 * n2))


def plane_value(planes, flags):
    return jnp.where(flags == 2, planes.astype(F32), jnp.where(flags == 1, 4.0, -4.0))


def halo_kernel(
    courant_ref,
    normals_ref,
    planes_ref,
    flags_ref,
    first_normals_ref,
    first_planes_ref,
    first_flags_ref,
    first_courant_ref,
    last_normals_ref,
    last_planes_ref,
    last_flags_ref,
    last_courant_ref,
    flux_ref,
    speed_ref,
    ends_ref,
    work,
    edge,
    edge_in,
    fields,
    code,
    code_in,
    packs,
    packs_in,
    row_send,
    row_recv,
    edge_send,
    edge_recv,
    code_send,
    code_recv,
):
    step = pl.program_id(0)
    half = pl.num_programs(0) // 2
    span, layers, cells = planes_ref.shape
    groups, group = code.shape[1:3]
    per_group = group // span
    tiles = cells // 128
    neighbours = []
    for axis in ("azim", "axial"):
        count, me = lax.axis_size(axis), lax.axis_index(axis)
        neighbours.append(
            ({axis: lax.rem(me + count - 1, count)}, {axis: lax.rem(me + 1, count)})
        )

    def remote(source, target, send, recv, device):
        return pltpu.make_async_remote_copy(
            src_ref=source,
            dst_ref=target,
            send_sem=send,
            recv_sem=recv,
            device_id=device,
            device_id_type=pl.DeviceIdType.MESH,
        )

    row_copies = [
        remote(packs.at[s], packs_in.at[1 - s], row_send.at[s], row_recv.at[1 - s], neighbours[0][s])
        for s in range(2)
    ]
    def edge_copy(s, g):
        return remote(
            edge.at[s, g],
            edge_in.at[1 - s, g],
            edge_send.at[s, g],
            edge_recv.at[1 - s, g],
            neighbours[1][s],
        )

    def code_copy(s, g):
        return remote(
            code.at[s, g],
            code_in.at[1 - s, g],
            code_send.at[s, g],
            code_recv.at[1 - s, g],
            neighbours[1][s],
        )

    @pl.when(step == 0)
    def _():
        barrier = pltpu.get_barrier_semaphore()
        for pair in neighbours:
            for device in pair:
                pl.semaphore_signal(
                    barrier, inc=1, device_id=device, device_id_type=pl.DeviceIdType.MESH
                )
        pl.semaphore_wait(barrier, 4)
        for s, (normals, planes, flags, courant) in enumerate(
            (
                (first_normals_ref, first_planes_ref, first_flags_ref, first_courant_ref),
                (last_normals_ref, last_planes_ref, last_flags_ref, last_courant_ref),
            )
        ):
            for k in range(3):
                packs[s, k] = normals[k, 0]
            packs[s, 3] = plane_value(planes[0], flags[0]).astype(BF16)
            packs[s, 4] = courant[0, 0]
        for copy in row_copies:
            copy.start()

    def layer_rows(tile, layer):
        return work[tile, pl.ds(layer, span, stride=layers), :]

    @pl.when(step < half)
    def _():
        place = step // per_group
        at = pl.ds(pl.multiple_of(lax.rem(step, per_group) * span, span), span)
        for tile in range(tiles):
            lanes = pl.ds(tile * 128, 128)
            work[tile] = courant_ref[0, :, :, lanes].astype(F32).reshape(span * layers, 128)
            for s, layer in ((0, 0), (1, layers - 1)):
                edge[s, place, at, lanes] = layer_rows(tile, layer).astype(BF16)

    for g in range(groups):

        @pl.when(step == (g + 1) * per_group - 1)
        def _(g=g):
            for s in range(2):
                edge_copy(s, g).start()

    @pl.when(step >= half)
    def _():
        at = pl.ds(pl.multiple_of((step - half) * span, span), span)
        for k in range(4):
            for tile in range(tiles):
                lanes = pl.ds(tile * 128, 128)
                if k < 3:
                    field = normals_ref[k, :, :, lanes].astype(F32)
                else:
                    field = plane_value(planes_ref[:, :, lanes], flags_ref[:, :, lanes])
                work[tile] = field.reshape(span * layers, 128)
                for s, layer in ((0, 0), (1, layers - 1)):
                    fields[s, k, at, lanes] = layer_rows(tile, layer)

    for g in range(groups):

        @pl.when(step == half + (g + 1) * per_group - 1)
        def _(g=g):
            for s in range(2):
                edge_copy(s, g).wait()
            for s in range(2):

                def donate(piece, _, s=s):
                    inside = pl.ds(pl.multiple_of(piece * 16, 16), 16)
                    at = pl.ds(pl.multiple_of(g * group + piece * 16, 16), 16)
                    normals = [fields[s, k, at, :] for k in range(3)]
                    own, beyond = edge[s, g, inside, :], edge_in[s, g, inside, :]
                    speed = 0.5 * (own.astype(F32) + beyond.astype(F32))
                    inverse = inverse_of(*normals)
                    flux = slab_flux(
                        normals[1],
                        jnp.abs(normals[0]),
                        jnp.abs(normals[2]),
                        fields[s, 3, at, :],
                        inverse if s == 1 else -inverse,
                        speed,
                    )
                    flux = jnp.where(speed > 0.0 if s == 1 else speed < 0.0, flux, 0.0)
                    flux_ref[s, at, :] = flux
                    speed_ref[s, at, :] = speed
                    code[s, g, inside, :] = to_codes(flux * FLUX_SCALE)
                    return 0

                lax.fori_loop(0, group // 16, donate, 0)
                code_copy(s, g).start()

    @pl.when(step == 2 * half - 1)
    def _():
        for copy in row_copies:
            copy.wait()
        ends_ref[...] = packs_in[...]
        for g in range(groups):
            for s in range(2):
                code_copy(s, g).wait()
            for s in range(2):
                at = pl.ds(g * group, group)
                received = code_in[s, g].astype(jnp.int32).astype(F32)
                flux_ref[s, at, :] += received * (1.0 / FLUX_SCALE)


def halos(normals, planes, flags, courant):
    rows, layers, cells = planes.shape
    span, groups = 32, 4
    half = rows // span

    def later(i):
        return jnp.maximum(i - half, 0)

    whole = pl.BlockSpec((span, layers, cells), lambda i: (later(i), 0, 0))
    in_specs = [
        pl.BlockSpec((1, span, layers, cells), lambda i: (1, jnp.minimum(i, half - 1), 0, 0)),
        pl.BlockSpec((3, span, layers, cells), lambda i: (0, later(i), 0, 0)),
        whole,
        whole,
    ]
    for row in (0, rows - 1):
        one = pl.BlockSpec((1, layers, cells), lambda i, row=row: (row, 0, 0))
        in_specs += [
            pl.BlockSpec((3, 1, layers, cells), lambda i, row=row: (0, row, 0, 0)),
            one,
            one,
            pl.BlockSpec((1, 1, layers, cells), lambda i, row=row: (0, row, 0, 0)),
        ]
    pair = pl.BlockSpec((2, rows, cells), lambda i: (0, 0, 0))
    ends = (2, 5, layers, cells)
    split_shape = (2, groups, rows // groups, cells)
    dma = pltpu.SemaphoreType.DMA
    return pl.pallas_call(
        halo_kernel,
        grid=(2 * half,),
        in_specs=in_specs,
        out_specs=[pair, pair, pl.BlockSpec(ends, lambda i: (0, 0, 0, 0))],
        out_shape=[
            jax.ShapeDtypeStruct((2, rows, cells), F32),
            jax.ShapeDtypeStruct((2, rows, cells), F32),
            jax.ShapeDtypeStruct(ends, BF16),
        ],
        scratch_shapes=[
            pltpu.VMEM((cells // 128, span * layers, 128), F32),
            pltpu.VMEM(split_shape, BF16),
            pltpu.VMEM(split_shape, BF16),
            pltpu.VMEM((2, 4, rows, cells), F32),
            pltpu.VMEM(split_shape, jnp.int16),
            pltpu.VMEM(split_shape, jnp.int16),
            pltpu.VMEM(ends, BF16),
            pltpu.VMEM(ends, BF16),
            dma((2,)),
            dma((2,)),
            dma((2, groups)),
            dma((2, groups)),
            dma((2, groups)),
            dma((2, groups)),
        ],
        compiler_params=pltpu.CompilerParams(
            collective_id=0, has_side_effects=True, vmem_limit_bytes=62 * 2**20
        ),
        name="halos",
    )(courant, normals, planes, flags, *(normals, planes, flags, courant) * 2)


def exponent_of(most):
    return jnp.clip(jnp.ceil(jnp.log2(jnp.maximum(most, 1e-29)) * 256.0) + 1.0, -25000.0, 30000.0)


def to_codes(values):
    return jnp.round(values).astype(jnp.int32).astype(jnp.int16)


def chunk_kernel(
    around,
    chunk_index,
    chunks,
    fraction_ref,
    normals_ref,
    planes_ref,
    flags_ref,
    courant_ref,
    next_normals_ref,
    next_planes_ref,
    next_flags_ref,
    next_courant_ref,
    last_normals_ref,
    last_planes_ref,
    last_flags_ref,
    last_courant_ref,
    ends_ref,
    axial_flux_ref,
    axial_speed_ref,
    basis_ref,
    *rest,
):
    if chunk_index:
        rest = rest[1:]
    updated_ref, sent_ref, parts, kept, source, wide, scales, turned = rest
    block, layers, cells = fraction_ref.shape
    steps = pl.num_programs(0)
    step = pl.program_id(0)
    chunk = source.shape[1] // layers
    lane_tiles = cells // 128
    backwards = lax.rem(lax.axis_index("azim"), around // 2) >= around // 4

    def put_field(slot, k, value):
        at = pl.ds(pl.multiple_of(slot * layers, layers), layers)
        for tile in range(lane_tiles):
            parts[k, tile, at, :] = value[:, tile * 128 : (tile + 1) * 128]

    def get_field(slot, k, shift=0):
        at = pl.ds(slot * layers + shift, layers)
        return jnp.concatenate([parts[k, tile, at, :] for tile in range(lane_tiles)], axis=1)

    def put_parts(slot, normals, plane, speed):
        inverse = inverse_of(*normals)
        for k, value in enumerate((*normals, plane, inverse, -inverse, 0.5 * speed)):
            put_field(slot, k, value)

    def put_packed(slot, side):
        values = [ends_ref[side, k].astype(F32) for k in range(5)]
        put_parts(slot, values[:3], values[3], values[4])

    def own_parts(row, _):
        put_parts(
            row,
            [normals_ref[k, row].astype(F32) for k in range(3)],
            plane_value(planes_ref[row], flags_ref[row]),
            courant_ref[0, row].astype(F32),
        )
        put_field(row, 7, 0.5 * courant_ref[1, row].astype(F32))
        return 0

    lax.fori_loop(0, block, own_parts, 0, unroll=2)

    def put_row(slot, normals, planes, flags, courant):
        put_parts(
            slot,
            [normals[k, 0].astype(F32) for k in range(3)],
            plane_value(planes[0], flags[0]),
            courant[0, 0].astype(F32),
        )

    def put_next():
        put_row(block, next_normals_ref, next_planes_ref, next_flags_ref, next_courant_ref)

    if chunk_index < chunks - 1:
        put_next()
    else:
        pl.when(step < steps - 1)(put_next)

        @pl.when(step == steps - 1)
        def _():
            put_packed(block, 1)

    def read_parts(slot):
        return [get_field(slot, k) for k in range(6)]

    @pl.when(step == 0)
    def _():
        if chunk_index == 0:
            put_packed(block + 1, 0)
        else:
            put_row(
                block + 1, last_normals_ref, last_planes_ref, last_flags_ref, last_courant_ref
            )
        turned[0], turned[1] = split(basis_ref[...].T)
        speed = get_field(block + 1, 6) + get_field(0, 6)
        kept[0] = upwind_flux(0, read_parts(block + 1), read_parts(0), speed)
        kept[1] = speed

    index = lax.broadcasted_iota(jnp.int32, (1, cells), 1)
    place = index.astype(F32)
    radius = 1.0 + (place + 0.5) / cells
    next_radius = 1.0 + (place + 1.5) / cells
    face_radius = 1.0 + (place + 1.0) / cells
    inverse_radius = 1.0 / radius
    inner = lax.broadcasted_iota(jnp.int32, (layers, cells), 1) < cells - 1
    layer = lax.broadcasted_iota(jnp.int32, (layers, cells), 0)
    last_layer = layer == layers - 1
    first_layer = layer == 0

    def one_row(row, _):
        own = read_parts(row)
        speed = get_field(row, 6) + get_field(row + 1, 6)
        flux = upwind_flux(0, own, read_parts(row + 1), speed)
        gained = flux - kept[0]
        divergence = speed - kept[1]
        kept[0] = flux
        kept[1] = speed

        above = [None if k == 4 else get_field(row, k, 1) for k in range(6)]
        speed = get_field(row, 7) + get_field(row, 7, 1)
        flux = upwind_flux(1, own, above, speed)
        flux = jnp.where(last_layer, axial_flux_ref[1, pl.ds(row, 1), :], flux)
        speed = jnp.where(last_layer, axial_speed_ref[1, pl.ds(row, 1), :], speed)
        gained = gained + (
            flux - jnp.where(first_layer, axial_flux_ref[0, pl.ds(row, 1), :], pltpu.roll(flux, 1, 0))
        )
        divergence = divergence + (
            speed - jnp.where(first_layer, axial_speed_ref[0, pl.ds(row, 1), :], pltpu.roll(speed, 1, 0))
        )

        half = 0.5 * courant_ref[2, row].astype(F32)
        outer = [None if k == 4 else pltpu.roll(field, cells - 1, 1) for k, field in enumerate(own)]
        speed = jnp.where(inner, half + pltpu.roll(half, cells - 1, 1), 0.0)
        flux = upwind_flux(2, own, outer, speed, radius, next_radius)
        gained = gained + (flux - pltpu.roll(flux, 1, 1)) * inverse_radius
        carried = face_radius * speed
        divergence = divergence + (carried - pltpu.roll(carried, 1, 1)) * inverse_radius
        updated = fraction_ref[row] - gained
        updated_ref[row] = updated
        result = divergence + BUOYANCY * updated
        at = step * block + row
        at = jnp.where(backwards, chunk - 1 - at, at)
        for tile in range(lane_tiles):
            source[tile, pl.ds(at, layers, stride=chunk), :] = result[
                :, tile * 128 : (tile + 1) * 128
            ]
        return 0

    lax.fori_loop(0, block, one_row, 0, unroll=2)

    @pl.when(step == steps - 1)
    def _():
        modes = basis_ref.shape[1]
        scales[...] = jnp.zeros_like(scales)

        def radial(z, _):
            at = pl.ds(pl.multiple_of(z * 2 * chunk, 2 * chunk), 2 * chunk)
            rows = jnp.concatenate([source[tile, at, :] for tile in range(lane_tiles)], axis=1)
            both = dot3((turned[0], turned[1]), split(rows), ((1,), (1,)))
            for half in range(2):
                got = both[:, half * chunk : (half + 1) * chunk]
                scales[...] = jnp.maximum(scales[...], jnp.abs(got))
                wide[pl.ds(z * 2 + half, modes, stride=layers), :] = got
            return 0

        lax.fori_loop(0, layers // 2, radial, 0, unroll=2)
        devices, slots, height, lanes = sent_ref.shape
        share = modes // devices
        most = scales[...].reshape(devices, share // height, height, lanes)
        exponent = exponent_of(jnp.max(most, axis=1))
        sent_ref[:, slots - 1] = exponent.astype(jnp.int32).astype(jnp.int16)
        factor = CODE_TOP / jnp.exp2(exponent * (1.0 / 256.0))
        scales[pl.ds(0, devices * height), :] = factor.reshape(devices * height, lanes)

        def coding(device, _):
            for mode in range(share):
                factor = scales[pl.ds(device * height + mode % height, 1), :]
                for part in range(layers // height):
                    at = (device * share + mode) * layers + part * height
                    values = wide[pl.ds(pl.multiple_of(at, height), height), :]
                    sent_ref[device, mode * (layers // height) + part] = to_codes(values * factor)
            return 0

        lax.fori_loop(0, devices, coding, 0)


def advect_chunk(arrays, ends, axial_flux, axial_speed, basis, chunk_index, chunk, around, devices, base):
    fraction, normals, planes, flags, courant = arrays
    rows, layers, cells = fraction.shape
    block = BLOCK
    steps = chunk // block
    first = chunk_index * steps
    share = cells // devices

    def here(i):
        return first + i

    def after(i):
        return jnp.minimum((first + i + 1) * block, rows - 1)

    whole = pl.BlockSpec((block, layers, cells), lambda i: (here(i), 0, 0))
    triple = pl.BlockSpec((3, block, layers, cells), lambda i: (0, here(i), 0, 0))
    row = pl.BlockSpec((1, layers, cells), lambda i: (after(i), 0, 0))
    before = max(first * block - 1, 0)
    last_row = pl.BlockSpec((1, layers, cells), lambda i: (before, 0, 0))
    edge = pl.BlockSpec((2, block, cells), lambda i: (0, here(i), 0))
    in_specs = [
        whole,
        triple,
        whole,
        whole,
        triple,
        pl.BlockSpec((3, 1, layers, cells), lambda i: (0, after(i), 0, 0)),
        row,
        row,
        pl.BlockSpec((1, 1, layers, cells), lambda i: (0, after(i), 0, 0)),
        pl.BlockSpec((3, 1, layers, cells), lambda i: (0, before, 0, 0)),
        last_row,
        last_row,
        pl.BlockSpec((1, 1, layers, cells), lambda i: (0, before, 0, 0)),
        pl.BlockSpec(ends.shape, lambda i: (0, 0, 0, 0)),
        edge,
        edge,
        pl.BlockSpec((cells, cells), lambda i: (0, 0), pipeline_mode=pl.Buffered(1)),
    ]
    operands = [
        fraction, normals, planes, flags, courant,
        normals, planes, flags, courant,
        normals, planes, flags, courant,
        ends, axial_flux, axial_speed, basis,
    ]
    aliases = {}
    if base is not None:
        in_specs.append(pl.BlockSpec(memory_space=pl.ANY))
        operands.append(base)
        aliases = {len(operands) - 1: 0}
    return pl.pallas_call(
        functools.partial(chunk_kernel, around, chunk_index, rows // chunk),
        grid=(steps,),
        in_specs=in_specs,
        out_specs=[
            whole,
            pl.BlockSpec((devices, 2 * share + 1, layers // 2, chunk), lambda i: (0, 0, 0, 0)),
        ],
        out_shape=[
            jax.ShapeDtypeStruct(fraction.shape, F32),
            jax.ShapeDtypeStruct((devices, 2 * share + 1, layers // 2, chunk), jnp.int16),
        ],
        scratch_shapes=[
            pltpu.VMEM((8, cells // 128, (block + 2) * layers, 128), F32),
            pltpu.VMEM((2, layers, cells), F32),
            pltpu.VMEM((cells // 128, layers * chunk, 128), F32),
            pltpu.VMEM((cells * layers, chunk), F32),
            pltpu.VMEM((cells, chunk), F32),
            pltpu.VMEM((2, cells, cells), BF16),
        ],
        input_output_aliases=aliases,
        compiler_params=pltpu.CompilerParams(vmem_limit_bytes=62 * 2**20),
        cost_estimate=pl.CostEstimate(
            flops=40000 * chunk * layers * cells, bytes_accessed=30 * chunk * layers * cells, transcendentals=0
        ),
        name="advect_chunk",
    )(*operands)


@functools.lru_cache(None)
def folded_tables(total):
    quarter = total // 4
    place = np.arange(quarter) + 0.5

    def halves(x):
        high = x.astype(jnp.bfloat16)
        return np.stack([high, (x - high.astype(np.float64)).astype(jnp.bfloat16)])

    tables, rates, weights = [], [], []
    for waves, wave in (
        (2 * np.arange(quarter), np.cos),
        (2 * np.arange(quarter) + 2, np.sin),
        (2 * np.arange(quarter) + 1, np.cos),
        (2 * np.arange(quarter) + 1, np.sin),
    ):
        doubled = waves[:, None] * (2 * np.arange(quarter) + 1)[None, :] % (2 * total)
        tables.append(wave(np.pi * doubled / total))
        rates.append(2.0 - 2.0 * np.cos(2.0 * np.pi * waves / total))
        weights.append(np.where((waves == 0) | (waves == total // 2), 1.0, 2.0) / total)
    tables = np.stack(tables)
    back = np.stack([halves(t) for t in tables])
    forth = np.stack([halves(t.T) for t in tables])
    return np.stack([forth, back]), np.stack(rates)[:, None].astype(np.float32), np.stack(weights)[:, None].astype(np.float32)


def decoded(values):
    return values.astype(jnp.int32).astype(F32)


def scale_of(codes):
    return jnp.exp2(decoded(codes) * (1.0 / 256.0)) * (1.0 / CODE_TOP)


def solve_kernel(around, along, chunks, start, *refs):
    got = refs[:chunks]
    extra = refs[chunks : 2 * chunks]
    refs = refs[2 * chunks :]
    mix, unmix, tables, rates, weights, shifts = refs[:6]
    sent, high, low, result, scale, exponents, forth, back, arrived = refs[6:]
    copies = [
        pltpu.make_async_copy(tables.at[0], forth, arrived.at[0]),
        pltpu.make_async_copy(tables.at[1], back, arrived.at[1]),
    ]
    for copy in copies:
        copy.start()
    devices, _, height, lanes = got[0].shape
    count, layers = (sent.shape[1] - 1) // (2 * chunks), 2 * height
    share = (sent.shape[1] - 1) // (2 * chunks)
    together = chunks * share // height
    pairs = around // 4
    for chunk in range(chunks):
        scale[chunk] = scale_of(extra[chunk][:, 0])
    def spots():
        for pair in range(pairs):
            for chunk in range(chunks):
                mirror = chunks - 1 - chunk
                at = pl.ds((pair * chunks + chunk) * lanes, lanes)
                yield at, (
                    (pair, chunk),
                    (pair + 2 * pairs, chunk),
                    (2 * pairs - 1 - pair, mirror),
                    (4 * pairs - 1 - pair, mirror),
                )

    def fold(index, _):
        mode, axial = index // along, index % along
        rows = pl.ds(pl.multiple_of(index * layers, layers), layers)
        row = pl.ds(lax.rem(start + mode, height), 1)
        for at, places in spots():
            u0, u1, r0, r1 = [
                jnp.concatenate(
                    [
                        decoded(got[chunk][azim * along + axial, 2 * mode + part])
                        * scale[chunk, azim * along + axial, row, :]
                        for part in range(2)
                    ]
                )
                for azim, chunk in places
            ]
            e0, o0, e1, o1 = u0 + u1, u0 - u1, r0 + r1, r0 - r1
            for k, folded in enumerate((e0 + e1, e0 - e1, o0 - o1, o0 + o1)):
                high[k, rows, at], low[k, rows, at] = split(folded)
        return 0

    lax.fori_loop(0, count * along, fold, 0)

    copies[0].wait()
    deep = mix.shape[1]
    parts = [pl.ds(at, deep) for at in range(0, high.shape[1], deep)]

    def waves(k, _):
        for at in parts:
            high[k, at], low[k, at] = split(
                dot3((mix[0], mix[1]), (high[k, at], low[k, at]))
            )
        spectrum = dot3((high[k], low[k]), (forth[k, 0], forth[k, 1]))
        high[k], low[k] = split(spectrum * weights[k] / (rates[k] + shifts[...]))
        pl.when(k == 0)(copies[1].wait)
        high[k], low[k] = split(dot3((high[k], low[k]), (back[k, 0], back[k, 1])))
        for at in parts:
            result[k, at] = dot3((unmix[0], unmix[1]), (high[k, at], low[k, at]))
        return 0

    lax.fori_loop(0, 4, waves, 0, unroll=2)

    apart = count // together

    def unfold(index, _):
        mode, axial = index // along, index % along
        for at, places in spots():
            found = []
            for part in range(together):
                row = ((mode + part * apart) * along + axial) * layers
                rows = pl.ds(pl.multiple_of(row, layers), layers)
                ec, es, oc, os = [result[k, rows, at] for k in range(4)]
                e0, e1, o0, o1 = ec + es, ec - es, oc + os, os - oc
                found.append((e0 + o0, e0 - o0, e1 + o1, e1 - o1))
            for (azim, chunk), values in zip(places, zip(*found)):
                device = azim * along + axial
                most = functools.reduce(jnp.maximum, [jnp.abs(x) for x in values])
                exponent = exponent_of(jnp.max(most, axis=0, keepdims=True))
                exponents[device, pl.ds(chunk * apart + mode, 1), :] = exponent
                factor = CODE_TOP / jnp.exp2(exponent * (1.0 / 256.0))
                for part, value in enumerate(values):
                    slot = 2 * (chunk * share + mode + part * apart)
                    for half in range(2):
                        piece = value[half * height : (half + 1) * height]
                        sent[device, slot + half] = to_codes(piece * factor)
        return 0

    lax.fori_loop(0, apart * along, unfold, 0)

    sent[:, 2 * chunks * share] = exponents[...].astype(jnp.int32).astype(jnp.int16)


def solve_group(got, mix, unmix, tables, shifts, start, share, around, along):
    chunks = len(got)
    devices, slots, height, lanes = got[0].shape
    rows = share * along * 2 * height
    tables, rates, weights = tables
    width = tables.shape[-1]

    def fixed(array):
        return pl.BlockSpec(
            array.shape, lambda i: (0,) * len(array.shape), pipeline_mode=pl.Buffered(1)
        )

    shifts = lax.slice_in_dim(shifts, start * along * 2 * height, start * along * 2 * height + rows)
    return pl.pallas_call(
        functools.partial(solve_kernel, around, along, chunks, start),
        grid=(1,),
        in_specs=[
            pl.BlockSpec(
                (devices, 2 * share, height, lanes),
                lambda i: (0, start // share, 0, 0),
                pipeline_mode=pl.Buffered(1),
            )
        ]
        * chunks
        + [
            pl.BlockSpec(
                (devices, 1, height, lanes),
                lambda i: (0, slots - 1, 0, 0),
                pipeline_mode=pl.Buffered(1),
            )
        ]
        * chunks
        + [fixed(mix), fixed(unmix)]
        + [pl.BlockSpec(memory_space=pl.ANY)]
        + [fixed(rates), fixed(weights), fixed(shifts)],
        out_specs=fixed(jax.ShapeDtypeStruct((devices, 2 * chunks * share + 1, height, lanes), jnp.int16)),
        out_shape=jax.ShapeDtypeStruct((devices, 2 * chunks * share + 1, height, lanes), jnp.int16),
        scratch_shapes=[
            pltpu.VMEM((4, rows, width), BF16),
            pltpu.VMEM((4, rows, width), BF16),
            pltpu.VMEM((4, rows, width), F32),
            pltpu.VMEM((chunks, devices, height, lanes), F32),
            pltpu.VMEM((devices, height, lanes), F32),
            pltpu.VMEM(tables.shape[1:], BF16),
            pltpu.VMEM(tables.shape[1:], BF16),
            pltpu.SemaphoreType.DMA((2,)),
        ],
        compiler_params=pltpu.CompilerParams(vmem_limit_bytes=SOLVE_VMEM * 2**20),
        cost_estimate=pl.CostEstimate(
            flops=60 * rows * width * width, bytes_accessed=20 * 2**20, transcendentals=0
        ),
        name="solve_group",
    )(*got, *got, mix, unmix, tables, rates, weights, shifts)


def pressure_kernel(around, groups, chunks, *refs):
    got = refs[:groups]
    basis = refs[groups]
    base = refs[groups + 1 : -4]
    out, flat, turned, scale = refs[-4:]
    devices, _, height, lanes = got[0].shape
    layers = 2 * height
    chunk = pl.program_id(0)
    backwards = lax.rem(lax.axis_index("azim"), around // 2) >= around // 4
    i = lax.broadcasted_iota(jnp.int32, (lanes, lanes), 0)
    j = lax.broadcasted_iota(jnp.int32, (lanes, lanes), 1)
    turned_place = jnp.where(backwards, lanes - 1, 0) + jnp.where(backwards, -1, 1) * i
    turn = jnp.where(j == turned_place, 1.0, 0.0).astype(BF16)
    spans, filled = [], 0
    for group in range(groups):
        share = (got[group].shape[1] - 1) // (2 * chunks)
        apart = height // chunks
        spans.append((filled, devices * share))
        scale[group] = scale_of(got[group][:, 2 * chunks * share])

        def unpack(device, _, group=group, share=share, filled=filled):
            for mode in range(share):
                factor = scale[group, device, pl.ds(chunk * apart + mode % apart, 1), :]
                for part in range(2):
                    at = (filled + device * share + mode) * layers + part * height
                    flat[pl.ds(pl.multiple_of(at, height), height), :] = (
                        decoded(got[group][device, 2 * (chunk * share + mode) + part]) * factor
                    )
            return 0

        lax.fori_loop(0, devices, unpack, 0)
        filled += devices * share

    def turning(z, _):
        for offset, height in spans:
            high, low = split(flat[pl.ds(offset * layers + z, height, stride=layers), :])
            rows = dot(turn, high, ((1,), (1,))) + dot(turn, low, ((1,), (1,)))
            for at in range(0, height, 128):
                turned[(offset + at) // 128, pl.ds(z, lanes, stride=layers), :] = rows[
                    :, at : at + 128
                ]
        return 0

    lax.fori_loop(0, layers, turning, 0, unroll=4)
    azimuths = 32
    height = azimuths * layers

    def radial(batch, _):
        at = pl.ds(pl.multiple_of(batch * height, height), height)
        rows = jnp.concatenate([turned[tile, at, :] for tile in range(filled // 128)], axis=1)
        high, low = split(rows)
        if filled > 128:
            total = dot3((high, low), (basis[0], basis[1]))
        else:
            rows = jnp.concatenate([high, low, high], axis=1)
            total = dot(rows, jnp.concatenate([basis[0], basis[0], basis[1]]), ((1,), (0,)))
        total = total.reshape(azimuths, layers, out.shape[2])
        at = pl.ds(pl.multiple_of(batch * azimuths, azimuths), azimuths)
        out[at] = total + base[0][at] if base else total
        return 0

    lax.fori_loop(0, lanes // azimuths, radial, 0, unroll=2)


def pressure_of(got, basis, around, chunks, base=None):
    groups = len(got)
    devices, _, height, lanes = got[0].shape
    layers = 2 * height
    inner, cells = basis.shape[1:]
    whole = pl.BlockSpec((lanes, layers, cells), lambda i: (i, 0, 0))
    return pl.pallas_call(
        functools.partial(pressure_kernel, around, groups, chunks),
        grid=(chunks,),
        in_specs=[pl.BlockSpec(memory_space=pltpu.VMEM)] * (groups + 1)
        + ([] if base is None else [whole]),
        out_specs=whole,
        out_shape=jax.ShapeDtypeStruct((lanes * chunks, layers, cells), F32),
        scratch_shapes=[
            pltpu.VMEM((inner * layers, lanes), F32),
            pltpu.VMEM((inner // 128, lanes * layers, 128), F32),
            pltpu.VMEM((groups, devices, height, lanes), F32),
        ],
        compiler_params=pltpu.CompilerParams(vmem_limit_bytes=PRESSURE_VMEM * 2**20),
        cost_estimate=pl.CostEstimate(
            flops=20 * lanes * chunks * layers * cells * inner,
            bytes_accessed=20 * 2**20,
            transcendentals=0,
        ),
        name="pressure_of",
    )(*got, basis, *([] if base is None else [base]))


def halves(values):
    high = lax.reduce_precision(values, 8, 7)
    return jnp.stack([high.astype(BF16), (values - high).astype(BF16)])


def exchanged(sent):
    return lax.all_to_all(sent, ("azim", "axial"), split_axis=0, concat_axis=0, tiled=True)


def following_kernel(values_ref, earlier_ref, out_ref):
    del values_ref, earlier_ref, out_ref


def following(values, earlier):
    anywhere = pl.BlockSpec(memory_space=pl.ANY)
    return pl.pallas_call(
        following_kernel,
        grid=(1,),
        in_specs=[
            anywhere,
            pl.BlockSpec((1, 1) + earlier.shape[2:], lambda i: (0, 0, 0, 0)),
        ],
        out_specs=anywhere,
        out_shape=jax.ShapeDtypeStruct(values.shape, values.dtype),
        input_output_aliases={0: 0},
        name="following",
    )(values, earlier)


def overlapped(
    fraction,
    normals,
    planes,
    cell_flags,
    courant,
    radial_basis,
    axial_basis,
    radial_rates,
    axial_rates,
):
    rows, layers, cells = fraction.shape
    around, along = lax.axis_size("azim"), lax.axis_size("axial")
    devices = around * along
    modes = cells // devices
    chunks = rows // CHUNK
    axial_flux, axial_speed, ends = halos(normals, planes, cell_flags, courant)
    arrays = (fraction, normals, planes, cell_flags, courant)
    updated, got = None, []
    for chunk in range(chunks):
        updated, sent = advect_chunk(
            arrays, ends, axial_flux, axial_speed, radial_basis, chunk, CHUNK, around, devices, updated
        )
        got.append(exchanged(following(sent, got[-1]) if got else sent))
    count = jnp.eye(4, dtype=F32)
    mix, unmix = halves(jnp.kron(count, axial_basis.T)), halves(jnp.kron(count, axial_basis))
    first = (lax.axis_index("azim") * along + lax.axis_index("axial")) * modes
    shifts = lax.dynamic_slice_in_dim(radial_rates, first, modes)[:, None] + axial_rates[None, :]
    shifts = shifts.reshape(modes * along * layers, 1)
    tables = [jnp.asarray(x) for x in folded_tables(rows * around)]
    returned, bases = [], []
    for start, share in SOLVED:
        sent = solve_group(got, mix, unmix, tables, shifts, start, share, around, along)
        returned.append(exchanged(sent))
        rows_of = radial_basis.T.reshape(devices, modes, cells)[:, start : start + share]
        bases.append(rows_of.reshape(devices * share, cells))
    pressure = pressure_of(returned[:-1], halves(jnp.concatenate(bases[:-1])), around, chunks)
    pressure = pressure_of(returned[-1:], halves(bases[-1]), around, chunks, pressure)
    return (updated, pressure)


def fits(fraction):
    rows, layers, cells = fraction.shape
    around, along = lax.axis_size("azim"), lax.axis_size("axial")
    modes = cells // (around * along)
    chunks = rows // CHUNK
    return (
        rows % CHUNK == 0
        and layers == 16
        and modes == 16
        and modes // 2 * chunks == layers
        and cells % 128 == 0
        and around % 4 == 0
        and along > 2
    )


def local(*arguments):
    return overlapped(*arguments) if fits(arguments[0]) else stepwise(*arguments)


def solution(mesh):
    placed = (
        P("azim", "axial", None),
        P(None, "azim", "axial", None),
        P("azim", "axial", None),
        P("azim", "axial", None),
        P(None, "azim", "axial", None),
        P(),
        P(),
        P(),
        P(),
    )
    return jax.shard_map(
        local,
        mesh=mesh,
        in_specs=placed,
        out_specs=(P("azim", "axial", None), P("azim", "axial", None)),
        check_vma=False,
    )
```
